32 devices in a mesh: leaf: 16 (over z, x, core), probe: 2 (over y).
Axes of the slice: x: 2, y: 2, z: 4, core: 2. Of those that a mesh axis runs over, the one named last changes fastest.
Arguments:
- coef_fine: bfloat16 [64, 65536], P('probe', 'leaf'), may hold values from -0.59765625 to 0.59765625
- points_fine: float32 [3, 65536], P(None, 'leaf'), may hold values from -1 to 1
- points_coarse: float32 [3, 32768], P(None, 'leaf'), may hold values from -1 to 1
- transfer: bfloat16 [64, 65536], P(None, 'leaf'), may hold values from -0.5 to 0.5
- send_fine: int32 [16, 16, 16], P('leaf'), may hold values from 0 to 63, as said below
- slots_fine: int32 [1024, 64], P('leaf'), may hold values from 0 to 319, as said below
- counts_fine: int32 [1024], P('leaf'), may hold values from 1 to 64, as said below
- send_coarse: int32 [16, 16, 8], P('leaf'), may hold values from 0 to 31, as said below
- slots_coarse: int32 [512, 64], P('leaf'), may hold values from 0 to 159, as said below
- counts_coarse: int32 [512], P('leaf'), may hold values from 1 to 64, as said below
Outputs:
- far_field: float32 [64, 65536], P('probe', 'leaf')
- probe_gram: float32 [64, 64], P('probe')
The draws below stay inside these ranges and needn't reach their ends.
Inputs may be any that keep to these rules, and one draw needn't show every extreme that they name: `send_fine`: entry [e, d, i] is the local index of a cluster of device e that device e sends to device d; every device sends exactly 16 distinct clusters to every device, itself included. `slots_fine`: A slot value v below 64 names the owning device's own cluster v; a value of 64 or more names entry [(v - 64) // 16, owner, (v - 64) % 16] of send_fine. Only the first counts_fine[c] slots of cluster c are live; every device has a cluster with all 64 slots live. `send_coarse`: entry [e, d, i] is the local index of a cluster of device e that device e sends to device d; every device sends exactly 8 distinct clusters to every device, itself included. `slots_coarse`: A slot value v below 32 names the owning device's own cluster v; a value of 32 or more names entry [(v - 32) // 8, owner, (v - 32) % 8] of send_coarse. Only the first counts_coarse[q] slots of cluster q are live; every device has a cluster with all 64 slots live.
All inputs are finite; a program needn't handle non-finite values.
Results may differ from the reference program's by a relative error of at most 0.0036.
Values may be sent and summed in bfloat16 or wider, within the bound.
No kernel may reach another device: no remote copies, remote signals or barrier semaphores. Data moves between devices by JAX's collectives and lax.ppermute only.
A program may use at most 64 MiB of HBM per device.

```python
import math
import jax
import jax.numpy as jnp
from jax import lax

K = 64
P_SIZE = 64
PAIRS = 64
CF = 64
CC = 32
CAP_F = 16
CAP_C = 8
OWNERS = 16
NF = 1024
NC = 512


def pick_lists(key, clusters, capacity):
    member_keys = jax.random.split(key, OWNERS * OWNERS)
    chosen_rows = jax.vmap(lambda member: jax.random.permutation(member, clusters)[:capacity])(member_keys)
    return chosen_rows.reshape(OWNERS, OWNERS, capacity).astype(jnp.int32)


def pick_slots(key, clusters, capacity):
    first_key, second_key, third_key = jax.random.split(key, 3)
    total = OWNERS * clusters
    chooser = jax.random.randint(first_key, (total, PAIRS), 0, 4)
    own_slot = jax.random.randint(second_key, (total, PAIRS), 0, clusters)
    remote_slot = clusters + jax.random.randint(third_key, (total, PAIRS), 0, OWNERS * capacity)
    return jnp.where(chooser == 0, own_slot, remote_slot).astype(jnp.int32)


def pick_counts(key, clusters):
    first_key, second_key, third_key = jax.random.split(key, 3)
    stride = max(1, PAIRS // 8)
    lowest = jax.random.randint(first_key, (OWNERS,), 1, 6) * stride
    drawn = jax.random.randint(second_key, (OWNERS, clusters), lowest[:, None], PAIRS + 1)
    position = jax.random.randint(third_key, (OWNERS,), 0, clusters)
    column = jnp.arange(clusters, dtype=jnp.int32)[None, :]
    filled = jnp.where(column == position[:, None], PAIRS, drawn)
    return filled.reshape(OWNERS * clusters).astype(jnp.int32)


def draw_send_fine(key, part):
    return pick_lists(jax.random.fold_in(key, 11), CF, CAP_F)


def draw_slots_fine(key, part):
    return pick_slots(jax.random.fold_in(key, 12), CF, CAP_F)


def draw_counts_fine(key, part):
    return pick_counts(jax.random.fold_in(key, 13), CF)


def draw_send_coarse(key, part):
    return pick_lists(jax.random.fold_in(key, 21), CC, CAP_C)


def draw_slots_coarse(key, part):
    return pick_slots(jax.random.fold_in(key, 22), CC, CAP_C)


def draw_counts_coarse(key, part):
    return pick_counts(jax.random.fold_in(key, 23), CC)


def block_scale(rng, shape, shards, low, largest):
    factor_of = 1.0
    for dim, parts in shards:
        draws = jax.random.uniform(jax.random.fold_in(jax.random.fold_in(rng, 6), dim), (parts,), jnp.float32, low / len(shards), largest / len(shards))
        factor_of = factor_of * jnp.repeat(jnp.exp(draws), shape[dim] // parts).reshape((-1,) + (1,) * (len(shape) - 1 - dim))
    return factor_of


def centred(stream_key, extent, deviation, most, cuts=(), kind=jnp.bfloat16):
    factor_of = block_scale(stream_key, extent, cuts, -0.22, 0.18) if cuts else 1.0
    values = jax.random.normal(stream_key, extent, jnp.float32) * deviation * factor_of
    return jnp.minimum(jnp.maximum(values, -most), most).astype(kind)


def setup_inputs(seed: int = 0) -> dict:
    seeds = jax.random.split(jax.random.key(seed), 11)
    return {
        "coef_fine": centred(seeds[0], (P_SIZE, NF * K), 0.1, 0.59765625, ((0, 2), (1, 16))),
        "points_fine": jnp.clip(jax.random.uniform(seeds[1], (3, NF * K), jnp.float32, -1.0, 1.0) * block_scale(seeds[1], (3, NF * K), ((1, 16),), -0.4, 0.0), -1.0, 1.0),
        "points_coarse": jnp.clip(jax.random.uniform(seeds[2], (3, NC * K), jnp.float32, -1.0, 1.0) * block_scale(seeds[2], (3, NC * K), ((1, 16),), -0.4, 0.0), -1.0, 1.0),
        "transfer": centred(seeds[3], (K, NF * K), (2 * K) ** -0.5, 0.5, ((1, 16),)),
        "send_fine": draw_send_fine(jax.random.fold_in(seeds[10], 71), 0),
        "slots_fine": draw_slots_fine(jax.random.fold_in(seeds[10], 71), 0),
        "counts_fine": draw_counts_fine(jax.random.fold_in(seeds[10], 71), 0),
        "send_coarse": draw_send_coarse(jax.random.fold_in(seeds[10], 71), 0),
        "slots_coarse": draw_slots_coarse(jax.random.fold_in(seeds[10], 71), 0),
        "counts_coarse": draw_counts_coarse(jax.random.fold_in(seeds[10], 71), 0),
    }


kernel_rate = 1.5

def kernel_block(target, source):
    squared = jnp.zeros((source.shape[0], target.shape[1], source.shape[2]), jnp.float32)
    for coord in range(3):
        coord_delta = target[coord][None, :, None] - source[:, coord][:, None, :]
        squared = squared + coord_delta * coord_delta
    return jnp.exp(-kernel_rate * squared)

def partner_ids(slot_row, owner_index, per_device, capacity, send_lists):
    offset = slot_row - per_device
    source = jnp.clip(offset // capacity, 0, OWNERS - 1).astype(jnp.int32)
    within = jnp.where(offset >= 0, offset % capacity, 0).astype(jnp.int32)
    remote = source * per_device + send_lists[source, owner_index, within]
    return jnp.where(slot_row < per_device, owner_index * per_device + slot_row, remote).astype(jnp.int32)

def level_sweep(coef_rows, point_rows, send_lists, slot_table, count_table, per_device, capacity):

    def one_cluster(cluster_item):
        target, slot_row, pair_count = cluster_item
        owner_index = (target // per_device).astype(jnp.int32)
        partner = partner_ids(slot_row, owner_index, per_device, capacity, send_lists)
        kernel_tile = kernel_block(point_rows[target], point_rows[partner])
        live_mask = jnp.arange(PAIRS, dtype=jnp.int32) < pair_count
        weights = jnp.where(live_mask[:, None, None], kernel_tile, 0.0).astype(jnp.bfloat16)
        return jnp.einsum('mkj,mpj->pk', weights.astype(jnp.float32), coef_rows[partner].astype(jnp.float32))
    return lax.map(one_cluster, (jnp.arange(coef_rows.shape[0], dtype=jnp.int32), slot_table, count_table))

def reference(coef_fine, points_fine, points_coarse, transfer, send_fine, slots_fine, counts_fine, send_coarse, slots_coarse, counts_coarse):
    coef_rows = coef_fine.reshape(P_SIZE, NF, K).transpose(1, 0, 2)
    fine_points = points_fine.reshape(3, NF, K).transpose(1, 0, 2)
    coarse_points = points_coarse.reshape(3, NC, K).transpose(1, 0, 2)
    matrices = transfer.reshape(K, NC, 2, K).astype(jnp.float32)
    children = coef_rows.reshape(NC, 2, P_SIZE, K).astype(jnp.float32)
    coarse_coef = jnp.einsum('qcpk,kqcj->qpj', children, matrices).astype(jnp.bfloat16)
    fine_far = level_sweep(coef_rows, fine_points, send_fine, slots_fine, counts_fine, CF, CAP_F)
    coarse_far = level_sweep(coarse_coef, coarse_points, send_coarse, slots_coarse, counts_coarse, CC, CAP_C).astype(jnp.bfloat16)
    downward = jnp.einsum('qpj,kqcj->qcpk', coarse_far.astype(jnp.float32), matrices).reshape(NF, P_SIZE, K)
    combined = fine_far + downward
    far_field = combined.transpose(1, 0, 2).reshape(P_SIZE, NF * K)
    probe_gram = jnp.dot(coef_fine.astype(jnp.float32), far_field.T, precision=lax.Precision.HIGHEST) * (1.0 / math.sqrt(NF * K))
    return (far_field, probe_gram)
```

```python
import functools
import math

import jax
import jax.numpy as jnp
from jax import lax
from jax.experimental import pallas as pl
from jax.experimental.pallas import tpu as pltpu
from jax.sharding import PartitionSpec as P

KERNEL_RATE = 1.5
POINT_SCALE = math.sqrt(2.0 * KERNEL_RATE * math.log2(math.e))
LANES = 128
TARGETS = 4
CHUNK = 8
FAR_AWAY = -30000.0
VMEM = 56 * 1024 * 1024

NT = (((1,), (1,)), ((), ()))
NN = (((1,), (0,)), ((), ()))


def bdot(a, b, dims):
    return lax.dot_general(a, b, dims, preferred_element_type=jnp.float32)


def split_rows(points):
    v = points * POINT_SCALE
    norm = -0.5 * (v[0:1] * v[0:1] + v[1:2] * v[1:2] + v[2:3] * v[2:3])
    full = jnp.concatenate([v, norm], axis=0)
    high = full.astype(jnp.bfloat16).astype(jnp.float32)
    rest = (full - high).astype(jnp.bfloat16).astype(jnp.float32)
    return jnp.concatenate([high, rest], axis=0)


def source_features(rows):
    place = lax.broadcasted_iota(jnp.int32, rows.shape, 0)
    one = jnp.where((place == 3) | (place == 7), 1.0, 0.0)
    return jnp.concatenate([rows, jnp.where(place < 3, rows, one)], axis=0)


def target_features(rows):
    place = lax.broadcasted_iota(jnp.int32, rows.shape, 0)
    turned = jnp.concatenate([rows[4:8], rows[0:4]], axis=0)
    one = jnp.where((place == 3) | (place == 7), 1.0, jnp.where(place < 3, rows, turned))
    return jnp.concatenate([one, turned], axis=0)


def halves(tile):
    lane = lax.broadcasted_iota(jnp.int32, tile.shape, 1)
    turned = pltpu.roll(tile, LANES // 2, 1)
    low = lane < LANES // 2
    return jnp.where(low, tile, turned), jnp.where(low, turned, tile)


def lane_tile(index):
    return pl.ds(pl.multiple_of(index * LANES, LANES), LANES)


def pack_send(send_ref, out_ref, dup_coef, dup_rows, owners, capacity, px):
    pairs = capacity // 2
    lane = lax.broadcasted_iota(jnp.int32, (px, LANES), 1) < LANES // 2
    lane8 = lax.broadcasted_iota(jnp.int32, (8, LANES), 1) < LANES // 2

    def one_owner(owner, carry):
        before = None
        for pair in range(pairs):
            first = send_ref[owner, 2 * pair]
            second = send_ref[owner, 2 * pair + 1]
            out_ref[owner, pair * px:(pair + 1) * px, :] = jnp.where(
                lane, dup_coef[first], dup_coef[second]
            ).astype(jnp.bfloat16)
            rows = jnp.where(lane8, dup_rows[first], dup_rows[second])
            if pair % 2 == 0:
                before = rows
            else:
                start = pairs * px + (pair - 1) * 8
                out_ref[owner, start:start + 16, :] = jnp.concatenate(
                    [before, rows], axis=0
                ).astype(jnp.bfloat16)
        return carry

    lax.fori_loop(0, owners, one_owner, 0)


def pack_fine_kernel(send_ref, coef_ref, points_ref, out_ref, rows_ref, dup_coef, dup_rows):
    owners, capacity = send_ref.shape
    px = coef_ref.shape[0]
    rows_ref[...] = split_rows(points_ref[...])

    def one_tile(index, carry):
        a, b = halves(coef_ref[:, lane_tile(index)].astype(jnp.float32))
        dup_coef[2 * index] = a
        dup_coef[2 * index + 1] = b
        a, b = halves(rows_ref[:, lane_tile(index)])
        dup_rows[2 * index] = a
        dup_rows[2 * index + 1] = b
        return carry

    lax.fori_loop(0, coef_ref.shape[1] // LANES, one_tile, 0, unroll=4)
    pack_send(send_ref, out_ref, dup_coef, dup_rows, owners, capacity, px)


def pack_coarse_kernel(
    send_ref, coef_ref, transfer_ref, points_ref, out_ref, rows_ref, coarse_ref, dup_coef, dup_rows
):
    owners, capacity = send_ref.shape
    px = coef_ref.shape[0]
    rows_ref[...] = split_rows(points_ref[...])

    def one_tile(index, carry):
        doubled = []
        for part in range(2):
            q = 2 * index + part
            a, b = halves(transfer_ref[:, lane_tile(q)].astype(jnp.float32))
            matrix = jnp.concatenate([a, b], axis=0).astype(jnp.bfloat16)
            block = bdot(coef_ref[:, lane_tile(q)], matrix, NN)
            dup_coef[q] = block
            doubled.append(block)
        lane = lax.broadcasted_iota(jnp.int32, (px, LANES), 1) < LANES // 2
        coarse_ref[:, lane_tile(index)] = jnp.where(lane, doubled[0], doubled[1]).astype(jnp.bfloat16)
        a, b = halves(rows_ref[:, lane_tile(index)])
        dup_rows[2 * index] = a
        dup_rows[2 * index + 1] = b
        return carry

    lax.fori_loop(0, coef_ref.shape[1] // (2 * LANES), one_tile, 0, unroll=2)
    pack_send(send_ref, out_ref, dup_coef, dup_rows, owners, capacity, px)


def build_tables(recv_ref, coef_ref, rows_ref, coef_table, feature_table):
    owners, recv_rows, _ = recv_ref.shape
    px = coef_ref.shape[0]
    pairs = recv_rows // (px + 8)
    own_tiles = coef_ref.shape[1] // LANES
    own = 2 * own_tiles
    row = lax.broadcasted_iota(jnp.int32, (LANES, LANES), 0)
    column = lax.broadcasted_iota(jnp.int32, (LANES, LANES), 1)
    unit = jnp.where(row == column, 1.0, 0.0).astype(jnp.bfloat16)

    def put(entry, coef, rows):
        a, b = halves(coef.astype(jnp.float32))
        coef_table[entry] = a.astype(jnp.bfloat16)
        coef_table[entry + 1] = b.astype(jnp.bfloat16)
        features = source_features(rows).astype(jnp.bfloat16)
        spread = jnp.concatenate([features] * 8, axis=0)
        turned = bdot(unit, spread, NT).astype(jnp.bfloat16)
        feature_table[entry] = turned[:64]
        feature_table[entry + 1] = turned[64:]

    def one_own(index, carry):
        put(2 * index, coef_ref[:, lane_tile(index)], rows_ref[:, lane_tile(index)])
        return carry

    lax.fori_loop(0, own_tiles, one_own, 0, unroll=4)

    def one_owner(owner, carry):
        for pair in range(0, pairs, 2):
            start = pairs * px + pair * 8
            both = recv_ref[owner, start:start + 16, :].astype(jnp.float32)
            for part in range(2):
                where = pair + part
                put(
                    own + owner * (2 * pairs) + 2 * where,
                    recv_ref[owner, where * px:(where + 1) * px, :],
                    both[8 * part:8 * part + 8],
                )
        return carry

    lax.fori_loop(0, owners, one_owner, 0)
    last = own + owners * pairs * 2
    coef_table[last] = jnp.zeros((px, LANES), jnp.bfloat16)
    place = lax.broadcasted_iota(jnp.int32, (8, LANES), 0)
    nothing = source_features(jnp.where(place == 3, FAR_AWAY, 0.0)).astype(jnp.bfloat16)
    feature_table[last] = bdot(unit, jnp.concatenate([nothing] * 8, axis=0), NT)[:64].astype(jnp.bfloat16)


def sweep_group(group, index_ref, turns_ref, rows_ref, coef_table, feature_table, acc):
    px = coef_table.shape[1]
    width = TARGETS * 64
    targets = target_features(rows_ref[:, pl.ds(pl.multiple_of(group * width, width), width)])
    targets = jnp.concatenate([targets] * 16, axis=0)
    row = lax.broadcasted_iota(jnp.int32, targets.shape, 0)
    column = lax.broadcasted_iota(jnp.int32, targets.shape, 1)
    owner_of_row = (row // LANES) * 2 + jnp.where(row % LANES < 16, 0, jnp.where(row % LANES < 32, 1, 9))
    weights = jnp.where(owner_of_row == column // 64, targets, 0.0).astype(jnp.bfloat16)
    lane = lax.broadcasted_iota(jnp.int32, (64, LANES), 1) < 16
    lane_x = lax.broadcasted_iota(jnp.int32, (px, LANES), 1) < 64
    acc[...] = jnp.zeros_like(acc)

    def one_turn(turn, carry):
        slot = turn * CHUNK
        total = None
        for part in range(0, CHUNK, 4):
            ids = [
                [index_ref[group * TARGETS + s, slot + part + m] for m in range(4)]
                for s in range(TARGETS)
            ]
            moving = []
            for m in range(4):
                moving.append(
                    jnp.concatenate(
                        [
                            jnp.where(lane, feature_table[ids[s][m]], feature_table[ids[s + 1][m]])
                            for s in (0, 2)
                        ],
                        axis=1,
                    )
                )
            values = jnp.exp2(bdot(jnp.concatenate(moving, axis=0), weights, NN)).astype(jnp.bfloat16)
            coefs = jnp.concatenate(
                [
                    jnp.concatenate(
                        [
                            jnp.where(lane_x, coef_table[ids[s][m]], coef_table[ids[s][m + 1]])
                            for m in (0, 2)
                        ],
                        axis=1,
                    )
                    for s in range(TARGETS)
                ],
                axis=0,
            )
            product = bdot(coefs, values, NN)
            total = product if total is None else total + product
        acc[...] += total
        return carry

    lax.fori_loop(0, turns_ref[group], one_turn, 0)
    block = lax.broadcasted_iota(jnp.int32, (px, width), 1) // 64
    result = acc[0:px, :]
    for s in range(1, TARGETS):
        result = jnp.where(block == s, acc[s * px:(s + 1) * px, :], result)
    return result


def fine_kernel(index_ref, turns_ref, recv_ref, coef_ref, rows_ref, out_ref, coef_table, feature_table, acc):
    build_tables(recv_ref, coef_ref, rows_ref, coef_table, feature_table)
    width = TARGETS * 64

    def one_group(group, carry):
        out_ref[:, pl.ds(pl.multiple_of(group * width, width), width)] = sweep_group(
            group, index_ref, turns_ref, rows_ref, coef_table, feature_table, acc
        )
        return carry

    lax.fori_loop(0, turns_ref.shape[0], one_group, 0)


def coarse_kernel(
    index_ref,
    turns_ref,
    recv_ref,
    coef_ref,
    rows_ref,
    fine_ref,
    transfer_ref,
    probes_ref,
    out_ref,
    gram_ref,
    coef_table,
    feature_table,
    acc,
):
    build_tables(recv_ref, coef_ref, rows_ref, coef_table, feature_table)
    gram_ref[...] = jnp.zeros_like(gram_ref)
    px = coef_ref.shape[0]

    def one_group(group, carry):
        far = sweep_group(group, index_ref, turns_ref, rows_ref, coef_table, feature_table, acc)
        for part in range(TARGETS):
            q = group * TARGETS + part
            tile = far[:, (part // 2) * LANES:(part // 2 + 1) * LANES]
            twice = halves(tile)[part % 2].astype(jnp.bfloat16)
            matrix = transfer_ref[:, lane_tile(q)].astype(jnp.float32)
            low = lax.broadcasted_iota(jnp.int32, matrix.shape, 1) < 64
            matrix = jnp.concatenate(
                [jnp.where(low, matrix, 0.0), jnp.where(low, 0.0, matrix)], axis=0
            ).astype(jnp.bfloat16)
            total = fine_ref[:, lane_tile(q)] + bdot(twice, matrix, NT)
            out_ref[:, lane_tile(q)] = total
            high = total.astype(jnp.bfloat16)
            rest = (total - high.astype(jnp.float32)).astype(jnp.bfloat16)
            probes = probes_ref[:, lane_tile(q)]
            gram_ref[...] += bdot(probes, high, NT) + bdot(probes, rest, NT)
        return carry

    lax.fori_loop(0, turns_ref.shape[0], one_group, 0)


def live_index(slots, counts, nothing):
    place = lax.broadcasted_iota(jnp.int32, slots.shape, 1)
    index = jnp.where(place < counts[:, None], slots, nothing)
    turns = (jnp.max(counts.reshape(-1, TARGETS), axis=1) + CHUNK - 1) // CHUNK
    return index, turns


def shards(
    coef_fine,
    points_fine,
    points_coarse,
    transfer,
    send_fine,
    slots_fine,
    counts_fine,
    send_coarse,
    slots_coarse,
    counts_coarse,
):
    probes = coef_fine.shape[0]
    fine_count = counts_fine.shape[0]
    coarse_count = counts_coarse.shape[0]
    owners = lax.axis_size("leaf")
    groups = lax.axis_size("probe")
    px = -(-probes // 16) * 16
    coef = coef_fine if px == probes else jnp.pad(coef_fine, ((0, px - probes), (0, 0)))
    send_fine = send_fine.reshape(owners, -1)
    send_coarse = send_coarse.reshape(owners, -1)
    cap_fine = send_fine.shape[1]
    cap_coarse = send_coarse.shape[1]
    params = pltpu.CompilerParams(vmem_limit_bytes=VMEM)
    smem = pl.BlockSpec(memory_space=pltpu.SMEM)
    vmem = pl.BlockSpec(memory_space=pltpu.VMEM)
    bf16, f32 = jnp.bfloat16, jnp.float32

    all_probes = lax.all_gather(coef_fine, "probe", axis=0, tiled=True)

    fine_send, fine_rows = pl.pallas_call(
        pack_fine_kernel,
        out_shape=(
            jax.ShapeDtypeStruct((owners, (cap_fine // 2) * (px + 8), LANES), bf16),
            jax.ShapeDtypeStruct((8, points_fine.shape[1]), f32),
        ),
        in_specs=[smem, vmem, vmem],
        out_specs=[vmem, vmem],
        scratch_shapes=[
            pltpu.VMEM((fine_count, px, LANES), f32),
            pltpu.VMEM((fine_count, 8, LANES), f32),
        ],
        compiler_params=params,
        name="pack_fine",
    )(send_fine, coef, points_fine)
    fine_recv = lax.all_to_all(fine_send, "leaf", split_axis=0, concat_axis=0, tiled=True)

    coarse_send, coarse_rows, coarse_coef = pl.pallas_call(
        pack_coarse_kernel,
        out_shape=(
            jax.ShapeDtypeStruct((owners, (cap_coarse // 2) * (px + 8), LANES), bf16),
            jax.ShapeDtypeStruct((8, points_coarse.shape[1]), f32),
            jax.ShapeDtypeStruct((px, points_coarse.shape[1]), bf16),
        ),
        in_specs=[smem, vmem, vmem, vmem],
        out_specs=[vmem, vmem, vmem],
        scratch_shapes=[
            pltpu.VMEM((coarse_count, px, LANES), f32),
            pltpu.VMEM((coarse_count, 8, LANES), f32),
        ],
        compiler_params=params,
        name="pack_coarse",
    )(send_coarse, coef, transfer, points_coarse)
    coarse_recv = lax.all_to_all(coarse_send, "leaf", split_axis=0, concat_axis=0, tiled=True)

    fine_total = fine_count + owners * cap_fine
    coarse_total = coarse_count + owners * cap_coarse
    fine_index, fine_turns = live_index(slots_fine, counts_fine, fine_total)
    coarse_index, coarse_turns = live_index(slots_coarse, counts_coarse, coarse_total)

    fine_far = pl.pallas_call(
        fine_kernel,
        out_shape=jax.ShapeDtypeStruct((px, points_fine.shape[1]), f32),
        in_specs=[smem, smem, vmem, vmem, vmem],
        out_specs=vmem,
        scratch_shapes=[
            pltpu.VMEM((fine_total + 1, px, LANES), bf16),
            pltpu.VMEM((fine_total + 1, 64, LANES), bf16),
            pltpu.VMEM((TARGETS * px, TARGETS * 64), f32),
        ],
        compiler_params=params,
        name="fine_sweep",
    )(fine_index, fine_turns, fine_recv, coef, fine_rows)

    far, gram = pl.pallas_call(
        coarse_kernel,
        out_shape=(
            jax.ShapeDtypeStruct((px, points_fine.shape[1]), f32),
            jax.ShapeDtypeStruct((all_probes.shape[0], px), f32),
        ),
        in_specs=[smem, smem] + [vmem] * 6,
        out_specs=[vmem, vmem],
        scratch_shapes=[
            pltpu.VMEM((coarse_total + 1, px, LANES), bf16),
            pltpu.VMEM((coarse_total + 1, 64, LANES), bf16),
            pltpu.VMEM((TARGETS * px, TARGETS * 64), f32),
        ],
        compiler_params=params,
        name="coarse_sweep",
    )(coarse_index, coarse_turns, coarse_recv, coarse_coef, coarse_rows, fine_far, transfer, all_probes)

    far_field = far[:probes]
    blocks = gram[:, :probes].reshape(groups, probes * probes)
    blocks = jnp.broadcast_to(blocks[None], (owners, groups, probes * probes))
    blocks = blocks.reshape(owners * groups, 1, probes * probes)
    blocks = lax.all_to_all(blocks, ("leaf", "probe"), split_axis=0, concat_axis=0, tiled=True)
    total = jnp.sum(blocks.reshape(owners, groups, probes, probes), axis=0)
    gram_scale = 1.0 / math.sqrt(owners * fine_count * 64)
    probe_gram = total.transpose(1, 0, 2).reshape(probes, groups * probes) * gram_scale
    return (far_field, probe_gram)


def solution(mesh):
    return jax.shard_map(
        shards,
        mesh=mesh,
        in_specs=(
            P("probe", "leaf"),
            P(None, "leaf"),
            P(None, "leaf"),
            P(None, "leaf"),
            P("leaf", None, None),
            P("leaf", None),
            P("leaf"),
            P("leaf", None, None),
            P("leaf", None),
            P("leaf"),
        ),
        out_specs=(P("probe", "leaf"), P("probe", None)),
        check_vma=False,
    )
```

```python
import functools
import math

import jax
import jax.numpy as jnp
from jax import lax
from jax.experimental import pallas as pl
from jax.experimental.pallas import tpu as pltpu
from jax.sharding import PartitionSpec as P

KERNEL_RATE = 1.5
POINT_SCALE = math.sqrt(2.0 * KERNEL_RATE * math.log2(math.e))
LANES = 128
TARGETS = 4
CHUNK = 8
FAR_AWAY = -30000.0
VMEM = 56 * 1024 * 1024

NT = (((1,), (1,)), ((), ()))
NN = (((1,), (0,)), ((), ()))


def bdot(a, b, dims):
    return lax.dot_general(a, b, dims, preferred_element_type=jnp.float32)


def split_rows(points):
    v = points * POINT_SCALE
    norm = -0.5 * (v[0:1] * v[0:1] + v[1:2] * v[1:2] + v[2:3] * v[2:3])
    full = jnp.concatenate([v, norm], axis=0)
    high = full.astype(jnp.bfloat16).astype(jnp.float32)
    rest = (full - high).astype(jnp.bfloat16).astype(jnp.float32)
    return jnp.concatenate([high, rest], axis=0)


def source_features(rows):
    place = lax.broadcasted_iota(jnp.int32, rows.shape, 0)
    one = jnp.where((place == 3) | (place == 7), 1.0, 0.0)
    return jnp.concatenate([rows, jnp.where(place < 3, rows, one)], axis=0)


def target_features(rows):
    place = lax.broadcasted_iota(jnp.int32, rows.shape, 0)
    turned = jnp.concatenate([rows[4:8], rows[0:4]], axis=0)
    one = jnp.where((place == 3) | (place == 7), 1.0, jnp.where(place < 3, rows, turned))
    return jnp.concatenate([one, turned], axis=0)


def halves(tile):
    lane = lax.broadcasted_iota(jnp.int32, tile.shape, 1)
    turned = pltpu.roll(tile, LANES // 2, 1)
    low = lane < LANES // 2
    return jnp.where(low, tile, turned), jnp.where(low, turned, tile)


def lane_tile(index):
    return pl.ds(pl.multiple_of(index * LANES, LANES), LANES)


def pack_send(send_ref, out_ref, dup_coef, dup_rows, owners, capacity, px):
    pairs = capacity // 2
    lane = lax.broadcasted_iota(jnp.int32, (px, LANES), 1) < LANES // 2
    lane8 = lax.broadcasted_iota(jnp.int32, (8, LANES), 1) < LANES // 2

    def one_owner(owner, carry):
        before = None
        for pair in range(pairs):
            first = send_ref[owner, 2 * pair]
            second = send_ref[owner, 2 * pair + 1]
            out_ref[owner, pair * px:(pair + 1) * px, :] = jnp.where(
                lane, dup_coef[first], dup_coef[second]
            ).astype(jnp.bfloat16)
            rows = jnp.where(lane8, dup_rows[first], dup_rows[second])
            if pair % 2 == 0:
                before = rows
            else:
                start = pairs * px + (pair - 1) * 8
                out_ref[owner, start:start + 16, :] = jnp.concatenate(
                    [before, rows], axis=0
                ).astype(jnp.bfloat16)
        return carry

    lax.fori_loop(0, owners, one_owner, 0)


def pack_fine_kernel(send_ref, coef_ref, points_ref, out_ref, rows_ref, dup_coef, dup_rows):
    owners, capacity = send_ref.shape
    px = coef_ref.shape[0]
    rows_ref[...] = split_rows(points_ref[...])

    def one_tile(index, carry):
        a, b = halves(coef_ref[:, lane_tile(index)].astype(jnp.float32))
        dup_coef[2 * index] = a
        dup_coef[2 * index + 1] = b
        a, b = halves(rows_ref[:, lane_tile(index)])
        dup_rows[2 * index] = a
        dup_rows[2 * index + 1] = b
        return carry

    lax.fori_loop(0, coef_ref.shape[1] // LANES, one_tile, 0, unroll=4)
    pack_send(send_ref, out_ref, dup_coef, dup_rows, owners, capacity, px)


def pack_coarse_kernel(
    send_ref, coef_ref, transfer_ref, points_ref, out_ref, rows_ref, coarse_ref, dup_coef, dup_rows
):
    owners, capacity = send_ref.shape
    px = coef_ref.shape[0]
    rows_ref[...] = split_rows(points_ref[...])

    def one_tile(index, carry):
        doubled = []
        for part in range(2):
            q = 2 * index + part
            a, b = halves(transfer_ref[:, lane_tile(q)].astype(jnp.float32))
            matrix = jnp.concatenate([a, b], axis=0).astype(jnp.bfloat16)
            block = bdot(coef_ref[:, lane_tile(q)], matrix, NN)
            dup_coef[q] = block
            doubled.append(block)
        lane = lax.broadcasted_iota(jnp.int32, (px, LANES), 1) < LANES // 2
        coarse_ref[:, lane_tile(index)] = jnp.where(lane, doubled[0], doubled[1]).astype(jnp.bfloat16)
        a, b = halves(rows_ref[:, lane_tile(index)])
        dup_rows[2 * index] = a
        dup_rows[2 * index + 1] = b
        return carry

    lax.fori_loop(0, coef_ref.shape[1] // (2 * LANES), one_tile, 0, unroll=2)
    pack_send(send_ref, out_ref, dup_coef, dup_rows, owners, capacity, px)


def build_tables(recv_ref, coef_ref, rows_ref, coef_table, feature_table, target_table):
    owners, recv_rows, _ = recv_ref.shape
    px = coef_ref.shape[0]
    pairs = recv_rows // (px + 8)
    own_tiles = coef_ref.shape[1] // LANES
    own = 2 * own_tiles
    row = lax.broadcasted_iota(jnp.int32, (LANES, LANES), 0)
    column = lax.broadcasted_iota(jnp.int32, (LANES, LANES), 1)
    unit = jnp.where(row == column, 1.0, 0.0).astype(jnp.bfloat16)

    def put(entry, coef, rows):
        a, b = halves(coef.astype(jnp.float32))
        coef_table[entry] = a.astype(jnp.bfloat16)
        coef_table[entry + 1] = b.astype(jnp.bfloat16)
        a, b = halves(source_features(rows))
        feature_table[entry] = a.astype(jnp.bfloat16)
        feature_table[entry + 1] = b.astype(jnp.bfloat16)

    def one_own(index, carry):
        rows = rows_ref[:, lane_tile(index)]
        put(2 * index, coef_ref[:, lane_tile(index)], rows)
        features = target_features(rows).astype(jnp.bfloat16)
        turned = bdot(unit, jnp.concatenate([features] * 8, axis=0), NT)
        place = 2 * (index % (TARGETS // 2)) + row // 64
        turned = jnp.where(column // 16 == place, turned, 0.0)
        target_table[index] = turned[:, :16 * TARGETS].astype(jnp.bfloat16)
        return carry

    lax.fori_loop(0, own_tiles, one_own, 0, unroll=4)

    def one_owner(owner, carry):
        for pair in range(0, pairs, 2):
            start = pairs * px + pair * 8
            both = recv_ref[owner, start:start + 16, :].astype(jnp.float32)
            for part in range(2):
                where = pair + part
                put(
                    own + owner * (2 * pairs) + 2 * where,
                    recv_ref[owner, where * px:(where + 1) * px, :],
                    both[8 * part:8 * part + 8],
                )
        return carry

    lax.fori_loop(0, owners, one_owner, 0)
    last = own + owners * pairs * 2
    coef_table[last] = jnp.zeros((px, LANES), jnp.bfloat16)
    place = lax.broadcasted_iota(jnp.int32, (8, LANES), 0)
    nothing = source_features(jnp.where(place == 3, FAR_AWAY, 0.0))
    feature_table[last] = nothing.astype(jnp.bfloat16)


def sweep(index_ref, turns_ref, coef_table, feature_table, target_table, first_buffer, second_buffer, acc):
    groups = turns_ref.shape[0]
    px = coef_table.shape[1]
    slots_end = index_ref.shape[1] // CHUNK - 1
    lane = lax.broadcasted_iota(jnp.int32, (16, LANES), 1) < 64
    lane_x = lax.broadcasted_iota(jnp.int32, (px, LANES), 1) < 64
    acc[...] = jnp.zeros_like(acc)

    def tiles(item, buffer):
        group, turn = item
        targets = target_table[pl.ds(2 * group, 2)].reshape(TARGETS * 64, 16 * TARGETS)
        for part in range(0, CHUNK, 4):
            sources = []
            for s in range(TARGETS):
                ids = [index_ref[group * TARGETS + s, turn * CHUNK + part + m] for m in range(4)]
                sources.append(
                    jnp.concatenate(
                        [
                            jnp.where(lane, feature_table[ids[m]], feature_table[ids[m + 1]])
                            for m in (0, 2)
                        ],
                        axis=1,
                    )
                )
            power = bdot(targets, jnp.concatenate(sources, axis=0), NN)
            buffer[:, part * 64:part * 64 + 256] = jnp.exp2(power).astype(jnp.bfloat16)

    def product(item, buffer):
        group, turn = item
        coefs = []
        for s in range(TARGETS):
            ids = [index_ref[group * TARGETS + s, turn * CHUNK + m] for m in range(CHUNK)]
            coefs.append(
                jnp.concatenate(
                    [
                        jnp.where(lane_x, coef_table[ids[m]], coef_table[ids[m + 1]])
                        for m in range(0, CHUNK, 2)
                    ],
                    axis=1,
                )
            )
        acc[group] += bdot(jnp.concatenate(coefs, axis=0), buffer[...], NT)

    def following(item):
        group, turn = item
        over = turn + 1 >= turns_ref[group]
        later = jnp.where(over, group + 1, group)
        end = later >= groups
        turn = jnp.where(end, slots_end, jnp.where(over, 0, turn + 1))
        return jnp.minimum(later, groups - 1), turn

    def two_items(_, item):
        second = following(item)
        third = following(second)
        tiles(second, second_buffer)
        product(item, first_buffer)
        tiles(third, first_buffer)
        product(second, second_buffer)
        return third

    items = lax.fori_loop(0, groups, lambda g, n: n + turns_ref[g], jnp.int32(0))
    start = (jnp.int32(0), jnp.int32(0))
    tiles(start, first_buffer)
    lax.fori_loop(0, (items + 1) // 2, two_items, start)


def diagonal(block, px):
    column = lax.broadcasted_iota(jnp.int32, (px, TARGETS * 64), 1) // 64
    result = block[0:px]
    for s in range(1, TARGETS):
        result = jnp.where(column == s, block[s * px:(s + 1) * px], result)
    return result


def fine_kernel(index_ref, turns_ref, recv_ref, coef_ref, rows_ref, out_ref, *scratch):
    tables, acc = scratch[:3], scratch[-1]
    build_tables(recv_ref, coef_ref, rows_ref, *tables)
    sweep(index_ref, turns_ref, *scratch)
    px = coef_ref.shape[0]
    width = TARGETS * 64

    def one_group(group, carry):
        out_ref[:, pl.ds(pl.multiple_of(group * width, width), width)] = diagonal(acc[group], px)
        return carry

    lax.fori_loop(0, turns_ref.shape[0], one_group, 0)


def coarse_kernel(
    index_ref,
    turns_ref,
    recv_ref,
    coef_ref,
    rows_ref,
    fine_ref,
    transfer_ref,
    probes_ref,
    out_ref,
    gram_ref,
    *scratch,
):
    tables, acc = scratch[:3], scratch[-1]
    build_tables(recv_ref, coef_ref, rows_ref, *tables)
    sweep(index_ref, turns_ref, *scratch)
    gram_ref[...] = jnp.zeros_like(gram_ref)
    px = coef_ref.shape[0]

    def one_group(group, carry):
        far = diagonal(acc[group], px)
        gram = None
        for part in range(TARGETS):
            q = group * TARGETS + part
            tile = far[:, (part // 2) * LANES:(part // 2 + 1) * LANES]
            twice = halves(tile)[part % 2].astype(jnp.bfloat16)
            matrix = transfer_ref[:, lane_tile(q)].astype(jnp.float32)
            low = lax.broadcasted_iota(jnp.int32, matrix.shape, 1) < 64
            matrix = jnp.concatenate(
                [jnp.where(low, matrix, 0.0), jnp.where(low, 0.0, matrix)], axis=0
            ).astype(jnp.bfloat16)
            total = fine_ref[:, lane_tile(q)] + bdot(twice, matrix, NT)
            out_ref[:, lane_tile(q)] = total
            high = total.astype(jnp.bfloat16)
            rest = (total - high.astype(jnp.float32)).astype(jnp.bfloat16)
            probes = probes_ref[:, lane_tile(q)]
            term = bdot(probes, high, NT) + bdot(probes, rest, NT)
            gram = term if gram is None else gram + term
        gram_ref[...] += gram
        return carry

    lax.fori_loop(0, turns_ref.shape[0], one_group, 0)


def sweep_scratch(total, clusters, px):
    return [
        pltpu.VMEM((total + 1, px, LANES), jnp.bfloat16),
        pltpu.VMEM((total + 1, 16, LANES), jnp.bfloat16),
        pltpu.VMEM((clusters // 2, LANES, 16 * TARGETS), jnp.bfloat16),
        pltpu.VMEM((TARGETS * 64, CHUNK * 64), jnp.bfloat16),
        pltpu.VMEM((TARGETS * 64, CHUNK * 64), jnp.bfloat16),
        pltpu.VMEM((clusters // TARGETS, TARGETS * px, TARGETS * 64), jnp.float32),
    ]


def live_index(slots, counts, nothing):
    place = lax.broadcasted_iota(jnp.int32, slots.shape, 1)
    index = jnp.where(place < counts[:, None], slots, nothing)
    index = jnp.pad(index, ((0, 0), (0, CHUNK)), constant_values=nothing)
    turns = (jnp.max(counts.reshape(-1, TARGETS), axis=1) + CHUNK - 1) // CHUNK
    return index, turns


def shards(
    coef_fine,
    points_fine,
    points_coarse,
    transfer,
    send_fine,
    slots_fine,
    counts_fine,
    send_coarse,
    slots_coarse,
    counts_coarse,
):
    probes = coef_fine.shape[0]
    fine_count = counts_fine.shape[0]
    coarse_count = counts_coarse.shape[0]
    owners = lax.axis_size("leaf")
    groups = lax.axis_size("probe")
    px = -(-probes // 16) * 16
    coef = coef_fine if px == probes else jnp.pad(coef_fine, ((0, px - probes), (0, 0)))
    send_fine = send_fine.reshape(owners, -1)
    send_coarse = send_coarse.reshape(owners, -1)
    cap_fine = send_fine.shape[1]
    cap_coarse = send_coarse.shape[1]
    params = pltpu.CompilerParams(vmem_limit_bytes=VMEM)
    smem = pl.BlockSpec(memory_space=pltpu.SMEM)
    vmem = pl.BlockSpec(memory_space=pltpu.VMEM)
    bf16, f32 = jnp.bfloat16, jnp.float32

    turned = [coef_fine]
    for step in range(1, groups):
        turned.append(lax.ppermute(coef_fine, "probe", [(i, (i + step) % groups) for i in range(groups)]))
    all_probes = jnp.concatenate(turned, axis=0)

    fine_send, fine_rows = pl.pallas_call(
        pack_fine_kernel,
        out_shape=(
            jax.ShapeDtypeStruct((owners, (cap_fine // 2) * (px + 8), LANES), bf16),
            jax.ShapeDtypeStruct((8, points_fine.shape[1]), f32),
        ),
        in_specs=[smem, vmem, vmem],
        out_specs=[vmem, vmem],
        scratch_shapes=[
            pltpu.VMEM((fine_count, px, LANES), f32),
            pltpu.VMEM((fine_count, 8, LANES), f32),
        ],
        compiler_params=params,
        name="pack_fine",
    )(send_fine, coef, points_fine)
    fine_recv = lax.all_to_all(fine_send, "leaf", split_axis=0, concat_axis=0, tiled=True)

    coarse_send, coarse_rows, coarse_coef = pl.pallas_call(
        pack_coarse_kernel,
        out_shape=(
            jax.ShapeDtypeStruct((owners, (cap_coarse // 2) * (px + 8), LANES), bf16),
            jax.ShapeDtypeStruct((8, points_coarse.shape[1]), f32),
            jax.ShapeDtypeStruct((px, points_coarse.shape[1]), bf16),
        ),
        in_specs=[smem, vmem, vmem, vmem],
        out_specs=[vmem, vmem, vmem],
        scratch_shapes=[
            pltpu.VMEM((coarse_count, px, LANES), f32),
            pltpu.VMEM((coarse_count, 8, LANES), f32),
        ],
        compiler_params=params,
        name="pack_coarse",
    )(send_coarse, coef, transfer, points_coarse)
    coarse_recv = lax.all_to_all(coarse_send, "leaf", split_axis=0, concat_axis=0, tiled=True)

    fine_total = fine_count + owners * cap_fine
    coarse_total = coarse_count + owners * cap_coarse
    fine_index, fine_turns = live_index(slots_fine, counts_fine, fine_total)
    coarse_index, coarse_turns = live_index(slots_coarse, counts_coarse, coarse_total)

    fine_far = pl.pallas_call(
        fine_kernel,
        out_shape=jax.ShapeDtypeStruct((px, points_fine.shape[1]), f32),
        in_specs=[smem, smem, vmem, vmem, vmem],
        out_specs=vmem,
        scratch_shapes=sweep_scratch(fine_total, fine_count, px),
        compiler_params=params,
        name="fine_sweep",
    )(fine_index, fine_turns, fine_recv, coef, fine_rows)

    far, gram = pl.pallas_call(
        coarse_kernel,
        out_shape=(
            jax.ShapeDtypeStruct((px, points_fine.shape[1]), f32),
            jax.ShapeDtypeStruct((all_probes.shape[0], px), f32),
        ),
        in_specs=[smem, smem] + [vmem] * 6,
        out_specs=[vmem, vmem],
        scratch_shapes=sweep_scratch(coarse_total, coarse_count, px),
        compiler_params=params,
        name="coarse_sweep",
    )(coarse_index, coarse_turns, coarse_recv, coarse_coef, coarse_rows, fine_far, transfer, all_probes)

    far_field = far[:probes]
    blocks = gram[:, :probes].reshape(groups, probes * probes)
    blocks = blocks[(lax.axis_index("probe") - jnp.arange(groups)) % groups]
    blocks = jnp.broadcast_to(blocks[None], (owners, groups, probes * probes))
    blocks = blocks.reshape(owners * groups, 1, probes * probes)
    blocks = lax.all_to_all(blocks, ("leaf", "probe"), split_axis=0, concat_axis=0, tiled=True)
    total = jnp.sum(blocks.reshape(owners, groups, probes, probes), axis=0)
    gram_scale = 1.0 / math.sqrt(owners * fine_count * 64)
    probe_gram = total.transpose(1, 0, 2).reshape(probes, groups * probes) * gram_scale
    return (far_field, probe_gram)


def solution(mesh):
    return jax.shard_map(
        shards,
        mesh=mesh,
        in_specs=(
            P("probe", "leaf"),
            P(None, "leaf"),
            P(None, "leaf"),
            P(None, "leaf"),
            P("leaf", None, None),
            P("leaf", None),
            P("leaf"),
            P("leaf", None, None),
            P("leaf", None),
            P("leaf"),
        ),
        out_specs=(P("probe", "leaf"), P("probe", None)),
        check_vma=False,
    )
```

```python
import functools
import math

import jax
import jax.numpy as jnp
from jax import lax
from jax.experimental import pallas as pl
from jax.experimental.pallas import tpu as pltpu
from jax.sharding import PartitionSpec as P

KERNEL_RATE = 1.5
POINT_SCALE = math.sqrt(2.0 * KERNEL_RATE * math.log2(math.e))
LANES = 128
UNITS = 4
CHUNK = 8
FAR_AWAY = -30000.0
VMEM = 56 * 1024 * 1024

NT = (((1,), (1,)), ((), ()))
NN = (((1,), (0,)), ((), ()))


def bdot(a, b, dims):
    return lax.dot_general(a, b, dims, preferred_element_type=jnp.float32)


def split_rows(points):
    v = points * POINT_SCALE
    norm = -0.5 * (v[0:1] * v[0:1] + v[1:2] * v[1:2] + v[2:3] * v[2:3])
    full = jnp.concatenate([v, norm], axis=0)
    high = full.astype(jnp.bfloat16).astype(jnp.float32)
    rest = (full - high).astype(jnp.bfloat16).astype(jnp.float32)
    return jnp.concatenate([high, rest], axis=0)


def source_features(rows):
    place = lax.broadcasted_iota(jnp.int32, rows.shape, 0)
    one = jnp.where((place == 3) | (place == 7), 1.0, 0.0)
    return jnp.concatenate([rows, jnp.where(place < 3, rows, one)], axis=0)


def target_features(rows):
    place = lax.broadcasted_iota(jnp.int32, rows.shape, 0)
    turned = jnp.concatenate([rows[4:8], rows[0:4]], axis=0)
    one = jnp.where((place == 3) | (place == 7), 1.0, jnp.where(place < 3, rows, turned))
    return jnp.concatenate([one, turned], axis=0)


def halves(tile):
    lane = lax.broadcasted_iota(jnp.int32, tile.shape, 1)
    turned = pltpu.roll(tile, LANES // 2, 1)
    low = lane < LANES // 2
    return jnp.where(low, tile, turned), jnp.where(low, turned, tile)


def lane_tile(index):
    return pl.ds(pl.multiple_of(index * LANES, LANES), LANES)


def pack_send(send_ref, out_ref, dup_coef, dup_rows, owners, capacity, px):
    pairs = capacity // 2
    lane = lax.broadcasted_iota(jnp.int32, (px, LANES), 1) < LANES // 2
    lane8 = lax.broadcasted_iota(jnp.int32, (8, LANES), 1) < LANES // 2

    def one_owner(owner, carry):
        before = None
        for pair in range(pairs):
            first = send_ref[owner, 2 * pair]
            second = send_ref[owner, 2 * pair + 1]
            out_ref[owner, pair * px:(pair + 1) * px, :] = jnp.where(
                lane, dup_coef[first], dup_coef[second]
            ).astype(jnp.bfloat16)
            rows = jnp.where(lane8, dup_rows[first], dup_rows[second])
            if pair % 2 == 0:
                before = rows
            else:
                start = pairs * px + (pair - 1) * 8
                out_ref[owner, start:start + 16, :] = jnp.concatenate(
                    [before, rows], axis=0
                ).astype(jnp.bfloat16)
        return carry

    lax.fori_loop(0, owners, one_owner, 0)


def pack_fine_kernel(send_ref, coef_ref, points_ref, out_ref, rows_ref, dup_coef, dup_rows):
    owners, capacity = send_ref.shape
    px = coef_ref.shape[0]
    rows_ref[...] = split_rows(points_ref[...])

    def one_tile(index, carry):
        a, b = halves(coef_ref[:, lane_tile(index)].astype(jnp.float32))
        dup_coef[2 * index] = a
        dup_coef[2 * index + 1] = b
        a, b = halves(rows_ref[:, lane_tile(index)])
        dup_rows[2 * index] = a
        dup_rows[2 * index + 1] = b
        return carry

    lax.fori_loop(0, coef_ref.shape[1] // LANES, one_tile, 0, unroll=4)
    pack_send(send_ref, out_ref, dup_coef, dup_rows, owners, capacity, px)


def pack_coarse_kernel(
    send_ref, coef_ref, transfer_ref, points_ref, out_ref, rows_ref, coarse_ref, dup_coef, dup_rows
):
    owners, capacity = send_ref.shape
    px = coef_ref.shape[0]
    rows_ref[...] = split_rows(points_ref[...])

    def one_tile(index, carry):
        doubled = []
        for part in range(2):
            q = 2 * index + part
            a, b = halves(transfer_ref[:, lane_tile(q)].astype(jnp.float32))
            matrix = jnp.concatenate([a, b], axis=0).astype(jnp.bfloat16)
            block = bdot(coef_ref[:, lane_tile(q)], matrix, NN)
            dup_coef[q] = block
            doubled.append(block)
        lane = lax.broadcasted_iota(jnp.int32, (px, LANES), 1) < LANES // 2
        coarse_ref[:, lane_tile(index)] = jnp.where(lane, doubled[0], doubled[1]).astype(jnp.bfloat16)
        a, b = halves(rows_ref[:, lane_tile(index)])
        dup_rows[2 * index] = a
        dup_rows[2 * index + 1] = b
        return carry

    lax.fori_loop(0, coef_ref.shape[1] // (2 * LANES), one_tile, 0, unroll=2)
    pack_send(send_ref, out_ref, dup_coef, dup_rows, owners, capacity, px)


def build_tables(recv_ref, coef_ref, rows_ref, coef_table, feature_table, target_table):
    owners, recv_rows, _ = recv_ref.shape
    px = coef_ref.shape[0]
    pairs = recv_rows // (px + 8)
    own_tiles = coef_ref.shape[1] // LANES
    own = 2 * own_tiles
    row = lax.broadcasted_iota(jnp.int32, (LANES, LANES), 0)
    column = lax.broadcasted_iota(jnp.int32, (LANES, LANES), 1)
    unit = jnp.where(row == column, 1.0, 0.0).astype(jnp.bfloat16)

    def put(entry, coef, rows):
        a, b = halves(coef.astype(jnp.float32))
        coef_table[entry] = a.astype(jnp.bfloat16)
        coef_table[entry + 1] = b.astype(jnp.bfloat16)
        a, b = halves(source_features(rows))
        feature_table[entry] = a.astype(jnp.bfloat16)
        feature_table[entry + 1] = b.astype(jnp.bfloat16)

    def one_own(index, carry):
        rows = rows_ref[:, lane_tile(index)]
        put(2 * index, coef_ref[:, lane_tile(index)], rows)
        features = target_features(rows).astype(jnp.bfloat16)
        turned = bdot(unit, jnp.concatenate([features] * 8, axis=0), NT)[:, :16]
        target_table[2 * index] = turned[:64].astype(jnp.bfloat16)
        target_table[2 * index + 1] = turned[64:].astype(jnp.bfloat16)
        return carry

    lax.fori_loop(0, own_tiles, one_own, 0, unroll=4)

    def one_owner(owner, carry):
        for pair in range(0, pairs, 2):
            start = pairs * px + pair * 8
            both = recv_ref[owner, start:start + 16, :].astype(jnp.float32)
            for part in range(2):
                where = pair + part
                put(
                    own + owner * (2 * pairs) + 2 * where,
                    recv_ref[owner, where * px:(where + 1) * px, :],
                    both[8 * part:8 * part + 8],
                )
        return carry

    lax.fori_loop(0, owners, one_owner, 0)
    last = own + owners * pairs * 2
    coef_table[last] = jnp.zeros((px, LANES), jnp.bfloat16)
    place = lax.broadcasted_iota(jnp.int32, (8, LANES), 0)
    nothing = source_features(jnp.where(place == 3, FAR_AWAY, 0.0))
    feature_table[last] = nothing.astype(jnp.bfloat16)


def sweep(index_ref, turns_ref, coef_table, feature_table, target_table, first_buffer, second_buffer, acc):
    clusters = turns_ref.shape[0]
    px = coef_table.shape[1]
    slots_end = index_ref.shape[1] // CHUNK - 1
    lane = lax.broadcasted_iota(jnp.int32, (16, LANES), 1) < 64
    lane_x = lax.broadcasted_iota(jnp.int32, (px, LANES), 1) < 64
    acc[...] = jnp.zeros_like(acc)

    def pairs_of(unit, table, low):
        target, turn = unit
        ids = [index_ref[target, turn * CHUNK + m] for m in range(CHUNK)]
        return jnp.concatenate(
            [jnp.where(low, table[ids[m]], table[ids[m + 1]]) for m in range(0, CHUNK, 2)], axis=1
        )

    def tiles(units, buffer):
        for place, unit in enumerate(units):
            power = bdot(target_table[unit[0]], pairs_of(unit, feature_table, lane), NN)
            buffer[place] = jnp.exp2(power).astype(jnp.bfloat16)

    def products(units, buffer):
        for place, unit in enumerate(units):
            acc[unit[0]] += bdot(pairs_of(unit, coef_table, lane_x), buffer[place], NT)

    def following(unit):
        target, turn = unit
        over = turn + 1 >= turns_ref[target]
        later = jnp.where(over, target + 1, target)
        end = later >= clusters
        turn = jnp.where(end, slots_end, jnp.where(over, 0, turn + 1))
        return jnp.minimum(later, clusters - 1), turn

    def next_units(unit):
        units = []
        for _ in range(UNITS):
            unit = following(unit)
            units.append(unit)
        return tuple(units)

    def two_sets(_, units):
        second = next_units(units[-1])
        third = next_units(second[-1])
        tiles(second, second_buffer)
        products(units, first_buffer)
        tiles(third, first_buffer)
        products(second, second_buffer)
        return third

    total = lax.fori_loop(0, clusters, lambda c, n: n + turns_ref[c], jnp.int32(0))
    unit = (jnp.int32(0), jnp.int32(0))
    start = (unit,) + next_units(unit)[:-1]
    tiles(start, first_buffer)
    lax.fori_loop(0, (total + 2 * UNITS - 1) // (2 * UNITS), two_sets, start)


def fine_kernel(index_ref, turns_ref, recv_ref, coef_ref, rows_ref, out_ref, *scratch):
    tables, acc = scratch[:3], scratch[-1]
    build_tables(recv_ref, coef_ref, rows_ref, *tables)
    sweep(index_ref, turns_ref, *scratch)
    low = lax.broadcasted_iota(jnp.int32, (coef_ref.shape[0], LANES), 1) < 64

    def one_tile(index, carry):
        pair = [jnp.concatenate([acc[2 * index + part]] * 2, axis=1) for part in range(2)]
        out_ref[:, lane_tile(index)] = jnp.where(low, pair[0], pair[1])
        return carry

    lax.fori_loop(0, turns_ref.shape[0] // 2, one_tile, 0, unroll=4)


def coarse_kernel(
    index_ref,
    turns_ref,
    recv_ref,
    coef_ref,
    rows_ref,
    fine_ref,
    transfer_ref,
    probes_ref,
    out_ref,
    gram_ref,
    *scratch,
):
    tables, acc = scratch[:3], scratch[-1]
    build_tables(recv_ref, coef_ref, rows_ref, *tables)
    sweep(index_ref, turns_ref, *scratch)
    gram_ref[...] = jnp.zeros_like(gram_ref)

    def one_group(group, carry):
        gram = None
        for part in range(4):
            q = group * 4 + part
            twice = jnp.concatenate([acc[q]] * 2, axis=1).astype(jnp.bfloat16)
            matrix = transfer_ref[:, lane_tile(q)].astype(jnp.float32)
            low = lax.broadcasted_iota(jnp.int32, matrix.shape, 1) < 64
            matrix = jnp.concatenate(
                [jnp.where(low, matrix, 0.0), jnp.where(low, 0.0, matrix)], axis=0
            ).astype(jnp.bfloat16)
            total = fine_ref[:, lane_tile(q)] + bdot(twice, matrix, NT)
            out_ref[:, lane_tile(q)] = total
            high = total.astype(jnp.bfloat16)
            rest = (total - high.astype(jnp.float32)).astype(jnp.bfloat16)
            probes = probes_ref[:, lane_tile(q)]
            term = bdot(probes, high, NT) + bdot(probes, rest, NT)
            gram = term if gram is None else gram + term
        gram_ref[...] += gram
        return carry

    lax.fori_loop(0, turns_ref.shape[0] // 4, one_group, 0)


def sweep_scratch(total, clusters, px):
    return [
        pltpu.VMEM((total + 1, px, LANES), jnp.bfloat16),
        pltpu.VMEM((total + 1, 16, LANES), jnp.bfloat16),
        pltpu.VMEM((clusters, 64, 16), jnp.bfloat16),
        pltpu.VMEM((UNITS, 64, CHUNK * 64), jnp.bfloat16),
        pltpu.VMEM((UNITS, 64, CHUNK * 64), jnp.bfloat16),
        pltpu.VMEM((clusters, px, 64), jnp.float32),
    ]


def live_index(slots, counts, nothing):
    place = lax.broadcasted_iota(jnp.int32, slots.shape, 1)
    index = jnp.where(place < counts[:, None], slots, nothing)
    index = jnp.pad(index, ((0, 0), (0, CHUNK)), constant_values=nothing)
    turns = (counts + CHUNK - 1) // CHUNK
    return index, turns


def shards(
    coef_fine,
    points_fine,
    points_coarse,
    transfer,
    send_fine,
    slots_fine,
    counts_fine,
    send_coarse,
    slots_coarse,
    counts_coarse,
):
    probes = coef_fine.shape[0]
    fine_count = counts_fine.shape[0]
    coarse_count = counts_coarse.shape[0]
    owners = lax.axis_size("leaf")
    groups = lax.axis_size("probe")
    px = -(-probes // 16) * 16
    coef = coef_fine if px == probes else jnp.pad(coef_fine, ((0, px - probes), (0, 0)))
    send_fine = send_fine.reshape(owners, -1)
    send_coarse = send_coarse.reshape(owners, -1)
    cap_fine = send_fine.shape[1]
    cap_coarse = send_coarse.shape[1]
    params = pltpu.CompilerParams(vmem_limit_bytes=VMEM)
    smem = pl.BlockSpec(memory_space=pltpu.SMEM)
    vmem = pl.BlockSpec(memory_space=pltpu.VMEM)
    bf16, f32 = jnp.bfloat16, jnp.float32

    turned = [coef_fine]
    for step in range(1, groups):
        turned.append(lax.ppermute(coef_fine, "probe", [(i, (i + step) % groups) for i in range(groups)]))
    all_probes = jnp.concatenate(turned, axis=0)

    fine_send, fine_rows = pl.pallas_call(
        pack_fine_kernel,
        out_shape=(
            jax.ShapeDtypeStruct((owners, (cap_fine // 2) * (px + 8), LANES), bf16),
            jax.ShapeDtypeStruct((8, points_fine.shape[1]), f32),
        ),
        in_specs=[smem, vmem, vmem],
        out_specs=[vmem, vmem],
        scratch_shapes=[
            pltpu.VMEM((fine_count, px, LANES), f32),
            pltpu.VMEM((fine_count, 8, LANES), f32),
        ],
        compiler_params=params,
        name="pack_fine",
    )(send_fine, coef, points_fine)
    fine_recv = lax.all_to_all(fine_send, "leaf", split_axis=0, concat_axis=0, tiled=True)

    coarse_send, coarse_rows, coarse_coef = pl.pallas_call(
        pack_coarse_kernel,
        out_shape=(
            jax.ShapeDtypeStruct((owners, (cap_coarse // 2) * (px + 8), LANES), bf16),
            jax.ShapeDtypeStruct((8, points_coarse.shape[1]), f32),
            jax.ShapeDtypeStruct((px, points_coarse.shape[1]), bf16),
        ),
        in_specs=[smem, vmem, vmem, vmem],
        out_specs=[vmem, vmem, vmem],
        scratch_shapes=[
            pltpu.VMEM((coarse_count, px, LANES), f32),
            pltpu.VMEM((coarse_count, 8, LANES), f32),
        ],
        compiler_params=params,
        name="pack_coarse",
    )(send_coarse, coef, transfer, points_coarse)
    coarse_recv = lax.all_to_all(coarse_send, "leaf", split_axis=0, concat_axis=0, tiled=True)

    fine_total = fine_count + owners * cap_fine
    coarse_total = coarse_count + owners * cap_coarse
    fine_index, fine_turns = live_index(slots_fine, counts_fine, fine_total)
    coarse_index, coarse_turns = live_index(slots_coarse, counts_coarse, coarse_total)

    fine_far = pl.pallas_call(
        fine_kernel,
        out_shape=jax.ShapeDtypeStruct((px, points_fine.shape[1]), f32),
        in_specs=[smem, smem, vmem, vmem, vmem],
        out_specs=vmem,
        scratch_shapes=sweep_scratch(fine_total, fine_count, px),
        compiler_params=params,
        name="fine_sweep",
    )(fine_index, fine_turns, fine_recv, coef, fine_rows)

    far, gram = pl.pallas_call(
        coarse_kernel,
        out_shape=(
            jax.ShapeDtypeStruct((px, points_fine.shape[1]), f32),
            jax.ShapeDtypeStruct((all_probes.shape[0], px), f32),
        ),
        in_specs=[smem, smem] + [vmem] * 6,
        out_specs=[vmem, vmem],
        scratch_shapes=sweep_scratch(coarse_total, coarse_count, px),
        compiler_params=params,
        name="coarse_sweep",
    )(coarse_index, coarse_turns, coarse_recv, coarse_coef, coarse_rows, fine_far, transfer, all_probes)

    far_field = far[:probes]
    blocks = gram[:, :probes].reshape(groups, probes * probes)
    blocks = blocks[(lax.axis_index("probe") - jnp.arange(groups)) % groups]
    blocks = jnp.broadcast_to(blocks[None], (owners, groups, probes * probes))
    blocks = blocks.reshape(owners * groups, 1, probes * probes)
    blocks = lax.all_to_all(blocks, ("leaf", "probe"), split_axis=0, concat_axis=0, tiled=True)
    total = jnp.sum(blocks.reshape(owners, groups, probes, probes), axis=0)
    gram_scale = 1.0 / math.sqrt(owners * fine_count * 64)
    probe_gram = total.transpose(1, 0, 2).reshape(probes, groups * probes) * gram_scale
    return (far_field, probe_gram)


def solution(mesh):
    return jax.shard_map(
        shards,
        mesh=mesh,
        in_specs=(
            P("probe", "leaf"),
            P(None, "leaf"),
            P(None, "leaf"),
            P(None, "leaf"),
            P("leaf", None, None),
            P("leaf", None),
            P("leaf"),
            P("leaf", None, None),
            P("leaf", None),
            P("leaf"),
        ),
        out_specs=(P("probe", "leaf"), P("probe", None)),
        check_vma=False,
    )
```

```python
import functools
import math

import jax
import jax.numpy as jnp
from jax import lax
from jax.experimental import pallas as pl
from jax.experimental.pallas import tpu as pltpu
from jax.sharding import PartitionSpec as P

KERNEL_RATE = 1.5
POINT_SCALE = math.sqrt(2.0 * KERNEL_RATE * math.log2(math.e))
LANES = 128
UNITS = 4
CHUNK = 8
FAR_AWAY = -30000.0
VMEM = 56 * 1024 * 1024

NT = (((1,), (1,)), ((), ()))
NN = (((1,), (0,)), ((), ()))


def bdot(a, b, dims):
    return lax.dot_general(a, b, dims, preferred_element_type=jnp.float32)


def split_rows(points):
    v = points * POINT_SCALE
    norm = -0.5 * (v[0:1] * v[0:1] + v[1:2] * v[1:2] + v[2:3] * v[2:3])
    full = jnp.concatenate([v, norm], axis=0)
    high = full.astype(jnp.bfloat16).astype(jnp.float32)
    rest = (full - high).astype(jnp.bfloat16).astype(jnp.float32)
    return jnp.concatenate([high, rest], axis=0)


def source_features(rows):
    place = lax.broadcasted_iota(jnp.int32, rows.shape, 0)
    one = jnp.where((place == 3) | (place == 7), 1.0, 0.0)
    return jnp.concatenate([rows, jnp.where(place < 3, rows, one)], axis=0)


def target_features(rows):
    place = lax.broadcasted_iota(jnp.int32, rows.shape, 0)
    turned = jnp.concatenate([rows[4:8], rows[0:4]], axis=0)
    one = jnp.where((place == 3) | (place == 7), 1.0, jnp.where(place < 3, rows, turned))
    return jnp.concatenate([one, turned], axis=0)


def halves(tile):
    lane = lax.broadcasted_iota(jnp.int32, tile.shape, 1)
    turned = pltpu.roll(tile, LANES // 2, 1)
    low = lane < LANES // 2
    return jnp.where(low, tile, turned), jnp.where(low, turned, tile)


def lane_tile(index):
    return pl.ds(pl.multiple_of(index * LANES, LANES), LANES)


def pack_send(send_ref, out_ref, dup_coef, dup_rows, owners, capacity, px):
    pairs = capacity // 2
    lane = lax.broadcasted_iota(jnp.int32, (px, LANES), 1) < LANES // 2
    lane8 = lax.broadcasted_iota(jnp.int32, (8, LANES), 1) < LANES // 2

    def one_owner(owner, carry):
        before = None
        for pair in range(pairs):
            first = send_ref[owner, 2 * pair]
            second = send_ref[owner, 2 * pair + 1]
            out_ref[owner, pair * px:(pair + 1) * px, :] = jnp.where(
                lane, dup_coef[first], dup_coef[second]
            ).astype(jnp.bfloat16)
            rows = jnp.where(lane8, dup_rows[first], dup_rows[second])
            if pair % 2 == 0:
                before = rows
            else:
                start = pairs * px + (pair - 1) * 8
                out_ref[owner, start:start + 16, :] = jnp.concatenate(
                    [before, rows], axis=0
                ).astype(jnp.bfloat16)
        return carry

    lax.fori_loop(0, owners, one_owner, 0)


def pack_fine_kernel(send_ref, coef_ref, points_ref, out_ref, rows_ref, dup_coef, dup_rows):
    owners, capacity = send_ref.shape
    px = coef_ref.shape[0]
    rows_ref[...] = split_rows(points_ref[...])

    def one_tile(index, carry):
        a, b = halves(coef_ref[:, lane_tile(index)].astype(jnp.float32))
        dup_coef[2 * index] = a
        dup_coef[2 * index + 1] = b
        a, b = halves(rows_ref[:, lane_tile(index)])
        dup_rows[2 * index] = a
        dup_rows[2 * index + 1] = b
        return carry

    lax.fori_loop(0, coef_ref.shape[1] // LANES, one_tile, 0, unroll=4)
    pack_send(send_ref, out_ref, dup_coef, dup_rows, owners, capacity, px)


def pack_coarse_kernel(
    send_ref, coef_ref, transfer_ref, points_ref, out_ref, rows_ref, coarse_ref, dup_coef, dup_rows
):
    owners, capacity = send_ref.shape
    px = coef_ref.shape[0]
    rows_ref[...] = split_rows(points_ref[...])

    def one_tile(index, carry):
        doubled = []
        for part in range(2):
            q = 2 * index + part
            a, b = halves(transfer_ref[:, lane_tile(q)].astype(jnp.float32))
            matrix = jnp.concatenate([a, b], axis=0).astype(jnp.bfloat16)
            block = bdot(coef_ref[:, lane_tile(q)], matrix, NN)
            dup_coef[q] = block
            doubled.append(block)
        lane = lax.broadcasted_iota(jnp.int32, (px, LANES), 1) < LANES // 2
        coarse_ref[:, lane_tile(index)] = jnp.where(lane, doubled[0], doubled[1]).astype(jnp.bfloat16)
        a, b = halves(rows_ref[:, lane_tile(index)])
        dup_rows[2 * index] = a
        dup_rows[2 * index + 1] = b
        return carry

    lax.fori_loop(0, coef_ref.shape[1] // (2 * LANES), one_tile, 0, unroll=2)
    pack_send(send_ref, out_ref, dup_coef, dup_rows, owners, capacity, px)


def build_tables(recv_ref, coef_ref, rows_ref, coef_table, feature_table, target_table):
    owners, recv_rows, _ = recv_ref.shape
    px = coef_ref.shape[0]
    pairs = recv_rows // (px + 8)
    own_tiles = coef_ref.shape[1] // LANES
    own = 2 * own_tiles
    row = lax.broadcasted_iota(jnp.int32, (LANES, LANES), 0)
    column = lax.broadcasted_iota(jnp.int32, (LANES, LANES), 1)
    unit = jnp.where(row == column, 1.0, 0.0).astype(jnp.bfloat16)

    def put(entry, coef, rows):
        turned = bdot(unit, coef, NT).astype(jnp.bfloat16)
        coef_table[entry] = turned[:64]
        coef_table[entry + 1] = turned[64:]
        a, b = halves(source_features(rows))
        feature_table[entry] = a.astype(jnp.bfloat16)
        feature_table[entry + 1] = b.astype(jnp.bfloat16)

    def one_own(index, carry):
        rows = rows_ref[:, lane_tile(index)]
        put(2 * index, coef_ref[:, lane_tile(index)], rows)
        features = target_features(rows).astype(jnp.bfloat16)
        turned = bdot(unit, jnp.concatenate([features] * 8, axis=0), NT)[:, :16]
        target_table[2 * index] = turned[:64].astype(jnp.bfloat16)
        target_table[2 * index + 1] = turned[64:].astype(jnp.bfloat16)
        return carry

    lax.fori_loop(0, own_tiles, one_own, 0, unroll=4)

    def one_owner(owner, carry):
        for pair in range(0, pairs, 2):
            start = pairs * px + pair * 8
            both = recv_ref[owner, start:start + 16, :].astype(jnp.float32)
            for part in range(2):
                where = pair + part
                put(
                    own + owner * (2 * pairs) + 2 * where,
                    recv_ref[owner, where * px:(where + 1) * px, :],
                    both[8 * part:8 * part + 8],
                )
        return carry

    lax.fori_loop(0, owners, one_owner, 0)
    last = own + owners * pairs * 2
    coef_table[last] = jnp.zeros((64, px), jnp.bfloat16)
    place = lax.broadcasted_iota(jnp.int32, (8, LANES), 0)
    nothing = source_features(jnp.where(place == 3, FAR_AWAY, 0.0))
    feature_table[last] = nothing.astype(jnp.bfloat16)


def sweep(index_ref, turns_ref, coef_table, feature_table, target_table, first_buffer, second_buffer, acc):
    clusters = turns_ref.shape[0]
    slots_end = index_ref.shape[1] // CHUNK - 1
    lane = lax.broadcasted_iota(jnp.int32, (16, LANES), 1) < 64
    acc[...] = jnp.zeros_like(acc)

    def partners(unit):
        target, turn = unit
        return [index_ref[target, turn * CHUNK + m] for m in range(CHUNK)]

    def tiles(units, buffer):
        for place, unit in enumerate(units):
            ids = partners(unit)
            sources = [
                jnp.where(lane, feature_table[ids[m]], feature_table[ids[m + 1]])
                for m in range(0, CHUNK, 2)
            ]
            power = bdot(target_table[unit[0]], jnp.concatenate(sources, axis=1), NN)
            buffer[place] = jnp.exp2(power).astype(jnp.bfloat16)

    def products(units, buffer):
        for place, unit in enumerate(units):
            coefs = jnp.concatenate([coef_table[i] for i in partners(unit)], axis=0)
            acc[unit[0]] += bdot(buffer[place], coefs, NN)

    def following(unit):
        target, turn = unit
        over = turn + 1 >= turns_ref[target]
        later = jnp.where(over, target + 1, target)
        end = later >= clusters
        turn = jnp.where(end, slots_end, jnp.where(over, 0, turn + 1))
        return jnp.minimum(later, clusters - 1), turn

    def next_units(unit):
        units = []
        for _ in range(UNITS):
            unit = following(unit)
            units.append(unit)
        return tuple(units)

    def two_sets(_, units):
        second = next_units(units[-1])
        third = next_units(second[-1])
        tiles(second, second_buffer)
        products(units, first_buffer)
        tiles(third, first_buffer)
        products(second, second_buffer)
        return third

    total = lax.fori_loop(0, clusters, lambda c, n: n + turns_ref[c], jnp.int32(0))
    unit = (jnp.int32(0), jnp.int32(0))
    start = (unit,) + next_units(unit)[:-1]
    tiles(start, first_buffer)
    lax.fori_loop(0, (total + 2 * UNITS - 1) // (2 * UNITS), two_sets, start)


def fine_kernel(index_ref, turns_ref, recv_ref, coef_ref, rows_ref, out_ref, *scratch):
    tables, acc = scratch[:3], scratch[-1]
    build_tables(recv_ref, coef_ref, rows_ref, *tables)
    sweep(index_ref, turns_ref, *scratch)

    def one_tile(index, carry):
        pair = jnp.concatenate([acc[2 * index], acc[2 * index + 1]], axis=0)
        out_ref[:, lane_tile(index)] = pair.T
        return carry

    lax.fori_loop(0, turns_ref.shape[0] // 2, one_tile, 0, unroll=4)


def coarse_kernel(
    index_ref,
    turns_ref,
    recv_ref,
    coef_ref,
    rows_ref,
    fine_ref,
    transfer_ref,
    probes_ref,
    out_ref,
    gram_ref,
    *scratch,
):
    tables, acc = scratch[:3], scratch[-1]
    build_tables(recv_ref, coef_ref, rows_ref, *tables)
    sweep(index_ref, turns_ref, *scratch)
    gram_ref[...] = jnp.zeros_like(gram_ref)

    def one_group(group, carry):
        gram = None
        for part in range(4):
            q = group * 4 + part
            twice = jnp.concatenate([acc[q]] * 2, axis=0).T.astype(jnp.bfloat16)
            matrix = transfer_ref[:, lane_tile(q)].astype(jnp.float32)
            low = lax.broadcasted_iota(jnp.int32, matrix.shape, 1) < 64
            matrix = jnp.concatenate(
                [jnp.where(low, matrix, 0.0), jnp.where(low, 0.0, matrix)], axis=0
            ).astype(jnp.bfloat16)
            total = fine_ref[:, lane_tile(q)] + bdot(twice, matrix, NT)
            out_ref[:, lane_tile(q)] = total
            high = total.astype(jnp.bfloat16)
            rest = (total - high.astype(jnp.float32)).astype(jnp.bfloat16)
            probes = probes_ref[:, lane_tile(q)]
            term = bdot(probes, high, NT) + bdot(probes, rest, NT)
            gram = term if gram is None else gram + term
        gram_ref[...] += gram
        return carry

    lax.fori_loop(0, turns_ref.shape[0] // 4, one_group, 0)


def sweep_scratch(total, clusters, px):
    return [
        pltpu.VMEM((total + 1, 64, px), jnp.bfloat16),
        pltpu.VMEM((total + 1, 16, LANES), jnp.bfloat16),
        pltpu.VMEM((clusters, 64, 16), jnp.bfloat16),
        pltpu.VMEM((UNITS, 64, CHUNK * 64), jnp.bfloat16),
        pltpu.VMEM((UNITS, 64, CHUNK * 64), jnp.bfloat16),
        pltpu.VMEM((clusters, 64, px), jnp.float32),
    ]


def live_index(slots, counts, nothing):
    place = lax.broadcasted_iota(jnp.int32, slots.shape, 1)
    index = jnp.where(place < counts[:, None], slots, nothing)
    index = jnp.pad(index, ((0, 0), (0, CHUNK)), constant_values=nothing)
    turns = (counts + CHUNK - 1) // CHUNK
    return index, turns


def shards(
    coef_fine,
    points_fine,
    points_coarse,
    transfer,
    send_fine,
    slots_fine,
    counts_fine,
    send_coarse,
    slots_coarse,
    counts_coarse,
):
    probes = coef_fine.shape[0]
    fine_count = counts_fine.shape[0]
    coarse_count = counts_coarse.shape[0]
    owners = lax.axis_size("leaf")
    groups = lax.axis_size("probe")
    px = -(-probes // 16) * 16
    coef = coef_fine if px == probes else jnp.pad(coef_fine, ((0, px - probes), (0, 0)))
    send_fine = send_fine.reshape(owners, -1)
    send_coarse = send_coarse.reshape(owners, -1)
    cap_fine = send_fine.shape[1]
    cap_coarse = send_coarse.shape[1]
    params = pltpu.CompilerParams(vmem_limit_bytes=VMEM)
    smem = pl.BlockSpec(memory_space=pltpu.SMEM)
    vmem = pl.BlockSpec(memory_space=pltpu.VMEM)
    bf16, f32 = jnp.bfloat16, jnp.float32

    turned = [coef_fine]
    for step in range(1, groups):
        turned.append(lax.ppermute(coef_fine, "probe", [(i, (i + step) % groups) for i in range(groups)]))
    all_probes = jnp.concatenate(turned, axis=0)

    fine_send, fine_rows = pl.pallas_call(
        pack_fine_kernel,
        out_shape=(
            jax.ShapeDtypeStruct((owners, (cap_fine // 2) * (px + 8), LANES), bf16),
            jax.ShapeDtypeStruct((8, points_fine.shape[1]), f32),
        ),
        in_specs=[smem, vmem, vmem],
        out_specs=[vmem, vmem],
        scratch_shapes=[
            pltpu.VMEM((fine_count, px, LANES), f32),
            pltpu.VMEM((fine_count, 8, LANES), f32),
        ],
        compiler_params=params,
        name="pack_fine",
    )(send_fine, coef, points_fine)
    fine_recv = lax.all_to_all(fine_send, "leaf", split_axis=0, concat_axis=0, tiled=True)

    coarse_send, coarse_rows, coarse_coef = pl.pallas_call(
        pack_coarse_kernel,
        out_shape=(
            jax.ShapeDtypeStruct((owners, (cap_coarse // 2) * (px + 8), LANES), bf16),
            jax.ShapeDtypeStruct((8, points_coarse.shape[1]), f32),
            jax.ShapeDtypeStruct((px, points_coarse.shape[1]), bf16),
        ),
        in_specs=[smem, vmem, vmem, vmem],
        out_specs=[vmem, vmem, vmem],
        scratch_shapes=[
            pltpu.VMEM((coarse_count, px, LANES), f32),
            pltpu.VMEM((coarse_count, 8, LANES), f32),
        ],
        compiler_params=params,
        name="pack_coarse",
    )(send_coarse, coef, transfer, points_coarse)
    coarse_recv = lax.all_to_all(coarse_send, "leaf", split_axis=0, concat_axis=0, tiled=True)

    fine_total = fine_count + owners * cap_fine
    coarse_total = coarse_count + owners * cap_coarse
    fine_index, fine_turns = live_index(slots_fine, counts_fine, fine_total)
    coarse_index, coarse_turns = live_index(slots_coarse, counts_coarse, coarse_total)

    fine_far = pl.pallas_call(
        fine_kernel,
        out_shape=jax.ShapeDtypeStruct((px, points_fine.shape[1]), f32),
        in_specs=[smem, smem, vmem, vmem, vmem],
        out_specs=vmem,
        scratch_shapes=sweep_scratch(fine_total, fine_count, px),
        compiler_params=params,
        name="fine_sweep",
    )(fine_index, fine_turns, fine_recv, coef, fine_rows)

    far, gram = pl.pallas_call(
        coarse_kernel,
        out_shape=(
            jax.ShapeDtypeStruct((px, points_fine.shape[1]), f32),
            jax.ShapeDtypeStruct((all_probes.shape[0], px), f32),
        ),
        in_specs=[smem, smem] + [vmem] * 6,
        out_specs=[vmem, vmem],
        scratch_shapes=sweep_scratch(coarse_total, coarse_count, px),
        compiler_params=params,
        name="coarse_sweep",
    )(coarse_index, coarse_turns, coarse_recv, coarse_coef, coarse_rows, fine_far, transfer, all_probes)

    far_field = far[:probes]
    blocks = gram[:, :probes].reshape(groups, probes * probes)
    blocks = blocks[(lax.axis_index("probe") - jnp.arange(groups)) % groups]
    blocks = jnp.broadcast_to(blocks[None], (owners, groups, probes * probes))
    blocks = blocks.reshape(owners * groups, 1, probes * probes)
    blocks = lax.all_to_all(blocks, ("leaf", "probe"), split_axis=0, concat_axis=0, tiled=True)
    total = jnp.sum(blocks.reshape(owners, groups, probes, probes), axis=0)
    gram_scale = 1.0 / math.sqrt(owners * fine_count * 64)
    probe_gram = total.transpose(1, 0, 2).reshape(probes, groups * probes) * gram_scale
    return (far_field, probe_gram)


def solution(mesh):
    return jax.shard_map(
        shards,
        mesh=mesh,
        in_specs=(
            P("probe", "leaf"),
            P(None, "leaf"),
            P(None, "leaf"),
            P(None, "leaf"),
            P("leaf", None, None),
            P("leaf", None),
            P("leaf"),
            P("leaf", None, None),
            P("leaf", None),
            P("leaf"),
        ),
        out_specs=(P("probe", "leaf"), P("probe", None)),
        check_vma=False,
    )
```

```python
import functools
import math

import jax
import jax.numpy as jnp
from jax import lax
from jax.experimental import pallas as pl
from jax.experimental.pallas import tpu as pltpu
from jax.sharding import PartitionSpec as P

KERNEL_RATE = 1.5
POINT_SCALE = math.sqrt(2.0 * KERNEL_RATE * math.log2(math.e))
LANES = 128
UNITS = 8
QUAD = 4
CHUNK = 8
FAR_AWAY = -30000.0
VMEM = 56 * 1024 * 1024

NT = (((1,), (1,)), ((), ()))
NN = (((1,), (0,)), ((), ()))


def bdot(a, b, dims):
    return lax.dot_general(a, b, dims, preferred_element_type=jnp.float32)


def split_rows(points):
    v = points * POINT_SCALE
    norm = -0.5 * (v[0:1] * v[0:1] + v[1:2] * v[1:2] + v[2:3] * v[2:3])
    full = jnp.concatenate([v, norm], axis=0)
    high = full.astype(jnp.bfloat16).astype(jnp.float32)
    rest = (full - high).astype(jnp.bfloat16).astype(jnp.float32)
    return jnp.concatenate([high, rest], axis=0)


def source_features(rows):
    place = lax.broadcasted_iota(jnp.int32, rows.shape, 0)
    one = jnp.where((place == 3) | (place == 7), 1.0, 0.0)
    return jnp.concatenate([rows, jnp.where(place < 3, rows, one)], axis=0)


def target_features(rows):
    place = lax.broadcasted_iota(jnp.int32, rows.shape, 0)
    turned = jnp.concatenate([rows[4:8], rows[0:4]], axis=0)
    one = jnp.where((place == 3) | (place == 7), 1.0, jnp.where(place < 3, rows, turned))
    return jnp.concatenate([one, turned], axis=0)


def halves(tile):
    lane = lax.broadcasted_iota(jnp.int32, tile.shape, 1)
    turned = pltpu.roll(tile, LANES // 2, 1)
    low = lane < LANES // 2
    return jnp.where(low, tile, turned), jnp.where(low, turned, tile)


def lane_tile(index):
    return pl.ds(pl.multiple_of(index * LANES, LANES), LANES)


def pack_send(send_ref, out_ref, dup_coef, dup_rows, owners, capacity, px):
    pairs = capacity // 2
    lane = lax.broadcasted_iota(jnp.int32, (px, LANES), 1) < LANES // 2
    lane8 = lax.broadcasted_iota(jnp.int32, (8, LANES), 1) < LANES // 2

    def one_owner(owner, carry):
        before = None
        for pair in range(pairs):
            first = send_ref[owner, 2 * pair]
            second = send_ref[owner, 2 * pair + 1]
            out_ref[owner, pair * px:(pair + 1) * px, :] = jnp.where(
                lane, dup_coef[first], dup_coef[second]
            ).astype(jnp.bfloat16)
            rows = jnp.where(lane8, dup_rows[first], dup_rows[second])
            if pair % 2 == 0:
                before = rows
            else:
                start = pairs * px + (pair - 1) * 8
                out_ref[owner, start:start + 16, :] = jnp.concatenate(
                    [before, rows], axis=0
                ).astype(jnp.bfloat16)
        return carry

    lax.fori_loop(0, owners, one_owner, 0)


def pack_fine_kernel(send_ref, coef_ref, points_ref, out_ref, rows_ref, dup_coef, dup_rows):
    owners, capacity = send_ref.shape
    px = coef_ref.shape[0]
    rows_ref[...] = split_rows(points_ref[...])

    def one_tile(index, carry):
        a, b = halves(coef_ref[:, lane_tile(index)].astype(jnp.float32))
        dup_coef[2 * index] = a
        dup_coef[2 * index + 1] = b
        a, b = halves(rows_ref[:, lane_tile(index)])
        dup_rows[2 * index] = a
        dup_rows[2 * index + 1] = b
        return carry

    lax.fori_loop(0, coef_ref.shape[1] // LANES, one_tile, 0, unroll=4)
    pack_send(send_ref, out_ref, dup_coef, dup_rows, owners, capacity, px)


def pack_coarse_kernel(
    send_ref, coef_ref, transfer_ref, points_ref, out_ref, rows_ref, coarse_ref, dup_coef, dup_rows
):
    owners, capacity = send_ref.shape
    px = coef_ref.shape[0]
    rows_ref[...] = split_rows(points_ref[...])

    def one_tile(index, carry):
        doubled = []
        for part in range(2):
            q = 2 * index + part
            a, b = halves(transfer_ref[:, lane_tile(q)].astype(jnp.float32))
            matrix = jnp.concatenate([a, b], axis=0).astype(jnp.bfloat16)
            block = bdot(coef_ref[:, lane_tile(q)], matrix, NN)
            dup_coef[q] = block
            doubled.append(block)
        lane = lax.broadcasted_iota(jnp.int32, (px, LANES), 1) < LANES // 2
        coarse_ref[:, lane_tile(index)] = jnp.where(lane, doubled[0], doubled[1]).astype(jnp.bfloat16)
        a, b = halves(rows_ref[:, lane_tile(index)])
        dup_rows[2 * index] = a
        dup_rows[2 * index + 1] = b
        return carry

    lax.fori_loop(0, coef_ref.shape[1] // (2 * LANES), one_tile, 0, unroll=2)
    pack_send(send_ref, out_ref, dup_coef, dup_rows, owners, capacity, px)


def build_tables(recv_ref, coef_ref, rows_ref, coef_table, feature_table, target_table):
    owners, recv_rows, _ = recv_ref.shape
    px = coef_ref.shape[0]
    pairs = recv_rows // (px + 8)
    own_tiles = coef_ref.shape[1] // LANES
    own = 2 * own_tiles
    row = lax.broadcasted_iota(jnp.int32, (LANES, LANES), 0)
    column = lax.broadcasted_iota(jnp.int32, (LANES, LANES), 1)
    unit = jnp.where(row == column, 1.0, 0.0).astype(jnp.bfloat16)

    def put(entry, coef, rows):
        a, b = halves(coef.astype(jnp.float32))
        coef_table[entry] = a.astype(jnp.bfloat16)
        coef_table[entry + 1] = b.astype(jnp.bfloat16)
        a, b = halves(source_features(rows))
        feature_table[entry] = a.astype(jnp.bfloat16)
        feature_table[entry + 1] = b.astype(jnp.bfloat16)

    def one_own(index, carry):
        rows = rows_ref[:, lane_tile(index)]
        put(2 * index, coef_ref[:, lane_tile(index)], rows)
        features = target_features(rows).astype(jnp.bfloat16)
        turned = bdot(unit, jnp.concatenate([features] * 8, axis=0), NT)[:, :16 * QUAD]
        target_table[2 * index] = turned[:64].astype(jnp.bfloat16)
        target_table[2 * index + 1] = turned[64:].astype(jnp.bfloat16)
        return carry

    lax.fori_loop(0, own_tiles, one_own, 0, unroll=4)

    def one_owner(owner, carry):
        for pair in range(0, pairs, 2):
            start = pairs * px + pair * 8
            both = recv_ref[owner, start:start + 16, :].astype(jnp.float32)
            for part in range(2):
                where = pair + part
                put(
                    own + owner * (2 * pairs) + 2 * where,
                    recv_ref[owner, where * px:(where + 1) * px, :],
                    both[8 * part:8 * part + 8],
                )
        return carry

    lax.fori_loop(0, owners, one_owner, 0)
    last = own + owners * pairs * 2
    coef_table[last] = jnp.zeros((px, LANES), jnp.bfloat16)
    place = lax.broadcasted_iota(jnp.int32, (8, LANES), 0)
    nothing = source_features(jnp.where(place == 3, FAR_AWAY, 0.0))
    feature_table[last] = nothing.astype(jnp.bfloat16)


def sweep(index_ref, turns_ref, coef_table, feature_table, target_table, first_buffer, second_buffer, acc):
    clusters = turns_ref.shape[0]
    px = coef_table.shape[1]
    slots_end = index_ref.shape[1] // CHUNK - 1
    lane = lax.broadcasted_iota(jnp.int32, (16, LANES), 1) < 64
    lane_x = lax.broadcasted_iota(jnp.int32, (px, LANES), 1) < 64
    owner = lax.broadcasted_iota(jnp.int32, (64, 16 * QUAD), 1) // 16
    blank = jnp.zeros((64, 16 * QUAD), jnp.bfloat16)
    acc[...] = jnp.zeros_like(acc)

    def pairs_of(unit, table, low):
        target, turn = unit
        ids = [index_ref[target, turn * CHUNK + m] for m in range(CHUNK)]
        return jnp.concatenate(
            [jnp.where(low, table[ids[m]], table[ids[m + 1]]) for m in range(0, CHUNK, 2)], axis=1
        )

    def tiles(units, buffer):
        for start in range(0, UNITS, QUAD):
            quad = units[start:start + QUAD]
            targets = jnp.concatenate(
                [jnp.where(owner == u, target_table[quad[u][0]], blank) for u in range(QUAD)], axis=0
            )
            sources = jnp.concatenate([pairs_of(unit, feature_table, lane) for unit in quad], axis=0)
            for part in range(0, CHUNK * 64, 256):
                power = bdot(targets, sources[:, part:part + 256], NN)
                buffer[start * 64:(start + QUAD) * 64, part:part + 256] = jnp.exp2(power).astype(
                    jnp.bfloat16
                )

    def products(units, buffer):
        for start in range(0, UNITS, QUAD):
            quad = units[start:start + QUAD]
            coefs = jnp.concatenate([pairs_of(unit, coef_table, lane_x) for unit in quad], axis=0)
            product = bdot(coefs, buffer[start * 64:(start + QUAD) * 64], NT)
            for u in range(QUAD):
                side = (u // 2) * LANES
                acc[u % 2, quad[u][0]] += product[u * px:(u + 1) * px, side:side + LANES]

    def following(unit):
        target, turn = unit
        over = turn + 1 >= turns_ref[target]
        later = jnp.where(over, target + 1, target)
        end = later >= clusters
        turn = jnp.where(end, slots_end, jnp.where(over, 0, turn + 1))
        return jnp.minimum(later, clusters - 1), turn

    def next_units(unit):
        units = []
        for _ in range(UNITS):
            unit = following(unit)
            units.append(unit)
        return tuple(units)

    def two_sets(_, units):
        second = next_units(units[-1])
        third = next_units(second[-1])
        tiles(second, second_buffer)
        products(units, first_buffer)
        tiles(third, first_buffer)
        products(second, second_buffer)
        return third

    total = lax.fori_loop(0, clusters, lambda c, n: n + turns_ref[c], jnp.int32(0))
    unit = (jnp.int32(0), jnp.int32(0))
    start = (unit,) + next_units(unit)[:-1]
    tiles(start, first_buffer)
    lax.fori_loop(0, (total + 2 * UNITS - 1) // (2 * UNITS), two_sets, start)


def summed(acc, target):
    low = lax.broadcasted_iota(jnp.int32, acc.shape[2:], 1) < 64
    here = jnp.where(low, acc[0, target], acc[1, target])
    return here + pltpu.roll(here, 64, 1)


def fine_kernel(index_ref, turns_ref, recv_ref, coef_ref, rows_ref, out_ref, *scratch):
    tables, acc = scratch[:3], scratch[-1]
    build_tables(recv_ref, coef_ref, rows_ref, *tables)
    sweep(index_ref, turns_ref, *scratch)
    low = lax.broadcasted_iota(jnp.int32, (coef_ref.shape[0], LANES), 1) < 64

    def one_tile(index, carry):
        out_ref[:, lane_tile(index)] = jnp.where(low, summed(acc, 2 * index), summed(acc, 2 * index + 1))
        return carry

    lax.fori_loop(0, turns_ref.shape[0] // 2, one_tile, 0, unroll=4)


def coarse_kernel(
    index_ref,
    turns_ref,
    recv_ref,
    coef_ref,
    rows_ref,
    fine_ref,
    transfer_ref,
    probes_ref,
    out_ref,
    gram_ref,
    *scratch,
):
    tables, acc = scratch[:3], scratch[-1]
    build_tables(recv_ref, coef_ref, rows_ref, *tables)
    sweep(index_ref, turns_ref, *scratch)
    gram_ref[...] = jnp.zeros_like(gram_ref)

    def one_group(group, carry):
        gram = None
        for part in range(4):
            q = group * 4 + part
            twice = summed(acc, q).astype(jnp.bfloat16)
            matrix = transfer_ref[:, lane_tile(q)].astype(jnp.float32)
            low = lax.broadcasted_iota(jnp.int32, matrix.shape, 1) < 64
            matrix = jnp.concatenate(
                [jnp.where(low, matrix, 0.0), jnp.where(low, 0.0, matrix)], axis=0
            ).astype(jnp.bfloat16)
            total = fine_ref[:, lane_tile(q)] + bdot(twice, matrix, NT)
            out_ref[:, lane_tile(q)] = total
            high = total.astype(jnp.bfloat16)
            rest = (total - high.astype(jnp.float32)).astype(jnp.bfloat16)
            probes = probes_ref[:, lane_tile(q)]
            term = bdot(probes, high, NT) + bdot(probes, rest, NT)
            gram = term if gram is None else gram + term
        gram_ref[...] += gram
        return carry

    lax.fori_loop(0, turns_ref.shape[0] // 4, one_group, 0)


def sweep_scratch(total, clusters, px):
    return [
        pltpu.VMEM((total + 1, px, LANES), jnp.bfloat16),
        pltpu.VMEM((total + 1, 16, LANES), jnp.bfloat16),
        pltpu.VMEM((clusters, 64, 16 * QUAD), jnp.bfloat16),
        pltpu.VMEM((UNITS * 64, CHUNK * 64), jnp.bfloat16),
        pltpu.VMEM((UNITS * 64, CHUNK * 64), jnp.bfloat16),
        pltpu.VMEM((2, clusters, px, LANES), jnp.float32),
    ]


def live_index(slots, counts, nothing):
    place = lax.broadcasted_iota(jnp.int32, slots.shape, 1)
    index = jnp.where(place < counts[:, None], slots, nothing)
    index = jnp.pad(index, ((0, 0), (0, CHUNK)), constant_values=nothing)
    turns = (counts + CHUNK - 1) // CHUNK
    return index, turns


def shards(
    coef_fine,
    points_fine,
    points_coarse,
    transfer,
    send_fine,
    slots_fine,
    counts_fine,
    send_coarse,
    slots_coarse,
    counts_coarse,
):
    probes = coef_fine.shape[0]
    fine_count = counts_fine.shape[0]
    coarse_count = counts_coarse.shape[0]
    owners = lax.axis_size("leaf")
    groups = lax.axis_size("probe")
    px = -(-probes // 16) * 16
    coef = coef_fine if px == probes else jnp.pad(coef_fine, ((0, px - probes), (0, 0)))
    send_fine = send_fine.reshape(owners, -1)
    send_coarse = send_coarse.reshape(owners, -1)
    cap_fine = send_fine.shape[1]
    cap_coarse = send_coarse.shape[1]
    params = pltpu.CompilerParams(vmem_limit_bytes=VMEM)
    smem = pl.BlockSpec(memory_space=pltpu.SMEM)
    vmem = pl.BlockSpec(memory_space=pltpu.VMEM)
    bf16, f32 = jnp.bfloat16, jnp.float32

    turned = [coef_fine]
    for step in range(1, groups):
        turned.append(lax.ppermute(coef_fine, "probe", [(i, (i + step) % groups) for i in range(groups)]))
    all_probes = jnp.concatenate(turned, axis=0)

    fine_send, fine_rows = pl.pallas_call(
        pack_fine_kernel,
        out_shape=(
            jax.ShapeDtypeStruct((owners, (cap_fine // 2) * (px + 8), LANES), bf16),
            jax.ShapeDtypeStruct((8, points_fine.shape[1]), f32),
        ),
        in_specs=[smem, vmem, vmem],
        out_specs=[vmem, vmem],
        scratch_shapes=[
            pltpu.VMEM((fine_count, px, LANES), f32),
            pltpu.VMEM((fine_count, 8, LANES), f32),
        ],
        compiler_params=params,
        name="pack_fine",
    )(send_fine, coef, points_fine)
    fine_recv = lax.all_to_all(fine_send, "leaf", split_axis=0, concat_axis=0, tiled=True)

    coarse_send, coarse_rows, coarse_coef = pl.pallas_call(
        pack_coarse_kernel,
        out_shape=(
            jax.ShapeDtypeStruct((owners, (cap_coarse // 2) * (px + 8), LANES), bf16),
            jax.ShapeDtypeStruct((8, points_coarse.shape[1]), f32),
            jax.ShapeDtypeStruct((px, points_coarse.shape[1]), bf16),
        ),
        in_specs=[smem, vmem, vmem, vmem],
        out_specs=[vmem, vmem, vmem],
        scratch_shapes=[
            pltpu.VMEM((coarse_count, px, LANES), f32),
            pltpu.VMEM((coarse_count, 8, LANES), f32),
        ],
        compiler_params=params,
        name="pack_coarse",
    )(send_coarse, coef, transfer, points_coarse)
    coarse_recv = lax.all_to_all(coarse_send, "leaf", split_axis=0, concat_axis=0, tiled=True)

    fine_total = fine_count + owners * cap_fine
    coarse_total = coarse_count + owners * cap_coarse
    fine_index, fine_turns = live_index(slots_fine, counts_fine, fine_total)
    coarse_index, coarse_turns = live_index(slots_coarse, counts_coarse, coarse_total)

    fine_far = pl.pallas_call(
        fine_kernel,
        out_shape=jax.ShapeDtypeStruct((px, points_fine.shape[1]), f32),
        in_specs=[smem, smem, vmem, vmem, vmem],
        out_specs=vmem,
        scratch_shapes=sweep_scratch(fine_total, fine_count, px),
        compiler_params=params,
        name="fine_sweep",
    )(fine_index, fine_turns, fine_recv, coef, fine_rows)

    far, gram = pl.pallas_call(
        coarse_kernel,
        out_shape=(
            jax.ShapeDtypeStruct((px, points_fine.shape[1]), f32),
            jax.ShapeDtypeStruct((all_probes.shape[0], px), f32),
        ),
        in_specs=[smem, smem] + [vmem] * 6,
        out_specs=[vmem, vmem],
        scratch_shapes=sweep_scratch(coarse_total, coarse_count, px),
        compiler_params=params,
        name="coarse_sweep",
    )(coarse_index, coarse_turns, coarse_recv, coarse_coef, coarse_rows, fine_far, transfer, all_probes)

    far_field = far[:probes]
    blocks = gram[:, :probes].reshape(groups, probes * probes)
    blocks = blocks[(lax.axis_index("probe") - jnp.arange(groups)) % groups]
    blocks = jnp.broadcast_to(blocks[None], (owners, groups, probes * probes))
    blocks = blocks.reshape(owners * groups, 1, probes * probes)
    blocks = lax.all_to_all(blocks, ("leaf", "probe"), split_axis=0, concat_axis=0, tiled=True)
    total = jnp.sum(blocks.reshape(owners, groups, probes, probes), axis=0)
    gram_scale = 1.0 / math.sqrt(owners * fine_count * 64)
    probe_gram = total.transpose(1, 0, 2).reshape(probes, groups * probes) * gram_scale
    return (far_field, probe_gram)


def solution(mesh):
    return jax.shard_map(
        shards,
        mesh=mesh,
        in_specs=(
            P("probe", "leaf"),
            P(None, "leaf"),
            P(None, "leaf"),
            P(None, "leaf"),
            P("leaf", None, None),
            P("leaf", None),
            P("leaf"),
            P("leaf", None, None),
            P("leaf", None),
            P("leaf"),
        ),
        out_specs=(P("probe", "leaf"), P("probe", None)),
        check_vma=False,
    )
```

```python
import functools
import math

import jax
import jax.numpy as jnp
from jax import lax
from jax.experimental import pallas as pl
from jax.experimental.pallas import tpu as pltpu
from jax.sharding import PartitionSpec as P

KERNEL_RATE = 1.5
POINT_SCALE = math.sqrt(2.0 * KERNEL_RATE * math.log2(math.e))
LANES = 128
UNITS = 8
QUAD = 4
CHUNK = 8
FAR_AWAY = -30000.0
VMEM = 56 * 1024 * 1024

NT = (((1,), (1,)), ((), ()))
NN = (((1,), (0,)), ((), ()))


def bdot(a, b, dims):
    return lax.dot_general(a, b, dims, preferred_element_type=jnp.float32)


def split_rows(points):
    v = points * POINT_SCALE
    norm = -0.5 * (v[0:1] * v[0:1] + v[1:2] * v[1:2] + v[2:3] * v[2:3])
    full = jnp.concatenate([v, norm], axis=0)
    high = full.astype(jnp.bfloat16).astype(jnp.float32)
    rest = (full - high).astype(jnp.bfloat16).astype(jnp.float32)
    return jnp.concatenate([high, rest], axis=0)


def source_features(rows):
    place = lax.broadcasted_iota(jnp.int32, rows.shape, 0)
    one = jnp.where((place == 3) | (place == 7), 1.0, 0.0)
    return jnp.concatenate([rows, jnp.where(place < 3, rows, one)], axis=0)


def target_features(rows):
    place = lax.broadcasted_iota(jnp.int32, rows.shape, 0)
    turned = jnp.concatenate([rows[4:8], rows[0:4]], axis=0)
    one = jnp.where((place == 3) | (place == 7), 1.0, jnp.where(place < 3, rows, turned))
    return jnp.concatenate([one, turned], axis=0)


def halves(tile):
    lane = lax.broadcasted_iota(jnp.int32, tile.shape, 1)
    turned = pltpu.roll(tile, LANES // 2, 1)
    low = lane < LANES // 2
    return jnp.where(low, tile, turned), jnp.where(low, turned, tile)


def lane_tile(index):
    return pl.ds(pl.multiple_of(index * LANES, LANES), LANES)


def pack_send(send_ref, out_ref, dup_coef, dup_rows, owners, capacity, px):
    pairs = capacity // 2
    lane = lax.broadcasted_iota(jnp.int32, (px, LANES), 1) < LANES // 2
    lane8 = lax.broadcasted_iota(jnp.int32, (8, LANES), 1) < LANES // 2

    def one_owner(owner, carry):
        before = None
        for pair in range(pairs):
            first = send_ref[owner, 2 * pair]
            second = send_ref[owner, 2 * pair + 1]
            out_ref[owner, pair * px:(pair + 1) * px, :] = jnp.where(
                lane, dup_coef[first], dup_coef[second]
            ).astype(jnp.bfloat16)
            rows = jnp.where(lane8, dup_rows[first], dup_rows[second])
            if pair % 2 == 0:
                before = rows
            else:
                start = pairs * px + (pair - 1) * 8
                out_ref[owner, start:start + 16, :] = jnp.concatenate(
                    [before, rows], axis=0
                ).astype(jnp.bfloat16)
        return carry

    lax.fori_loop(0, owners, one_owner, 0)


def pack_fine_kernel(send_ref, coef_ref, points_ref, out_ref, rows_ref, dup_coef, dup_rows):
    owners, capacity = send_ref.shape
    px = coef_ref.shape[0]
    rows_ref[...] = split_rows(points_ref[...])

    def one_tile(index, carry):
        a, b = halves(coef_ref[:, lane_tile(index)].astype(jnp.float32))
        dup_coef[2 * index] = a
        dup_coef[2 * index + 1] = b
        a, b = halves(rows_ref[:, lane_tile(index)])
        dup_rows[2 * index] = a
        dup_rows[2 * index + 1] = b
        return carry

    lax.fori_loop(0, coef_ref.shape[1] // LANES, one_tile, 0, unroll=4)
    pack_send(send_ref, out_ref, dup_coef, dup_rows, owners, capacity, px)


def pack_coarse_kernel(
    send_ref, coef_ref, transfer_ref, points_ref, out_ref, rows_ref, coarse_ref, dup_coef, dup_rows
):
    owners, capacity = send_ref.shape
    px = coef_ref.shape[0]
    rows_ref[...] = split_rows(points_ref[...])

    def one_tile(index, carry):
        doubled = []
        for part in range(2):
            q = 2 * index + part
            a, b = halves(transfer_ref[:, lane_tile(q)].astype(jnp.float32))
            matrix = jnp.concatenate([a, b], axis=0).astype(jnp.bfloat16)
            block = bdot(coef_ref[:, lane_tile(q)], matrix, NN)
            dup_coef[q] = block
            doubled.append(block)
        lane = lax.broadcasted_iota(jnp.int32, (px, LANES), 1) < LANES // 2
        coarse_ref[:, lane_tile(index)] = jnp.where(lane, doubled[0], doubled[1]).astype(jnp.bfloat16)
        a, b = halves(rows_ref[:, lane_tile(index)])
        dup_rows[2 * index] = a
        dup_rows[2 * index + 1] = b
        return carry

    lax.fori_loop(0, coef_ref.shape[1] // (2 * LANES), one_tile, 0, unroll=2)
    pack_send(send_ref, out_ref, dup_coef, dup_rows, owners, capacity, px)


def put_pair(entry, coef, rows, coef_table, feature_table):
    a, b = halves(coef.astype(jnp.float32))
    coef_table[entry] = a.astype(jnp.bfloat16)
    coef_table[entry + 1] = b.astype(jnp.bfloat16)
    a, b = halves(source_features(rows))
    feature_table[entry] = a.astype(jnp.bfloat16)
    feature_table[entry + 1] = b.astype(jnp.bfloat16)


def put_nothing(entry, coef_table, feature_table):
    coef_table[entry] = jnp.zeros(coef_table.shape[1:], jnp.bfloat16)
    place = lax.broadcasted_iota(jnp.int32, (8, LANES), 0)
    nothing = source_features(jnp.where(place == 3, FAR_AWAY, 0.0))
    feature_table[entry] = nothing.astype(jnp.bfloat16)


def build_own(coef_ref, rows_ref, coef_table, feature_table):
    tiles = coef_ref.shape[1] // LANES

    def one_tile(index, carry):
        tile = lane_tile(index)
        put_pair(2 * index, coef_ref[:, tile], rows_ref[:, tile], coef_table, feature_table)
        return carry

    lax.fori_loop(0, tiles, one_tile, 0, unroll=4)
    put_nothing(2 * tiles, coef_table, feature_table)


def build_received(recv_ref, coef_table, feature_table):
    owners, recv_rows, _ = recv_ref.shape
    px = coef_table.shape[1]
    pairs = recv_rows // (px + 8)

    def one_owner(owner, carry):
        for pair in range(0, pairs, 2):
            start = pairs * px + pair * 8
            both = recv_ref[owner, start:start + 16, :].astype(jnp.float32)
            for part in range(2):
                where = pair + part
                put_pair(
                    owner * (2 * pairs) + 2 * where,
                    recv_ref[owner, where * px:(where + 1) * px, :],
                    both[8 * part:8 * part + 8],
                    coef_table,
                    feature_table,
                )
        return carry

    lax.fori_loop(0, owners, one_owner, 0)
    put_nothing(owners * pairs * 2, coef_table, feature_table)


def build_targets(rows_ref, target_table):
    row = lax.broadcasted_iota(jnp.int32, (LANES, LANES), 0)
    column = lax.broadcasted_iota(jnp.int32, (LANES, LANES), 1)
    unit = jnp.where(row == column, 1.0, 0.0).astype(jnp.bfloat16)

    def one_tile(index, carry):
        features = target_features(rows_ref[:, lane_tile(index)]).astype(jnp.bfloat16)
        turned = bdot(unit, jnp.concatenate([features] * 8, axis=0), NT)[:, :16 * QUAD]
        target_table[2 * index] = turned[:64].astype(jnp.bfloat16)
        target_table[2 * index + 1] = turned[64:].astype(jnp.bfloat16)
        return carry

    lax.fori_loop(0, rows_ref.shape[1] // LANES, one_tile, 0, unroll=4)


def sweep(index_ref, turns_ref, coef_table, feature_table, target_table, first_buffer, second_buffer, acc):
    clusters = turns_ref.shape[0]
    px = coef_table.shape[1]
    slots_end = index_ref.shape[1] // CHUNK - 1
    lane = lax.broadcasted_iota(jnp.int32, (16, LANES), 1) < 64
    lane_x = lax.broadcasted_iota(jnp.int32, (px, LANES), 1) < 64
    owner = lax.broadcasted_iota(jnp.int32, (64, 16 * QUAD), 1) // 16
    blank = jnp.zeros((64, 16 * QUAD), jnp.bfloat16)
    acc[...] = jnp.zeros_like(acc)

    def pairs_of(unit, table, low):
        target, turn = unit
        ids = [index_ref[target, turn * CHUNK + m] for m in range(CHUNK)]
        return jnp.concatenate(
            [jnp.where(low, table[ids[m]], table[ids[m + 1]]) for m in range(0, CHUNK, 2)], axis=1
        )

    def tiles(units, buffer):
        for start in range(0, UNITS, QUAD):
            quad = units[start:start + QUAD]
            targets = jnp.concatenate(
                [jnp.where(owner == u, target_table[quad[u][0]], blank) for u in range(QUAD)], axis=0
            )
            sources = jnp.concatenate([pairs_of(unit, feature_table, lane) for unit in quad], axis=0)
            for part in range(0, CHUNK * 64, 256):
                power = bdot(targets, sources[:, part:part + 256], NN)
                buffer[start * 64:(start + QUAD) * 64, part:part + 256] = jnp.exp2(power).astype(
                    jnp.bfloat16
                )

    def products(units, buffer):
        for start in range(0, UNITS, QUAD):
            quad = units[start:start + QUAD]
            coefs = jnp.concatenate([pairs_of(unit, coef_table, lane_x) for unit in quad], axis=0)
            product = bdot(coefs, buffer[start * 64:(start + QUAD) * 64], NT)
            for u in range(QUAD):
                side = (u // 2) * LANES
                acc[u % 2, quad[u][0]] += product[u * px:(u + 1) * px, side:side + LANES]

    def following(unit):
        target, turn = unit
        over = turn + 1 >= turns_ref[target]
        later = jnp.where(over, target + 1, target)
        end = later >= clusters
        turn = jnp.where(end, slots_end, jnp.where(over, 0, turn + 1))
        return jnp.minimum(later, clusters - 1), turn

    def next_units(unit):
        units = []
        for _ in range(UNITS):
            unit = following(unit)
            units.append(unit)
        return tuple(units)

    def two_sets(_, units):
        second = next_units(units[-1])
        third = next_units(second[-1])
        tiles(second, second_buffer)
        products(units, first_buffer)
        tiles(third, first_buffer)
        products(second, second_buffer)
        return third

    total = lax.fori_loop(0, clusters, lambda c, n: n + turns_ref[c], jnp.int32(0))
    unit = (jnp.int32(0), jnp.int32(0))
    start = (unit,) + next_units(unit)[:-1]
    tiles(start, first_buffer)
    lax.fori_loop(0, (total + 2 * UNITS - 1) // (2 * UNITS), two_sets, start)


def summed(acc, target):
    low = lax.broadcasted_iota(jnp.int32, acc.shape[2:], 1) < 64
    here = jnp.where(low, acc[0, target], acc[1, target])
    return here + pltpu.roll(here, 64, 1)


def put_sums(acc, clusters, out_ref, before_ref=None):
    low = lax.broadcasted_iota(jnp.int32, acc.shape[2:], 1) < 64

    def one_tile(index, carry):
        tile = lane_tile(index)
        sums = jnp.where(low, summed(acc, 2 * index), summed(acc, 2 * index + 1))
        out_ref[:, tile] = sums if before_ref is None else before_ref[:, tile] + sums
        return carry

    lax.fori_loop(0, clusters // 2, one_tile, 0, unroll=4)


def own_kernel(
    fine_index_ref,
    fine_turns_ref,
    coarse_index_ref,
    coarse_turns_ref,
    fine_coef_ref,
    fine_rows_ref,
    coarse_coef_ref,
    coarse_rows_ref,
    fine_out_ref,
    coarse_out_ref,
    *scratch,
):
    acc = scratch[-1]
    for index_ref, turns_ref, coef_ref, rows_ref, out_ref in (
        (fine_index_ref, fine_turns_ref, fine_coef_ref, fine_rows_ref, fine_out_ref),
        (coarse_index_ref, coarse_turns_ref, coarse_coef_ref, coarse_rows_ref, coarse_out_ref),
    ):
        build_own(coef_ref, rows_ref, *scratch[:2])
        build_targets(rows_ref, scratch[2])
        sweep(index_ref, turns_ref, *scratch)
        put_sums(acc, turns_ref.shape[0], out_ref)


def fine_kernel(index_ref, turns_ref, recv_ref, rows_ref, own_ref, out_ref, *scratch):
    build_received(recv_ref, *scratch[:2])
    build_targets(rows_ref, scratch[2])
    sweep(index_ref, turns_ref, *scratch)
    put_sums(scratch[-1], turns_ref.shape[0], out_ref, own_ref)


def coarse_kernel(
    index_ref,
    turns_ref,
    recv_ref,
    rows_ref,
    own_ref,
    fine_ref,
    transfer_ref,
    probes_ref,
    out_ref,
    gram_ref,
    *scratch,
):
    acc = scratch[-1]
    build_received(recv_ref, *scratch[:2])
    build_targets(rows_ref, scratch[2])
    sweep(index_ref, turns_ref, *scratch)
    gram_ref[...] = jnp.zeros_like(gram_ref)

    def one_group(group, carry):
        gram = None
        for part in range(4):
            q = group * 4 + part
            own = halves(own_ref[:, lane_tile(group * 2 + part // 2)])[part % 2]
            twice = (summed(acc, q) + own).astype(jnp.bfloat16)
            matrix = transfer_ref[:, lane_tile(q)].astype(jnp.float32)
            low = lax.broadcasted_iota(jnp.int32, matrix.shape, 1) < 64
            matrix = jnp.concatenate(
                [jnp.where(low, matrix, 0.0), jnp.where(low, 0.0, matrix)], axis=0
            ).astype(jnp.bfloat16)
            total = fine_ref[:, lane_tile(q)] + bdot(twice, matrix, NT)
            out_ref[:, lane_tile(q)] = total
            high = total.astype(jnp.bfloat16)
            rest = (total - high.astype(jnp.float32)).astype(jnp.bfloat16)
            probes = probes_ref[:, lane_tile(q)]
            term = bdot(probes, high, NT) + bdot(probes, rest, NT)
            gram = term if gram is None else gram + term
        gram_ref[...] += gram
        return carry

    lax.fori_loop(0, turns_ref.shape[0] // 4, one_group, 0)


def sweep_scratch(total, clusters, px):
    return [
        pltpu.VMEM((total + 1, px, LANES), jnp.bfloat16),
        pltpu.VMEM((total + 1, 16, LANES), jnp.bfloat16),
        pltpu.VMEM((clusters, 64, 16 * QUAD), jnp.bfloat16),
        pltpu.VMEM((UNITS * 64, CHUNK * 64), jnp.bfloat16),
        pltpu.VMEM((UNITS * 64, CHUNK * 64), jnp.bfloat16),
        pltpu.VMEM((2, clusters, px, LANES), jnp.float32),
    ]


def slot_list(slots, chosen, nothing):
    width = slots.shape[1]
    before = jnp.tril(jnp.ones((width, width), jnp.float32)).T
    rank = jnp.dot(chosen.astype(jnp.float32), before).astype(jnp.int32) - 1
    place = lax.broadcasted_iota(jnp.int32, (1, 1, width + CHUNK), 2)
    moved = jnp.where(chosen, rank, -1)[:, :, None] == place
    index = nothing + jnp.sum(jnp.where(moved, (slots - nothing)[:, :, None], 0), axis=1)
    turns = (rank[:, -1] + CHUNK) // CHUNK
    return index, jnp.maximum(turns, 1)


def slot_lists(slots, counts, entries):
    clusters, width = slots.shape
    live = lax.broadcasted_iota(jnp.int32, slots.shape, 1) < counts[:, None]
    own = slot_list(slots, live & (slots < clusters), clusters)
    received = slot_list(slots - clusters, live & (slots >= clusters), entries)
    return own, received


def shards(
    coef_fine,
    points_fine,
    points_coarse,
    transfer,
    send_fine,
    slots_fine,
    counts_fine,
    send_coarse,
    slots_coarse,
    counts_coarse,
):
    probes = coef_fine.shape[0]
    fine_count = counts_fine.shape[0]
    coarse_count = counts_coarse.shape[0]
    owners = lax.axis_size("leaf")
    groups = lax.axis_size("probe")
    px = -(-probes // 16) * 16
    coef = coef_fine if px == probes else jnp.pad(coef_fine, ((0, px - probes), (0, 0)))
    send_fine = send_fine.reshape(owners, -1)
    send_coarse = send_coarse.reshape(owners, -1)
    cap_fine = send_fine.shape[1]
    cap_coarse = send_coarse.shape[1]
    params = pltpu.CompilerParams(vmem_limit_bytes=VMEM)
    smem = pl.BlockSpec(memory_space=pltpu.SMEM)
    vmem = pl.BlockSpec(memory_space=pltpu.VMEM)
    bf16, f32 = jnp.bfloat16, jnp.float32

    turned = [coef_fine]
    for step in range(1, groups):
        turned.append(lax.ppermute(coef_fine, "probe", [(i, (i + step) % groups) for i in range(groups)]))
    all_probes = jnp.concatenate(turned, axis=0)

    fine_send, fine_rows = pl.pallas_call(
        pack_fine_kernel,
        out_shape=(
            jax.ShapeDtypeStruct((owners, (cap_fine // 2) * (px + 8), LANES), bf16),
            jax.ShapeDtypeStruct((8, points_fine.shape[1]), f32),
        ),
        in_specs=[smem, vmem, vmem],
        out_specs=[vmem, vmem],
        scratch_shapes=[
            pltpu.VMEM((fine_count, px, LANES), f32),
            pltpu.VMEM((fine_count, 8, LANES), f32),
        ],
        compiler_params=params,
        name="pack_fine",
    )(send_fine, coef, points_fine)
    fine_recv = lax.all_to_all(fine_send, "leaf", split_axis=0, concat_axis=0, tiled=True)

    coarse_send, coarse_rows, coarse_coef = pl.pallas_call(
        pack_coarse_kernel,
        out_shape=(
            jax.ShapeDtypeStruct((owners, (cap_coarse // 2) * (px + 8), LANES), bf16),
            jax.ShapeDtypeStruct((8, points_coarse.shape[1]), f32),
            jax.ShapeDtypeStruct((px, points_coarse.shape[1]), bf16),
        ),
        in_specs=[smem, vmem, vmem, vmem],
        out_specs=[vmem, vmem, vmem],
        scratch_shapes=[
            pltpu.VMEM((coarse_count, px, LANES), f32),
            pltpu.VMEM((coarse_count, 8, LANES), f32),
        ],
        compiler_params=params,
        name="pack_coarse",
    )(send_coarse, coef, transfer, points_coarse)
    fine_total = owners * cap_fine
    coarse_total = owners * cap_coarse
    (fine_own, fine_own_turns), (fine_index, fine_turns) = slot_lists(slots_fine, counts_fine, fine_total)
    (coarse_own, coarse_own_turns), (coarse_index, coarse_turns) = slot_lists(
        slots_coarse, counts_coarse, coarse_total
    )
    fine_sums, coarse_sums = pl.pallas_call(
        own_kernel,
        out_shape=(
            jax.ShapeDtypeStruct((px, points_fine.shape[1]), f32),
            jax.ShapeDtypeStruct((px, points_coarse.shape[1]), f32),
        ),
        in_specs=[smem] * 4 + [vmem] * 4,
        out_specs=[vmem, vmem],
        scratch_shapes=sweep_scratch(fine_count, fine_count, px),
        compiler_params=params,
        cost_estimate=pl.CostEstimate(flops=10**10, bytes_accessed=10**7, transcendentals=10**7),
        name="own_sweep",
    )(fine_own, fine_own_turns, coarse_own, coarse_own_turns, coef, fine_rows, coarse_coef, coarse_rows)

    coarse_send, coarse_sums = lax.optimization_barrier((coarse_send, coarse_sums))
    coarse_recv = lax.all_to_all(coarse_send, "leaf", split_axis=0, concat_axis=0, tiled=True)

    fine_far = pl.pallas_call(
        fine_kernel,
        out_shape=jax.ShapeDtypeStruct((px, points_fine.shape[1]), f32),
        in_specs=[smem, smem, vmem, vmem, vmem],
        out_specs=vmem,
        scratch_shapes=sweep_scratch(fine_total, fine_count, px),
        compiler_params=params,
        name="fine_sweep",
    )(fine_index, fine_turns, fine_recv, fine_rows, fine_sums)

    far, gram = pl.pallas_call(
        coarse_kernel,
        out_shape=(
            jax.ShapeDtypeStruct((px, points_fine.shape[1]), f32),
            jax.ShapeDtypeStruct((all_probes.shape[0], px), f32),
        ),
        in_specs=[smem, smem] + [vmem] * 6,
        out_specs=[vmem, vmem],
        scratch_shapes=sweep_scratch(coarse_total, coarse_count, px),
        compiler_params=params,
        name="coarse_sweep",
    )(coarse_index, coarse_turns, coarse_recv, coarse_rows, coarse_sums, fine_far, transfer, all_probes)

    far_field = far[:probes]
    blocks = gram[:, :probes].reshape(groups, probes * probes)
    blocks = blocks[(lax.axis_index("probe") - jnp.arange(groups)) % groups]
    blocks = jnp.broadcast_to(blocks[None], (owners, groups, probes * probes))
    blocks = blocks.reshape(owners * groups, 1, probes * probes)
    blocks = lax.all_to_all(blocks, ("leaf", "probe"), split_axis=0, concat_axis=0, tiled=True)
    total = jnp.sum(blocks.reshape(owners, groups, probes, probes), axis=0)
    gram_scale = 1.0 / math.sqrt(owners * fine_count * 64)
    probe_gram = total.transpose(1, 0, 2).reshape(probes, groups * probes) * gram_scale
    return (far_field, probe_gram)


def solution(mesh):
    return jax.shard_map(
        shards,
        mesh=mesh,
        in_specs=(
            P("probe", "leaf"),
            P(None, "leaf"),
            P(None, "leaf"),
            P(None, "leaf"),
            P("leaf", None, None),
            P("leaf", None),
            P("leaf"),
            P("leaf", None, None),
            P("leaf", None),
            P("leaf"),
        ),
        out_specs=(P("probe", "leaf"), P("probe", None)),
        check_vma=False,
    )
```

```python
import functools
import math

import jax
import jax.numpy as jnp
from jax import lax
from jax.experimental import pallas as pl
from jax.experimental.pallas import tpu as pltpu
from jax.sharding import PartitionSpec as P

KERNEL_RATE = 1.5
POINT_SCALE = math.sqrt(2.0 * KERNEL_RATE)
LANES = 128
UNITS = 8
QUAD = 4
CHUNK = 8
FAR_AWAY = -30000.0
VMEM = 56 * 1024 * 1024

NT = (((1,), (1,)), ((), ()))
NN = (((1,), (0,)), ((), ()))


def bdot(a, b, dims):
    return lax.dot_general(a, b, dims, preferred_element_type=jnp.float32)


def split_rows(points):
    v = points * POINT_SCALE
    norm = -0.5 * (v[0:1] * v[0:1] + v[1:2] * v[1:2] + v[2:3] * v[2:3])
    full = jnp.concatenate([v, norm], axis=0)
    high = full.astype(jnp.bfloat16).astype(jnp.float32)
    rest = (full - high).astype(jnp.bfloat16).astype(jnp.float32)
    return jnp.concatenate([high, rest], axis=0)


def source_features(rows):
    place = lax.broadcasted_iota(jnp.int32, rows.shape, 0)
    one = jnp.where((place == 3) | (place == 7), 1.0, 0.0)
    return jnp.concatenate([rows, jnp.where(place < 3, rows, one)], axis=0)


def target_features(rows):
    place = lax.broadcasted_iota(jnp.int32, rows.shape, 0)
    turned = jnp.concatenate([rows[4:8], rows[0:4]], axis=0)
    one = jnp.where((place == 3) | (place == 7), 1.0, jnp.where(place < 3, rows, turned))
    return jnp.concatenate([one, turned], axis=0)


def halves(tile):
    lane = lax.broadcasted_iota(jnp.int32, tile.shape, 1)
    turned = pltpu.roll(tile, LANES // 2, 1)
    low = lane < LANES // 2
    return jnp.where(low, tile, turned), jnp.where(low, turned, tile)


def lane_tile(index):
    return pl.ds(pl.multiple_of(index * LANES, LANES), LANES)


def pack_send(send_ref, out_ref, dup_coef, dup_rows, owners, capacity, px):
    pairs = capacity // 2
    lane = lax.broadcasted_iota(jnp.int32, (px, LANES), 1) < LANES // 2
    lane8 = lax.broadcasted_iota(jnp.int32, (8, LANES), 1) < LANES // 2

    def one_owner(owner, carry):
        before = None
        for pair in range(pairs):
            first = send_ref[owner, 2 * pair]
            second = send_ref[owner, 2 * pair + 1]
            out_ref[owner, pair * px:(pair + 1) * px, :] = jnp.where(
                lane, dup_coef[first], dup_coef[second]
            ).astype(jnp.bfloat16)
            rows = jnp.where(lane8, dup_rows[first], dup_rows[second])
            if pair % 2 == 0:
                before = rows
            else:
                start = pairs * px + (pair - 1) * 8
                out_ref[owner, start:start + 16, :] = jnp.concatenate(
                    [before, rows], axis=0
                ).astype(jnp.bfloat16)
        return carry

    lax.fori_loop(0, owners, one_owner, 0)


def pack_fine_kernel(send_ref, coef_ref, points_ref, out_ref, rows_ref, dup_coef, dup_rows):
    owners, capacity = send_ref.shape
    px = coef_ref.shape[0]
    rows_ref[...] = split_rows(points_ref[...])

    def one_tile(index, carry):
        a, b = halves(coef_ref[:, lane_tile(index)].astype(jnp.float32))
        dup_coef[2 * index] = a
        dup_coef[2 * index + 1] = b
        a, b = halves(rows_ref[:, lane_tile(index)])
        dup_rows[2 * index] = a
        dup_rows[2 * index + 1] = b
        return carry

    lax.fori_loop(0, coef_ref.shape[1] // LANES, one_tile, 0, unroll=4)
    pack_send(send_ref, out_ref, dup_coef, dup_rows, owners, capacity, px)


def pack_coarse_kernel(
    send_ref, coef_ref, transfer_ref, points_ref, out_ref, rows_ref, coarse_ref, dup_coef, dup_rows
):
    owners, capacity = send_ref.shape
    px = coef_ref.shape[0]
    rows_ref[...] = split_rows(points_ref[...])

    def one_tile(index, carry):
        doubled = []
        for part in range(2):
            q = 2 * index + part
            a, b = halves(transfer_ref[:, lane_tile(q)].astype(jnp.float32))
            matrix = jnp.concatenate([a, b], axis=0).astype(jnp.bfloat16)
            block = bdot(coef_ref[:, lane_tile(q)], matrix, NN)
            dup_coef[q] = block
            doubled.append(block)
        lane = lax.broadcasted_iota(jnp.int32, (px, LANES), 1) < LANES // 2
        coarse_ref[:, lane_tile(index)] = jnp.where(lane, doubled[0], doubled[1]).astype(jnp.bfloat16)
        a, b = halves(rows_ref[:, lane_tile(index)])
        dup_rows[2 * index] = a
        dup_rows[2 * index + 1] = b
        return carry

    lax.fori_loop(0, coef_ref.shape[1] // (2 * LANES), one_tile, 0, unroll=2)
    pack_send(send_ref, out_ref, dup_coef, dup_rows, owners, capacity, px)


def turned(rows):
    row = lax.broadcasted_iota(jnp.int32, (LANES, LANES), 0)
    column = lax.broadcasted_iota(jnp.int32, (LANES, LANES), 1)
    unit = jnp.where(row == column, 1.0, 0.0).astype(jnp.bfloat16)
    return bdot(unit, rows, NT).astype(jnp.bfloat16)


def put_pair(entry, coef, rows, coef_table, feature_table):
    a, b = halves(coef.astype(jnp.float32))
    coef_table[entry] = a.astype(jnp.bfloat16)
    coef_table[entry + 1] = b.astype(jnp.bfloat16)
    features = turned(jnp.concatenate([source_features(rows).astype(jnp.bfloat16)] * 8, axis=0))
    feature_table[entry] = features[:64]
    feature_table[entry + 1] = features[64:]


def put_nothing(entry, coef_table, feature_table):
    coef_table[entry] = jnp.zeros(coef_table.shape[1:], jnp.bfloat16)
    place = lax.broadcasted_iota(jnp.int32, (8, LANES), 0)
    nothing = source_features(jnp.where(place == 3, FAR_AWAY, 0.0)).astype(jnp.bfloat16)
    feature_table[entry] = turned(jnp.concatenate([nothing] * 8, axis=0))[:64]


def build_own(coef_ref, rows_ref, coef_table, feature_table):
    tiles = coef_ref.shape[1] // LANES

    def one_tile(index, carry):
        tile = lane_tile(index)
        put_pair(2 * index, coef_ref[:, tile], rows_ref[:, tile], coef_table, feature_table)
        return carry

    lax.fori_loop(0, tiles, one_tile, 0, unroll=4)
    put_nothing(2 * tiles, coef_table, feature_table)


def build_received(recv_ref, coef_table, feature_table):
    owners, recv_rows, _ = recv_ref.shape
    px = coef_table.shape[1]
    pairs = recv_rows // (px + 8)

    def one_owner(owner, carry):
        for pair in range(0, pairs, 2):
            start = pairs * px + pair * 8
            both = recv_ref[owner, start:start + 16, :].astype(jnp.float32)
            for part in range(2):
                where = pair + part
                put_pair(
                    owner * (2 * pairs) + 2 * where,
                    recv_ref[owner, where * px:(where + 1) * px, :],
                    both[8 * part:8 * part + 8],
                    coef_table,
                    feature_table,
                )
        return carry

    lax.fori_loop(0, owners, one_owner, 0)
    put_nothing(owners * pairs * 2, coef_table, feature_table)


def build_targets(rows_ref, target_table):
    def one_tile(index, carry):
        a, b = halves(target_features(rows_ref[:, lane_tile(index)]))
        target_table[2 * index] = a.astype(jnp.bfloat16)
        target_table[2 * index + 1] = b.astype(jnp.bfloat16)
        return carry

    lax.fori_loop(0, rows_ref.shape[1] // LANES, one_tile, 0, unroll=4)


def sweep(index_ref, turns_ref, coef_table, feature_table, target_table, first_buffer, second_buffer, acc):
    clusters = turns_ref.shape[0]
    px = coef_table.shape[1]
    slots_end = index_ref.shape[1] // CHUNK - 1
    lane = lax.broadcasted_iota(jnp.int32, (64, LANES), 1) // 16
    lane_t = lax.broadcasted_iota(jnp.int32, (16, LANES), 1) // 64
    lane_x = lax.broadcasted_iota(jnp.int32, (px, LANES), 1) < 64
    blank = jnp.zeros((16, LANES), jnp.bfloat16)
    acc[...] = jnp.zeros_like(acc)

    def partners(unit):
        target, turn = unit
        return [index_ref[target, turn * CHUNK + m] for m in range(CHUNK)]

    def tiles(units, buffer):
        for start in range(0, UNITS, QUAD):
            quad = units[start:start + QUAD]
            weights = []
            for u in range(QUAD):
                own = jnp.where(lane_t == u % 2, target_table[quad[u][0]], blank)
                weights.append(jnp.concatenate([own if v == u // 2 else blank for v in range(QUAD // 2)], axis=1))
            weights = jnp.concatenate(weights, axis=0)
            ids = [partners(unit) for unit in quad]
            for part in range(0, CHUNK, 4):
                rows = []
                for m in range(part, part + 4):
                    tile = feature_table[ids[0][m]]
                    for u in range(1, QUAD):
                        tile = jnp.where(lane == u, feature_table[ids[u][m]], tile)
                    rows.append(tile[:, :16 * QUAD])
                power = bdot(jnp.concatenate(rows, axis=0), weights, NN)
                buffer[start // QUAD, part * 64:(part + 4) * 64] = jnp.exp(power).astype(jnp.bfloat16)

    def products(units, buffer):
        for start in range(0, UNITS, QUAD):
            quad = units[start:start + QUAD]
            coefs = []
            for unit in quad:
                ids = partners(unit)
                coefs.append(
                    jnp.concatenate(
                        [
                            jnp.where(lane_x, coef_table[ids[m]], coef_table[ids[m + 1]])
                            for m in range(0, CHUNK, 2)
                        ],
                        axis=1,
                    )
                )
            product = bdot(jnp.concatenate(coefs, axis=0), buffer[start // QUAD], NN)
            for u in range(QUAD):
                side = (u // 2) * LANES
                acc[u % 2, quad[u][0]] += product[u * px:(u + 1) * px, side:side + LANES]

    def following(unit):
        target, turn = unit
        over = turn + 1 >= turns_ref[target]
        later = jnp.where(over, target + 1, target)
        end = later >= clusters
        turn = jnp.where(end, slots_end, jnp.where(over, 0, turn + 1))
        return jnp.minimum(later, clusters - 1), turn

    def next_units(unit):
        units = []
        for _ in range(UNITS):
            unit = following(unit)
            units.append(unit)
        return tuple(units)

    def two_sets(_, units):
        second = next_units(units[-1])
        third = next_units(second[-1])
        tiles(second, second_buffer)
        products(units, first_buffer)
        tiles(third, first_buffer)
        products(second, second_buffer)
        return third

    total = lax.fori_loop(0, clusters, lambda c, n: n + turns_ref[c], jnp.int32(0))
    unit = (jnp.int32(0), jnp.int32(0))
    start = (unit,) + next_units(unit)[:-1]
    tiles(start, first_buffer)
    lax.fori_loop(0, (total + 2 * UNITS - 1) // (2 * UNITS), two_sets, start)


def summed(acc, target):
    low = lax.broadcasted_iota(jnp.int32, acc.shape[2:], 1) < 64
    here = jnp.where(low, acc[0, target], acc[1, target])
    return here + pltpu.roll(here, 64, 1)


def put_sums(acc, clusters, out_ref, before_ref=None):
    low = lax.broadcasted_iota(jnp.int32, acc.shape[2:], 1) < 64

    def one_tile(index, carry):
        tile = lane_tile(index)
        sums = jnp.where(low, summed(acc, 2 * index), summed(acc, 2 * index + 1))
        out_ref[:, tile] = sums if before_ref is None else before_ref[:, tile] + sums
        return carry

    lax.fori_loop(0, clusters // 2, one_tile, 0, unroll=4)


def own_kernel(
    fine_index_ref,
    fine_turns_ref,
    coarse_index_ref,
    coarse_turns_ref,
    fine_coef_ref,
    fine_rows_ref,
    coarse_coef_ref,
    coarse_rows_ref,
    fine_out_ref,
    coarse_out_ref,
    *scratch,
):
    acc = scratch[-1]
    for index_ref, turns_ref, coef_ref, rows_ref, out_ref in (
        (fine_index_ref, fine_turns_ref, fine_coef_ref, fine_rows_ref, fine_out_ref),
        (coarse_index_ref, coarse_turns_ref, coarse_coef_ref, coarse_rows_ref, coarse_out_ref),
    ):
        build_own(coef_ref, rows_ref, *scratch[:2])
        build_targets(rows_ref, scratch[2])
        sweep(index_ref, turns_ref, *scratch)
        put_sums(acc, turns_ref.shape[0], out_ref)


def fine_kernel(index_ref, turns_ref, recv_ref, rows_ref, own_ref, out_ref, *scratch):
    build_received(recv_ref, *scratch[:2])
    build_targets(rows_ref, scratch[2])
    sweep(index_ref, turns_ref, *scratch)
    put_sums(scratch[-1], turns_ref.shape[0], out_ref, own_ref)


def coarse_kernel(
    index_ref,
    turns_ref,
    recv_ref,
    rows_ref,
    own_ref,
    fine_ref,
    transfer_ref,
    probes_ref,
    out_ref,
    gram_ref,
    *scratch,
):
    acc = scratch[-1]
    build_received(recv_ref, *scratch[:2])
    build_targets(rows_ref, scratch[2])
    sweep(index_ref, turns_ref, *scratch)
    gram_ref[...] = jnp.zeros_like(gram_ref)

    def one_group(group, carry):
        gram = None
        for part in range(4):
            q = group * 4 + part
            own = halves(own_ref[:, lane_tile(group * 2 + part // 2)])[part % 2]
            twice = (summed(acc, q) + own).astype(jnp.bfloat16)
            matrix = transfer_ref[:, lane_tile(q)].astype(jnp.float32)
            low = lax.broadcasted_iota(jnp.int32, matrix.shape, 1) < 64
            matrix = jnp.concatenate(
                [jnp.where(low, matrix, 0.0), jnp.where(low, 0.0, matrix)], axis=0
            ).astype(jnp.bfloat16)
            total = fine_ref[:, lane_tile(q)] + bdot(twice, matrix, NT)
            out_ref[:, lane_tile(q)] = total
            high = total.astype(jnp.bfloat16)
            rest = (total - high.astype(jnp.float32)).astype(jnp.bfloat16)
            probes = probes_ref[:, lane_tile(q)]
            term = bdot(probes, high, NT) + bdot(probes, rest, NT)
            gram = term if gram is None else gram + term
        gram_ref[...] += gram
        return carry

    lax.fori_loop(0, turns_ref.shape[0] // 4, one_group, 0)


def sweep_scratch(total, clusters, px):
    return [
        pltpu.VMEM((total + 1, px, LANES), jnp.bfloat16),
        pltpu.VMEM((total + 1, 64, LANES), jnp.bfloat16),
        pltpu.VMEM((clusters, 16, LANES), jnp.bfloat16),
        pltpu.VMEM((UNITS // QUAD, CHUNK * 64, QUAD * 64), jnp.bfloat16),
        pltpu.VMEM((UNITS // QUAD, CHUNK * 64, QUAD * 64), jnp.bfloat16),
        pltpu.VMEM((2, clusters, px, LANES), jnp.float32),
    ]


def slot_list(slots, chosen, nothing):
    width = slots.shape[1]
    before = jnp.tril(jnp.ones((width, width), jnp.float32)).T
    rank = jnp.dot(chosen.astype(jnp.float32), before).astype(jnp.int32) - 1
    place = lax.broadcasted_iota(jnp.int32, (1, 1, width + CHUNK), 2)
    moved = jnp.where(chosen, rank, -1)[:, :, None] == place
    index = nothing + jnp.sum(jnp.where(moved, (slots - nothing)[:, :, None], 0), axis=1)
    turns = (rank[:, -1] + CHUNK) // CHUNK
    return index, jnp.maximum(turns, 1)


def slot_lists(slots, counts, entries):
    clusters, width = slots.shape
    live = lax.broadcasted_iota(jnp.int32, slots.shape, 1) < counts[:, None]
    own = slot_list(slots, live & (slots < clusters), clusters)
    received = slot_list(slots - clusters, live & (slots >= clusters), entries)
    return own, received


def shards(
    coef_fine,
    points_fine,
    points_coarse,
    transfer,
    send_fine,
    slots_fine,
    counts_fine,
    send_coarse,
    slots_coarse,
    counts_coarse,
):
    probes = coef_fine.shape[0]
    fine_count = counts_fine.shape[0]
    coarse_count = counts_coarse.shape[0]
    owners = lax.axis_size("leaf")
    groups = lax.axis_size("probe")
    px = -(-probes // 16) * 16
    coef = coef_fine if px == probes else jnp.pad(coef_fine, ((0, px - probes), (0, 0)))
    send_fine = send_fine.reshape(owners, -1)
    send_coarse = send_coarse.reshape(owners, -1)
    cap_fine = send_fine.shape[1]
    cap_coarse = send_coarse.shape[1]
    params = pltpu.CompilerParams(vmem_limit_bytes=VMEM)
    smem = pl.BlockSpec(memory_space=pltpu.SMEM)
    vmem = pl.BlockSpec(memory_space=pltpu.VMEM)
    bf16, f32 = jnp.bfloat16, jnp.float32

    turned = [coef_fine]
    for step in range(1, groups):
        turned.append(lax.ppermute(coef_fine, "probe", [(i, (i + step) % groups) for i in range(groups)]))
    all_probes = jnp.concatenate(turned, axis=0)

    fine_send, fine_rows = pl.pallas_call(
        pack_fine_kernel,
        out_shape=(
            jax.ShapeDtypeStruct((owners, (cap_fine // 2) * (px + 8), LANES), bf16),
            jax.ShapeDtypeStruct((8, points_fine.shape[1]), f32),
        ),
        in_specs=[smem, vmem, vmem],
        out_specs=[vmem, vmem],
        scratch_shapes=[
            pltpu.VMEM((fine_count, px, LANES), f32),
            pltpu.VMEM((fine_count, 8, LANES), f32),
        ],
        compiler_params=params,
        name="pack_fine",
    )(send_fine, coef, points_fine)
    fine_recv = lax.all_to_all(fine_send, "leaf", split_axis=0, concat_axis=0, tiled=True)

    coarse_send, coarse_rows, coarse_coef = pl.pallas_call(
        pack_coarse_kernel,
        out_shape=(
            jax.ShapeDtypeStruct((owners, (cap_coarse // 2) * (px + 8), LANES), bf16),
            jax.ShapeDtypeStruct((8, points_coarse.shape[1]), f32),
            jax.ShapeDtypeStruct((px, points_coarse.shape[1]), bf16),
        ),
        in_specs=[smem, vmem, vmem, vmem],
        out_specs=[vmem, vmem, vmem],
        scratch_shapes=[
            pltpu.VMEM((coarse_count, px, LANES), f32),
            pltpu.VMEM((coarse_count, 8, LANES), f32),
        ],
        compiler_params=params,
        name="pack_coarse",
    )(send_coarse, coef, transfer, points_coarse)
    fine_total = owners * cap_fine
    coarse_total = owners * cap_coarse
    (fine_own, fine_own_turns), (fine_index, fine_turns) = slot_lists(slots_fine, counts_fine, fine_total)
    (coarse_own, coarse_own_turns), (coarse_index, coarse_turns) = slot_lists(
        slots_coarse, counts_coarse, coarse_total
    )
    fine_sums, coarse_sums = pl.pallas_call(
        own_kernel,
        out_shape=(
            jax.ShapeDtypeStruct((px, points_fine.shape[1]), f32),
            jax.ShapeDtypeStruct((px, points_coarse.shape[1]), f32),
        ),
        in_specs=[smem] * 4 + [vmem] * 4,
        out_specs=[vmem, vmem],
        scratch_shapes=sweep_scratch(fine_count, fine_count, px),
        compiler_params=params,
        cost_estimate=pl.CostEstimate(flops=10**10, bytes_accessed=10**7, transcendentals=10**7),
        name="own_sweep",
    )(fine_own, fine_own_turns, coarse_own, coarse_own_turns, coef, fine_rows, coarse_coef, coarse_rows)

    coarse_send, coarse_sums = lax.optimization_barrier((coarse_send, coarse_sums))
    coarse_recv = lax.all_to_all(coarse_send, "leaf", split_axis=0, concat_axis=0, tiled=True)

    fine_far = pl.pallas_call(
        fine_kernel,
        out_shape=jax.ShapeDtypeStruct((px, points_fine.shape[1]), f32),
        in_specs=[smem, smem, vmem, vmem, vmem],
        out_specs=vmem,
        scratch_shapes=sweep_scratch(fine_total, fine_count, px),
        compiler_params=params,
        name="fine_sweep",
    )(fine_index, fine_turns, fine_recv, fine_rows, fine_sums)

    far, gram = pl.pallas_call(
        coarse_kernel,
        out_shape=(
            jax.ShapeDtypeStruct((px, points_fine.shape[1]), f32),
            jax.ShapeDtypeStruct((all_probes.shape[0], px), f32),
        ),
        in_specs=[smem, smem] + [vmem] * 6,
        out_specs=[vmem, vmem],
        scratch_shapes=sweep_scratch(coarse_total, coarse_count, px),
        compiler_params=params,
        name="coarse_sweep",
    )(coarse_index, coarse_turns, coarse_recv, coarse_rows, coarse_sums, fine_far, transfer, all_probes)

    far_field = far[:probes]
    blocks = gram[:, :probes].reshape(groups, probes * probes)
    blocks = blocks[(lax.axis_index("probe") - jnp.arange(groups)) % groups]
    blocks = jnp.broadcast_to(blocks[None], (owners, groups, probes * probes))
    blocks = blocks.reshape(owners * groups, 1, probes * probes)
    blocks = lax.all_to_all(blocks, ("leaf", "probe"), split_axis=0, concat_axis=0, tiled=True)
    total = jnp.sum(blocks.reshape(owners, groups, probes, probes), axis=0)
    gram_scale = 1.0 / math.sqrt(owners * fine_count * 64)
    probe_gram = total.transpose(1, 0, 2).reshape(probes, groups * probes) * gram_scale
    return (far_field, probe_gram)


def solution(mesh):
    return jax.shard_map(
        shards,
        mesh=mesh,
        in_specs=(
            P("probe", "leaf"),
            P(None, "leaf"),
            P(None, "leaf"),
            P(None, "leaf"),
            P("leaf", None, None),
            P("leaf", None),
            P("leaf"),
            P("leaf", None, None),
            P("leaf", None),
            P("leaf"),
        ),
        out_specs=(P("probe", "leaf"), P("probe", None)),
        check_vma=False,
    )
```

```python
import functools
import functools
import math

import jax
import jax.numpy as jnp
from jax import lax
from jax.experimental import pallas as pl
from jax.experimental.pallas import tpu as pltpu
from jax.sharding import PartitionSpec as P

KERNEL_RATE = 1.5
POINT_SCALE = math.sqrt(2.0 * KERNEL_RATE)
LANES = 128
UNITS = 16
QUAD = 4
CHUNK = 4
FAR_AWAY = -30000.0
SLOTS = 64
TURNS = LANES - 1
VMEM = 56 * 1024 * 1024

NT = (((1,), (1,)), ((), ()))
NN = (((1,), (0,)), ((), ()))


def bdot(a, b, dims):
    return lax.dot_general(a, b, dims, preferred_element_type=jnp.float32)


def split_rows(points):
    v = points * POINT_SCALE
    norm = -0.5 * (v[0:1] * v[0:1] + v[1:2] * v[1:2] + v[2:3] * v[2:3])
    full = jnp.concatenate([v, norm], axis=0)
    high = full.astype(jnp.bfloat16).astype(jnp.float32)
    rest = (full - high).astype(jnp.bfloat16).astype(jnp.float32)
    return jnp.concatenate([high, rest], axis=0)


def source_features(rows):
    place = lax.broadcasted_iota(jnp.int32, rows.shape, 0)
    one = jnp.where((place == 3) | (place == 7), 1.0, 0.0)
    return jnp.concatenate([rows, jnp.where(place < 3, rows, one)], axis=0)


def target_features(rows):
    place = lax.broadcasted_iota(jnp.int32, rows.shape, 0)
    turned = jnp.concatenate([rows[4:8], rows[0:4]], axis=0)
    one = jnp.where((place == 3) | (place == 7), 1.0, jnp.where(place < 3, rows, turned))
    return jnp.concatenate([one, turned], axis=0)


def halves(tile):
    lane = lax.broadcasted_iota(jnp.int32, tile.shape, 1)
    turned = pltpu.roll(tile, LANES // 2, 1)
    low = lane < LANES // 2
    return jnp.where(low, tile, turned), jnp.where(low, turned, tile)


def lane_tile(index):
    return pl.ds(pl.multiple_of(index * LANES, LANES), LANES)


def list_slots(slots_ref, counts_ref, out_ref, entries):
    clusters, width = slots_ref.shape
    slots = slots_ref[...]
    place = lax.broadcasted_iota(jnp.int32, slots.shape, 1)
    live = place < counts_ref[...]
    own = live & (slots < clusters)
    received = live & (slots >= clusters)
    row = lax.broadcasted_iota(jnp.int32, (width, width), 0)
    column = lax.broadcasted_iota(jnp.int32, (width, width), 1)
    upto = jnp.where(row <= column, 1.0, 0.0).astype(jnp.bfloat16)
    rank = [
        bdot(jnp.where(chosen, 1.0, 0.0).astype(jnp.bfloat16), upto, NN).astype(jnp.int32)
        for chosen in (own, received)
    ]
    spot = jnp.where(own, rank[0] - 1, jnp.where(received, rank[1] + (LANES - 1), -1))
    value = jnp.where(own, slots - clusters, slots - clusters - entries)
    lane = lax.broadcasted_iota(jnp.int32, (clusters, 2 * LANES), 1)
    table = jnp.where(lane < LANES, clusters, entries)
    for m in range(width):
        table = table + jnp.where(lane == spot[:, m:m + 1], value[:, m:m + 1], 0)
    for side in range(2):
        turns = jnp.maximum((rank[side][:, width - 1:] + CHUNK - 1) // CHUNK, 1)
        table = jnp.where(lane == side * LANES + TURNS, turns, table)
    out_ref[...] = table


def list_slots_kernel(
    fine_slots_ref, fine_counts_ref, coarse_slots_ref, coarse_counts_ref, fine_out_ref, coarse_out_ref, *, entries
):
    list_slots(fine_slots_ref, fine_counts_ref, fine_out_ref, entries[0])
    list_slots(coarse_slots_ref, coarse_counts_ref, coarse_out_ref, entries[1])


def pack_send(send_ref, out_ref, dup_coef, dup_rows, owners, capacity, px):
    pairs = capacity // 2
    lane = lax.broadcasted_iota(jnp.int32, (px, LANES), 1) < LANES // 2
    lane8 = lax.broadcasted_iota(jnp.int32, (8, LANES), 1) < LANES // 2

    def one_owner(owner, carry):
        before = None
        for pair in range(pairs):
            first = send_ref[0, owner, 2 * pair]
            second = send_ref[0, owner, 2 * pair + 1]
            out_ref[owner, pair * px:(pair + 1) * px, :] = jnp.where(
                lane, dup_coef[first], dup_coef[second]
            ).astype(jnp.bfloat16)
            rows = jnp.where(lane8, dup_rows[first], dup_rows[second])
            if pair % 2 == 0:
                before = rows
            else:
                start = pairs * px + (pair - 1) * 8
                out_ref[owner, start:start + 16, :] = jnp.concatenate(
                    [before, rows], axis=0
                ).astype(jnp.bfloat16)
        return carry

    lax.fori_loop(0, owners, one_owner, 0)


def pack_fine_kernel(send_ref, coef_ref, points_ref, out_ref, rows_ref, dup_coef, dup_rows):
    _, owners, capacity = send_ref.shape
    px = coef_ref.shape[0]
    rows_ref[...] = split_rows(points_ref[...])

    def one_tile(index, carry):
        a, b = halves(coef_ref[:, lane_tile(index)].astype(jnp.float32))
        dup_coef[2 * index] = a
        dup_coef[2 * index + 1] = b
        a, b = halves(rows_ref[:, lane_tile(index)])
        dup_rows[2 * index] = a
        dup_rows[2 * index + 1] = b
        return carry

    lax.fori_loop(0, coef_ref.shape[1] // LANES, one_tile, 0, unroll=4)
    pack_send(send_ref, out_ref, dup_coef, dup_rows, owners, capacity, px)


def pack_coarse_kernel(
    send_ref, coef_ref, transfer_ref, points_ref, out_ref, rows_ref, coarse_ref, dup_coef, dup_rows
):
    _, owners, capacity = send_ref.shape
    px = coef_ref.shape[0]
    rows_ref[...] = split_rows(points_ref[...])

    def one_tile(index, carry):
        doubled = []
        for part in range(2):
            q = 2 * index + part
            a, b = halves(transfer_ref[:, lane_tile(q)].astype(jnp.float32))
            matrix = jnp.concatenate([a, b], axis=0).astype(jnp.bfloat16)
            block = bdot(coef_ref[:, lane_tile(q)], matrix, NN)
            dup_coef[q] = block
            doubled.append(block)
        lane = lax.broadcasted_iota(jnp.int32, (px, LANES), 1) < LANES // 2
        coarse_ref[:, lane_tile(index)] = jnp.where(lane, doubled[0], doubled[1]).astype(jnp.bfloat16)
        a, b = halves(rows_ref[:, lane_tile(index)])
        dup_rows[2 * index] = a
        dup_rows[2 * index + 1] = b
        return carry

    lax.fori_loop(0, coef_ref.shape[1] // (2 * LANES), one_tile, 0, unroll=2)
    pack_send(send_ref, out_ref, dup_coef, dup_rows, owners, capacity, px)


def turned(rows):
    row = lax.broadcasted_iota(jnp.int32, (LANES, LANES), 0)
    column = lax.broadcasted_iota(jnp.int32, (LANES, LANES), 1)
    unit = jnp.where(row == column, 1.0, 0.0).astype(jnp.bfloat16)
    return bdot(unit, rows, NT).astype(jnp.bfloat16)


def put_pair(entry, coef, rows, coef_table, feature_table):
    a, b = halves(coef.astype(jnp.float32))
    coef_table[entry] = a.astype(jnp.bfloat16)
    coef_table[entry + 1] = b.astype(jnp.bfloat16)
    features = turned(jnp.concatenate([source_features(rows).astype(jnp.bfloat16)] * 8, axis=0))
    feature_table[entry] = features[:64]
    feature_table[entry + 1] = features[64:]


def put_nothing(entry, coef_table, feature_table):
    coef_table[entry] = jnp.zeros(coef_table.shape[1:], jnp.bfloat16)
    place = lax.broadcasted_iota(jnp.int32, (8, LANES), 0)
    nothing = source_features(jnp.where(place == 3, FAR_AWAY, 0.0)).astype(jnp.bfloat16)
    feature_table[entry] = turned(jnp.concatenate([nothing] * 8, axis=0))[:64]


def build_own(coef_ref, rows_ref, coef_table, feature_table):
    tiles = coef_ref.shape[1] // LANES

    def one_tile(index, carry):
        tile = lane_tile(index)
        put_pair(2 * index, coef_ref[:, tile], rows_ref[:, tile], coef_table, feature_table)
        return carry

    lax.fori_loop(0, tiles, one_tile, 0, unroll=4)
    put_nothing(2 * tiles, coef_table, feature_table)


def build_received(recv_ref, coef_table, feature_table):
    owners, recv_rows, _ = recv_ref.shape
    px = coef_table.shape[1]
    pairs = recv_rows // (px + 8)

    def one_owner(owner, carry):
        for pair in range(0, pairs, 2):
            start = pairs * px + pair * 8
            both = recv_ref[owner, start:start + 16, :].astype(jnp.float32)
            for part in range(2):
                where = pair + part
                put_pair(
                    owner * (2 * pairs) + 2 * where,
                    recv_ref[owner, where * px:(where + 1) * px, :],
                    both[8 * part:8 * part + 8],
                    coef_table,
                    feature_table,
                )
        return carry

    lax.fori_loop(0, owners, one_owner, 0)
    put_nothing(owners * pairs * 2, coef_table, feature_table)


def build_targets(rows_ref, target_table):
    def one_tile(index, carry):
        a, b = halves(target_features(rows_ref[:, lane_tile(index)]))
        target_table[2 * index] = a.astype(jnp.bfloat16)
        target_table[2 * index + 1] = b.astype(jnp.bfloat16)
        return carry

    lax.fori_loop(0, rows_ref.shape[1] // LANES, one_tile, 0, unroll=4)


def sweep(index_ref, base, coef_table, feature_table, target_table, first_buffer, second_buffer, acc):
    clusters = index_ref.shape[0]
    px = coef_table.shape[1]
    slots_end = SLOTS // CHUNK
    lane = lax.broadcasted_iota(jnp.int32, (64, LANES), 1) // 16
    lane_t = lax.broadcasted_iota(jnp.int32, (16, LANES), 1) // 64
    lane_x = lax.broadcasted_iota(jnp.int32, (px, LANES), 1) < 64
    blank = jnp.zeros((16, LANES), jnp.bfloat16)
    acc[...] = jnp.zeros_like(acc)

    def partners(unit):
        target, turn = unit
        return [index_ref[target, base + turn * CHUNK + m] for m in range(CHUNK)]

    def tiles(units, buffer):
        for start in range(0, UNITS, QUAD):
            quad = units[start:start + QUAD]
            weights = []
            for u in range(QUAD):
                own = jnp.where(lane_t == u % 2, target_table[quad[u][0]], blank)
                weights.append(jnp.concatenate([own if v == u // 2 else blank for v in range(QUAD // 2)], axis=1))
            weights = jnp.concatenate(weights, axis=0)
            ids = [partners(unit) for unit in quad]
            for part in range(0, CHUNK, 4):
                rows = []
                for m in range(part, part + 4):
                    tile = feature_table[ids[0][m]]
                    for u in range(1, QUAD):
                        tile = jnp.where(lane == u, feature_table[ids[u][m]], tile)
                    rows.append(tile[:, :16 * QUAD])
                power = bdot(jnp.concatenate(rows, axis=0), weights, NN)
                buffer[start // QUAD, part * 64:(part + 4) * 64] = jnp.exp(power).astype(jnp.bfloat16)

    def products(units, buffer):
        for start in range(0, UNITS, QUAD):
            quad = units[start:start + QUAD]
            coefs = []
            for unit in quad:
                ids = partners(unit)
                coefs.append(
                    jnp.concatenate(
                        [
                            jnp.where(lane_x, coef_table[ids[m]], coef_table[ids[m + 1]])
                            for m in range(0, CHUNK, 2)
                        ],
                        axis=1,
                    )
                )
            product = bdot(jnp.concatenate(coefs, axis=0), buffer[start // QUAD], NN)
            for u in range(QUAD):
                side = (u // 2) * LANES
                acc[u % 2, quad[u][0]] += product[u * px:(u + 1) * px, side:side + LANES]

    def following(unit):
        target, turn = unit
        over = turn + 1 >= index_ref[target, base + TURNS]
        later = jnp.where(over, target + 1, target)
        end = later >= clusters
        turn = jnp.where(end, slots_end, jnp.where(over, 0, turn + 1))
        return jnp.minimum(later, clusters - 1), turn

    def next_units(unit):
        units = []
        for _ in range(UNITS):
            unit = following(unit)
            units.append(unit)
        return tuple(units)

    def two_sets(_, units):
        second = next_units(units[-1])
        third = next_units(second[-1])
        tiles(second, second_buffer)
        products(units, first_buffer)
        tiles(third, first_buffer)
        products(second, second_buffer)
        return third

    total = lax.fori_loop(0, clusters, lambda c, n: n + index_ref[c, base + TURNS], jnp.int32(0))
    unit = (jnp.int32(0), jnp.int32(0))
    start = (unit,) + next_units(unit)[:-1]
    tiles(start, first_buffer)
    lax.fori_loop(0, (total + 2 * UNITS - 1) // (2 * UNITS), two_sets, start)


def summed(acc, target):
    low = lax.broadcasted_iota(jnp.int32, acc.shape[2:], 1) < 64
    here = jnp.where(low, acc[0, target], acc[1, target])
    return here + pltpu.roll(here, 64, 1)


def put_sums(acc, clusters, out_ref, before_ref=None):
    low = lax.broadcasted_iota(jnp.int32, acc.shape[2:], 1) < 64

    def one_tile(index, carry):
        tile = lane_tile(index)
        sums = jnp.where(low, summed(acc, 2 * index), summed(acc, 2 * index + 1))
        out_ref[:, tile] = sums if before_ref is None else before_ref[:, tile] + sums
        return carry

    lax.fori_loop(0, clusters // 2, one_tile, 0, unroll=4)


def own_kernel(
    fine_list_ref,
    coarse_list_ref,
    fine_coef_ref,
    fine_rows_ref,
    coarse_coef_ref,
    coarse_rows_ref,
    fine_out_ref,
    coarse_out_ref,
    *scratch,
):
    for list_ref, coef_ref, rows_ref, out_ref in (
        (fine_list_ref, fine_coef_ref, fine_rows_ref, fine_out_ref),
        (coarse_list_ref, coarse_coef_ref, coarse_rows_ref, coarse_out_ref),
    ):
        build_own(coef_ref, rows_ref, *scratch[:2])
        build_targets(rows_ref, scratch[2])
        sweep(list_ref, 0, *scratch)
        put_sums(scratch[-1], list_ref.shape[0], out_ref)


def fine_kernel(list_ref, recv_ref, rows_ref, own_ref, out_ref, *scratch):
    build_received(recv_ref, *scratch[:2])
    build_targets(rows_ref, scratch[2])
    sweep(list_ref, LANES, *scratch)
    put_sums(scratch[-1], list_ref.shape[0], out_ref, own_ref)


def coarse_kernel(groups, *refs):
    list_ref, recv_ref, rows_ref, own_ref, fine_ref, transfer_ref = refs[:6]
    probes_refs = refs[6:6 + groups]
    out_ref, terms_ref = refs[6 + groups:8 + groups]
    gram_ref, *scratch = refs[8 + groups:]
    probes = probes_refs[0].shape[0]
    acc = scratch[-1]
    build_received(recv_ref, *scratch[:2])
    build_targets(rows_ref, scratch[2])
    sweep(list_ref, LANES, *scratch)
    gram_ref[...] = jnp.zeros_like(gram_ref)

    def one_group(group, carry):
        grams = [None] * groups
        for part in range(4):
            q = group * 4 + part
            own = halves(own_ref[:, lane_tile(group * 2 + part // 2)])[part % 2]
            twice = (summed(acc, q) + own).astype(jnp.bfloat16)
            matrix = transfer_ref[:, lane_tile(q)].astype(jnp.float32)
            low = lax.broadcasted_iota(jnp.int32, matrix.shape, 1) < 64
            matrix = jnp.concatenate(
                [jnp.where(low, matrix, 0.0), jnp.where(low, 0.0, matrix)], axis=0
            ).astype(jnp.bfloat16)
            total = fine_ref[:, lane_tile(q)] + bdot(twice, matrix, NT)
            out_ref[:, lane_tile(q)] = total
            high = total.astype(jnp.bfloat16)
            rest = (total - high.astype(jnp.float32)).astype(jnp.bfloat16)
            for block, probes_ref in enumerate(probes_refs):
                tile = probes_ref[:, lane_tile(q)]
                term = bdot(tile, high, NT) + bdot(tile, rest, NT)
                grams[block] = term if grams[block] is None else grams[block] + term
        for block in range(groups):
            gram_ref[block] += grams[block]
        return carry

    lax.fori_loop(0, list_ref.shape[0] // 4, one_group, 0)
    place = lax.axis_index("probe")
    for b in range(groups):
        block = gram_ref[lax.rem(place - b + groups, groups)]
        packed = jnp.concatenate([block[i:i + 8, :probes] for i in range(0, probes, 8)], axis=1)

        def one_owner(owner, carry):
            terms_ref[owner * groups + b] = packed
            return carry

        lax.fori_loop(0, terms_ref.shape[0] // groups, one_owner, 0)


def gram_kernel(terms_ref, out_ref, *, groups, scale):
    probes = out_ref.shape[0]
    columns = []
    for b in range(groups):
        total = terms_ref[b]
        for owner in range(1, terms_ref.shape[0] // groups):
            total = total + terms_ref[owner * groups + b]
        columns.append(
            jnp.concatenate([total[:, i * probes:(i + 1) * probes] for i in range(probes // 8)], axis=0)
        )
    out_ref[...] = jnp.concatenate(columns, axis=1) * scale


def sweep_scratch(total, clusters, px):
    return [
        pltpu.VMEM((total + 1, px, LANES), jnp.bfloat16),
        pltpu.VMEM((total + 1, 64, LANES), jnp.bfloat16),
        pltpu.VMEM((clusters, 16, LANES), jnp.bfloat16),
        pltpu.VMEM((UNITS // QUAD, CHUNK * 64, QUAD * 64), jnp.bfloat16),
        pltpu.VMEM((UNITS // QUAD, CHUNK * 64, QUAD * 64), jnp.bfloat16),
        pltpu.VMEM((2, clusters, px, LANES), jnp.float32),
    ]


def shards(
    coef_fine,
    points_fine,
    points_coarse,
    transfer,
    send_fine,
    slots_fine,
    counts_fine,
    send_coarse,
    slots_coarse,
    counts_coarse,
):
    probes = coef_fine.shape[0]
    fine_count = counts_fine.shape[0]
    coarse_count = counts_coarse.shape[0]
    owners = lax.axis_size("leaf")
    groups = lax.axis_size("probe")
    px = -(-probes // 16) * 16
    coef = coef_fine if px == probes else jnp.pad(coef_fine, ((0, px - probes), (0, 0)))
    cap_fine = send_fine.shape[2]
    cap_coarse = send_coarse.shape[2]
    params = pltpu.CompilerParams(vmem_limit_bytes=VMEM)
    smem = pl.BlockSpec(memory_space=pltpu.SMEM)
    vmem = pl.BlockSpec(memory_space=pltpu.VMEM)
    bf16, f32 = jnp.bfloat16, jnp.float32

    turned = [coef_fine]
    for step in range(1, groups):
        turned.append(lax.ppermute(coef_fine, "probe", [(i, (i + step) % groups) for i in range(groups)]))

    fine_send, fine_rows = pl.pallas_call(
        pack_fine_kernel,
        out_shape=(
            jax.ShapeDtypeStruct((owners, (cap_fine // 2) * (px + 8), LANES), bf16),
            jax.ShapeDtypeStruct((8, points_fine.shape[1]), f32),
        ),
        in_specs=[smem, vmem, vmem],
        out_specs=[vmem, vmem],
        scratch_shapes=[
            pltpu.VMEM((fine_count, px, LANES), f32),
            pltpu.VMEM((fine_count, 8, LANES), f32),
        ],
        compiler_params=params,
        name="pack_fine",
    )(send_fine, coef, points_fine)
    fine_recv = lax.all_to_all(fine_send, "leaf", split_axis=0, concat_axis=0, tiled=True)

    coarse_send, coarse_rows, coarse_coef = pl.pallas_call(
        pack_coarse_kernel,
        out_shape=(
            jax.ShapeDtypeStruct((owners, (cap_coarse // 2) * (px + 8), LANES), bf16),
            jax.ShapeDtypeStruct((8, points_coarse.shape[1]), f32),
            jax.ShapeDtypeStruct((px, points_coarse.shape[1]), bf16),
        ),
        in_specs=[smem, vmem, vmem, vmem],
        out_specs=[vmem, vmem, vmem],
        scratch_shapes=[
            pltpu.VMEM((coarse_count, px, LANES), f32),
            pltpu.VMEM((coarse_count, 8, LANES), f32),
        ],
        compiler_params=params,
        name="pack_coarse",
    )(send_coarse, coef, transfer, points_coarse)
    fine_total = owners * cap_fine
    coarse_total = owners * cap_coarse
    fine_list, coarse_list = pl.pallas_call(
        functools.partial(list_slots_kernel, entries=(fine_total, coarse_total)),
        out_shape=(
            jax.ShapeDtypeStruct((fine_count, 2 * LANES), jnp.int32),
            jax.ShapeDtypeStruct((coarse_count, 2 * LANES), jnp.int32),
        ),
        in_specs=[vmem] * 4,
        out_specs=[vmem, vmem],
        compiler_params=params,
        name="list_slots",
    )(slots_fine, counts_fine[:, None], slots_coarse, counts_coarse[:, None])
    fine_sums, coarse_sums = pl.pallas_call(
        own_kernel,
        out_shape=(
            jax.ShapeDtypeStruct((px, points_fine.shape[1]), f32),
            jax.ShapeDtypeStruct((px, points_coarse.shape[1]), f32),
        ),
        in_specs=[smem] * 2 + [vmem] * 4,
        out_specs=[vmem, vmem],
        scratch_shapes=sweep_scratch(fine_count, fine_count, px),
        compiler_params=params,
        cost_estimate=pl.CostEstimate(flops=10**10, bytes_accessed=10**7, transcendentals=10**7),
        name="own_sweep",
    )(fine_list, coarse_list, coef, fine_rows, coarse_coef, coarse_rows)

    coarse_send, coarse_sums = lax.optimization_barrier((coarse_send, coarse_sums))
    coarse_recv = lax.all_to_all(coarse_send, "leaf", split_axis=0, concat_axis=0, tiled=True)

    fine_far = pl.pallas_call(
        fine_kernel,
        out_shape=jax.ShapeDtypeStruct((px, points_fine.shape[1]), f32),
        in_specs=[smem, vmem, vmem, vmem],
        out_specs=vmem,
        scratch_shapes=sweep_scratch(fine_total, fine_count, px),
        compiler_params=params,
        name="fine_sweep",
    )(fine_list, fine_recv, fine_rows, fine_sums)

    term_shape = (owners * groups, 8, probes * probes // 8)
    far, terms = pl.pallas_call(
        functools.partial(coarse_kernel, groups),
        out_shape=(
            jax.ShapeDtypeStruct((px, points_fine.shape[1]), f32),
            jax.ShapeDtypeStruct(term_shape, f32),
        ),
        in_specs=[smem] + [vmem] * (5 + groups),
        out_specs=[vmem, vmem],
        scratch_shapes=[pltpu.VMEM((groups, probes, px), f32)]
        + sweep_scratch(coarse_total, coarse_count, px),
        compiler_params=params,
        name="coarse_sweep",
    )(coarse_list, coarse_recv, coarse_rows, coarse_sums, fine_far, transfer, *turned)

    terms = lax.all_to_all(terms, ("leaf", "probe"), split_axis=0, concat_axis=0, tiled=True)
    probe_gram = pl.pallas_call(
        functools.partial(
            gram_kernel, groups=groups, scale=1.0 / math.sqrt(owners * fine_count * 64)
        ),
        out_shape=jax.ShapeDtypeStruct((probes, groups * probes), f32),
        in_specs=[vmem],
        out_specs=vmem,
        name="gram_sum",
    )(terms)
    return (far[:probes], probe_gram)


def solution(mesh):
    return jax.shard_map(
        shards,
        mesh=mesh,
        in_specs=(
            P("probe", "leaf"),
            P(None, "leaf"),
            P(None, "leaf"),
            P(None, "leaf"),
            P("leaf", None, None),
            P("leaf", None),
            P("leaf"),
            P("leaf", None, None),
            P("leaf", None),
            P("leaf"),
        ),
        out_specs=(P("probe", "leaf"), P("probe", None)),
        check_vma=False,
    )
```

```python
import functools
import functools
import math

import jax
import jax.numpy as jnp
from jax import lax
from jax.experimental import pallas as pl
from jax.experimental.pallas import tpu as pltpu
from jax.sharding import PartitionSpec as P

KERNEL_RATE = 1.5
POINT_SCALE = math.sqrt(2.0 * KERNEL_RATE)
LANES = 128
UNITS = 8
QUAD = 4
CHUNK = 8
FAR_AWAY = -30000.0
SLOTS = 64
RECEIVED = SLOTS + CHUNK
SPARE = 6 * 1024 * 1024

NT = (((1,), (1,)), ((), ()))
NN = (((1,), (0,)), ((), ()))


def bdot(a, b, dims):
    return lax.dot_general(a, b, dims, preferred_element_type=jnp.float32)


def split_rows(points):
    v = points * POINT_SCALE
    norm = -0.5 * (v[0:1] * v[0:1] + v[1:2] * v[1:2] + v[2:3] * v[2:3])
    full = jnp.concatenate([v, norm], axis=0)
    high = full.astype(jnp.bfloat16).astype(jnp.float32)
    rest = (full - high).astype(jnp.bfloat16).astype(jnp.float32)
    return jnp.concatenate([high, rest], axis=0)


def source_features(rows):
    place = lax.broadcasted_iota(jnp.int32, rows.shape, 0)
    one = jnp.where((place == 3) | (place == 7), 1.0, 0.0)
    return jnp.concatenate([rows, jnp.where(place < 3, rows, one)], axis=0)


def target_features(rows):
    place = lax.broadcasted_iota(jnp.int32, rows.shape, 0)
    turned = jnp.concatenate([rows[4:8], rows[0:4]], axis=0)
    one = jnp.where((place == 3) | (place == 7), 1.0, jnp.where(place < 3, rows, turned))
    return jnp.concatenate([one, turned], axis=0)


def halves(tile):
    lane = lax.broadcasted_iota(jnp.int32, tile.shape, 1)
    turned = pltpu.roll(tile, LANES // 2, 1)
    low = lane < LANES // 2
    return jnp.where(low, tile, turned), jnp.where(low, turned, tile)


def lane_tile(index):
    return pl.ds(pl.multiple_of(index * LANES, LANES), LANES)


def list_slots_kernel(
    fine_slots_ref, fine_counts_ref, coarse_slots_ref, coarse_counts_ref, out_ref, *units_refs, entries
):
    fine, coarse = fine_slots_ref.shape[0], coarse_slots_ref.shape[0]
    spare = LANES - fine - coarse
    slots = jnp.concatenate(
        [fine_slots_ref[...], coarse_slots_ref[...], jnp.zeros((spare, SLOTS), jnp.int32)], axis=0
    )
    slots = slots.astype(jnp.float32).T.astype(jnp.int32)
    counts = jnp.concatenate(
        [fine_counts_ref[...], coarse_counts_ref[...], jnp.zeros((1, spare), jnp.int32)], axis=1
    )
    shape = (SLOTS, LANES)
    in_fine = lax.broadcasted_iota(jnp.int32, shape, 1) < fine
    clusters = jnp.where(in_fine, fine, coarse)
    nothing = jnp.where(in_fine, entries[0], entries[1])
    live = lax.broadcasted_iota(jnp.int32, shape, 0) < counts
    own = live & (slots < clusters)
    received = live & (slots >= clusters)
    row = lax.broadcasted_iota(jnp.int32, (SLOTS, SLOTS), 0)
    column = lax.broadcasted_iota(jnp.int32, (SLOTS, SLOTS), 1)
    upto = jnp.where(column <= row, 1.0, 0.0).astype(jnp.bfloat16)
    turns = []
    for start, chosen, value, blank in (
        (0, own, slots, clusters),
        (RECEIVED, received, slots - clusters, nothing),
    ):
        rank = bdot(upto, jnp.where(chosen, 1.0, 0.0).astype(jnp.bfloat16), NN).astype(jnp.int32)
        spot = jnp.where(chosen, rank - 1, -1)
        value = value - blank
        for first in range(0, SLOTS, 8):
            rows = [
                blank[:1] + jnp.sum(jnp.where(spot == place, value, 0), axis=0, keepdims=True)
                for place in range(first, first + 8)
            ]
            out_ref[start + first:start + first + 8] = jnp.concatenate(rows, axis=0)
        out_ref[start + SLOTS:start + SLOTS + CHUNK] = jnp.broadcast_to(blank[:1], (CHUNK, LANES))
        turns.append(jnp.maximum((rank[SLOTS - 1:] + CHUNK - 1) // CHUNK, 1))
    turns = jnp.concatenate(turns + [jnp.zeros((6, LANES), jnp.int32)], axis=0).astype(jnp.float32).T
    row = lax.broadcasted_iota(jnp.int32, (LANES, LANES), 0)
    column = lax.broadcasted_iota(jnp.int32, (LANES, LANES), 1)
    upto = (column <= row) & ((row < fine) == (column < fine))
    ends = bdot(jnp.where(upto, 1.0, 0.0).astype(jnp.bfloat16), turns.astype(jnp.bfloat16), NN)
    ends, turns = ends.astype(jnp.int32), turns.astype(jnp.int32)
    for side in range(2):
        for level, (low, count) in enumerate(((0, fine), (fine, coarse))):
            units_ref = units_refs[2 * side + level]
            end = ends[low:low + count, side:side + 1]
            took = turns[low:low + count, side:side + 1]
            lane = lax.broadcasted_iota(jnp.int32, (1, LANES), 1)
            for tile in range(units_ref.shape[0]):
                place = tile * LANES + lane
                passed = end <= place
                target = jnp.sum(jnp.where(passed, 1, 0), axis=0, keepdims=True)
                turn = place - jnp.sum(jnp.where(passed, took, 0), axis=0, keepdims=True)
                over = target >= count
                start = side * RECEIVED + jnp.where(over, SLOTS, turn * CHUNK)
                code = start * LANES + low + jnp.where(over, count - 1, target)
                if tile == units_ref.shape[0] - 1:
                    code = jnp.where(lane == LANES - 1, end[count - 1:], code)
                units_ref[tile:tile + 1] = code


def pack_send(send_ref, out_ref, dup_coef, dup_rows, owners, capacity, px, entry_first=False):
    pairs = capacity // 2
    lane = lax.broadcasted_iota(jnp.int32, (px, LANES), 1) < LANES // 2
    lane8 = lax.broadcasted_iota(jnp.int32, (8, LANES), 1) < LANES // 2

    def one_owner(owner, carry):
        before = None
        for pair in range(pairs):
            first, second = [
                send_ref[0, entry, owner] if entry_first else send_ref[0, owner, entry]
                for entry in (2 * pair, 2 * pair + 1)
            ]
            out_ref[owner, pair * px:(pair + 1) * px, :] = jnp.where(
                lane, dup_coef[first], dup_coef[second]
            ).astype(jnp.bfloat16)
            rows = jnp.where(lane8, dup_rows[first], dup_rows[second])
            if pair % 2 == 0:
                before = rows
            else:
                start = pairs * px + (pair - 1) * 8
                out_ref[owner, start:start + 16, :] = jnp.concatenate(
                    [before, rows], axis=0
                ).astype(jnp.bfloat16)
        return carry

    lax.fori_loop(0, owners, one_owner, 0)


def pack_fine_kernel(send_ref, coef_ref, points_ref, out_ref, rows_ref, dup_coef, dup_rows):
    _, owners, capacity = send_ref.shape
    px = coef_ref.shape[0]
    rows_ref[...] = split_rows(points_ref[...])

    def one_tile(index, carry):
        a, b = halves(coef_ref[:, lane_tile(index)].astype(jnp.float32))
        dup_coef[2 * index] = a
        dup_coef[2 * index + 1] = b
        a, b = halves(rows_ref[:, lane_tile(index)])
        dup_rows[2 * index] = a
        dup_rows[2 * index + 1] = b
        return carry

    lax.fori_loop(0, coef_ref.shape[1] // LANES, one_tile, 0, unroll=4)
    pack_send(send_ref, out_ref, dup_coef, dup_rows, owners, capacity, px)


def pack_coarse_kernel(
    send_ref, coef_ref, transfer_ref, points_ref, out_ref, rows_ref, coarse_ref, dup_coef, dup_rows
):
    _, capacity, owners = send_ref.shape
    px = coef_ref.shape[0]
    rows_ref[...] = split_rows(points_ref[...])

    def one_tile(index, carry):
        doubled = []
        for part in range(2):
            q = 2 * index + part
            a, b = halves(transfer_ref[:, lane_tile(q)].astype(jnp.float32))
            matrix = jnp.concatenate([a, b], axis=0).astype(jnp.bfloat16)
            block = bdot(coef_ref[:, lane_tile(q)], matrix, NN)
            dup_coef[q] = block
            doubled.append(block)
        lane = lax.broadcasted_iota(jnp.int32, (px, LANES), 1) < LANES // 2
        coarse_ref[:, lane_tile(index)] = jnp.where(lane, doubled[0], doubled[1]).astype(jnp.bfloat16)
        a, b = halves(rows_ref[:, lane_tile(index)])
        dup_rows[2 * index] = a
        dup_rows[2 * index + 1] = b
        return carry

    lax.fori_loop(0, coef_ref.shape[1] // (2 * LANES), one_tile, 0, unroll=2)
    pack_send(send_ref, out_ref, dup_coef, dup_rows, owners, capacity, px, entry_first=True)


def turned(rows):
    row = lax.broadcasted_iota(jnp.int32, (LANES, LANES), 0)
    column = lax.broadcasted_iota(jnp.int32, (LANES, LANES), 1)
    unit = jnp.where(row == column, 1.0, 0.0).astype(jnp.bfloat16)
    return bdot(unit, rows, NT).astype(jnp.bfloat16)


def put_pair(entry, coef, rows, coef_table, feature_table):
    a, b = halves(coef.astype(jnp.float32))
    coef_table[entry] = a.astype(jnp.bfloat16)
    coef_table[entry + 1] = b.astype(jnp.bfloat16)
    features = turned(jnp.concatenate([source_features(rows).astype(jnp.bfloat16)] * QUAD, axis=0))
    feature_table[entry] = features[:64]
    feature_table[entry + 1] = features[64:]


def put_nothing(entry, coef_table, feature_table):
    coef_table[entry] = jnp.zeros(coef_table.shape[1:], jnp.bfloat16)
    place = lax.broadcasted_iota(jnp.int32, (8, LANES), 0)
    nothing = source_features(jnp.where(place == 3, FAR_AWAY, 0.0)).astype(jnp.bfloat16)
    feature_table[entry] = turned(jnp.concatenate([nothing] * QUAD, axis=0))[:64]


def build_own(coef_ref, rows_ref, coef_table, feature_table):
    tiles = coef_ref.shape[1] // LANES

    def one_tile(index, carry):
        tile = lane_tile(index)
        put_pair(2 * index, coef_ref[:, tile], rows_ref[:, tile], coef_table, feature_table)
        return carry

    lax.fori_loop(0, tiles, one_tile, 0, unroll=4)
    put_nothing(2 * tiles, coef_table, feature_table)


def build_received(recv_ref, coef_table, feature_table):
    owners, recv_rows, _ = recv_ref.shape
    px = coef_table.shape[1]
    pairs = recv_rows // (px + 8)

    def one_owner(owner, carry):
        for pair in range(0, pairs, 2):
            start = pairs * px + pair * 8
            both = recv_ref[owner, start:start + 16, :].astype(jnp.float32)
            for part in range(2):
                where = pair + part
                put_pair(
                    owner * (2 * pairs) + 2 * where,
                    recv_ref[owner, where * px:(where + 1) * px, :],
                    both[8 * part:8 * part + 8],
                    coef_table,
                    feature_table,
                )
        return carry

    lax.fori_loop(0, owners, one_owner, 0)
    put_nothing(owners * pairs * 2, coef_table, feature_table)


def build_targets(rows_ref, target_table):
    def one_tile(index, carry):
        a, b = halves(target_features(rows_ref[:, lane_tile(index)]))
        target_table[2 * index] = a.astype(jnp.bfloat16)
        target_table[2 * index + 1] = b.astype(jnp.bfloat16)
        return carry

    lax.fori_loop(0, rows_ref.shape[1] // LANES, one_tile, 0, unroll=4)


def sweep(list_ref, units_ref, first, coef_table, feature_table, target_table, first_buffer, second_buffer, acc):
    px = coef_table.shape[1]
    lane = lax.broadcasted_iota(jnp.int32, (64, 16 * QUAD), 1) // 16
    lane_t = lax.broadcasted_iota(jnp.int32, (16, LANES), 1) // 64
    lane_x = lax.broadcasted_iota(jnp.int32, (px, LANES), 1) < 64
    blank = jnp.zeros((16, LANES), jnp.bfloat16)
    acc[...] = jnp.zeros_like(acc)

    def partners(unit):
        row, column = unit
        return [list_ref[row + m, column] for m in range(CHUNK)]

    def units_of(place):
        codes = [units_ref[place >> 7, (place & (LANES - 1)) + u] for u in range(UNITS)]
        return [(code >> 7, code & (LANES - 1)) for code in codes]

    def tiles(units, buffer):
        for start in range(0, UNITS, QUAD):
            quad = units[start:start + QUAD]
            weights = []
            for u in range(QUAD):
                own = jnp.where(lane_t == u % 2, target_table[quad[u][1] - first], blank)
                weights.append(jnp.concatenate([own if v == u // 2 else blank for v in range(QUAD // 2)], axis=1))
            weights = jnp.concatenate(weights, axis=0)
            ids = [partners(unit) for unit in quad]
            for part in range(0, CHUNK, 4):
                rows = []
                for m in range(part, part + 4):
                    tile = feature_table[ids[0][m]]
                    for u in range(1, QUAD):
                        tile = jnp.where(lane == u, feature_table[ids[u][m]], tile)
                    rows.append(tile)
                power = bdot(jnp.concatenate(rows, axis=0), weights, NN)
                buffer[start // QUAD, part * 64:(part + 4) * 64] = jnp.exp(power).astype(jnp.bfloat16)

    def products(units, buffer):
        for start in range(0, UNITS, QUAD):
            quad = units[start:start + QUAD]
            coefs = []
            for unit in quad:
                ids = partners(unit)
                coefs.append(
                    jnp.concatenate(
                        [
                            jnp.where(lane_x, coef_table[ids[m]], coef_table[ids[m + 1]])
                            for m in range(0, CHUNK, 2)
                        ],
                        axis=1,
                    )
                )
            product = bdot(jnp.concatenate(coefs, axis=0), buffer[start // QUAD], NN)
            for u in range(QUAD):
                side = (u // 2) * LANES
                acc[u % 2, quad[u][1] - first] += product[u * px:(u + 1) * px, side:side + LANES]

    def two_sets(index, carry):
        here = index * (2 * UNITS)
        second = units_of(here + UNITS)
        tiles(second, second_buffer)
        products(units_of(here), first_buffer)
        tiles(units_of(here + 2 * UNITS), first_buffer)
        products(second, second_buffer)
        return carry

    total = units_ref[units_ref.shape[0] - 1, LANES - 1]
    tiles(units_of(0), first_buffer)
    lax.fori_loop(0, (total + 2 * UNITS - 1) // (2 * UNITS), two_sets, 0)


def summed(acc, target):
    low = lax.broadcasted_iota(jnp.int32, acc.shape[2:], 1) < 64
    here = jnp.where(low, acc[0, target], acc[1, target])
    return here + pltpu.roll(here, 64, 1)


def put_sums(acc, clusters, out_ref, before_ref=None):
    low = lax.broadcasted_iota(jnp.int32, acc.shape[2:], 1) < 64

    def one_tile(index, carry):
        tile = lane_tile(index)
        sums = jnp.where(low, summed(acc, 2 * index), summed(acc, 2 * index + 1))
        out_ref[:, tile] = sums if before_ref is None else before_ref[:, tile] + sums
        return carry

    lax.fori_loop(0, clusters // 2, one_tile, 0, unroll=4)


def own_kernel(
    list_ref,
    fine_units_ref,
    coarse_units_ref,
    fine_coef_ref,
    fine_rows_ref,
    coarse_coef_ref,
    coarse_rows_ref,
    fine_out_ref,
    coarse_out_ref,
    *scratch,
):
    first = 0
    for units_ref, coef_ref, rows_ref, out_ref in (
        (fine_units_ref, fine_coef_ref, fine_rows_ref, fine_out_ref),
        (coarse_units_ref, coarse_coef_ref, coarse_rows_ref, coarse_out_ref),
    ):
        clusters = rows_ref.shape[1] // 64
        build_own(coef_ref, rows_ref, *scratch[:2])
        build_targets(rows_ref, scratch[2])
        sweep(list_ref, units_ref, first, *scratch)
        put_sums(scratch[-1], clusters, out_ref)
        first += clusters


def fine_kernel(list_ref, units_ref, recv_ref, rows_ref, own_ref, out_ref, *scratch):
    build_received(recv_ref, *scratch[:2])
    build_targets(rows_ref, scratch[2])
    sweep(list_ref, units_ref, 0, *scratch)
    put_sums(scratch[-1], rows_ref.shape[1] // 64, out_ref, own_ref)


def coarse_kernel(groups, *refs):
    list_ref, units_ref, recv_ref, rows_ref, own_ref, fine_ref, transfer_ref = refs[:7]
    probes_refs = refs[7:7 + groups]
    out_ref, terms_ref = refs[7 + groups:9 + groups]
    gram_ref, *scratch = refs[9 + groups:]
    clusters = rows_ref.shape[1] // 64
    probes = probes_refs[0].shape[0]
    acc = scratch[-1]
    build_received(recv_ref, *scratch[:2])
    build_targets(rows_ref, scratch[2])
    sweep(list_ref, units_ref, fine_ref.shape[1] // 64, *scratch)
    gram_ref[...] = jnp.zeros_like(gram_ref)

    def one_group(group, carry):
        grams = [None] * groups
        for part in range(4):
            q = group * 4 + part
            own = halves(own_ref[:, lane_tile(group * 2 + part // 2)])[part % 2]
            twice = (summed(acc, q) + own).astype(jnp.bfloat16)
            matrix = transfer_ref[:, lane_tile(q)].astype(jnp.float32)
            low = lax.broadcasted_iota(jnp.int32, matrix.shape, 1) < 64
            matrix = jnp.concatenate(
                [jnp.where(low, matrix, 0.0), jnp.where(low, 0.0, matrix)], axis=0
            ).astype(jnp.bfloat16)
            total = fine_ref[:, lane_tile(q)] + bdot(twice, matrix, NT)
            out_ref[:, lane_tile(q)] = total
            high = total.astype(jnp.bfloat16)
            rest = (total - high.astype(jnp.float32)).astype(jnp.bfloat16)
            for block, probes_ref in enumerate(probes_refs):
                tile = probes_ref[:, lane_tile(q)]
                term = bdot(tile, high, NT) + bdot(tile, rest, NT)
                grams[block] = term if grams[block] is None else grams[block] + term
        for block in range(groups):
            gram_ref[block] += grams[block]
        return carry

    lax.fori_loop(0, clusters // 4, one_group, 0)
    place = lax.axis_index("probe")
    for b in range(groups):
        block = gram_ref[lax.rem(place - b + groups, groups)]
        packed = jnp.concatenate([block[i:i + 8, :probes] for i in range(0, probes, 8)], axis=1)

        def one_owner(owner, carry):
            terms_ref[owner * groups + b] = packed
            return carry

        lax.fori_loop(0, terms_ref.shape[0] // groups, one_owner, 0)


def gram_kernel(terms_ref, out_ref, *, groups, scale):
    probes = out_ref.shape[0]
    columns = []
    for b in range(groups):
        total = terms_ref[b]
        for owner in range(1, terms_ref.shape[0] // groups):
            total = total + terms_ref[owner * groups + b]
        columns.append(
            jnp.concatenate([total[:, i * probes:(i + 1) * probes] for i in range(probes // 8)], axis=0)
        )
    out_ref[...] = jnp.concatenate(columns, axis=1) * scale


def sweep_scratch(total, clusters, px):
    return [
        pltpu.VMEM((total + 1, px, LANES), jnp.bfloat16),
        pltpu.VMEM((total + 1, 64, 16 * QUAD), jnp.bfloat16),
        pltpu.VMEM((clusters, 16, LANES), jnp.bfloat16),
        pltpu.VMEM((UNITS // QUAD, CHUNK * 64, QUAD * 64), jnp.bfloat16),
        pltpu.VMEM((UNITS // QUAD, CHUNK * 64, QUAD * 64), jnp.bfloat16),
        pltpu.VMEM((2, clusters, px, LANES), jnp.float32),
    ]


def shards(
    coef_fine,
    points_fine,
    points_coarse,
    transfer,
    send_fine,
    slots_fine,
    counts_fine,
    send_coarse,
    slots_coarse,
    counts_coarse,
):
    probes = coef_fine.shape[0]
    fine_count = counts_fine.shape[0]
    coarse_count = counts_coarse.shape[0]
    owners = lax.axis_size("leaf")
    groups = lax.axis_size("probe")
    px = -(-probes // 16) * 16
    coef = coef_fine if px == probes else jnp.pad(coef_fine, ((0, px - probes), (0, 0)))
    cap_fine = send_fine.shape[2]
    cap_coarse = send_coarse.shape[2]

    def params(scratch, blocks):
        size = SPARE + blocks * px * points_fine.shape[1] * 4
        for ref in scratch:
            size += math.prod(ref.shape[:-1]) * -(-ref.shape[-1] // LANES) * LANES * ref.dtype.itemsize
        return pltpu.CompilerParams(vmem_limit_bytes=size)

    fine_pack = [
        pltpu.VMEM((fine_count, px, LANES), jnp.float32),
        pltpu.VMEM((fine_count, 8, LANES), jnp.float32),
    ]
    coarse_pack = [
        pltpu.VMEM((coarse_count, px, LANES), jnp.float32),
        pltpu.VMEM((coarse_count, 8, LANES), jnp.float32),
    ]
    own_scratch = sweep_scratch(fine_count, fine_count, px)
    fine_scratch = sweep_scratch(owners * cap_fine, fine_count, px)
    coarse_scratch = sweep_scratch(owners * cap_coarse, coarse_count, px)
    smem = pl.BlockSpec(memory_space=pltpu.SMEM)
    vmem = pl.BlockSpec(memory_space=pltpu.VMEM)
    bf16, f32 = jnp.bfloat16, jnp.float32

    turned = [coef_fine]
    for step in range(1, groups):
        turned.append(lax.ppermute(coef_fine, "probe", [(i, (i + step) % groups) for i in range(groups)]))

    fine_send, fine_rows = pl.pallas_call(
        pack_fine_kernel,
        out_shape=(
            jax.ShapeDtypeStruct((owners, (cap_fine // 2) * (px + 8), LANES), bf16),
            jax.ShapeDtypeStruct((8, points_fine.shape[1]), f32),
        ),
        in_specs=[smem, vmem, vmem],
        out_specs=[vmem, vmem],
        scratch_shapes=fine_pack,
        compiler_params=params(fine_pack, owners // 4),
        name="pack_fine",
    )(send_fine, coef, points_fine)
    fine_recv = lax.all_to_all(fine_send, "leaf", split_axis=0, concat_axis=0, tiled=True)

    coarse_send, coarse_rows, coarse_coef = pl.pallas_call(
        pack_coarse_kernel,
        out_shape=(
            jax.ShapeDtypeStruct((owners, (cap_coarse // 2) * (px + 8), LANES), bf16),
            jax.ShapeDtypeStruct((8, points_coarse.shape[1]), f32),
            jax.ShapeDtypeStruct((px, points_coarse.shape[1]), bf16),
        ),
        in_specs=[smem, vmem, vmem, vmem],
        out_specs=[vmem, vmem, vmem],
        scratch_shapes=coarse_pack,
        compiler_params=params(coarse_pack, owners // 4),
        name="pack_coarse",
    )(jnp.swapaxes(send_coarse, 1, 2), coef, transfer, points_coarse)
    fine_total = owners * cap_fine
    coarse_total = owners * cap_coarse
    unit_rows = [-(-(count * (SLOTS // CHUNK) + 2 * UNITS + 1) // LANES) for count in (fine_count, coarse_count)]
    slot_list, fine_own, coarse_own, fine_units, coarse_units = pl.pallas_call(
        functools.partial(list_slots_kernel, entries=(fine_total, coarse_total)),
        out_shape=[jax.ShapeDtypeStruct((RECEIVED + SLOTS + CHUNK, LANES), jnp.int32)]
        + [jax.ShapeDtypeStruct((rows, LANES), jnp.int32) for rows in unit_rows * 2],
        in_specs=[vmem] * 4,
        out_specs=[vmem] * 5,
        name="list_slots",
    )(slots_fine, counts_fine.reshape(1, -1), slots_coarse, counts_coarse.reshape(1, -1))
    fine_sums, coarse_sums = pl.pallas_call(
        own_kernel,
        out_shape=(
            jax.ShapeDtypeStruct((px, points_fine.shape[1]), f32),
            jax.ShapeDtypeStruct((px, points_coarse.shape[1]), f32),
        ),
        in_specs=[smem] * 3 + [vmem] * 4,
        out_specs=[vmem, vmem],
        scratch_shapes=own_scratch,
        compiler_params=params(own_scratch, 4),
        cost_estimate=pl.CostEstimate(flops=10**10, bytes_accessed=10**7, transcendentals=10**7),
        name="own_sweep",
    )(slot_list, fine_own, coarse_own, coef, fine_rows, coarse_coef, coarse_rows)

    coarse_send, coarse_sums = lax.optimization_barrier((coarse_send, coarse_sums))
    coarse_recv = lax.all_to_all(coarse_send, "leaf", split_axis=0, concat_axis=0, tiled=True)

    fine_far = pl.pallas_call(
        fine_kernel,
        out_shape=jax.ShapeDtypeStruct((px, points_fine.shape[1]), f32),
        in_specs=[smem] * 2 + [vmem] * 3,
        out_specs=vmem,
        scratch_shapes=fine_scratch,
        compiler_params=params(fine_scratch, owners // 4 + 4),
        name="fine_sweep",
    )(slot_list, fine_units, fine_recv, fine_rows, fine_sums)

    term_shape = (owners * groups, 8, probes * probes // 8)
    far, terms = pl.pallas_call(
        functools.partial(coarse_kernel, groups),
        out_shape=(
            jax.ShapeDtypeStruct((px, points_fine.shape[1]), f32),
            jax.ShapeDtypeStruct(term_shape, f32),
        ),
        in_specs=[smem] * 2 + [vmem] * (5 + groups),
        out_specs=[vmem, vmem],
        scratch_shapes=[pltpu.VMEM((groups, probes, px), f32)] + coarse_scratch,
        compiler_params=params(coarse_scratch, owners // 4 + 6),
        name="coarse_sweep",
    )(slot_list, coarse_units, coarse_recv, coarse_rows, coarse_sums, fine_far, transfer, *turned)

    terms = lax.all_to_all(terms, ("leaf", "probe"), split_axis=0, concat_axis=0, tiled=True)
    probe_gram = pl.pallas_call(
        functools.partial(
            gram_kernel, groups=groups, scale=1.0 / math.sqrt(owners * fine_count * 64)
        ),
        out_shape=jax.ShapeDtypeStruct((probes, groups * probes), f32),
        in_specs=[vmem],
        out_specs=vmem,
        name="gram_sum",
    )(terms)
    return (far[:probes], probe_gram)


def solution(mesh):
    return jax.shard_map(
        shards,
        mesh=mesh,
        in_specs=(
            P("probe", "leaf"),
            P(None, "leaf"),
            P(None, "leaf"),
            P(None, "leaf"),
            P("leaf", None, None),
            P("leaf", None),
            P("leaf"),
            P("leaf", None, None),
            P("leaf", None),
            P("leaf"),
        ),
        out_specs=(P("probe", "leaf"), P("probe", None)),
        check_vma=False,
    )
```

```python
import functools
import functools
import math

import jax
import jax.numpy as jnp
from jax import lax
from jax.experimental import pallas as pl
from jax.experimental.pallas import tpu as pltpu
from jax.sharding import PartitionSpec as P

KERNEL_RATE = 1.5
POINT_SCALE = math.sqrt(2.0 * KERNEL_RATE)
LANES = 128
UNITS = 8
QUAD = 4
CHUNK = 8
FAR_AWAY = -30000.0
SLOTS = 64
RECEIVED = SLOTS + CHUNK
VMEM = 56 * 1024 * 1024
SPARE = 6 * 1024 * 1024

NT = (((1,), (1,)), ((), ()))
NN = (((1,), (0,)), ((), ()))


def bdot(a, b, dims):
    return lax.dot_general(a, b, dims, preferred_element_type=jnp.float32)


def split_rows(points):
    v = points * POINT_SCALE
    norm = -0.5 * (v[0:1] * v[0:1] + v[1:2] * v[1:2] + v[2:3] * v[2:3])
    full = jnp.concatenate([v, norm], axis=0)
    high = full.astype(jnp.bfloat16).astype(jnp.float32)
    rest = (full - high).astype(jnp.bfloat16).astype(jnp.float32)
    return jnp.concatenate([high, rest], axis=0)


def source_features(rows):
    place = lax.broadcasted_iota(jnp.int32, rows.shape, 0)
    one = jnp.where((place == 3) | (place == 7), 1.0, 0.0)
    return jnp.concatenate([rows, jnp.where(place < 3, rows, one)], axis=0)


def target_features(rows):
    place = lax.broadcasted_iota(jnp.int32, rows.shape, 0)
    turned = jnp.concatenate([rows[4:8], rows[0:4]], axis=0)
    one = jnp.where((place == 3) | (place == 7), 1.0, jnp.where(place < 3, rows, turned))
    return jnp.concatenate([one, turned], axis=0)


def halves(tile):
    lane = lax.broadcasted_iota(jnp.int32, tile.shape, 1)
    turned = pltpu.roll(tile, LANES // 2, 1)
    low = lane < LANES // 2
    return jnp.where(low, tile, turned), jnp.where(low, turned, tile)


def lane_tile(index):
    return pl.ds(pl.multiple_of(index * LANES, LANES), LANES)


def list_slots(
    fine_slots_ref, fine_counts_ref, coarse_slots_ref, coarse_counts_ref, out_ref, *units_refs, entries
):
    fine, coarse = fine_slots_ref.shape[0], coarse_slots_ref.shape[0]
    spare = LANES - fine - coarse
    slots = jnp.concatenate(
        [fine_slots_ref[...], coarse_slots_ref[...], jnp.zeros((spare, SLOTS), jnp.int32)], axis=0
    )
    slots = slots.astype(jnp.float32).T.astype(jnp.int32)
    counts = jnp.concatenate(
        [fine_counts_ref[...], coarse_counts_ref[...], jnp.zeros((1, spare), jnp.int32)], axis=1
    )
    shape = (SLOTS, LANES)
    in_fine = lax.broadcasted_iota(jnp.int32, shape, 1) < fine
    clusters = jnp.where(in_fine, fine, coarse)
    nothing = jnp.where(in_fine, entries[0], entries[1])
    live = lax.broadcasted_iota(jnp.int32, shape, 0) < counts
    own = live & (slots < clusters)
    received = live & (slots >= clusters)
    row = lax.broadcasted_iota(jnp.int32, (SLOTS, SLOTS), 0)
    column = lax.broadcasted_iota(jnp.int32, (SLOTS, SLOTS), 1)
    upto = jnp.where(column <= row, 1.0, 0.0).astype(jnp.bfloat16)
    turns = []
    for start, chosen, value, blank in (
        (0, own, slots, clusters),
        (RECEIVED, received, slots - clusters, nothing),
    ):
        rank = bdot(upto, jnp.where(chosen, 1.0, 0.0).astype(jnp.bfloat16), NN).astype(jnp.int32)
        spot = jnp.where(chosen, rank - 1, -1)
        value = value - blank
        for first in range(0, SLOTS, 8):
            rows = [
                blank[:1] + jnp.sum(jnp.where(spot == place, value, 0), axis=0, keepdims=True)
                for place in range(first, first + 8)
            ]
            out_ref[start + first:start + first + 8] = jnp.concatenate(rows, axis=0)
        out_ref[start + SLOTS:start + SLOTS + CHUNK] = jnp.broadcast_to(blank[:1], (CHUNK, LANES))
        turns.append(jnp.maximum((rank[SLOTS - 1:] + CHUNK - 1) // CHUNK, 1))
    turns = jnp.concatenate(turns + [jnp.zeros((6, LANES), jnp.int32)], axis=0).astype(jnp.float32).T
    row = lax.broadcasted_iota(jnp.int32, (LANES, LANES), 0)
    column = lax.broadcasted_iota(jnp.int32, (LANES, LANES), 1)
    upto = (column <= row) & ((row < fine) == (column < fine))
    ends = bdot(jnp.where(upto, 1.0, 0.0).astype(jnp.bfloat16), turns.astype(jnp.bfloat16), NN)
    ends, turns = ends.astype(jnp.int32), turns.astype(jnp.int32)
    for side in range(2):
        for level, (low, count) in enumerate(((0, fine), (fine, coarse))):
            units_ref = units_refs[2 * side + level]
            end = ends[low:low + count, side:side + 1]
            took = turns[low:low + count, side:side + 1]
            lane = lax.broadcasted_iota(jnp.int32, (1, LANES), 1)
            for tile in range(units_ref.shape[0]):
                place = tile * LANES + lane
                passed = end <= place
                target = jnp.sum(jnp.where(passed, 1, 0), axis=0, keepdims=True)
                turn = place - jnp.sum(jnp.where(passed, took, 0), axis=0, keepdims=True)
                over = target >= count
                start = side * RECEIVED + jnp.where(over, SLOTS, turn * CHUNK)
                code = start * LANES + low + jnp.where(over, count - 1, target)
                if tile == units_ref.shape[0] - 1:
                    code = jnp.where(lane == LANES - 1, end[count - 1:], code)
                units_ref[tile:tile + 1] = code


def pack_send(send_ref, out_ref, dup_coef, dup_rows, owners, capacity, px, entry_first=False):
    pairs = capacity // 2
    lane = lax.broadcasted_iota(jnp.int32, (px, LANES), 1) < LANES // 2
    lane8 = lax.broadcasted_iota(jnp.int32, (8, LANES), 1) < LANES // 2

    def one_owner(owner, carry):
        before = None
        for pair in range(pairs):
            first, second = [
                send_ref[0, entry, owner] if entry_first else send_ref[0, owner, entry]
                for entry in (2 * pair, 2 * pair + 1)
            ]
            out_ref[owner, pair * px:(pair + 1) * px, :] = jnp.where(
                lane, dup_coef[first], dup_coef[second]
            ).astype(jnp.bfloat16)
            rows = jnp.where(lane8, dup_rows[first], dup_rows[second])
            if pair % 2 == 0:
                before = rows
            else:
                start = pairs * px + (pair - 1) * 8
                out_ref[owner, start:start + 16, :] = jnp.concatenate(
                    [before, rows], axis=0
                ).astype(jnp.bfloat16)
        return carry

    lax.fori_loop(0, owners, one_owner, 0, unroll=4)


def pack_fine_kernel(send_ref, coef_ref, points_ref, out_ref, rows_ref, dup_coef, dup_rows):
    _, owners, capacity = send_ref.shape
    px = coef_ref.shape[0]
    rows_ref[...] = split_rows(points_ref[...])

    def one_tile(index, carry):
        a, b = halves(coef_ref[:, lane_tile(index)].astype(jnp.float32))
        dup_coef[2 * index] = a
        dup_coef[2 * index + 1] = b
        a, b = halves(rows_ref[:, lane_tile(index)])
        dup_rows[2 * index] = a
        dup_rows[2 * index + 1] = b
        return carry

    lax.fori_loop(0, coef_ref.shape[1] // LANES, one_tile, 0, unroll=8)
    pack_send(send_ref, out_ref, dup_coef, dup_rows, owners, capacity, px)


def pack_coarse(
    send_ref, coef_ref, transfer_ref, points_ref, out_ref, rows_ref, coarse_ref, dup_coef, dup_rows
):
    _, capacity, owners = send_ref.shape
    px = coef_ref.shape[0]
    rows_ref[...] = split_rows(points_ref[...])

    def one_tile(index, carry):
        doubled = []
        for part in range(2):
            q = 2 * index + part
            a, b = halves(transfer_ref[:, lane_tile(q)].astype(jnp.float32))
            matrix = jnp.concatenate([a, b], axis=0).astype(jnp.bfloat16)
            block = bdot(coef_ref[:, lane_tile(q)], matrix, NN)
            dup_coef[q] = block
            doubled.append(block)
        lane = lax.broadcasted_iota(jnp.int32, (px, LANES), 1) < LANES // 2
        coarse_ref[:, lane_tile(index)] = jnp.where(lane, doubled[0], doubled[1]).astype(jnp.bfloat16)
        a, b = halves(rows_ref[:, lane_tile(index)])
        dup_rows[2 * index] = a
        dup_rows[2 * index + 1] = b
        return carry

    lax.fori_loop(0, coef_ref.shape[1] // (2 * LANES), one_tile, 0, unroll=8)
    pack_send(send_ref, out_ref, dup_coef, dup_rows, owners, capacity, px, entry_first=True)


def turned(rows):
    row = lax.broadcasted_iota(jnp.int32, (LANES, LANES), 0)
    column = lax.broadcasted_iota(jnp.int32, (LANES, LANES), 1)
    unit = jnp.where(row == column, 1.0, 0.0).astype(jnp.bfloat16)
    return bdot(unit, rows, NT).astype(jnp.bfloat16)


def put_pair(entry, coef, rows, coef_table, feature_table):
    a, b = halves(coef.astype(jnp.float32))
    coef_table[entry] = a.astype(jnp.bfloat16)
    coef_table[entry + 1] = b.astype(jnp.bfloat16)
    features = turned(jnp.concatenate([source_features(rows).astype(jnp.bfloat16)] * QUAD, axis=0))
    feature_table[entry] = features[:64]
    feature_table[entry + 1] = features[64:]


def put_nothing(entry, coef_table, feature_table):
    coef_table[entry] = jnp.zeros(coef_table.shape[1:], jnp.bfloat16)
    place = lax.broadcasted_iota(jnp.int32, (8, LANES), 0)
    nothing = source_features(jnp.where(place == 3, FAR_AWAY, 0.0)).astype(jnp.bfloat16)
    feature_table[entry] = turned(jnp.concatenate([nothing] * QUAD, axis=0))[:64]


def build_own(coef_ref, rows_ref, coef_table, feature_table):
    tiles = coef_ref.shape[1] // LANES

    def one_tile(index, carry):
        tile = lane_tile(index)
        put_pair(2 * index, coef_ref[:, tile], rows_ref[:, tile], coef_table, feature_table)
        return carry

    lax.fori_loop(0, tiles, one_tile, 0, unroll=16)
    put_nothing(2 * tiles, coef_table, feature_table)


def build_received(recv_ref, coef_table, feature_table):
    owners, recv_rows, _ = recv_ref.shape
    px = coef_table.shape[1]
    pairs = recv_rows // (px + 8)

    def one_owner(owner, carry):
        for pair in range(0, pairs, 2):
            start = pairs * px + pair * 8
            both = recv_ref[owner, start:start + 16, :].astype(jnp.float32)
            for part in range(2):
                where = pair + part
                put_pair(
                    owner * (2 * pairs) + 2 * where,
                    recv_ref[owner, where * px:(where + 1) * px, :],
                    both[8 * part:8 * part + 8],
                    coef_table,
                    feature_table,
                )
        return carry

    lax.fori_loop(0, owners, one_owner, 0, unroll=32 // pairs)
    put_nothing(owners * pairs * 2, coef_table, feature_table)


def build_targets(rows_ref, target_table):
    def one_tile(index, carry):
        a, b = halves(target_features(rows_ref[:, lane_tile(index)]))
        target_table[2 * index] = a.astype(jnp.bfloat16)
        target_table[2 * index + 1] = b.astype(jnp.bfloat16)
        return carry

    lax.fori_loop(0, rows_ref.shape[1] // LANES, one_tile, 0, unroll=16)


def sweep(list_ref, units_ref, first, coef_table, feature_table, target_table, first_buffer, second_buffer, acc):
    px = coef_table.shape[1]
    lane = lax.broadcasted_iota(jnp.int32, (64, 16 * QUAD), 1) // 16
    lane_t = lax.broadcasted_iota(jnp.int32, (16, LANES), 1) // 64
    lane_x = lax.broadcasted_iota(jnp.int32, (px, LANES), 1) < 64
    blank = jnp.zeros((16, LANES), jnp.bfloat16)
    acc[...] = jnp.zeros_like(acc)

    def partners(unit):
        row, column = unit
        return [list_ref[row + m, column] for m in range(CHUNK)]

    def units_of(place):
        codes = [units_ref[place >> 7, (place & (LANES - 1)) + u] for u in range(UNITS)]
        return [(code >> 7, code & (LANES - 1)) for code in codes]

    def tiles(units, buffer):
        for start in range(0, UNITS, QUAD):
            quad = units[start:start + QUAD]
            weights = []
            for u in range(QUAD):
                own = jnp.where(lane_t == u % 2, target_table[quad[u][1] - first], blank)
                weights.append(jnp.concatenate([own if v == u // 2 else blank for v in range(QUAD // 2)], axis=1))
            weights = jnp.concatenate(weights, axis=0)
            ids = [partners(unit) for unit in quad]
            for part in range(0, CHUNK, 4):
                rows = []
                for m in range(part, part + 4):
                    tile = feature_table[ids[0][m]]
                    for u in range(1, QUAD):
                        tile = jnp.where(lane == u, feature_table[ids[u][m]], tile)
                    rows.append(tile)
                power = bdot(jnp.concatenate(rows, axis=0), weights, NN)
                buffer[start // QUAD, part * 64:(part + 4) * 64] = jnp.exp(power).astype(jnp.bfloat16)

    def products(units, buffer):
        for start in range(0, UNITS, QUAD):
            quad = units[start:start + QUAD]
            coefs = []
            for unit in quad:
                ids = partners(unit)
                coefs.append(
                    jnp.concatenate(
                        [
                            jnp.where(lane_x, coef_table[ids[m]], coef_table[ids[m + 1]])
                            for m in range(0, CHUNK, 2)
                        ],
                        axis=1,
                    )
                )
            product = bdot(jnp.concatenate(coefs, axis=0), buffer[start // QUAD], NN)
            for u in range(QUAD):
                side = (u // 2) * LANES
                acc[u % 2, quad[u][1] - first] += product[u * px:(u + 1) * px, side:side + LANES]

    def two_sets(index, carry):
        here = index * (2 * UNITS)
        second = units_of(here + UNITS)
        tiles(second, second_buffer)
        products(units_of(here), first_buffer)
        tiles(units_of(here + 2 * UNITS), first_buffer)
        products(second, second_buffer)
        return carry

    total = units_ref[units_ref.shape[0] - 1, LANES - 1]
    tiles(units_of(0), first_buffer)
    lax.fori_loop(0, (total + 2 * UNITS - 1) // (2 * UNITS), two_sets, 0)


def summed(acc, target):
    low = lax.broadcasted_iota(jnp.int32, acc.shape[2:], 1) < 64
    here = jnp.where(low, acc[0, target], acc[1, target])
    return here + pltpu.roll(here, 64, 1)


def put_sums(acc, clusters, out_ref, before_ref=None):
    low = lax.broadcasted_iota(jnp.int32, acc.shape[2:], 1) < 64

    def one_tile(index, carry):
        tile = lane_tile(index)
        sums = jnp.where(low, summed(acc, 2 * index), summed(acc, 2 * index + 1))
        out_ref[:, tile] = sums if before_ref is None else before_ref[:, tile] + sums
        return carry

    lax.fori_loop(0, clusters // 2, one_tile, 0, unroll=8)


def own_kernel(
    send_ref,
    fine_slots_ref,
    fine_counts_ref,
    coarse_slots_ref,
    coarse_counts_ref,
    coef_ref,
    transfer_ref,
    points_ref,
    fine_rows_ref,
    send_out_ref,
    coarse_rows_ref,
    list_out_ref,
    fine_units_ref,
    coarse_units_ref,
    fine_out_ref,
    coarse_out_ref,
    coarse_coef_ref,
    dup_coef,
    dup_rows,
    fine_own_units,
    coarse_own_units,
    list_ref,
    fine_own_ref,
    coarse_own_ref,
    list_sem,
    fine_sem,
    coarse_sem,
    *scratch,
    entries,
):
    list_slots(
        fine_slots_ref,
        fine_counts_ref,
        coarse_slots_ref,
        coarse_counts_ref,
        list_out_ref,
        fine_own_units,
        coarse_own_units,
        fine_units_ref,
        coarse_units_ref,
        entries=entries,
    )
    copies = [
        pltpu.make_async_copy(list_out_ref, list_ref, list_sem),
        pltpu.make_async_copy(fine_own_units, fine_own_ref, fine_sem),
        pltpu.make_async_copy(coarse_own_units, coarse_own_ref, coarse_sem),
    ]
    for copy in copies:
        copy.start()
    pack_coarse(
        send_ref,
        coef_ref,
        transfer_ref,
        points_ref,
        send_out_ref,
        coarse_rows_ref,
        coarse_coef_ref,
        dup_coef,
        dup_rows,
    )
    for copy in copies:
        copy.wait()
    first = 0
    for units_ref, source_ref, rows_ref, out_ref in (
        (fine_own_ref, coef_ref, fine_rows_ref, fine_out_ref),
        (coarse_own_ref, coarse_coef_ref, coarse_rows_ref, coarse_out_ref),
    ):
        clusters = rows_ref.shape[1] // 64
        build_own(source_ref, rows_ref, *scratch[:2])
        build_targets(rows_ref, scratch[2])
        sweep(list_ref, units_ref, first, *scratch)
        put_sums(scratch[-1], clusters, out_ref)
        first += clusters


def fine_kernel(list_ref, units_ref, recv_ref, rows_ref, own_ref, out_ref, *scratch):
    build_received(recv_ref, *scratch[:2])
    build_targets(rows_ref, scratch[2])
    sweep(list_ref, units_ref, 0, *scratch)
    put_sums(scratch[-1], rows_ref.shape[1] // 64, out_ref, own_ref)


def coarse_kernel(groups, *refs):
    list_ref, units_ref, recv_ref, rows_ref, own_ref, fine_ref, transfer_ref = refs[:7]
    probes_refs = refs[7:7 + groups]
    out_ref, terms_ref = refs[7 + groups:9 + groups]
    gram_ref, split_ref, *scratch = refs[9 + groups:]
    clusters = rows_ref.shape[1] // 64
    px = split_ref.shape[0] // 2
    probes = probes_refs[0].shape[0]
    acc = scratch[-1]
    build_received(recv_ref, *scratch[:2])
    build_targets(rows_ref, scratch[2])
    sweep(list_ref, units_ref, fine_ref.shape[1] // 64, *scratch)

    def one_parent(q, carry):
        own = halves(own_ref[:, lane_tile(q >> 1)])
        own = jnp.where((q & 1) == 0, own[0], own[1])
        twice = (summed(acc, q) + own).astype(jnp.bfloat16)
        matrix = transfer_ref[:, lane_tile(q)].astype(jnp.float32)
        low = lax.broadcasted_iota(jnp.int32, matrix.shape, 1) < 64
        matrix = jnp.concatenate(
            [jnp.where(low, matrix, 0.0), jnp.where(low, 0.0, matrix)], axis=0
        ).astype(jnp.bfloat16)
        total = fine_ref[:, lane_tile(q)] + bdot(twice, matrix, NT)
        out_ref[:, lane_tile(q)] = total
        high = total.astype(jnp.bfloat16)
        split_ref[:px, lane_tile(q)] = high
        split_ref[px:, lane_tile(q)] = (total - high.astype(jnp.float32)).astype(jnp.bfloat16)
        return carry

    lax.fori_loop(0, clusters, one_parent, 0, unroll=8)
    for block, probes_ref in enumerate(probes_refs):
        term = bdot(probes_ref[...], split_ref[...], NT)
        gram_ref[block] = term[:, :px] + term[:, px:]
    place = lax.axis_index("probe")
    for b in range(groups):
        block = gram_ref[lax.rem(place - b + groups, groups)]
        packed = jnp.concatenate([block[i:i + 8, :probes] for i in range(0, probes, 8)], axis=1)

        def one_owner(owner, carry):
            terms_ref[owner * groups + b] = packed
            return carry

        lax.fori_loop(0, terms_ref.shape[0] // groups, one_owner, 0)


def gram_kernel(terms_ref, out_ref, *, groups, scale):
    probes = out_ref.shape[0]
    columns = []
    for b in range(groups):
        total = terms_ref[b]
        for owner in range(1, terms_ref.shape[0] // groups):
            total = total + terms_ref[owner * groups + b]
        columns.append(
            jnp.concatenate([total[:, i * probes:(i + 1) * probes] for i in range(probes // 8)], axis=0)
        )
    out_ref[...] = jnp.concatenate(columns, axis=1) * scale


def sweep_scratch(total, clusters, px):
    return [
        pltpu.VMEM((total + 1, px, LANES), jnp.bfloat16),
        pltpu.VMEM((total + 1, 64, 16 * QUAD), jnp.bfloat16),
        pltpu.VMEM((clusters, 16, LANES), jnp.bfloat16),
        pltpu.VMEM((UNITS // QUAD, CHUNK * 64, QUAD * 64), jnp.bfloat16),
        pltpu.VMEM((UNITS // QUAD, CHUNK * 64, QUAD * 64), jnp.bfloat16),
        pltpu.VMEM((2, clusters, px, LANES), jnp.float32),
    ]


def shards(
    coef_fine,
    points_fine,
    points_coarse,
    transfer,
    send_fine,
    slots_fine,
    counts_fine,
    send_coarse,
    slots_coarse,
    counts_coarse,
):
    probes = coef_fine.shape[0]
    fine_count = counts_fine.shape[0]
    coarse_count = counts_coarse.shape[0]
    owners = lax.axis_size("leaf")
    groups = lax.axis_size("probe")
    px = -(-probes // 16) * 16
    coef = coef_fine if px == probes else jnp.pad(coef_fine, ((0, px - probes), (0, 0)))
    cap_fine = send_fine.shape[2]
    cap_coarse = send_coarse.shape[2]

    def params(scratch, blocks):
        size = SPARE + blocks * px * points_fine.shape[1] * 4
        for ref in scratch:
            size += math.prod(ref.shape[:-1]) * -(-ref.shape[-1] // LANES) * LANES * ref.dtype.itemsize
        return pltpu.CompilerParams(vmem_limit_bytes=size)

    whole_vmem = pltpu.CompilerParams(vmem_limit_bytes=VMEM)
    fine_scratch = sweep_scratch(owners * cap_fine, fine_count, px)
    coarse_scratch = sweep_scratch(owners * cap_coarse, coarse_count, px)
    smem = pl.BlockSpec(memory_space=pltpu.SMEM)
    vmem = pl.BlockSpec(memory_space=pltpu.VMEM)
    bf16, f32 = jnp.bfloat16, jnp.float32

    turned = [coef_fine]
    for step in range(1, groups):
        turned.append(lax.ppermute(coef_fine, "probe", [(i, (i + step) % groups) for i in range(groups)]))

    fine_send, fine_rows = pl.pallas_call(
        pack_fine_kernel,
        out_shape=(
            jax.ShapeDtypeStruct((owners, (cap_fine // 2) * (px + 8), LANES), bf16),
            jax.ShapeDtypeStruct((8, points_fine.shape[1]), f32),
        ),
        in_specs=[smem, vmem, vmem],
        out_specs=[vmem, vmem],
        scratch_shapes=[
            pltpu.VMEM((fine_count, px, LANES), f32),
            pltpu.VMEM((fine_count, 8, LANES), f32),
        ],
        compiler_params=whole_vmem,
        name="pack_fine",
    )(send_fine, coef, points_fine)
    fine_recv = lax.all_to_all(fine_send, "leaf", split_axis=0, concat_axis=0, tiled=True)

    fine_total = owners * cap_fine
    coarse_total = owners * cap_coarse
    unit_rows = [-(-(count * (SLOTS // CHUNK) + 2 * UNITS + 1) // LANES) for count in (fine_count, coarse_count)]
    list_shape = (RECEIVED + SLOTS + CHUNK, LANES)
    i32 = jnp.int32
    coarse_send, coarse_rows, slot_list, fine_units, coarse_units, fine_sums, coarse_sums = pl.pallas_call(
        functools.partial(own_kernel, entries=(fine_total, coarse_total)),
        out_shape=(
            jax.ShapeDtypeStruct((owners, (cap_coarse // 2) * (px + 8), LANES), bf16),
            jax.ShapeDtypeStruct((8, points_coarse.shape[1]), f32),
            jax.ShapeDtypeStruct(list_shape, i32),
            jax.ShapeDtypeStruct((unit_rows[0], LANES), i32),
            jax.ShapeDtypeStruct((unit_rows[1], LANES), i32),
            jax.ShapeDtypeStruct((px, points_fine.shape[1]), f32),
            jax.ShapeDtypeStruct((px, points_coarse.shape[1]), f32),
        ),
        in_specs=[smem] + [vmem] * 8,
        out_specs=[vmem] * 7,
        scratch_shapes=[
            pltpu.VMEM((px, points_coarse.shape[1]), bf16),
            pltpu.VMEM((coarse_count, px, LANES), f32),
            pltpu.VMEM((coarse_count, 8, LANES), f32),
            pltpu.VMEM((unit_rows[0], LANES), i32),
            pltpu.VMEM((unit_rows[1], LANES), i32),
            pltpu.SMEM(list_shape, i32),
            pltpu.SMEM((unit_rows[0], LANES), i32),
            pltpu.SMEM((unit_rows[1], LANES), i32),
            pltpu.SemaphoreType.DMA,
            pltpu.SemaphoreType.DMA,
            pltpu.SemaphoreType.DMA,
        ]
        + sweep_scratch(fine_count, fine_count, px),
        compiler_params=whole_vmem,
        cost_estimate=pl.CostEstimate(flops=10**10, bytes_accessed=10**7, transcendentals=10**7),
        name="own_sweep",
    )(
        jnp.swapaxes(send_coarse, 1, 2),
        slots_fine,
        counts_fine.reshape(1, -1),
        slots_coarse,
        counts_coarse.reshape(1, -1),
        coef,
        transfer,
        points_coarse,
        fine_rows,
    )

    coarse_send, coarse_sums = lax.optimization_barrier((coarse_send, coarse_sums))
    coarse_recv = lax.all_to_all(coarse_send, "leaf", split_axis=0, concat_axis=0, tiled=True)

    fine_far = pl.pallas_call(
        fine_kernel,
        out_shape=jax.ShapeDtypeStruct((px, points_fine.shape[1]), f32),
        in_specs=[smem] * 2 + [vmem] * 3,
        out_specs=vmem,
        scratch_shapes=fine_scratch,
        compiler_params=params(fine_scratch, owners // 4 + 4),
        name="fine_sweep",
    )(slot_list, fine_units, fine_recv, fine_rows, fine_sums)

    term_shape = (owners * groups, 8, probes * probes // 8)
    far, terms = pl.pallas_call(
        functools.partial(coarse_kernel, groups),
        out_shape=(
            jax.ShapeDtypeStruct((px, points_fine.shape[1]), f32),
            jax.ShapeDtypeStruct(term_shape, f32),
        ),
        in_specs=[smem] * 2 + [vmem] * (5 + groups),
        out_specs=[vmem, vmem],
        scratch_shapes=[
            pltpu.VMEM((groups, probes, px), f32),
            pltpu.VMEM((2 * px, points_fine.shape[1]), bf16),
        ]
        + coarse_scratch,
        compiler_params=params(coarse_scratch, owners // 4 + 6),
        name="coarse_sweep",
    )(slot_list, coarse_units, coarse_recv, coarse_rows, coarse_sums, fine_far, transfer, *turned)

    terms = lax.all_to_all(terms, ("leaf", "probe"), split_axis=0, concat_axis=0, tiled=True)
    probe_gram = pl.pallas_call(
        functools.partial(
            gram_kernel, groups=groups, scale=1.0 / math.sqrt(owners * fine_count * 64)
        ),
        out_shape=jax.ShapeDtypeStruct((probes, groups * probes), f32),
        in_specs=[vmem],
        out_specs=vmem,
        name="gram_sum",
    )(terms)
    return (far[:probes], probe_gram)


def solution(mesh):
    return jax.shard_map(
        shards,
        mesh=mesh,
        in_specs=(
            P("probe", "leaf"),
            P(None, "leaf"),
            P(None, "leaf"),
            P(None, "leaf"),
            P("leaf", None, None),
            P("leaf", None),
            P("leaf"),
            P("leaf", None, None),
            P("leaf", None),
            P("leaf"),
        ),
        out_specs=(P("probe", "leaf"), P("probe", None)),
        check_vma=False,
    )
```

```python
import functools
import functools
import math

import jax
import jax.numpy as jnp
from jax import lax
from jax.experimental import pallas as pl
from jax.experimental.pallas import tpu as pltpu
from jax.sharding import PartitionSpec as P

KERNEL_RATE = 1.5
POINT_SCALE = math.sqrt(2.0 * KERNEL_RATE)
LANES = 128
UNITS = 16
QUAD = 4
CHUNK = 8
FAR_AWAY = -30000.0
SLOTS = 64
RECEIVED = SLOTS + CHUNK
VMEM = 56 * 1024 * 1024
SPARE = 6 * 1024 * 1024

NT = (((1,), (1,)), ((), ()))
NN = (((1,), (0,)), ((), ()))


def bdot(a, b, dims):
    return lax.dot_general(a, b, dims, preferred_element_type=jnp.float32)


def split_rows(points):
    v = points * POINT_SCALE
    norm = -0.5 * (v[0:1] * v[0:1] + v[1:2] * v[1:2] + v[2:3] * v[2:3])
    full = jnp.concatenate([v, norm], axis=0)
    high = full.astype(jnp.bfloat16).astype(jnp.float32)
    rest = (full - high).astype(jnp.bfloat16).astype(jnp.float32)
    return jnp.concatenate([high, rest], axis=0)


def source_features(rows):
    place = lax.broadcasted_iota(jnp.int32, rows.shape, 0)
    one = jnp.where((place == 3) | (place == 7), 1.0, 0.0)
    return jnp.concatenate([rows, jnp.where(place < 3, rows, one)], axis=0)


def target_features(rows):
    place = lax.broadcasted_iota(jnp.int32, rows.shape, 0)
    turned = jnp.concatenate([rows[4:8], rows[0:4]], axis=0)
    one = jnp.where((place == 3) | (place == 7), 1.0, jnp.where(place < 3, rows, turned))
    return jnp.concatenate([one, turned], axis=0)


def halves(tile):
    lane = lax.broadcasted_iota(jnp.int32, tile.shape, 1)
    turned = pltpu.roll(tile, LANES // 2, 1)
    low = lane < LANES // 2
    return jnp.where(low, tile, turned), jnp.where(low, turned, tile)


def lane_tile(index):
    return pl.ds(pl.multiple_of(index * LANES, LANES), LANES)


def list_slots(
    fine_slots_ref, fine_counts_ref, coarse_slots_ref, coarse_counts_ref, out_ref, *units_refs, entries
):
    fine, coarse = fine_slots_ref.shape[0], coarse_slots_ref.shape[0]
    spare = LANES - fine - coarse
    slots = jnp.concatenate(
        [fine_slots_ref[...], coarse_slots_ref[...], jnp.zeros((spare, SLOTS), jnp.int32)], axis=0
    )
    slots = slots.astype(jnp.float32).T.astype(jnp.int32)
    counts = jnp.concatenate(
        [fine_counts_ref[...], coarse_counts_ref[...], jnp.zeros((1, spare), jnp.int32)], axis=1
    )
    shape = (SLOTS, LANES)
    in_fine = lax.broadcasted_iota(jnp.int32, shape, 1) < fine
    clusters = jnp.where(in_fine, fine, coarse)
    nothing = jnp.where(in_fine, entries[0], entries[1])
    live = lax.broadcasted_iota(jnp.int32, shape, 0) < counts
    own = live & (slots < clusters)
    received = live & (slots >= clusters)
    row = lax.broadcasted_iota(jnp.int32, (SLOTS, SLOTS), 0)
    column = lax.broadcasted_iota(jnp.int32, (SLOTS, SLOTS), 1)
    upto = jnp.where(column <= row, 1.0, 0.0).astype(jnp.bfloat16)
    turns = []
    for start, chosen, value, blank in (
        (0, own, slots, clusters),
        (RECEIVED, received, slots - clusters, nothing),
    ):
        rank = bdot(upto, jnp.where(chosen, 1.0, 0.0).astype(jnp.bfloat16), NN).astype(jnp.int32)
        spot = jnp.where(chosen, rank - 1, -1)
        value = value - blank
        for first in range(0, SLOTS, 8):
            rows = [
                blank[:1] + jnp.sum(jnp.where(spot == place, value, 0), axis=0, keepdims=True)
                for place in range(first, first + 8)
            ]
            out_ref[start + first:start + first + 8] = jnp.concatenate(rows, axis=0)
        out_ref[start + SLOTS:start + SLOTS + CHUNK] = jnp.broadcast_to(blank[:1], (CHUNK, LANES))
        turns.append(jnp.maximum((rank[SLOTS - 1:] + CHUNK - 1) // CHUNK, 1))
    turns = jnp.concatenate(turns + [jnp.zeros((6, LANES), jnp.int32)], axis=0).astype(jnp.float32).T
    row = lax.broadcasted_iota(jnp.int32, (LANES, LANES), 0)
    column = lax.broadcasted_iota(jnp.int32, (LANES, LANES), 1)
    upto = (column <= row) & ((row < fine) == (column < fine))
    ends = bdot(jnp.where(upto, 1.0, 0.0).astype(jnp.bfloat16), turns.astype(jnp.bfloat16), NN)
    ends, turns = ends.astype(jnp.int32), turns.astype(jnp.int32)
    for side in range(2):
        for level, (low, count) in enumerate(((0, fine), (fine, coarse))):
            units_ref = units_refs[2 * side + level]
            end = ends[low:low + count, side:side + 1]
            took = turns[low:low + count, side:side + 1]
            lane = lax.broadcasted_iota(jnp.int32, (1, LANES), 1)
            for tile in range(units_ref.shape[0]):
                place = tile * LANES + lane
                passed = end <= place
                target = jnp.sum(jnp.where(passed, 1, 0), axis=0, keepdims=True)
                turn = place - jnp.sum(jnp.where(passed, took, 0), axis=0, keepdims=True)
                over = target >= count
                start = side * RECEIVED + jnp.where(over, SLOTS, turn * CHUNK)
                code = start * LANES + low + jnp.where(over, count - 1, target)
                if tile == units_ref.shape[0] - 1:
                    code = jnp.where(lane == LANES - 1, end[count - 1:], code)
                units_ref[tile:tile + 1] = code


def pack_send(send_ref, out_ref, dup_coef, dup_rows, owners, capacity, px, entry_first=False):
    pairs = capacity // 2
    lane = lax.broadcasted_iota(jnp.int32, (px, LANES), 1) < LANES // 2
    lane8 = lax.broadcasted_iota(jnp.int32, (8, LANES), 1) < LANES // 2

    def one_owner(owner, carry):
        before = None
        for pair in range(pairs):
            first, second = [
                send_ref[0, entry, owner] if entry_first else send_ref[0, owner, entry]
                for entry in (2 * pair, 2 * pair + 1)
            ]
            out_ref[owner, pair * px:(pair + 1) * px, :] = jnp.where(lane, dup_coef[first], dup_coef[second])
            rows = jnp.where(lane8, dup_rows[first], dup_rows[second])
            if pair % 2 == 0:
                before = rows
            else:
                start = pairs * px + (pair - 1) * 8
                out_ref[owner, start:start + 16, :] = jnp.concatenate(
                    [before, rows], axis=0
                ).astype(jnp.bfloat16)
        return carry

    lax.fori_loop(0, owners, one_owner, 0, unroll=4)


def pack_fine_kernel(send_ref, coef_ref, points_ref, out_ref, rows_ref, dup_coef, dup_rows):
    _, owners, capacity = send_ref.shape
    px = coef_ref.shape[0]
    rows_ref[...] = split_rows(points_ref[...])

    def one_tile(index, carry):
        a, b = halves(coef_ref[:, lane_tile(index)].astype(jnp.float32))
        dup_coef[2 * index] = a.astype(jnp.bfloat16)
        dup_coef[2 * index + 1] = b.astype(jnp.bfloat16)
        a, b = halves(rows_ref[:, lane_tile(index)])
        dup_rows[2 * index] = a
        dup_rows[2 * index + 1] = b
        return carry

    lax.fori_loop(0, coef_ref.shape[1] // LANES, one_tile, 0, unroll=8)
    pack_send(send_ref, out_ref, dup_coef, dup_rows, owners, capacity, px)


def pack_coarse(
    send_ref, coef_ref, transfer_ref, points_ref, out_ref, rows_ref, coarse_ref, dup_coef, dup_rows
):
    _, capacity, owners = send_ref.shape
    px = coef_ref.shape[0]
    rows_ref[...] = split_rows(points_ref[...])

    def one_tile(index, carry):
        doubled = []
        for part in range(2):
            q = 2 * index + part
            a, b = halves(transfer_ref[:, lane_tile(q)].astype(jnp.float32))
            matrix = jnp.concatenate([a, b], axis=0).astype(jnp.bfloat16)
            block = bdot(coef_ref[:, lane_tile(q)], matrix, NN).astype(jnp.bfloat16)
            dup_coef[q] = block
            doubled.append(block)
        lane = lax.broadcasted_iota(jnp.int32, (px, LANES), 1) < LANES // 2
        coarse_ref[:, lane_tile(index)] = jnp.where(lane, doubled[0], doubled[1])
        a, b = halves(rows_ref[:, lane_tile(index)])
        dup_rows[2 * index] = a
        dup_rows[2 * index + 1] = b
        return carry

    lax.fori_loop(0, coef_ref.shape[1] // (2 * LANES), one_tile, 0, unroll=8)
    pack_send(send_ref, out_ref, dup_coef, dup_rows, owners, capacity, px, entry_first=True)


def turned(rows):
    row = lax.broadcasted_iota(jnp.int32, (LANES, LANES), 0)
    column = lax.broadcasted_iota(jnp.int32, (LANES, LANES), 1)
    unit = jnp.where(row == column, 1.0, 0.0).astype(jnp.bfloat16)
    return bdot(unit, rows, NT).astype(jnp.bfloat16)


def put_pair(entry, coef, rows, coef_table, feature_table):
    a, b = halves(coef.astype(jnp.float32))
    coef_table[entry] = a.astype(jnp.bfloat16)
    coef_table[entry + 1] = b.astype(jnp.bfloat16)
    features = turned(jnp.concatenate([source_features(rows).astype(jnp.bfloat16)] * QUAD, axis=0))
    feature_table[entry] = features[:64]
    feature_table[entry + 1] = features[64:]


def put_nothing(entry, coef_table, feature_table):
    coef_table[entry] = jnp.zeros(coef_table.shape[1:], jnp.bfloat16)
    place = lax.broadcasted_iota(jnp.int32, (8, LANES), 0)
    nothing = source_features(jnp.where(place == 3, FAR_AWAY, 0.0)).astype(jnp.bfloat16)
    feature_table[entry] = turned(jnp.concatenate([nothing] * QUAD, axis=0))[:64]


def build_own(coef_ref, rows_ref, coef_table, feature_table):
    tiles = coef_ref.shape[1] // LANES

    def one_tile(index, carry):
        tile = lane_tile(index)
        put_pair(2 * index, coef_ref[:, tile], rows_ref[:, tile], coef_table, feature_table)
        return carry

    lax.fori_loop(0, tiles, one_tile, 0, unroll=16)
    put_nothing(2 * tiles, coef_table, feature_table)


def build_received(recv_ref, coef_table, feature_table):
    owners, recv_rows, _ = recv_ref.shape
    px = coef_table.shape[1]
    pairs = recv_rows // (px + 8)

    def one_owner(owner, carry):
        for pair in range(0, pairs, 2):
            start = pairs * px + pair * 8
            both = recv_ref[owner, start:start + 16, :].astype(jnp.float32)
            for part in range(2):
                where = pair + part
                put_pair(
                    owner * (2 * pairs) + 2 * where,
                    recv_ref[owner, where * px:(where + 1) * px, :],
                    both[8 * part:8 * part + 8],
                    coef_table,
                    feature_table,
                )
        return carry

    lax.fori_loop(0, owners, one_owner, 0, unroll=32 // pairs)
    put_nothing(owners * pairs * 2, coef_table, feature_table)


def build_targets(rows_ref, target_table):
    def one_tile(index, carry):
        a, b = halves(target_features(rows_ref[:, lane_tile(index)]))
        target_table[2 * index] = a.astype(jnp.bfloat16)
        target_table[2 * index + 1] = b.astype(jnp.bfloat16)
        return carry

    lax.fori_loop(0, rows_ref.shape[1] // LANES, one_tile, 0, unroll=16)


def sweep(list_ref, units_ref, first, coef_table, feature_table, target_table, acc):
    px = coef_table.shape[1]
    lane = lax.broadcasted_iota(jnp.int32, (64, 16 * QUAD), 1) // 16
    lane_t = lax.broadcasted_iota(jnp.int32, (16, LANES), 1) // 64
    lane_x = lax.broadcasted_iota(jnp.int32, (px, LANES), 1) < 64
    blank = jnp.zeros((16, LANES), jnp.bfloat16)
    acc[...] = jnp.zeros_like(acc)

    def partners(unit):
        row, column = unit
        return [list_ref[row + m, column] for m in range(CHUNK)]

    def units_of(place):
        codes = [units_ref[place >> 7, (place & (LANES - 1)) + u] for u in range(UNITS)]
        return [(code >> 7, code & (LANES - 1)) for code in codes]

    def one_quad(quad):
        weights = []
        for u in range(QUAD):
            own = jnp.where(lane_t == u % 2, target_table[quad[u][1] - first], blank)
            weights.append(jnp.concatenate([own if v == u // 2 else blank for v in range(QUAD // 2)], axis=1))
        weights = jnp.concatenate(weights, axis=0)
        ids = [partners(unit) for unit in quad]
        product = None
        for part in range(0, CHUNK, 4):
            rows = []
            coefs = []
            for m in range(part, part + 4):
                tile = feature_table[ids[0][m]]
                for u in range(1, QUAD):
                    tile = jnp.where(lane == u, feature_table[ids[u][m]], tile)
                rows.append(tile)
            power = bdot(jnp.concatenate(rows, axis=0), weights, NN)
            values = jnp.exp(power).astype(jnp.bfloat16)
            for u in range(QUAD):
                coefs.append(
                    jnp.concatenate(
                        [
                            jnp.where(lane_x, coef_table[ids[u][m]], coef_table[ids[u][m + 1]])
                            for m in (part, part + 2)
                        ],
                        axis=1,
                    )
                )
            term = bdot(jnp.concatenate(coefs, axis=0), values, NN)
            product = term if product is None else product + term
        return product

    def one_set(index, carry):
        units = units_of(index * UNITS)
        products = [one_quad(units[start:start + QUAD]) for start in range(0, UNITS, QUAD)]
        for place, (row, column) in enumerate(units):
            u = place % QUAD
            side = (u // 2) * LANES
            acc[u % 2, column - first] += products[place // QUAD][u * px:(u + 1) * px, side:side + LANES]
        return carry

    total = units_ref[units_ref.shape[0] - 1, LANES - 1]
    lax.fori_loop(0, (total + UNITS - 1) // UNITS, one_set, 0)


def summed(acc, target):
    low = lax.broadcasted_iota(jnp.int32, acc.shape[2:], 1) < 64
    here = jnp.where(low, acc[0, target], acc[1, target])
    return here + pltpu.roll(here, 64, 1)


def put_sums(acc, clusters, out_ref, before_ref=None):
    low = lax.broadcasted_iota(jnp.int32, acc.shape[2:], 1) < 64

    def one_tile(index, carry):
        tile = lane_tile(index)
        sums = jnp.where(low, summed(acc, 2 * index), summed(acc, 2 * index + 1))
        out_ref[:, tile] = sums if before_ref is None else before_ref[:, tile] + sums
        return carry

    lax.fori_loop(0, clusters // 2, one_tile, 0, unroll=8)


def own_kernel(
    send_ref,
    fine_slots_ref,
    fine_counts_ref,
    coarse_slots_ref,
    coarse_counts_ref,
    coef_ref,
    transfer_ref,
    points_ref,
    fine_rows_ref,
    send_out_ref,
    coarse_rows_ref,
    list_out_ref,
    fine_units_ref,
    coarse_units_ref,
    fine_out_ref,
    coarse_out_ref,
    coarse_coef_ref,
    dup_coef,
    dup_rows,
    fine_own_units,
    coarse_own_units,
    list_ref,
    fine_own_ref,
    coarse_own_ref,
    list_sem,
    fine_sem,
    coarse_sem,
    *scratch,
    entries,
):
    list_slots(
        fine_slots_ref,
        fine_counts_ref,
        coarse_slots_ref,
        coarse_counts_ref,
        list_out_ref,
        fine_own_units,
        coarse_own_units,
        fine_units_ref,
        coarse_units_ref,
        entries=entries,
    )
    copies = [
        pltpu.make_async_copy(list_out_ref, list_ref, list_sem),
        pltpu.make_async_copy(fine_own_units, fine_own_ref, fine_sem),
        pltpu.make_async_copy(coarse_own_units, coarse_own_ref, coarse_sem),
    ]
    for copy in copies:
        copy.start()
    pack_coarse(
        send_ref,
        coef_ref,
        transfer_ref,
        points_ref,
        send_out_ref,
        coarse_rows_ref,
        coarse_coef_ref,
        dup_coef,
        dup_rows,
    )
    for copy in copies:
        copy.wait()
    first = 0
    for units_ref, source_ref, rows_ref, out_ref in (
        (fine_own_ref, coef_ref, fine_rows_ref, fine_out_ref),
        (coarse_own_ref, coarse_coef_ref, coarse_rows_ref, coarse_out_ref),
    ):
        clusters = rows_ref.shape[1] // 64
        build_own(source_ref, rows_ref, *scratch[:2])
        build_targets(rows_ref, scratch[2])
        sweep(list_ref, units_ref, first, *scratch)
        put_sums(scratch[-1], clusters, out_ref)
        first += clusters


def fine_kernel(list_ref, units_ref, recv_ref, rows_ref, own_ref, out_ref, *scratch):
    build_received(recv_ref, *scratch[:2])
    build_targets(rows_ref, scratch[2])
    sweep(list_ref, units_ref, 0, *scratch)
    put_sums(scratch[-1], rows_ref.shape[1] // 64, out_ref, own_ref)


def coarse_kernel(groups, *refs):
    late = 3 + groups
    list_ref, units_ref, recv_ref, rows_ref = refs[:4]
    out_ref, terms_ref = refs[4 + late:6 + late]
    late_refs = refs[6 + late:6 + 2 * late]
    late_sems = refs[6 + 2 * late:6 + 3 * late]
    gram_ref, split_ref, *scratch = refs[6 + 3 * late:]
    copies = [pltpu.make_async_copy(*pair) for pair in zip(refs[4:4 + late], late_refs, late_sems)]
    for copy in copies:
        copy.start()
    own_ref, fine_ref, transfer_ref, *probes_refs = late_refs
    clusters = rows_ref.shape[1] // 64
    px = split_ref.shape[0] // 2
    probes = probes_refs[0].shape[0]
    acc = scratch[-1]
    build_received(recv_ref, *scratch[:2])
    build_targets(rows_ref, scratch[2])
    sweep(list_ref, units_ref, fine_ref.shape[1] // 64, *scratch)
    for copy in copies:
        copy.wait()

    def one_parent(q, carry):
        own = halves(own_ref[:, lane_tile(q >> 1)])
        own = jnp.where((q & 1) == 0, own[0], own[1])
        twice = (summed(acc, q) + own).astype(jnp.bfloat16)
        matrix = transfer_ref[:, lane_tile(q)].astype(jnp.float32)
        low = lax.broadcasted_iota(jnp.int32, matrix.shape, 1) < 64
        matrix = jnp.concatenate(
            [jnp.where(low, matrix, 0.0), jnp.where(low, 0.0, matrix)], axis=0
        ).astype(jnp.bfloat16)
        total = fine_ref[:, lane_tile(q)] + bdot(twice, matrix, NT)
        out_ref[:, lane_tile(q)] = total
        high = total.astype(jnp.bfloat16)
        split_ref[:px, lane_tile(q)] = high
        split_ref[px:, lane_tile(q)] = (total - high.astype(jnp.float32)).astype(jnp.bfloat16)
        return carry

    lax.fori_loop(0, clusters, one_parent, 0, unroll=8)
    for block, probes_ref in enumerate(probes_refs):
        term = bdot(probes_ref[...], split_ref[...], NT)
        gram_ref[block] = term[:, :px] + term[:, px:]
    place = lax.axis_index("probe")
    for b in range(groups):
        block = gram_ref[lax.rem(place - b + groups, groups)]
        packed = jnp.concatenate([block[i:i + 8, :probes] for i in range(0, probes, 8)], axis=1)

        def one_owner(owner, carry):
            terms_ref[owner * groups + b] = packed
            return carry

        lax.fori_loop(0, terms_ref.shape[0] // groups, one_owner, 0)


def gram_kernel(terms_ref, out_ref, *, groups, scale):
    probes = out_ref.shape[0]
    columns = []
    for b in range(groups):
        total = terms_ref[b]
        for owner in range(1, terms_ref.shape[0] // groups):
            total = total + terms_ref[owner * groups + b]
        columns.append(
            jnp.concatenate([total[:, i * probes:(i + 1) * probes] for i in range(probes // 8)], axis=0)
        )
    out_ref[...] = jnp.concatenate(columns, axis=1) * scale


def sweep_scratch(total, clusters, px):
    return [
        pltpu.VMEM((total + 1, px, LANES), jnp.bfloat16),
        pltpu.VMEM((total + 1, 64, 16 * QUAD), jnp.bfloat16),
        pltpu.VMEM((clusters, 16, LANES), jnp.bfloat16),
        pltpu.VMEM((2, clusters, px, LANES), jnp.float32),
    ]


def shards(
    coef_fine,
    points_fine,
    points_coarse,
    transfer,
    send_fine,
    slots_fine,
    counts_fine,
    send_coarse,
    slots_coarse,
    counts_coarse,
):
    probes = coef_fine.shape[0]
    fine_count = counts_fine.shape[0]
    coarse_count = counts_coarse.shape[0]
    owners = lax.axis_size("leaf")
    groups = lax.axis_size("probe")
    px = -(-probes // 16) * 16
    coef = coef_fine if px == probes else jnp.pad(coef_fine, ((0, px - probes), (0, 0)))
    cap_fine = send_fine.shape[2]
    cap_coarse = send_coarse.shape[2]

    def params(scratch, blocks):
        size = SPARE + blocks * px * points_fine.shape[1] * 4
        for ref in scratch:
            size += math.prod(ref.shape[:-1]) * -(-ref.shape[-1] // LANES) * LANES * ref.dtype.itemsize
        return pltpu.CompilerParams(vmem_limit_bytes=size)

    whole_vmem = pltpu.CompilerParams(vmem_limit_bytes=VMEM)
    fine_scratch = sweep_scratch(owners * cap_fine, fine_count, px)
    coarse_scratch = sweep_scratch(owners * cap_coarse, coarse_count, px)
    smem = pl.BlockSpec(memory_space=pltpu.SMEM)
    vmem = pl.BlockSpec(memory_space=pltpu.VMEM)
    bf16, f32 = jnp.bfloat16, jnp.float32

    fine_send, fine_rows = pl.pallas_call(
        pack_fine_kernel,
        out_shape=(
            jax.ShapeDtypeStruct((owners, (cap_fine // 2) * (px + 8), LANES), bf16),
            jax.ShapeDtypeStruct((8, points_fine.shape[1]), f32),
        ),
        in_specs=[smem, vmem, vmem],
        out_specs=[vmem, vmem],
        scratch_shapes=[
            pltpu.VMEM((fine_count, px, LANES), bf16),
            pltpu.VMEM((fine_count, 8, LANES), f32),
        ],
        compiler_params=whole_vmem,
        name="pack_fine",
    )(send_fine, coef, points_fine)
    fine_recv = lax.all_to_all(fine_send, "leaf", split_axis=0, concat_axis=0, tiled=True)

    fine_total = owners * cap_fine
    coarse_total = owners * cap_coarse
    unit_rows = [-(-(count * (SLOTS // CHUNK) + 2 * UNITS + 1) // LANES) for count in (fine_count, coarse_count)]
    list_shape = (RECEIVED + SLOTS + CHUNK, LANES)
    i32 = jnp.int32
    coarse_send, coarse_rows, slot_list, fine_units, coarse_units, fine_sums, coarse_sums = pl.pallas_call(
        functools.partial(own_kernel, entries=(fine_total, coarse_total)),
        out_shape=(
            jax.ShapeDtypeStruct((owners, (cap_coarse // 2) * (px + 8), LANES), bf16),
            jax.ShapeDtypeStruct((8, points_coarse.shape[1]), f32),
            jax.ShapeDtypeStruct(list_shape, i32),
            jax.ShapeDtypeStruct((unit_rows[0], LANES), i32),
            jax.ShapeDtypeStruct((unit_rows[1], LANES), i32),
            jax.ShapeDtypeStruct((px, points_fine.shape[1]), f32),
            jax.ShapeDtypeStruct((px, points_coarse.shape[1]), f32),
        ),
        in_specs=[smem] + [vmem] * 8,
        out_specs=[vmem] * 7,
        scratch_shapes=[
            pltpu.VMEM((px, points_coarse.shape[1]), bf16),
            pltpu.VMEM((coarse_count, px, LANES), bf16),
            pltpu.VMEM((coarse_count, 8, LANES), f32),
            pltpu.VMEM((unit_rows[0], LANES), i32),
            pltpu.VMEM((unit_rows[1], LANES), i32),
            pltpu.SMEM(list_shape, i32),
            pltpu.SMEM((unit_rows[0], LANES), i32),
            pltpu.SMEM((unit_rows[1], LANES), i32),
            pltpu.SemaphoreType.DMA,
            pltpu.SemaphoreType.DMA,
            pltpu.SemaphoreType.DMA,
        ]
        + sweep_scratch(fine_count, fine_count, px),
        compiler_params=whole_vmem,
        cost_estimate=pl.CostEstimate(flops=10**10, bytes_accessed=10**7, transcendentals=10**7),
        name="own_sweep",
    )(
        jnp.swapaxes(send_coarse, 1, 2),
        slots_fine,
        counts_fine.reshape(1, -1),
        slots_coarse,
        counts_coarse.reshape(1, -1),
        coef,
        transfer,
        points_coarse,
        fine_rows,
    )

    coarse_sums, own_probes = lax.optimization_barrier((coarse_sums, coef_fine))
    turned = [coef_fine]
    for step in range(1, groups):
        turned.append(lax.ppermute(own_probes, "probe", [(i, (i + step) % groups) for i in range(groups)]))
    coarse_send, turned = lax.optimization_barrier((coarse_send, turned))
    coarse_recv = lax.all_to_all(coarse_send, "leaf", split_axis=0, concat_axis=0, tiled=True)

    fine_far = pl.pallas_call(
        fine_kernel,
        out_shape=jax.ShapeDtypeStruct((px, points_fine.shape[1]), f32),
        in_specs=[smem] * 2 + [vmem] * 3,
        out_specs=vmem,
        scratch_shapes=fine_scratch,
        compiler_params=params(fine_scratch, owners // 4 + 4),
        name="fine_sweep",
    )(slot_list, fine_units, fine_recv, fine_rows, fine_sums)

    late = (coarse_sums, fine_far, transfer, *turned)
    term_shape = (owners * groups, 8, probes * probes // 8)
    far, terms = pl.pallas_call(
        functools.partial(coarse_kernel, groups),
        out_shape=(
            jax.ShapeDtypeStruct((px, points_fine.shape[1]), f32),
            jax.ShapeDtypeStruct(term_shape, f32),
        ),
        in_specs=[smem] * 2 + [vmem] * 2 + [pl.BlockSpec(memory_space=pl.ANY)] * (3 + groups),
        out_specs=[vmem, vmem],
        scratch_shapes=[pltpu.VMEM(operand.shape, operand.dtype) for operand in late]
        + [pltpu.SemaphoreType.DMA] * len(late)
        + [
            pltpu.VMEM((groups, probes, px), f32),
            pltpu.VMEM((2 * px, points_fine.shape[1]), bf16),
        ]
        + coarse_scratch,
        compiler_params=params(coarse_scratch, owners // 4 + 6),
        name="coarse_sweep",
    )(slot_list, coarse_units, coarse_recv, coarse_rows, *late)

    terms = lax.all_to_all(terms, ("leaf", "probe"), split_axis=0, concat_axis=0, tiled=True)
    probe_gram = pl.pallas_call(
        functools.partial(
            gram_kernel, groups=groups, scale=1.0 / math.sqrt(owners * fine_count * 64)
        ),
        out_shape=jax.ShapeDtypeStruct((probes, groups * probes), f32),
        in_specs=[vmem],
        out_specs=vmem,
        name="gram_sum",
    )(terms)
    return (far[:probes], probe_gram)


def solution(mesh):
    return jax.shard_map(
        shards,
        mesh=mesh,
        in_specs=(
            P("probe", "leaf"),
            P(None, "leaf"),
            P(None, "leaf"),
            P(None, "leaf"),
            P("leaf", None, None),
            P("leaf", None),
            P("leaf"),
            P("leaf", None, None),
            P("leaf", None),
            P("leaf"),
        ),
        out_specs=(P("probe", "leaf"), P("probe", None)),
        check_vma=False,
    )
```

```python
import functools
import functools
import math

import jax
import jax.numpy as jnp
from jax import lax
from jax.experimental import pallas as pl
from jax.experimental.pallas import tpu as pltpu
from jax.sharding import PartitionSpec as P

KERNEL_RATE = 1.5
POINT_SCALE = math.sqrt(2.0 * KERNEL_RATE)
LANES = 128
UNITS = 16
QUAD = 4
CHUNK = 8
FAR_AWAY = -30000.0
SLOTS = 64
RECEIVED = SLOTS + CHUNK
VMEM = 56 * 1024 * 1024
SPARE = 6 * 1024 * 1024

NT = (((1,), (1,)), ((), ()))
NN = (((1,), (0,)), ((), ()))


def bdot(a, b, dims):
    return lax.dot_general(a, b, dims, preferred_element_type=jnp.float32)


def split_rows(points):
    v = points * POINT_SCALE
    norm = -0.5 * (v[0:1] * v[0:1] + v[1:2] * v[1:2] + v[2:3] * v[2:3])
    full = jnp.concatenate([v, norm], axis=0)
    high = full.astype(jnp.bfloat16).astype(jnp.float32)
    rest = (full - high).astype(jnp.bfloat16).astype(jnp.float32)
    return jnp.concatenate([high, rest], axis=0)


def source_features(rows):
    place = lax.broadcasted_iota(jnp.int32, rows.shape, 0)
    one = jnp.where((place == 3) | (place == 7), 1.0, 0.0)
    return jnp.concatenate([rows, jnp.where(place < 3, rows, one)], axis=0)


def target_features(rows):
    place = lax.broadcasted_iota(jnp.int32, rows.shape, 0)
    turned = jnp.concatenate([rows[4:8], rows[0:4]], axis=0)
    one = jnp.where((place == 3) | (place == 7), 1.0, jnp.where(place < 3, rows, turned))
    return jnp.concatenate([one, turned], axis=0)


def halves(tile):
    lane = lax.broadcasted_iota(jnp.int32, tile.shape, 1)
    turned = pltpu.roll(tile, LANES // 2, 1)
    low = lane < LANES // 2
    return jnp.where(low, tile, turned), jnp.where(low, turned, tile)


def lane_tile(index):
    return pl.ds(pl.multiple_of(index * LANES, LANES), LANES)


def list_slots(
    fine_slots_ref, fine_counts_ref, coarse_slots_ref, coarse_counts_ref, out_ref, *units_refs, entries
):
    fine, coarse = fine_slots_ref.shape[0], coarse_slots_ref.shape[0]
    spare = LANES - fine - coarse
    slots = jnp.concatenate(
        [fine_slots_ref[...], coarse_slots_ref[...], jnp.zeros((spare, SLOTS), jnp.int32)], axis=0
    )
    slots = slots.astype(jnp.float32).T.astype(jnp.int32)
    counts = jnp.concatenate(
        [fine_counts_ref[...], coarse_counts_ref[...], jnp.zeros((1, spare), jnp.int32)], axis=1
    )
    shape = (SLOTS, LANES)
    in_fine = lax.broadcasted_iota(jnp.int32, shape, 1) < fine
    clusters = jnp.where(in_fine, fine, coarse)
    nothing = jnp.where(in_fine, entries[0], entries[1])
    live = lax.broadcasted_iota(jnp.int32, shape, 0) < counts
    own = live & (slots < clusters)
    received = live & (slots >= clusters)
    row = lax.broadcasted_iota(jnp.int32, (SLOTS, SLOTS), 0)
    column = lax.broadcasted_iota(jnp.int32, (SLOTS, SLOTS), 1)
    upto = jnp.where(column <= row, 1.0, 0.0).astype(jnp.bfloat16)
    turns = []
    for start, chosen, value, blank in (
        (0, own, slots, clusters),
        (RECEIVED, received, slots - clusters, nothing),
    ):
        rank = bdot(upto, jnp.where(chosen, 1.0, 0.0).astype(jnp.bfloat16), NN).astype(jnp.int32)
        spot = jnp.where(chosen, rank - 1, -1)
        value = value - blank
        for first in range(0, SLOTS, 8):
            rows = [
                blank[:1] + jnp.sum(jnp.where(spot == place, value, 0), axis=0, keepdims=True)
                for place in range(first, first + 8)
            ]
            out_ref[start + first:start + first + 8] = jnp.concatenate(rows, axis=0)
        out_ref[start + SLOTS:start + SLOTS + CHUNK] = jnp.broadcast_to(blank[:1], (CHUNK, LANES))
        turns.append(jnp.maximum((rank[SLOTS - 1:] + CHUNK - 1) // CHUNK, 1))
    turns = jnp.concatenate(turns + [jnp.zeros((6, LANES), jnp.int32)], axis=0).astype(jnp.float32).T
    row = lax.broadcasted_iota(jnp.int32, (LANES, LANES), 0)
    column = lax.broadcasted_iota(jnp.int32, (LANES, LANES), 1)
    upto = (column <= row) & ((row < fine) == (column < fine))
    ends = bdot(jnp.where(upto, 1.0, 0.0).astype(jnp.bfloat16), turns.astype(jnp.bfloat16), NN)
    ends, turns = ends.astype(jnp.int32), turns.astype(jnp.int32)
    for side in range(2):
        for level, (low, count) in enumerate(((0, fine), (fine, coarse))):
            units_ref = units_refs[2 * side + level]
            end = ends[low:low + count, side:side + 1]
            took = turns[low:low + count, side:side + 1]
            lane = lax.broadcasted_iota(jnp.int32, (1, LANES), 1)
            for tile in range(units_ref.shape[0]):
                place = tile * LANES + lane
                passed = end <= place
                target = jnp.sum(jnp.where(passed, 1, 0), axis=0, keepdims=True)
                turn = place - jnp.sum(jnp.where(passed, took, 0), axis=0, keepdims=True)
                over = target >= count
                start = side * RECEIVED + jnp.where(over, SLOTS, turn * CHUNK)
                code = start * LANES + low + jnp.where(over, count - 1, target)
                if tile == units_ref.shape[0] - 1:
                    code = jnp.where(lane == LANES - 1, end[count - 1:], code)
                units_ref[tile:tile + 1] = code


def pack_send(send_ref, out_ref, dup_coef, dup_rows, owners, capacity, px, entry_first=False):
    pairs = capacity // 2
    lane = lax.broadcasted_iota(jnp.int32, (px, LANES), 1) < LANES // 2
    lane8 = lax.broadcasted_iota(jnp.int32, (8, LANES), 1) < LANES // 2

    def one_owner(owner, carry):
        before = None
        for pair in range(pairs):
            first, second = [
                send_ref[0, entry, owner] if entry_first else send_ref[0, owner, entry]
                for entry in (2 * pair, 2 * pair + 1)
            ]
            out_ref[owner, pair * px:(pair + 1) * px, :] = jnp.where(lane, dup_coef[first], dup_coef[second])
            rows = jnp.where(lane8, dup_rows[first], dup_rows[second])
            if pair % 2 == 0:
                before = rows
            else:
                start = pairs * px + (pair - 1) * 8
                out_ref[owner, start:start + 16, :] = jnp.concatenate(
                    [before, rows], axis=0
                ).astype(jnp.bfloat16)
        return carry

    lax.fori_loop(0, owners, one_owner, 0, unroll=4)


def pack_fine_kernel(send_ref, coef_ref, points_ref, out_ref, rows_ref, dup_coef, dup_rows):
    _, owners, capacity = send_ref.shape
    px = coef_ref.shape[0]
    rows_ref[...] = split_rows(points_ref[...])

    def one_tile(index, carry):
        a, b = halves(coef_ref[:, lane_tile(index)].astype(jnp.float32))
        dup_coef[2 * index] = a.astype(jnp.bfloat16)
        dup_coef[2 * index + 1] = b.astype(jnp.bfloat16)
        a, b = halves(rows_ref[:, lane_tile(index)])
        dup_rows[2 * index] = a
        dup_rows[2 * index + 1] = b
        return carry

    lax.fori_loop(0, coef_ref.shape[1] // LANES, one_tile, 0, unroll=8)
    pack_send(send_ref, out_ref, dup_coef, dup_rows, owners, capacity, px)


def pack_coarse(
    send_ref, coef_ref, transfer_ref, points_ref, out_ref, rows_ref, coarse_ref, dup_coef, dup_rows
):
    _, capacity, owners = send_ref.shape
    px = coef_ref.shape[0]
    rows_ref[...] = split_rows(points_ref[...])

    def one_tile(index, carry):
        doubled = []
        for part in range(2):
            q = 2 * index + part
            a, b = halves(transfer_ref[:, lane_tile(q)].astype(jnp.float32))
            matrix = jnp.concatenate([a, b], axis=0).astype(jnp.bfloat16)
            block = bdot(coef_ref[:, lane_tile(q)], matrix, NN).astype(jnp.bfloat16)
            dup_coef[q] = block
            doubled.append(block)
        lane = lax.broadcasted_iota(jnp.int32, (px, LANES), 1) < LANES // 2
        coarse_ref[:, lane_tile(index)] = jnp.where(lane, doubled[0], doubled[1])
        a, b = halves(rows_ref[:, lane_tile(index)])
        dup_rows[2 * index] = a
        dup_rows[2 * index + 1] = b
        return carry

    lax.fori_loop(0, coef_ref.shape[1] // (2 * LANES), one_tile, 0, unroll=8)
    pack_send(send_ref, out_ref, dup_coef, dup_rows, owners, capacity, px, entry_first=True)


def turned(rows):
    row = lax.broadcasted_iota(jnp.int32, (LANES, LANES), 0)
    column = lax.broadcasted_iota(jnp.int32, (LANES, LANES), 1)
    unit = jnp.where(row == column, 1.0, 0.0).astype(jnp.bfloat16)
    return bdot(unit, rows, NT).astype(jnp.bfloat16)


def put_pair(entry, coef, rows, coef_table, feature_table):
    a, b = halves(coef.astype(jnp.float32))
    coef_table[entry] = a.astype(jnp.bfloat16)
    coef_table[entry + 1] = b.astype(jnp.bfloat16)
    features = turned(jnp.concatenate([source_features(rows).astype(jnp.bfloat16)] * QUAD, axis=0))
    feature_table[entry] = features[:64]
    feature_table[entry + 1] = features[64:]


def put_nothing(entry, coef_table, feature_table):
    coef_table[entry] = jnp.zeros(coef_table.shape[1:], jnp.bfloat16)
    place = lax.broadcasted_iota(jnp.int32, (8, LANES), 0)
    nothing = source_features(jnp.where(place == 3, FAR_AWAY, 0.0)).astype(jnp.bfloat16)
    feature_table[entry] = turned(jnp.concatenate([nothing] * QUAD, axis=0))[:64]


def build_own(coef_ref, rows_ref, coef_table, feature_table):
    tiles = coef_ref.shape[1] // LANES

    def one_tile(index, carry):
        tile = lane_tile(index)
        put_pair(2 * index, coef_ref[:, tile], rows_ref[:, tile], coef_table, feature_table)
        return carry

    lax.fori_loop(0, tiles, one_tile, 0, unroll=16)
    put_nothing(2 * tiles, coef_table, feature_table)


def build_received(recv_ref, coef_table, feature_table):
    owners, recv_rows, _ = recv_ref.shape
    px = coef_table.shape[1]
    pairs = recv_rows // (px + 8)

    def one_owner(owner, carry):
        for pair in range(0, pairs, 2):
            start = pairs * px + pair * 8
            both = recv_ref[owner, start:start + 16, :].astype(jnp.float32)
            for part in range(2):
                where = pair + part
                put_pair(
                    owner * (2 * pairs) + 2 * where,
                    recv_ref[owner, where * px:(where + 1) * px, :],
                    both[8 * part:8 * part + 8],
                    coef_table,
                    feature_table,
                )
        return carry

    lax.fori_loop(0, owners, one_owner, 0, unroll=32 // pairs)
    put_nothing(owners * pairs * 2, coef_table, feature_table)


def build_targets(rows_ref, target_table):
    def one_tile(index, carry):
        a, b = halves(target_features(rows_ref[:, lane_tile(index)]))
        target_table[2 * index] = a.astype(jnp.bfloat16)
        target_table[2 * index + 1] = b.astype(jnp.bfloat16)
        return carry

    lax.fori_loop(0, rows_ref.shape[1] // LANES, one_tile, 0, unroll=16)


def sweep(list_ref, units_ref, first, coef_table, feature_table, target_table, first_buffer, second_buffer, acc):
    px = coef_table.shape[1]
    lane = lax.broadcasted_iota(jnp.int32, (64, 16 * QUAD), 1) // 16
    lane_t = lax.broadcasted_iota(jnp.int32, (16, LANES), 1) // 64
    lane_x = lax.broadcasted_iota(jnp.int32, (px, LANES), 1) < 64
    blank = jnp.zeros((16, LANES), jnp.bfloat16)
    acc[...] = jnp.zeros_like(acc)

    def partners(unit):
        row, column = unit
        return [list_ref[row + m, column] for m in range(CHUNK)]

    def units_of(place):
        codes = [units_ref[place >> 7, (place & (LANES - 1)) + u] for u in range(UNITS)]
        return [(code >> 7, code & (LANES - 1)) for code in codes]

    def tiles(units, buffer):
        for start in range(0, UNITS, QUAD):
            quad = units[start:start + QUAD]
            weights = []
            for u in range(QUAD):
                own = jnp.where(lane_t == u % 2, target_table[quad[u][1] - first], blank)
                weights.append(jnp.concatenate([own if v == u // 2 else blank for v in range(QUAD // 2)], axis=1))
            weights = jnp.concatenate(weights, axis=0)
            ids = [partners(unit) for unit in quad]
            for part in range(0, CHUNK, 4):
                rows = []
                for m in range(part, part + 4):
                    tile = feature_table[ids[0][m]]
                    for u in range(1, QUAD):
                        tile = jnp.where(lane == u, feature_table[ids[u][m]], tile)
                    rows.append(tile)
                power = bdot(jnp.concatenate(rows, axis=0), weights, NN)
                buffer[start // QUAD, part * 64:(part + 4) * 64] = jnp.exp(power).astype(jnp.bfloat16)

    def products(units, buffer):
        for start in range(0, UNITS, QUAD):
            quad = units[start:start + QUAD]
            coefs = []
            for unit in quad:
                ids = partners(unit)
                coefs.append(
                    jnp.concatenate(
                        [
                            jnp.where(lane_x, coef_table[ids[m]], coef_table[ids[m + 1]])
                            for m in range(0, CHUNK, 2)
                        ],
                        axis=1,
                    )
                )
            product = bdot(jnp.concatenate(coefs, axis=0), buffer[start // QUAD], NN)
            for u in range(QUAD):
                side = (u // 2) * LANES
                acc[u % 2, quad[u][1] - first] += product[u * px:(u + 1) * px, side:side + LANES]

    def two_sets(index, carry):
        here = index * (2 * UNITS)
        second = units_of(here + UNITS)
        tiles(second, second_buffer)
        products(units_of(here), first_buffer)
        tiles(units_of(here + 2 * UNITS), first_buffer)
        products(second, second_buffer)
        return carry

    total = units_ref[units_ref.shape[0] - 1, LANES - 1]
    tiles(units_of(0), first_buffer)
    lax.fori_loop(0, (total + 2 * UNITS - 1) // (2 * UNITS), two_sets, 0)


def summed(acc, target):
    low = lax.broadcasted_iota(jnp.int32, acc.shape[2:], 1) < 64
    here = jnp.where(low, acc[0, target], acc[1, target])
    return here + pltpu.roll(here, 64, 1)


def put_sums(acc, clusters, out_ref, before_ref=None):
    low = lax.broadcasted_iota(jnp.int32, acc.shape[2:], 1) < 64

    def one_tile(index, carry):
        tile = lane_tile(index)
        sums = jnp.where(low, summed(acc, 2 * index), summed(acc, 2 * index + 1))
        out_ref[:, tile] = sums if before_ref is None else before_ref[:, tile] + sums
        return carry

    lax.fori_loop(0, clusters // 2, one_tile, 0, unroll=8)


def own_kernel(
    send_ref,
    fine_slots_ref,
    fine_counts_ref,
    coarse_slots_ref,
    coarse_counts_ref,
    coef_ref,
    transfer_ref,
    points_ref,
    fine_rows_ref,
    send_out_ref,
    coarse_rows_ref,
    list_out_ref,
    fine_units_ref,
    coarse_units_ref,
    fine_out_ref,
    coarse_out_ref,
    coarse_coef_ref,
    dup_coef,
    dup_rows,
    fine_own_units,
    coarse_own_units,
    list_ref,
    fine_own_ref,
    coarse_own_ref,
    list_sem,
    fine_sem,
    coarse_sem,
    *scratch,
    entries,
):
    list_slots(
        fine_slots_ref,
        fine_counts_ref,
        coarse_slots_ref,
        coarse_counts_ref,
        list_out_ref,
        fine_own_units,
        coarse_own_units,
        fine_units_ref,
        coarse_units_ref,
        entries=entries,
    )
    copies = [
        pltpu.make_async_copy(list_out_ref, list_ref, list_sem),
        pltpu.make_async_copy(fine_own_units, fine_own_ref, fine_sem),
        pltpu.make_async_copy(coarse_own_units, coarse_own_ref, coarse_sem),
    ]
    for copy in copies:
        copy.start()
    pack_coarse(
        send_ref,
        coef_ref,
        transfer_ref,
        points_ref,
        send_out_ref,
        coarse_rows_ref,
        coarse_coef_ref,
        dup_coef,
        dup_rows,
    )
    for copy in copies:
        copy.wait()
    first = 0
    for units_ref, source_ref, rows_ref, out_ref in (
        (fine_own_ref, coef_ref, fine_rows_ref, fine_out_ref),
        (coarse_own_ref, coarse_coef_ref, coarse_rows_ref, coarse_out_ref),
    ):
        clusters = rows_ref.shape[1] // 64
        build_own(source_ref, rows_ref, *scratch[:2])
        build_targets(rows_ref, scratch[2])
        sweep(list_ref, units_ref, first, *scratch)
        put_sums(scratch[-1], clusters, out_ref)
        first += clusters


def fine_kernel(list_ref, units_ref, recv_ref, rows_ref, own_ref, out_ref, *scratch):
    build_received(recv_ref, *scratch[:2])
    build_targets(rows_ref, scratch[2])
    sweep(list_ref, units_ref, 0, *scratch)
    put_sums(scratch[-1], rows_ref.shape[1] // 64, out_ref, own_ref)


def coarse_kernel(groups, *refs):
    late = 3 + groups
    list_ref, units_ref, recv_ref, rows_ref = refs[:4]
    out_ref, terms_ref = refs[4 + late:6 + late]
    late_refs = refs[6 + late:6 + 2 * late]
    late_sems = refs[6 + 2 * late:6 + 3 * late]
    gram_ref, split_ref, *scratch = refs[6 + 3 * late:]
    copies = [pltpu.make_async_copy(*pair) for pair in zip(refs[4:4 + late], late_refs, late_sems)]
    for copy in copies:
        copy.start()
    own_ref, fine_ref, transfer_ref, *probes_refs = late_refs
    clusters = rows_ref.shape[1] // 64
    px = split_ref.shape[0] // 2
    probes = probes_refs[0].shape[0]
    acc = scratch[-1]
    build_received(recv_ref, *scratch[:2])
    build_targets(rows_ref, scratch[2])
    sweep(list_ref, units_ref, fine_ref.shape[1] // 64, *scratch)
    for copy in copies:
        copy.wait()

    def one_parent(q, carry):
        own = halves(own_ref[:, lane_tile(q >> 1)])
        own = jnp.where((q & 1) == 0, own[0], own[1])
        twice = (summed(acc, q) + own).astype(jnp.bfloat16)
        matrix = transfer_ref[:, lane_tile(q)].astype(jnp.float32)
        low = lax.broadcasted_iota(jnp.int32, matrix.shape, 1) < 64
        matrix = jnp.concatenate(
            [jnp.where(low, matrix, 0.0), jnp.where(low, 0.0, matrix)], axis=0
        ).astype(jnp.bfloat16)
        total = fine_ref[:, lane_tile(q)] + bdot(twice, matrix, NT)
        out_ref[:, lane_tile(q)] = total
        high = total.astype(jnp.bfloat16)
        split_ref[:px, lane_tile(q)] = high
        split_ref[px:, lane_tile(q)] = (total - high.astype(jnp.float32)).astype(jnp.bfloat16)
        return carry

    lax.fori_loop(0, clusters, one_parent, 0, unroll=8)
    for block, probes_ref in enumerate(probes_refs):
        term = bdot(probes_ref[...], split_ref[...], NT)
        gram_ref[block] = term[:, :px] + term[:, px:]
    place = lax.axis_index("probe")
    for b in range(groups):
        block = gram_ref[lax.rem(place - b + groups, groups)]
        packed = jnp.concatenate([block[i:i + 8, :probes] for i in range(0, probes, 8)], axis=1)

        def one_owner(owner, carry):
            terms_ref[owner * groups + b] = packed
            return carry

        lax.fori_loop(0, terms_ref.shape[0] // groups, one_owner, 0)


def gram_kernel(terms_ref, out_ref, *, groups, scale):
    probes = out_ref.shape[0]
    columns = []
    for b in range(groups):
        total = terms_ref[b]
        for owner in range(1, terms_ref.shape[0] // groups):
            total = total + terms_ref[owner * groups + b]
        columns.append(
            jnp.concatenate([total[:, i * probes:(i + 1) * probes] for i in range(probes // 8)], axis=0)
        )
    out_ref[...] = jnp.concatenate(columns, axis=1) * scale


def sweep_scratch(total, clusters, px):
    return [
        pltpu.VMEM((total + 1, px, LANES), jnp.bfloat16),
        pltpu.VMEM((total + 1, 64, 16 * QUAD), jnp.bfloat16),
        pltpu.VMEM((clusters, 16, LANES), jnp.bfloat16),
        pltpu.VMEM((UNITS // QUAD, CHUNK * 64, QUAD * 64), jnp.bfloat16),
        pltpu.VMEM((UNITS // QUAD, CHUNK * 64, QUAD * 64), jnp.bfloat16),
        pltpu.VMEM((2, clusters, px, LANES), jnp.float32),
    ]


def shards(
    coef_fine,
    points_fine,
    points_coarse,
    transfer,
    send_fine,
    slots_fine,
    counts_fine,
    send_coarse,
    slots_coarse,
    counts_coarse,
):
    probes = coef_fine.shape[0]
    fine_count = counts_fine.shape[0]
    coarse_count = counts_coarse.shape[0]
    owners = lax.axis_size("leaf")
    groups = lax.axis_size("probe")
    px = -(-probes // 16) * 16
    coef = coef_fine if px == probes else jnp.pad(coef_fine, ((0, px - probes), (0, 0)))
    cap_fine = send_fine.shape[2]
    cap_coarse = send_coarse.shape[2]

    def params(scratch, blocks):
        size = SPARE + blocks * px * points_fine.shape[1] * 4
        for ref in scratch:
            size += math.prod(ref.shape[:-1]) * -(-ref.shape[-1] // LANES) * LANES * ref.dtype.itemsize
        return pltpu.CompilerParams(vmem_limit_bytes=size)

    whole_vmem = pltpu.CompilerParams(vmem_limit_bytes=VMEM)
    fine_scratch = sweep_scratch(owners * cap_fine, fine_count, px)
    coarse_scratch = sweep_scratch(owners * cap_coarse, coarse_count, px)
    smem = pl.BlockSpec(memory_space=pltpu.SMEM)
    vmem = pl.BlockSpec(memory_space=pltpu.VMEM)
    bf16, f32 = jnp.bfloat16, jnp.float32

    fine_send, fine_rows = pl.pallas_call(
        pack_fine_kernel,
        out_shape=(
            jax.ShapeDtypeStruct((owners, (cap_fine // 2) * (px + 8), LANES), bf16),
            jax.ShapeDtypeStruct((8, points_fine.shape[1]), f32),
        ),
        in_specs=[smem, vmem, vmem],
        out_specs=[vmem, vmem],
        scratch_shapes=[
            pltpu.VMEM((fine_count, px, LANES), bf16),
            pltpu.VMEM((fine_count, 8, LANES), f32),
        ],
        compiler_params=whole_vmem,
        name="pack_fine",
    )(send_fine, coef, points_fine)
    fine_recv = lax.all_to_all(fine_send, "leaf", split_axis=0, concat_axis=0, tiled=True)

    fine_total = owners * cap_fine
    coarse_total = owners * cap_coarse
    unit_rows = [-(-(count * (SLOTS // CHUNK) + 2 * UNITS + 1) // LANES) for count in (fine_count, coarse_count)]
    list_shape = (RECEIVED + SLOTS + CHUNK, LANES)
    i32 = jnp.int32
    coarse_send, coarse_rows, slot_list, fine_units, coarse_units, fine_sums, coarse_sums = pl.pallas_call(
        functools.partial(own_kernel, entries=(fine_total, coarse_total)),
        out_shape=(
            jax.ShapeDtypeStruct((owners, (cap_coarse // 2) * (px + 8), LANES), bf16),
            jax.ShapeDtypeStruct((8, points_coarse.shape[1]), f32),
            jax.ShapeDtypeStruct(list_shape, i32),
            jax.ShapeDtypeStruct((unit_rows[0], LANES), i32),
            jax.ShapeDtypeStruct((unit_rows[1], LANES), i32),
            jax.ShapeDtypeStruct((px, points_fine.shape[1]), f32),
            jax.ShapeDtypeStruct((px, points_coarse.shape[1]), f32),
        ),
        in_specs=[smem] + [vmem] * 8,
        out_specs=[vmem] * 7,
        scratch_shapes=[
            pltpu.VMEM((px, points_coarse.shape[1]), bf16),
            pltpu.VMEM((coarse_count, px, LANES), bf16),
            pltpu.VMEM((coarse_count, 8, LANES), f32),
            pltpu.VMEM((unit_rows[0], LANES), i32),
            pltpu.VMEM((unit_rows[1], LANES), i32),
            pltpu.SMEM(list_shape, i32),
            pltpu.SMEM((unit_rows[0], LANES), i32),
            pltpu.SMEM((unit_rows[1], LANES), i32),
            pltpu.SemaphoreType.DMA,
            pltpu.SemaphoreType.DMA,
            pltpu.SemaphoreType.DMA,
        ]
        + sweep_scratch(fine_count, fine_count, px),
        compiler_params=whole_vmem,
        cost_estimate=pl.CostEstimate(flops=10**10, bytes_accessed=10**7, transcendentals=10**7),
        name="own_sweep",
    )(
        jnp.swapaxes(send_coarse, 1, 2),
        slots_fine,
        counts_fine.reshape(1, -1),
        slots_coarse,
        counts_coarse.reshape(1, -1),
        coef,
        transfer,
        points_coarse,
        fine_rows,
    )

    turned = [coef_fine]
    for step in range(1, groups):
        turned.append(lax.ppermute(coef_fine, "probe", [(i, (i + step) % groups) for i in range(groups)]))
    coarse_recv = lax.all_to_all(coarse_send, "leaf", split_axis=0, concat_axis=0, tiled=True)

    fine_far = pl.pallas_call(
        fine_kernel,
        out_shape=jax.ShapeDtypeStruct((px, points_fine.shape[1]), f32),
        in_specs=[smem] * 2 + [vmem] * 3,
        out_specs=vmem,
        scratch_shapes=fine_scratch,
        compiler_params=params(fine_scratch, owners // 4 + 4),
        name="fine_sweep",
    )(slot_list, fine_units, fine_recv, fine_rows, fine_sums)

    late = (coarse_sums, fine_far, transfer, *turned)
    term_shape = (owners * groups, 8, probes * probes // 8)
    far, terms = pl.pallas_call(
        functools.partial(coarse_kernel, groups),
        out_shape=(
            jax.ShapeDtypeStruct((px, points_fine.shape[1]), f32),
            jax.ShapeDtypeStruct(term_shape, f32),
        ),
        in_specs=[smem] * 2 + [vmem] * 2 + [pl.BlockSpec(memory_space=pl.ANY)] * (3 + groups),
        out_specs=[vmem, vmem],
        scratch_shapes=[pltpu.VMEM(operand.shape, operand.dtype) for operand in late]
        + [pltpu.SemaphoreType.DMA] * len(late)
        + [
            pltpu.VMEM((groups, probes, px), f32),
            pltpu.VMEM((2 * px, points_fine.shape[1]), bf16),
        ]
        + coarse_scratch,
        compiler_params=whole_vmem,
        name="coarse_sweep",
    )(slot_list, coarse_units, coarse_recv, coarse_rows, *late)

    terms = lax.all_to_all(terms, ("leaf", "probe"), split_axis=0, concat_axis=0, tiled=True)
    probe_gram = pl.pallas_call(
        functools.partial(
            gram_kernel, groups=groups, scale=1.0 / math.sqrt(owners * fine_count * 64)
        ),
        out_shape=jax.ShapeDtypeStruct((probes, groups * probes), f32),
        in_specs=[vmem],
        out_specs=vmem,
        name="gram_sum",
    )(terms)
    return (far[:probes], probe_gram)


def solution(mesh):
    return jax.shard_map(
        shards,
        mesh=mesh,
        in_specs=(
            P("probe", "leaf"),
            P(None, "leaf"),
            P(None, "leaf"),
            P(None, "leaf"),
            P("leaf", None, None),
            P("leaf", None),
            P("leaf"),
            P("leaf", None, None),
            P("leaf", None),
            P("leaf"),
        ),
        out_specs=(P("probe", "leaf"), P("probe", None)),
        check_vma=False,
    )
```

```python
import functools
import functools
import math

import jax
import jax.numpy as jnp
from jax import lax
from jax.experimental import pallas as pl
from jax.experimental.pallas import tpu as pltpu
from jax.sharding import PartitionSpec as P

KERNEL_RATE = 1.5
POINT_SCALE = math.sqrt(2.0 * KERNEL_RATE)
LANES = 128
UNITS = 16
QUAD = 4
CHUNK = 8
FAR_AWAY = -30000.0
SLOTS = 64
RECEIVED = SLOTS + CHUNK
VMEM = 56 * 1024 * 1024

NT = (((1,), (1,)), ((), ()))
NN = (((1,), (0,)), ((), ()))


def bdot(a, b, dims):
    return lax.dot_general(a, b, dims, preferred_element_type=jnp.float32)


def split_rows(points):
    v = points * POINT_SCALE
    norm = -0.5 * (v[0:1] * v[0:1] + v[1:2] * v[1:2] + v[2:3] * v[2:3])
    full = jnp.concatenate([v, norm], axis=0)
    high = full.astype(jnp.bfloat16).astype(jnp.float32)
    rest = (full - high).astype(jnp.bfloat16).astype(jnp.float32)
    return jnp.concatenate([high, rest], axis=0)


def source_features(rows):
    place = lax.broadcasted_iota(jnp.int32, rows.shape, 0)
    one = jnp.where((place == 3) | (place == 7), 1.0, 0.0)
    return jnp.concatenate([rows, jnp.where(place < 3, rows, one)], axis=0)


def target_features(rows):
    place = lax.broadcasted_iota(jnp.int32, rows.shape, 0)
    turned = jnp.concatenate([rows[4:8], rows[0:4]], axis=0)
    one = jnp.where((place == 3) | (place == 7), 1.0, jnp.where(place < 3, rows, turned))
    return jnp.concatenate([one, turned], axis=0)


def halves(tile):
    lane = lax.broadcasted_iota(jnp.int32, tile.shape, 1)
    turned = pltpu.roll(tile, LANES // 2, 1)
    low = lane < LANES // 2
    return jnp.where(low, tile, turned), jnp.where(low, turned, tile)


def lane_tile(index):
    return pl.ds(pl.multiple_of(index * LANES, LANES), LANES)


def list_slots(
    fine_slots_ref, fine_counts_ref, coarse_slots_ref, coarse_counts_ref, out_ref, *units_refs, entries
):
    fine, coarse = fine_slots_ref.shape[0], coarse_slots_ref.shape[0]
    spare = LANES - fine - coarse
    slots = jnp.concatenate(
        [fine_slots_ref[...], coarse_slots_ref[...], jnp.zeros((spare, SLOTS), jnp.int32)], axis=0
    )
    slots = slots.astype(jnp.float32).T.astype(jnp.int32)
    counts = jnp.concatenate(
        [fine_counts_ref[...], coarse_counts_ref[...], jnp.zeros((1, spare), jnp.int32)], axis=1
    )
    shape = (SLOTS, LANES)
    in_fine = lax.broadcasted_iota(jnp.int32, shape, 1) < fine
    clusters = jnp.where(in_fine, fine, coarse)
    nothing = jnp.where(in_fine, entries[0], entries[1])
    live = lax.broadcasted_iota(jnp.int32, shape, 0) < counts
    own = live & (slots < clusters)
    received = live & (slots >= clusters)
    row = lax.broadcasted_iota(jnp.int32, (SLOTS, SLOTS), 0)
    column = lax.broadcasted_iota(jnp.int32, (SLOTS, SLOTS), 1)
    upto = jnp.where(column <= row, 1.0, 0.0).astype(jnp.bfloat16)
    turns = []
    for start, chosen, value, blank in (
        (0, own, slots, clusters),
        (RECEIVED, received, slots - clusters, nothing),
    ):
        rank = bdot(upto, jnp.where(chosen, 1.0, 0.0).astype(jnp.bfloat16), NN).astype(jnp.int32)
        spot = jnp.where(chosen, rank - 1, -1)
        value = value - blank
        for first in range(0, SLOTS, 8):
            rows = [
                blank[:1] + jnp.sum(jnp.where(spot == place, value, 0), axis=0, keepdims=True)
                for place in range(first, first + 8)
            ]
            out_ref[start + first:start + first + 8] = jnp.concatenate(rows, axis=0)
        out_ref[start + SLOTS:start + SLOTS + CHUNK] = jnp.broadcast_to(blank[:1], (CHUNK, LANES))
        turns.append(jnp.maximum((rank[SLOTS - 1:] + CHUNK - 1) // CHUNK, 1))
    turns = jnp.concatenate(turns + [jnp.zeros((6, LANES), jnp.int32)], axis=0).astype(jnp.float32).T
    row = lax.broadcasted_iota(jnp.int32, (LANES, LANES), 0)
    column = lax.broadcasted_iota(jnp.int32, (LANES, LANES), 1)
    upto = (column <= row) & ((row < fine) == (column < fine))
    ends = bdot(jnp.where(upto, 1.0, 0.0).astype(jnp.bfloat16), turns.astype(jnp.bfloat16), NN)
    ends, turns = ends.astype(jnp.int32), turns.astype(jnp.int32)
    for side in range(2):
        for level, (low, count) in enumerate(((0, fine), (fine, coarse))):
            units_ref = units_refs[2 * side + level]
            end = ends[low:low + count, side:side + 1]
            took = turns[low:low + count, side:side + 1]
            lane = lax.broadcasted_iota(jnp.int32, (1, LANES), 1)
            for tile in range(units_ref.shape[0]):
                place = tile * LANES + lane
                passed = end <= place
                target = jnp.sum(jnp.where(passed, 1, 0), axis=0, keepdims=True)
                turn = place - jnp.sum(jnp.where(passed, took, 0), axis=0, keepdims=True)
                over = target >= count
                start = side * RECEIVED + jnp.where(over, SLOTS, turn * CHUNK)
                code = start * LANES + low + jnp.where(over, count - 1, target)
                if tile == units_ref.shape[0] - 1:
                    code = jnp.where(lane == LANES - 1, end[count - 1:], code)
                units_ref[tile:tile + 1] = code


def pack_send(send_ref, out_ref, dup_coef, dup_rows, owners, capacity, px, entry_first=False):
    pairs = capacity // 2
    lane = lax.broadcasted_iota(jnp.int32, (px, LANES), 1) < LANES // 2
    lane8 = lax.broadcasted_iota(jnp.int32, (8, LANES), 1) < LANES // 2

    def one_owner(owner, carry):
        before = None
        for pair in range(pairs):
            first, second = [
                send_ref[0, entry, owner] if entry_first else send_ref[0, owner, entry]
                for entry in (2 * pair, 2 * pair + 1)
            ]
            out_ref[owner, pair * px:(pair + 1) * px, :] = jnp.where(lane, dup_coef[first], dup_coef[second])
            rows = jnp.where(lane8, dup_rows[first], dup_rows[second])
            if pair % 2 == 0:
                before = rows
            else:
                start = pairs * px + (pair - 1) * 8
                out_ref[owner, start:start + 16, :] = jnp.concatenate(
                    [before, rows], axis=0
                ).astype(jnp.bfloat16)
        return carry

    lax.fori_loop(0, owners, one_owner, 0, unroll=4)


def pack_fine(send_ref, coef_ref, points_ref, out_ref, rows_ref, dup_coef, dup_rows):
    _, owners, capacity = send_ref.shape
    px = coef_ref.shape[0]
    rows_ref[...] = split_rows(points_ref[...])

    def one_tile(index, carry):
        a, b = halves(coef_ref[:, lane_tile(index)].astype(jnp.float32))
        dup_coef[2 * index] = a.astype(jnp.bfloat16)
        dup_coef[2 * index + 1] = b.astype(jnp.bfloat16)
        a, b = halves(rows_ref[:, lane_tile(index)])
        dup_rows[2 * index] = a
        dup_rows[2 * index + 1] = b
        return carry

    lax.fori_loop(0, coef_ref.shape[1] // LANES, one_tile, 0, unroll=8)
    pack_send(send_ref, out_ref, dup_coef, dup_rows, owners, capacity, px)


def pack_coarse(
    send_ref, coef_ref, transfer_ref, points_ref, out_ref, rows_ref, coarse_ref, dup_coef, dup_rows
):
    _, capacity, owners = send_ref.shape
    px = coef_ref.shape[0]
    rows_ref[...] = split_rows(points_ref[...])

    def one_tile(index, carry):
        doubled = []
        for part in range(2):
            q = 2 * index + part
            a, b = halves(transfer_ref[:, lane_tile(q)].astype(jnp.float32))
            matrix = jnp.concatenate([a, b], axis=0).astype(jnp.bfloat16)
            block = bdot(coef_ref[:, lane_tile(q)], matrix, NN).astype(jnp.bfloat16)
            dup_coef[q] = block
            doubled.append(block)
        lane = lax.broadcasted_iota(jnp.int32, (px, LANES), 1) < LANES // 2
        coarse_ref[:, lane_tile(index)] = jnp.where(lane, doubled[0], doubled[1])
        a, b = halves(rows_ref[:, lane_tile(index)])
        dup_rows[2 * index] = a
        dup_rows[2 * index + 1] = b
        return carry

    lax.fori_loop(0, coef_ref.shape[1] // (2 * LANES), one_tile, 0, unroll=8)
    pack_send(send_ref, out_ref, dup_coef, dup_rows, owners, capacity, px, entry_first=True)


def turned(rows):
    row = lax.broadcasted_iota(jnp.int32, (LANES, LANES), 0)
    column = lax.broadcasted_iota(jnp.int32, (LANES, LANES), 1)
    unit = jnp.where(row == column, 1.0, 0.0).astype(jnp.bfloat16)
    return bdot(unit, rows, NT).astype(jnp.bfloat16)


def put_pair(entry, coef, rows, coef_table, feature_table):
    a, b = halves(coef.astype(jnp.float32))
    coef_table[entry] = a.astype(jnp.bfloat16)
    coef_table[entry + 1] = b.astype(jnp.bfloat16)
    features = turned(jnp.concatenate([source_features(rows).astype(jnp.bfloat16)] * QUAD, axis=0))
    feature_table[entry] = features[:64]
    feature_table[entry + 1] = features[64:]


def put_nothing(entry, coef_table, feature_table):
    coef_table[entry] = jnp.zeros(coef_table.shape[1:], jnp.bfloat16)
    place = lax.broadcasted_iota(jnp.int32, (8, LANES), 0)
    nothing = source_features(jnp.where(place == 3, FAR_AWAY, 0.0)).astype(jnp.bfloat16)
    feature_table[entry] = turned(jnp.concatenate([nothing] * QUAD, axis=0))[:64]


def build_own(coef_ref, rows_ref, coef_table, feature_table):
    tiles = coef_ref.shape[1] // LANES

    def one_tile(index, carry):
        tile = lane_tile(index)
        put_pair(2 * index, coef_ref[:, tile], rows_ref[:, tile], coef_table, feature_table)
        return carry

    lax.fori_loop(0, tiles, one_tile, 0, unroll=16)
    put_nothing(2 * tiles, coef_table, feature_table)


def build_received(recv_ref, coef_table, feature_table):
    owners, recv_rows, _ = recv_ref.shape
    px = coef_table.shape[1]
    pairs = recv_rows // (px + 8)

    def one_owner(owner, carry):
        for pair in range(0, pairs, 2):
            start = pairs * px + pair * 8
            both = recv_ref[owner, start:start + 16, :].astype(jnp.float32)
            for part in range(2):
                where = pair + part
                put_pair(
                    owner * (2 * pairs) + 2 * where,
                    recv_ref[owner, where * px:(where + 1) * px, :],
                    both[8 * part:8 * part + 8],
                    coef_table,
                    feature_table,
                )
        return carry

    lax.fori_loop(0, owners, one_owner, 0, unroll=32 // pairs)
    put_nothing(owners * pairs * 2, coef_table, feature_table)


def build_targets(rows_ref, target_table):
    def one_tile(index, carry):
        a, b = halves(target_features(rows_ref[:, lane_tile(index)]))
        target_table[2 * index] = a.astype(jnp.bfloat16)
        target_table[2 * index + 1] = b.astype(jnp.bfloat16)
        return carry

    lax.fori_loop(0, rows_ref.shape[1] // LANES, one_tile, 0, unroll=16)


def sweep(list_ref, units_ref, first, coef_table, feature_table, target_table, first_buffer, second_buffer, acc):
    px = coef_table.shape[1]
    lane = lax.broadcasted_iota(jnp.int32, (64, 16 * QUAD), 1) // 16
    lane_t = lax.broadcasted_iota(jnp.int32, (16, LANES), 1) // 64
    lane_x = lax.broadcasted_iota(jnp.int32, (px, LANES), 1) < 64
    blank = jnp.zeros((16, LANES), jnp.bfloat16)
    acc[...] = jnp.zeros_like(acc)

    def partners(unit):
        row, column = unit
        return [list_ref[row + m, column] for m in range(CHUNK)]

    def units_of(place):
        codes = [units_ref[place >> 7, (place & (LANES - 1)) + u] for u in range(UNITS)]
        return [(code >> 7, code & (LANES - 1)) for code in codes]

    def tiles(units, buffer):
        for start in range(0, UNITS, QUAD):
            quad = units[start:start + QUAD]
            weights = []
            for u in range(QUAD):
                own = jnp.where(lane_t == u % 2, target_table[quad[u][1] - first], blank)
                weights.append(jnp.concatenate([own if v == u // 2 else blank for v in range(QUAD // 2)], axis=1))
            weights = jnp.concatenate(weights, axis=0)
            ids = [partners(unit) for unit in quad]
            for part in range(0, CHUNK, 4):
                rows = []
                for m in range(part, part + 4):
                    tile = feature_table[ids[0][m]]
                    for u in range(1, QUAD):
                        tile = jnp.where(lane == u, feature_table[ids[u][m]], tile)
                    rows.append(tile)
                power = bdot(jnp.concatenate(rows, axis=0), weights, NN)
                buffer[start // QUAD, part * 64:(part + 4) * 64] = jnp.exp(power).astype(jnp.bfloat16)

    def products(units, buffer):
        for start in range(0, UNITS, QUAD):
            quad = units[start:start + QUAD]
            coefs = []
            for unit in quad:
                ids = partners(unit)
                coefs.append(
                    jnp.concatenate(
                        [
                            jnp.where(lane_x, coef_table[ids[m]], coef_table[ids[m + 1]])
                            for m in range(0, CHUNK, 2)
                        ],
                        axis=1,
                    )
                )
            product = bdot(jnp.concatenate(coefs, axis=0), buffer[start // QUAD], NN)
            for u in range(QUAD):
                side = (u // 2) * LANES
                acc[u % 2, quad[u][1] - first] += product[u * px:(u + 1) * px, side:side + LANES]

    def two_sets(index, carry):
        here = index * (2 * UNITS)
        second = units_of(here + UNITS)
        tiles(second, second_buffer)
        products(units_of(here), first_buffer)
        tiles(units_of(here + 2 * UNITS), first_buffer)
        products(second, second_buffer)
        return carry

    total = units_ref[units_ref.shape[0] - 1, LANES - 1]
    sets = (total + UNITS - 1) // UNITS
    bodies = (sets - 1) // 2
    last = bodies * (2 * UNITS)
    tiles(units_of(0), first_buffer)
    lax.fori_loop(0, bodies, two_sets, 0)

    @pl.when(sets == 2 * bodies + 2)
    def _():
        second = units_of(last + UNITS)
        tiles(second, second_buffer)
        products(units_of(last), first_buffer)
        products(second, second_buffer)

    @pl.when(sets == 2 * bodies + 1)
    def _():
        products(units_of(last), first_buffer)


def summed(acc, target):
    low = lax.broadcasted_iota(jnp.int32, acc.shape[2:], 1) < 64
    here = jnp.where(low, acc[0, target], acc[1, target])
    return here + pltpu.roll(here, 64, 1)


def put_sums(acc, clusters, out_ref, before_ref=None):
    low = lax.broadcasted_iota(jnp.int32, acc.shape[2:], 1) < 64

    def one_tile(index, carry):
        tile = lane_tile(index)
        sums = jnp.where(low, summed(acc, 2 * index), summed(acc, 2 * index + 1))
        out_ref[:, tile] = sums if before_ref is None else before_ref[:, tile] + sums
        return carry

    lax.fori_loop(0, clusters // 2, one_tile, 0, unroll=8)


def prepare_kernel(
    send_ref,
    fine_slots_ref,
    fine_counts_ref,
    coarse_slots_ref,
    coarse_counts_ref,
    coef_ref,
    points_ref,
    coarse_coef_ref,
    coarse_rows_ref,
    send_out_ref,
    fine_rows_ref,
    list_out_ref,
    fine_own_ref,
    fine_units_ref,
    coarse_units_ref,
    coarse_out_ref,
    dup_coef,
    dup_rows,
    coarse_own_ref,
    list_ref,
    units_ref,
    list_sem,
    units_sem,
    *scratch,
    entries,
):
    list_slots(
        fine_slots_ref,
        fine_counts_ref,
        coarse_slots_ref,
        coarse_counts_ref,
        list_out_ref,
        fine_own_ref,
        coarse_own_ref,
        fine_units_ref,
        coarse_units_ref,
        entries=entries,
    )
    copies = [
        pltpu.make_async_copy(list_out_ref, list_ref, list_sem),
        pltpu.make_async_copy(coarse_own_ref, units_ref, units_sem),
    ]
    for copy in copies:
        copy.start()
    pack_fine(send_ref, coef_ref, points_ref, send_out_ref, fine_rows_ref, dup_coef, dup_rows)
    build_own(coarse_coef_ref, coarse_rows_ref, *scratch[:2])
    build_targets(coarse_rows_ref, scratch[2])
    for copy in copies:
        copy.wait()
    sweep(list_ref, units_ref, fine_rows_ref.shape[1] // 64, *scratch)
    put_sums(scratch[-1], coarse_rows_ref.shape[1] // 64, coarse_out_ref)


def coarse_kernel(
    list_ref,
    own_units_ref,
    units_ref,
    coef_ref,
    fine_rows_ref,
    recv_ref,
    rows_ref,
    own_ref,
    fine_out_ref,
    out_ref,
    *scratch,
):
    fine = fine_rows_ref.shape[1] // 64
    build_own(coef_ref, fine_rows_ref, *scratch[:2])
    build_targets(fine_rows_ref, scratch[2])
    sweep(list_ref, own_units_ref, 0, *scratch)
    put_sums(scratch[-1], fine, fine_out_ref)
    build_received(recv_ref, *scratch[:2])
    build_targets(rows_ref, scratch[2])
    sweep(list_ref, units_ref, fine, *scratch)
    put_sums(scratch[-1], rows_ref.shape[1] // 64, out_ref, own_ref)


def fine_kernel(groups, *refs):
    late = 3 + groups
    list_ref, units_ref, recv_ref, rows_ref = refs[:4]
    out_ref, terms_ref = refs[4 + late:6 + late]
    late_refs = refs[6 + late:6 + 2 * late]
    late_sems = refs[6 + 2 * late:6 + 3 * late]
    gram_ref, split_ref, *scratch = refs[6 + 3 * late:]
    copies = [pltpu.make_async_copy(*pair) for pair in zip(refs[4:4 + late], late_refs, late_sems)]
    for copy in copies:
        copy.start()
    own_ref, coarse_ref, transfer_ref, *probes_refs = late_refs
    px = split_ref.shape[0] // 2
    probes = probes_refs[0].shape[0]
    acc = scratch[-1]
    build_received(recv_ref, *scratch[:2])
    build_targets(rows_ref, scratch[2])
    sweep(list_ref, units_ref, 0, *scratch)
    for copy in copies:
        copy.wait()
    low_x = lax.broadcasted_iota(jnp.int32, (px, LANES), 1) < 64

    def one_parent(q, carry):
        far = halves(coarse_ref[:, lane_tile(q >> 1)])
        twice = jnp.where((q & 1) == 0, far[0], far[1]).astype(jnp.bfloat16)
        matrix = transfer_ref[:, lane_tile(q)].astype(jnp.float32)
        low = lax.broadcasted_iota(jnp.int32, matrix.shape, 1) < 64
        matrix = jnp.concatenate(
            [jnp.where(low, matrix, 0.0), jnp.where(low, 0.0, matrix)], axis=0
        ).astype(jnp.bfloat16)
        sums = jnp.where(low_x, summed(acc, 2 * q), summed(acc, 2 * q + 1))
        total = own_ref[:, lane_tile(q)] + sums + bdot(twice, matrix, NT)
        out_ref[:, lane_tile(q)] = total
        high = total.astype(jnp.bfloat16)
        split_ref[:px, lane_tile(q)] = high
        split_ref[px:, lane_tile(q)] = (total - high.astype(jnp.float32)).astype(jnp.bfloat16)
        return carry

    lax.fori_loop(0, coarse_ref.shape[1] // 64, one_parent, 0, unroll=8)
    for block, probes_ref in enumerate(probes_refs):
        term = bdot(probes_ref[...], split_ref[...], NT)
        gram_ref[block] = term[:, :px] + term[:, px:]
    place = lax.axis_index("probe")
    for b in range(groups):
        block = gram_ref[lax.rem(place - b + groups, groups)]
        packed = jnp.concatenate([block[i:i + 8, :probes] for i in range(0, probes, 8)], axis=1)

        def one_owner(owner, carry):
            terms_ref[owner * groups + b] = packed
            return carry

        lax.fori_loop(0, terms_ref.shape[0] // groups, one_owner, 0)


def gram_kernel(terms_ref, out_ref, *, groups, scale):
    probes = out_ref.shape[0]
    columns = []
    for b in range(groups):
        total = terms_ref[b]
        for owner in range(1, terms_ref.shape[0] // groups):
            total = total + terms_ref[owner * groups + b]
        columns.append(
            jnp.concatenate([total[:, i * probes:(i + 1) * probes] for i in range(probes // 8)], axis=0)
        )
    out_ref[...] = jnp.concatenate(columns, axis=1) * scale


def sweep_scratch(total, clusters, px):
    return [
        pltpu.VMEM((total + 1, px, LANES), jnp.bfloat16),
        pltpu.VMEM((total + 1, 64, 16 * QUAD), jnp.bfloat16),
        pltpu.VMEM((clusters, 16, LANES), jnp.bfloat16),
        pltpu.VMEM((UNITS // QUAD, CHUNK * 64, QUAD * 64), jnp.bfloat16),
        pltpu.VMEM((UNITS // QUAD, CHUNK * 64, QUAD * 64), jnp.bfloat16),
        pltpu.VMEM((2, clusters, px, LANES), jnp.float32),
    ]


def shards(
    coef_fine,
    points_fine,
    points_coarse,
    transfer,
    send_fine,
    slots_fine,
    counts_fine,
    send_coarse,
    slots_coarse,
    counts_coarse,
):
    probes = coef_fine.shape[0]
    fine_count = counts_fine.shape[0]
    coarse_count = counts_coarse.shape[0]
    owners = lax.axis_size("leaf")
    groups = lax.axis_size("probe")
    px = -(-probes // 16) * 16
    coef = coef_fine if px == probes else jnp.pad(coef_fine, ((0, px - probes), (0, 0)))
    cap_fine = send_fine.shape[2]
    cap_coarse = send_coarse.shape[2]

    whole_vmem = pltpu.CompilerParams(vmem_limit_bytes=VMEM)
    smem = pl.BlockSpec(memory_space=pltpu.SMEM)
    vmem = pl.BlockSpec(memory_space=pltpu.VMEM)
    bf16, f32 = jnp.bfloat16, jnp.float32

    fine_total = owners * cap_fine
    coarse_total = owners * cap_coarse
    unit_rows = [-(-(count * (SLOTS // CHUNK) + 2 * UNITS + 1) // LANES) for count in (fine_count, coarse_count)]
    list_shape = (RECEIVED + SLOTS + CHUNK, LANES)
    i32 = jnp.int32
    fine_columns, coarse_columns = points_fine.shape[1], points_coarse.shape[1]

    coarse_send, coarse_rows, coarse_coef = pl.pallas_call(
        pack_coarse,
        out_shape=(
            jax.ShapeDtypeStruct((owners, (cap_coarse // 2) * (px + 8), LANES), bf16),
            jax.ShapeDtypeStruct((8, coarse_columns), f32),
            jax.ShapeDtypeStruct((px, coarse_columns), bf16),
        ),
        in_specs=[smem, vmem, vmem, vmem],
        out_specs=[vmem] * 3,
        scratch_shapes=[
            pltpu.VMEM((coarse_count, px, LANES), bf16),
            pltpu.VMEM((coarse_count, 8, LANES), f32),
        ],
        compiler_params=whole_vmem,
        name="pack_coarse",
    )(jnp.swapaxes(send_coarse, 1, 2), coef, transfer, points_coarse)
    coarse_recv = lax.all_to_all(coarse_send, "leaf", split_axis=0, concat_axis=0, tiled=True)

    turned = [coef_fine]
    for step in range(1, groups):
        turned.append(lax.ppermute(coef_fine, "probe", [(i, (i + step) % groups) for i in range(groups)]))

    fine_send, fine_rows, slot_list, fine_own, fine_units, coarse_units, coarse_own_sums = pl.pallas_call(
        functools.partial(prepare_kernel, entries=(fine_total, coarse_total)),
        out_shape=(
            jax.ShapeDtypeStruct((owners, (cap_fine // 2) * (px + 8), LANES), bf16),
            jax.ShapeDtypeStruct((8, fine_columns), f32),
            jax.ShapeDtypeStruct(list_shape, i32),
            jax.ShapeDtypeStruct((unit_rows[0], LANES), i32),
            jax.ShapeDtypeStruct((unit_rows[0], LANES), i32),
            jax.ShapeDtypeStruct((unit_rows[1], LANES), i32),
            jax.ShapeDtypeStruct((px, coarse_columns), f32),
        ),
        in_specs=[smem] + [vmem] * 8,
        out_specs=[vmem] * 7,
        scratch_shapes=[
            pltpu.VMEM((fine_count, px, LANES), bf16),
            pltpu.VMEM((fine_count, 8, LANES), f32),
            pltpu.VMEM((unit_rows[1], LANES), i32),
            pltpu.SMEM(list_shape, i32),
            pltpu.SMEM((unit_rows[1], LANES), i32),
            pltpu.SemaphoreType.DMA,
            pltpu.SemaphoreType.DMA,
        ]
        + sweep_scratch(coarse_count, coarse_count, px),
        compiler_params=whole_vmem,
        cost_estimate=pl.CostEstimate(flops=10**10, bytes_accessed=10**7, transcendentals=10**7),
        name="prepare",
    )(
        send_fine,
        slots_fine,
        counts_fine.reshape(1, -1),
        slots_coarse,
        counts_coarse.reshape(1, -1),
        coef,
        points_fine,
        coarse_coef,
        coarse_rows,
    )
    fine_recv = lax.all_to_all(fine_send, "leaf", split_axis=0, concat_axis=0, tiled=True)

    fine_sums, coarse_far = pl.pallas_call(
        coarse_kernel,
        out_shape=(
            jax.ShapeDtypeStruct((px, fine_columns), f32),
            jax.ShapeDtypeStruct((px, coarse_columns), f32),
        ),
        in_specs=[smem] * 3 + [vmem] * 5,
        out_specs=[vmem, vmem],
        scratch_shapes=sweep_scratch(max(fine_count, coarse_total), fine_count, px),
        compiler_params=whole_vmem,
        cost_estimate=pl.CostEstimate(flops=10**10, bytes_accessed=10**7, transcendentals=10**7),
        name="coarse_sweep",
    )(slot_list, fine_own, coarse_units, coef, fine_rows, coarse_recv, coarse_rows, coarse_own_sums)

    late = (fine_sums, coarse_far, transfer, *turned)
    term_shape = (owners * groups, 8, probes * probes // 8)
    far, terms = pl.pallas_call(
        functools.partial(fine_kernel, groups),
        out_shape=(
            jax.ShapeDtypeStruct((px, points_fine.shape[1]), f32),
            jax.ShapeDtypeStruct(term_shape, f32),
        ),
        in_specs=[smem] * 2 + [vmem] * 2 + [pl.BlockSpec(memory_space=pl.ANY)] * (3 + groups),
        out_specs=[vmem, vmem],
        scratch_shapes=[pltpu.VMEM(operand.shape, operand.dtype) for operand in late]
        + [pltpu.SemaphoreType.DMA] * len(late)
        + [
            pltpu.VMEM((groups, probes, px), f32),
            pltpu.VMEM((2 * px, points_fine.shape[1]), bf16),
        ]
        + sweep_scratch(fine_total, fine_count, px),
        compiler_params=whole_vmem,
        name="fine_sweep",
    )(slot_list, fine_units, fine_recv, fine_rows, *late)

    terms = lax.all_to_all(terms, ("leaf", "probe"), split_axis=0, concat_axis=0, tiled=True)
    probe_gram = pl.pallas_call(
        functools.partial(
            gram_kernel, groups=groups, scale=1.0 / math.sqrt(owners * fine_count * 64)
        ),
        out_shape=jax.ShapeDtypeStruct((probes, groups * probes), f32),
        in_specs=[vmem],
        out_specs=vmem,
        name="gram_sum",
    )(terms)
    return (far[:probes], probe_gram)


def solution(mesh):
    return jax.shard_map(
        shards,
        mesh=mesh,
        in_specs=(
            P("probe", "leaf"),
            P(None, "leaf"),
            P(None, "leaf"),
            P(None, "leaf"),
            P("leaf", None, None),
            P("leaf", None),
            P("leaf"),
            P("leaf", None, None),
            P("leaf", None),
            P("leaf"),
        ),
        out_specs=(P("probe", "leaf"), P("probe", None)),
        check_vma=False,
    )
```

```python
import functools
import functools
import math

import jax
import jax.numpy as jnp
from jax import lax
from jax.experimental import pallas as pl
from jax.experimental.pallas import tpu as pltpu
from jax.sharding import PartitionSpec as P

KERNEL_RATE = 1.5
POINT_SCALE = math.sqrt(2.0 * KERNEL_RATE)
LANES = 128
UNITS = 16
QUAD = 4
CHUNK = 8
FAR_AWAY = -30000.0
SLOTS = 64
SECTION = SLOTS + CHUNK
EARLY = 3
VMEM = 56 * 1024 * 1024

NT = (((1,), (1,)), ((), ()))
NN = (((1,), (0,)), ((), ()))


def bdot(a, b, dims):
    return lax.dot_general(a, b, dims, preferred_element_type=jnp.float32)


def split_rows(points):
    v = points * POINT_SCALE
    norm = -0.5 * (v[0:1] * v[0:1] + v[1:2] * v[1:2] + v[2:3] * v[2:3])
    full = jnp.concatenate([v, norm], axis=0)
    high = full.astype(jnp.bfloat16).astype(jnp.float32)
    rest = (full - high).astype(jnp.bfloat16).astype(jnp.float32)
    return jnp.concatenate([high, rest], axis=0)


def source_features(rows):
    place = lax.broadcasted_iota(jnp.int32, rows.shape, 0)
    one = jnp.where((place == 3) | (place == 7), 1.0, 0.0)
    return jnp.concatenate([rows, jnp.where(place < 3, rows, one)], axis=0)


def target_features(rows):
    place = lax.broadcasted_iota(jnp.int32, rows.shape, 0)
    turned = jnp.concatenate([rows[4:8], rows[0:4]], axis=0)
    one = jnp.where((place == 3) | (place == 7), 1.0, jnp.where(place < 3, rows, turned))
    return jnp.concatenate([one, turned], axis=0)


def halves(tile):
    lane = lax.broadcasted_iota(jnp.int32, tile.shape, 1)
    turned = pltpu.roll(tile, LANES // 2, 1)
    low = lane < LANES // 2
    return jnp.where(low, tile, turned), jnp.where(low, turned, tile)


def lane_tile(index):
    return pl.ds(pl.multiple_of(index * LANES, LANES), LANES)


def list_slots(
    fine_slots_ref, fine_counts_ref, coarse_slots_ref, coarse_counts_ref, out_ref, *units_refs, owners, caps, splits
):
    fine, coarse = fine_slots_ref.shape[0], coarse_slots_ref.shape[0]
    spare = LANES - fine - coarse
    slots = jnp.concatenate(
        [fine_slots_ref[...], coarse_slots_ref[...], jnp.zeros((spare, SLOTS), jnp.int32)], axis=0
    )
    slots = slots.astype(jnp.float32).T.astype(jnp.int32)
    counts = jnp.concatenate(
        [fine_counts_ref[...], coarse_counts_ref[...], jnp.zeros((1, spare), jnp.int32)], axis=1
    )
    shape = (SLOTS, LANES)
    in_fine = lax.broadcasted_iota(jnp.int32, shape, 1) < fine

    def by_level(values):
        return jnp.where(in_fine, values[0], values[1])

    clusters = by_level((fine, coarse))
    split = by_level(splits)
    live = lax.broadcasted_iota(jnp.int32, shape, 0) < counts
    own = live & (slots < clusters)
    received = live & (slots >= clusters)
    entry = slots - clusters
    source = by_level([entry >> (cap.bit_length() - 1) for cap in caps])
    within = by_level([entry & (cap - 1) for cap in caps])
    later = by_level([cap - first for cap, first in zip(caps, splits)])
    row = lax.broadcasted_iota(jnp.int32, (SLOTS, SLOTS), 0)
    column = lax.broadcasted_iota(jnp.int32, (SLOTS, SLOTS), 1)
    upto = jnp.where(column <= row, 1.0, 0.0).astype(jnp.bfloat16)
    turns = []
    for side, (chosen, value, blank) in enumerate(
        (
            (own, slots, clusters),
            (received & (within < split), source * split + within, owners * split),
            (received & (within >= split), source * later + within - split, owners * later),
        )
    ):
        start = side * SECTION
        rank = bdot(upto, jnp.where(chosen, 1.0, 0.0).astype(jnp.bfloat16), NN).astype(jnp.int32)
        spot = jnp.where(chosen, rank - 1, -1)
        value = value - blank
        for first in range(0, SLOTS, 8):
            rows = [
                blank[:1] + jnp.sum(jnp.where(spot == place, value, 0), axis=0, keepdims=True)
                for place in range(first, first + 8)
            ]
            out_ref[start + first:start + first + 8] = jnp.concatenate(rows, axis=0)
        out_ref[start + SLOTS:start + SLOTS + CHUNK] = jnp.broadcast_to(blank[:1], (CHUNK, LANES))
        turns.append(jnp.maximum((rank[SLOTS - 1:] + CHUNK - 1) // CHUNK, 1))
    turns = jnp.concatenate(turns + [jnp.zeros((5, LANES), jnp.int32)], axis=0).astype(jnp.float32).T
    row = lax.broadcasted_iota(jnp.int32, (LANES, LANES), 0)
    column = lax.broadcasted_iota(jnp.int32, (LANES, LANES), 1)
    upto = (column <= row) & ((row < fine) == (column < fine))
    ends = bdot(jnp.where(upto, 1.0, 0.0).astype(jnp.bfloat16), turns.astype(jnp.bfloat16), NN)
    ends, turns = ends.astype(jnp.int32), turns.astype(jnp.int32)
    for side in range(3):
        for level, (low, count) in enumerate(((0, fine), (fine, coarse))):
            if side == 2 and level == 1:
                continue
            units_ref = units_refs[2 * side + level]
            end = ends[low:low + count, side:side + 1]
            took = turns[low:low + count, side:side + 1]
            lane = lax.broadcasted_iota(jnp.int32, (1, LANES), 1)
            for tile in range(units_ref.shape[0]):
                place = tile * LANES + lane
                passed = end <= place
                target = jnp.sum(jnp.where(passed, 1, 0), axis=0, keepdims=True)
                turn = place - jnp.sum(jnp.where(passed, took, 0), axis=0, keepdims=True)
                over = target >= count
                start = side * SECTION + jnp.where(over, SLOTS, turn * CHUNK)
                code = start * LANES + low + jnp.where(over, count - 1, target)
                if tile == units_ref.shape[0] - 1:
                    code = jnp.where(lane == LANES - 1, end[count - 1:], code)
                units_ref[tile:tile + 1] = code


def sent_rows(pairs, px):
    return pairs * px + -(-pairs // 2) * 16


def pack_send(send_ref, out_ref, dup_coef, dup_rows, px, pairs, base=0, entry_first=False):
    owners = out_ref.shape[0]
    points = base + len(pairs) * px
    lane = lax.broadcasted_iota(jnp.int32, (px, LANES), 1) < LANES // 2
    lane8 = lax.broadcasted_iota(jnp.int32, (8, LANES), 1) < LANES // 2

    def one_owner(owner, carry):
        rows = []
        for place, pair in enumerate(pairs):
            first, second = [
                send_ref[0, entry, owner] if entry_first else send_ref[0, owner, entry]
                for entry in (2 * pair, 2 * pair + 1)
            ]
            start = base + place * px
            out_ref[owner, start:start + px, :] = jnp.where(lane, dup_coef[first], dup_coef[second])
            rows.append(jnp.where(lane8, dup_rows[first], dup_rows[second]))
        if len(rows) % 2:
            rows.append(rows[-1])
        for place in range(0, len(rows), 2):
            start = points + place * 8
            out_ref[owner, start:start + 16, :] = jnp.concatenate(rows[place:place + 2], axis=0).astype(
                jnp.bfloat16
            )
        return carry

    lax.fori_loop(0, owners, one_owner, 0, unroll=4)


def double_fine(coef_ref, rows_ref, dup_coef, dup_rows):
    def one_tile(index, carry):
        a, b = halves(coef_ref[:, lane_tile(index)].astype(jnp.float32))
        dup_coef[2 * index] = a.astype(jnp.bfloat16)
        dup_coef[2 * index + 1] = b.astype(jnp.bfloat16)
        a, b = halves(rows_ref[:, lane_tile(index)])
        dup_rows[2 * index] = a
        dup_rows[2 * index + 1] = b
        return carry

    lax.fori_loop(0, coef_ref.shape[1] // LANES, one_tile, 0, unroll=8)


def pack_kernel(
    send_ref,
    send_fine_ref,
    coef_ref,
    transfer_ref,
    points_ref,
    points_fine_ref,
    out_ref,
    rows_ref,
    coarse_ref,
    fine_rows_ref,
    dup_coef,
    dup_rows,
    dup_fine,
    dup_fine_rows,
    *,
    early,
):
    px = coef_ref.shape[0]
    pairs = send_ref.shape[1] // 2
    rows_ref[...] = split_rows(points_ref[...])
    fine_rows_ref[...] = split_rows(points_fine_ref[...])
    double_fine(coef_ref, fine_rows_ref, dup_fine, dup_fine_rows)

    def one_tile(index, carry):
        doubled = []
        for part in range(2):
            q = 2 * index + part
            a, b = halves(transfer_ref[:, lane_tile(q)].astype(jnp.float32))
            matrix = jnp.concatenate([a, b], axis=0).astype(jnp.bfloat16)
            block = bdot(coef_ref[:, lane_tile(q)], matrix, NN).astype(jnp.bfloat16)
            dup_coef[q] = block
            doubled.append(block)
        lane = lax.broadcasted_iota(jnp.int32, (px, LANES), 1) < LANES // 2
        coarse_ref[:, lane_tile(index)] = jnp.where(lane, doubled[0], doubled[1])
        a, b = halves(rows_ref[:, lane_tile(index)])
        dup_rows[2 * index] = a
        dup_rows[2 * index + 1] = b
        return carry

    lax.fori_loop(0, coef_ref.shape[1] // (2 * LANES), one_tile, 0, unroll=8)
    pack_send(send_ref, out_ref, dup_coef, dup_rows, px, range(pairs), entry_first=True)
    pack_send(send_fine_ref, out_ref, dup_fine, dup_fine_rows, px, range(early), base=sent_rows(pairs, px))


def turned(rows):
    row = lax.broadcasted_iota(jnp.int32, (LANES, LANES), 0)
    column = lax.broadcasted_iota(jnp.int32, (LANES, LANES), 1)
    unit = jnp.where(row == column, 1.0, 0.0).astype(jnp.bfloat16)
    return bdot(unit, rows, NT).astype(jnp.bfloat16)


def put_pair(entry, coef, rows, coef_table, feature_table):
    a, b = halves(coef.astype(jnp.float32))
    coef_table[entry] = a.astype(jnp.bfloat16)
    coef_table[entry + 1] = b.astype(jnp.bfloat16)
    features = turned(jnp.concatenate([source_features(rows).astype(jnp.bfloat16)] * QUAD, axis=0))
    feature_table[entry] = features[:64]
    feature_table[entry + 1] = features[64:]


def put_nothing(entry, coef_table, feature_table):
    coef_table[entry] = jnp.zeros(coef_table.shape[1:], jnp.bfloat16)
    place = lax.broadcasted_iota(jnp.int32, (8, LANES), 0)
    nothing = source_features(jnp.where(place == 3, FAR_AWAY, 0.0)).astype(jnp.bfloat16)
    feature_table[entry] = turned(jnp.concatenate([nothing] * QUAD, axis=0))[:64]


def build_own(coef_ref, rows_ref, coef_table, feature_table):
    tiles = coef_ref.shape[1] // LANES

    def one_tile(index, carry):
        tile = lane_tile(index)
        put_pair(2 * index, coef_ref[:, tile], rows_ref[:, tile], coef_table, feature_table)
        return carry

    lax.fori_loop(0, tiles, one_tile, 0, unroll=16)
    put_nothing(2 * tiles, coef_table, feature_table)


def build_received(recv_ref, base, pairs, coef_table, feature_table):
    owners = recv_ref.shape[0]
    px = coef_table.shape[1]
    points = base + pairs * px

    def one_owner(owner, carry):
        for pair in range(0, pairs, 2):
            start = points + pair * 8
            both = recv_ref[owner, start:start + 16, :].astype(jnp.float32)
            for part in range(min(2, pairs - pair)):
                where = pair + part
                start = base + where * px
                put_pair(
                    owner * (2 * pairs) + 2 * where,
                    recv_ref[owner, start:start + px, :],
                    both[8 * part:8 * part + 8],
                    coef_table,
                    feature_table,
                )
        return carry

    lax.fori_loop(0, owners, one_owner, 0, unroll=8 if pairs <= 4 else 4)
    put_nothing(owners * pairs * 2, coef_table, feature_table)


def build_targets(rows_ref, target_table):
    def one_tile(index, carry):
        a, b = halves(target_features(rows_ref[:, lane_tile(index)]))
        target_table[2 * index] = a.astype(jnp.bfloat16)
        target_table[2 * index + 1] = b.astype(jnp.bfloat16)
        return carry

    lax.fori_loop(0, rows_ref.shape[1] // LANES, one_tile, 0, unroll=16)


def sweep(list_ref, units_ref, first, coef_table, feature_table, target_table, first_buffer, second_buffer, acc):
    px = coef_table.shape[1]
    lane = lax.broadcasted_iota(jnp.int32, (64, 16 * QUAD), 1) // 16
    lane_t = lax.broadcasted_iota(jnp.int32, (16, LANES), 1) // 64
    lane_x = lax.broadcasted_iota(jnp.int32, (px, LANES), 1) < 64
    blank = jnp.zeros((16, LANES), jnp.bfloat16)
    acc[...] = jnp.zeros_like(acc)

    def partners(unit):
        row, column = unit
        return [list_ref[row + m, column] for m in range(CHUNK)]

    def units_of(place):
        codes = [units_ref[place >> 7, (place & (LANES - 1)) + u] for u in range(UNITS)]
        return [(code >> 7, code & (LANES - 1)) for code in codes]

    def tiles(units, buffer):
        for start in range(0, UNITS, QUAD):
            quad = units[start:start + QUAD]
            weights = []
            for u in range(QUAD):
                own = jnp.where(lane_t == u % 2, target_table[quad[u][1] - first], blank)
                weights.append(jnp.concatenate([own if v == u // 2 else blank for v in range(QUAD // 2)], axis=1))
            weights = jnp.concatenate(weights, axis=0)
            ids = [partners(unit) for unit in quad]
            for part in range(0, CHUNK, 4):
                rows = []
                for m in range(part, part + 4):
                    tile = feature_table[ids[0][m]]
                    for u in range(1, QUAD):
                        tile = jnp.where(lane == u, feature_table[ids[u][m]], tile)
                    rows.append(tile)
                power = bdot(jnp.concatenate(rows, axis=0), weights, NN)
                buffer[start // QUAD, part * 64:(part + 4) * 64] = jnp.exp(power).astype(jnp.bfloat16)

    def products(units, buffer):
        for start in range(0, UNITS, QUAD):
            quad = units[start:start + QUAD]
            coefs = []
            for unit in quad:
                ids = partners(unit)
                coefs.append(
                    jnp.concatenate(
                        [
                            jnp.where(lane_x, coef_table[ids[m]], coef_table[ids[m + 1]])
                            for m in range(0, CHUNK, 2)
                        ],
                        axis=1,
                    )
                )
            product = bdot(jnp.concatenate(coefs, axis=0), buffer[start // QUAD], NN)
            for u in range(QUAD):
                side = (u // 2) * LANES
                acc[u % 2, quad[u][1] - first] += product[u * px:(u + 1) * px, side:side + LANES]

    def two_sets(index, carry):
        here = index * (2 * UNITS)
        second = units_of(here + UNITS)
        tiles(second, second_buffer)
        products(units_of(here), first_buffer)
        tiles(units_of(here + 2 * UNITS), first_buffer)
        products(second, second_buffer)
        return carry

    total = units_ref[units_ref.shape[0] - 1, LANES - 1]
    sets = (total + UNITS - 1) // UNITS
    bodies = (sets - 1) // 2
    last = bodies * (2 * UNITS)
    tiles(units_of(0), first_buffer)
    lax.fori_loop(0, bodies, two_sets, 0)

    @pl.when(sets == 2 * bodies + 2)
    def _():
        second = units_of(last + UNITS)
        tiles(second, second_buffer)
        products(units_of(last), first_buffer)
        products(second, second_buffer)

    @pl.when(sets == 2 * bodies + 1)
    def _():
        products(units_of(last), first_buffer)


def summed(acc, target):
    low = lax.broadcasted_iota(jnp.int32, acc.shape[2:], 1) < 64
    here = jnp.where(low, acc[0, target], acc[1, target])
    return here + pltpu.roll(here, 64, 1)


def put_sums(acc, clusters, out_ref, before_ref=None):
    low = lax.broadcasted_iota(jnp.int32, acc.shape[2:], 1) < 64

    def one_tile(index, carry):
        tile = lane_tile(index)
        sums = jnp.where(low, summed(acc, 2 * index), summed(acc, 2 * index + 1))
        out_ref[:, tile] = sums if before_ref is None else before_ref[:, tile] + sums
        return carry

    lax.fori_loop(0, clusters // 2, one_tile, 0, unroll=8)


def prepare_kernel(
    send_ref,
    fine_slots_ref,
    fine_counts_ref,
    coarse_slots_ref,
    coarse_counts_ref,
    coef_ref,
    fine_rows_ref,
    coarse_coef_ref,
    coarse_rows_ref,
    send_out_ref,
    list_out_ref,
    early_units_ref,
    coarse_units_ref,
    fine_units_ref,
    fine_out_ref,
    coarse_out_ref,
    dup_coef,
    dup_rows,
    fine_own_ref,
    coarse_own_ref,
    list_ref,
    fine_own_units,
    coarse_own_units,
    list_sem,
    fine_sem,
    coarse_sem,
    *scratch,
    owners,
    caps,
    splits,
):
    list_slots(
        fine_slots_ref,
        fine_counts_ref,
        coarse_slots_ref,
        coarse_counts_ref,
        list_out_ref,
        fine_own_ref,
        coarse_own_ref,
        early_units_ref,
        coarse_units_ref,
        fine_units_ref,
        owners=owners,
        caps=caps,
        splits=splits,
    )
    copies = [
        pltpu.make_async_copy(list_out_ref, list_ref, list_sem),
        pltpu.make_async_copy(fine_own_ref, fine_own_units, fine_sem),
        pltpu.make_async_copy(coarse_own_ref, coarse_own_units, coarse_sem),
    ]
    for copy in copies:
        copy.start()
    double_fine(coef_ref, fine_rows_ref, dup_coef, dup_rows)
    pack_send(
        send_ref, send_out_ref, dup_coef, dup_rows, coef_ref.shape[0], range(splits[0] // 2, caps[0] // 2)
    )
    for copy in copies:
        copy.wait()
    first = 0
    for units_ref, source_ref, rows_ref, out_ref in (
        (fine_own_units, coef_ref, fine_rows_ref, fine_out_ref),
        (coarse_own_units, coarse_coef_ref, coarse_rows_ref, coarse_out_ref),
    ):
        clusters = rows_ref.shape[1] // 64
        build_own(source_ref, rows_ref, *scratch[:2])
        build_targets(rows_ref, scratch[2])
        sweep(list_ref, units_ref, first, *scratch)
        put_sums(scratch[-1], clusters, out_ref)
        first += clusters


def first_kernel(
    list_ref,
    early_units_ref,
    units_ref,
    recv_ref,
    fine_rows_ref,
    rows_ref,
    fine_own_ref,
    own_ref,
    fine_out_ref,
    out_ref,
    *scratch,
    pairs,
    early,
):
    px = own_ref.shape[0]
    fine = fine_rows_ref.shape[1] // 64
    build_received(recv_ref, 0, pairs, *scratch[:2])
    build_targets(rows_ref, scratch[2])
    sweep(list_ref, units_ref, fine, *scratch)
    put_sums(scratch[-1], rows_ref.shape[1] // 64, out_ref, own_ref)
    build_received(recv_ref, sent_rows(pairs, px), early, *scratch[:2])
    build_targets(fine_rows_ref, scratch[2])
    sweep(list_ref, early_units_ref, 0, *scratch)
    put_sums(scratch[-1], fine, fine_out_ref, fine_own_ref)


def fine_kernel(groups, pairs, *refs):
    late = 3 + groups
    list_ref, units_ref, recv_ref, rows_ref = refs[:4]
    out_ref, terms_ref = refs[4 + late:6 + late]
    late_refs = refs[6 + late:6 + 2 * late]
    late_sems = refs[6 + 2 * late:6 + 3 * late]
    gram_ref, split_ref, *scratch = refs[6 + 3 * late:]
    copies = [pltpu.make_async_copy(*pair) for pair in zip(refs[4:4 + late], late_refs, late_sems)]
    for copy in copies:
        copy.start()
    own_ref, coarse_ref, transfer_ref, *probes_refs = late_refs
    px = split_ref.shape[0] // 2
    probes = probes_refs[0].shape[0]
    acc = scratch[-1]
    build_received(recv_ref, 0, pairs, *scratch[:2])
    build_targets(rows_ref, scratch[2])
    sweep(list_ref, units_ref, 0, *scratch)
    for copy in copies:
        copy.wait()
    low_x = lax.broadcasted_iota(jnp.int32, (px, LANES), 1) < 64

    def one_parent(q, carry):
        far = halves(coarse_ref[:, lane_tile(q >> 1)])
        twice = jnp.where((q & 1) == 0, far[0], far[1]).astype(jnp.bfloat16)
        matrix = transfer_ref[:, lane_tile(q)].astype(jnp.float32)
        low = lax.broadcasted_iota(jnp.int32, matrix.shape, 1) < 64
        matrix = jnp.concatenate(
            [jnp.where(low, matrix, 0.0), jnp.where(low, 0.0, matrix)], axis=0
        ).astype(jnp.bfloat16)
        sums = jnp.where(low_x, summed(acc, 2 * q), summed(acc, 2 * q + 1))
        total = own_ref[:, lane_tile(q)] + sums + bdot(twice, matrix, NT)
        out_ref[:, lane_tile(q)] = total
        high = total.astype(jnp.bfloat16)
        split_ref[:px, lane_tile(q)] = high
        split_ref[px:, lane_tile(q)] = (total - high.astype(jnp.float32)).astype(jnp.bfloat16)
        return carry

    lax.fori_loop(0, coarse_ref.shape[1] // 64, one_parent, 0, unroll=8)
    for block, probes_ref in enumerate(probes_refs):
        term = bdot(probes_ref[...], split_ref[...], NT)
        gram_ref[block] = term[:, :px] + term[:, px:]
    place = lax.axis_index("probe")
    for b in range(groups):
        block = gram_ref[lax.rem(place - b + groups, groups)]
        packed = jnp.concatenate([block[i:i + 8, :probes] for i in range(0, probes, 8)], axis=1)

        def one_owner(owner, carry):
            terms_ref[owner * groups + b] = packed
            return carry

        lax.fori_loop(0, terms_ref.shape[0] // groups, one_owner, 0)


def gram_kernel(terms_ref, out_ref, *, groups, scale):
    probes = out_ref.shape[0]
    columns = []
    for b in range(groups):
        total = terms_ref[b]
        for owner in range(1, terms_ref.shape[0] // groups):
            total = total + terms_ref[owner * groups + b]
        columns.append(
            jnp.concatenate([total[:, i * probes:(i + 1) * probes] for i in range(probes // 8)], axis=0)
        )
    out_ref[...] = jnp.concatenate(columns, axis=1) * scale


def sweep_scratch(total, clusters, px):
    return [
        pltpu.VMEM((total + 1, px, LANES), jnp.bfloat16),
        pltpu.VMEM((total + 1, 64, 16 * QUAD), jnp.bfloat16),
        pltpu.VMEM((clusters, 16, LANES), jnp.bfloat16),
        pltpu.VMEM((UNITS // QUAD, CHUNK * 64, QUAD * 64), jnp.bfloat16),
        pltpu.VMEM((UNITS // QUAD, CHUNK * 64, QUAD * 64), jnp.bfloat16),
        pltpu.VMEM((2, clusters, px, LANES), jnp.float32),
    ]


def shards(
    coef_fine,
    points_fine,
    points_coarse,
    transfer,
    send_fine,
    slots_fine,
    counts_fine,
    send_coarse,
    slots_coarse,
    counts_coarse,
):
    probes = coef_fine.shape[0]
    fine_count = counts_fine.shape[0]
    coarse_count = counts_coarse.shape[0]
    owners = lax.axis_size("leaf")
    groups = lax.axis_size("probe")
    px = -(-probes // 16) * 16
    coef = coef_fine if px == probes else jnp.pad(coef_fine, ((0, px - probes), (0, 0)))
    cap_fine = send_fine.shape[2]
    cap_coarse = send_coarse.shape[2]

    whole_vmem = pltpu.CompilerParams(vmem_limit_bytes=VMEM)
    smem = pl.BlockSpec(memory_space=pltpu.SMEM)
    vmem = pl.BlockSpec(memory_space=pltpu.VMEM)
    bf16, f32 = jnp.bfloat16, jnp.float32

    coarse_pairs = cap_coarse // 2
    early_pairs = EARLY * (cap_fine // 2) // 8
    late_pairs = cap_fine // 2 - early_pairs
    early_total = owners * 2 * early_pairs
    late_total = owners * 2 * late_pairs
    coarse_total = owners * cap_coarse
    unit_rows = [-(-(count * (SLOTS // CHUNK) + 2 * UNITS + 1) // LANES) for count in (fine_count, coarse_count)]
    list_shape = (3 * SECTION, LANES)
    i32 = jnp.int32
    fine_units_shape, coarse_units_shape = [(rows, LANES) for rows in unit_rows]
    fine_columns, coarse_columns = points_fine.shape[1], points_coarse.shape[1]
    heavy = pl.CostEstimate(flops=10**10, bytes_accessed=10**7, transcendentals=10**7)

    first_send, coarse_rows, coarse_coef, fine_rows = pl.pallas_call(
        functools.partial(pack_kernel, early=early_pairs),
        out_shape=(
            jax.ShapeDtypeStruct(
                (owners, sent_rows(coarse_pairs, px) + sent_rows(early_pairs, px), LANES), bf16
            ),
            jax.ShapeDtypeStruct((8, coarse_columns), f32),
            jax.ShapeDtypeStruct((px, coarse_columns), bf16),
            jax.ShapeDtypeStruct((8, fine_columns), f32),
        ),
        in_specs=[smem] * 2 + [vmem] * 4,
        out_specs=[vmem] * 4,
        scratch_shapes=[
            pltpu.VMEM((coarse_count, px, LANES), bf16),
            pltpu.VMEM((coarse_count, 8, LANES), f32),
            pltpu.VMEM((fine_count, px, LANES), bf16),
            pltpu.VMEM((fine_count, 8, LANES), f32),
        ],
        compiler_params=whole_vmem,
        name="pack_first",
    )(jnp.swapaxes(send_coarse, 1, 2), send_fine, coef, transfer, points_coarse, points_fine)
    first_recv = lax.all_to_all(first_send, "leaf", split_axis=0, concat_axis=0, tiled=True)

    turned = [coef_fine]
    for step in range(1, groups):
        turned.append(lax.ppermute(coef_fine, "probe", [(i, (i + step) % groups) for i in range(groups)]))

    fine_send, slot_list, early_units, coarse_units, fine_units, fine_own_sums, coarse_own_sums = pl.pallas_call(
        functools.partial(
            prepare_kernel,
            owners=owners,
            caps=(cap_fine, cap_coarse),
            splits=(2 * early_pairs, cap_coarse),
        ),
        out_shape=(
            jax.ShapeDtypeStruct((owners, sent_rows(late_pairs, px), LANES), bf16),
            jax.ShapeDtypeStruct(list_shape, i32),
            jax.ShapeDtypeStruct(fine_units_shape, i32),
            jax.ShapeDtypeStruct(coarse_units_shape, i32),
            jax.ShapeDtypeStruct(fine_units_shape, i32),
            jax.ShapeDtypeStruct((px, fine_columns), f32),
            jax.ShapeDtypeStruct((px, coarse_columns), f32),
        ),
        in_specs=[smem] + [vmem] * 8,
        out_specs=[vmem] * 7,
        scratch_shapes=[
            pltpu.VMEM((fine_count, px, LANES), bf16),
            pltpu.VMEM((fine_count, 8, LANES), f32),
            pltpu.VMEM(fine_units_shape, i32),
            pltpu.VMEM(coarse_units_shape, i32),
            pltpu.SMEM(list_shape, i32),
            pltpu.SMEM(fine_units_shape, i32),
            pltpu.SMEM(coarse_units_shape, i32),
            pltpu.SemaphoreType.DMA,
            pltpu.SemaphoreType.DMA,
            pltpu.SemaphoreType.DMA,
        ]
        + sweep_scratch(fine_count, fine_count, px),
        compiler_params=whole_vmem,
        cost_estimate=heavy,
        name="prepare",
    )(
        send_fine,
        slots_fine,
        counts_fine.reshape(1, -1),
        slots_coarse,
        counts_coarse.reshape(1, -1),
        coef,
        fine_rows,
        coarse_coef,
        coarse_rows,
    )
    fine_recv = lax.all_to_all(fine_send, "leaf", split_axis=0, concat_axis=0, tiled=True)

    fine_sums, coarse_far = pl.pallas_call(
        functools.partial(first_kernel, pairs=coarse_pairs, early=early_pairs),
        out_shape=(
            jax.ShapeDtypeStruct((px, fine_columns), f32),
            jax.ShapeDtypeStruct((px, coarse_columns), f32),
        ),
        in_specs=[smem] * 3 + [vmem] * 5,
        out_specs=[vmem, vmem],
        scratch_shapes=sweep_scratch(max(early_total, coarse_total), fine_count, px),
        compiler_params=whole_vmem,
        cost_estimate=heavy,
        name="first_sweep",
    )(slot_list, early_units, coarse_units, first_recv, fine_rows, coarse_rows, fine_own_sums, coarse_own_sums)

    late = (fine_sums, coarse_far, transfer, *turned)
    term_shape = (owners * groups, 8, probes * probes // 8)
    far, terms = pl.pallas_call(
        functools.partial(fine_kernel, groups, late_pairs),
        out_shape=(
            jax.ShapeDtypeStruct((px, points_fine.shape[1]), f32),
            jax.ShapeDtypeStruct(term_shape, f32),
        ),
        in_specs=[smem] * 2 + [vmem] * 2 + [pl.BlockSpec(memory_space=pl.ANY)] * (3 + groups),
        out_specs=[vmem, vmem],
        scratch_shapes=[pltpu.VMEM(operand.shape, operand.dtype) for operand in late]
        + [pltpu.SemaphoreType.DMA] * len(late)
        + [
            pltpu.VMEM((groups, probes, px), f32),
            pltpu.VMEM((2 * px, points_fine.shape[1]), bf16),
        ]
        + sweep_scratch(late_total, fine_count, px),
        compiler_params=whole_vmem,
        name="fine_sweep",
    )(slot_list, fine_units, fine_recv, fine_rows, *late)

    terms = lax.all_to_all(terms, ("leaf", "probe"), split_axis=0, concat_axis=0, tiled=True)
    probe_gram = pl.pallas_call(
        functools.partial(
            gram_kernel, groups=groups, scale=1.0 / math.sqrt(owners * fine_count * 64)
        ),
        out_shape=jax.ShapeDtypeStruct((probes, groups * probes), f32),
        in_specs=[vmem],
        out_specs=vmem,
        name="gram_sum",
    )(terms)
    return (far[:probes], probe_gram)


def solution(mesh):
    return jax.shard_map(
        shards,
        mesh=mesh,
        in_specs=(
            P("probe", "leaf"),
            P(None, "leaf"),
            P(None, "leaf"),
            P(None, "leaf"),
            P("leaf", None, None),
            P("leaf", None),
            P("leaf"),
            P("leaf", None, None),
            P("leaf", None),
            P("leaf"),
        ),
        out_specs=(P("probe", "leaf"), P("probe", None)),
        check_vma=False,
    )
```

```python
import functools
import functools
import math

import jax
import jax.numpy as jnp
from jax import lax
from jax.experimental import pallas as pl
from jax.experimental.pallas import tpu as pltpu
from jax.sharding import PartitionSpec as P

KERNEL_RATE = 1.5
POINT_SCALE = math.sqrt(2.0 * KERNEL_RATE * math.log2(math.e))
LANES = 128
UNITS = 16
QUAD = 4
CHUNK = 8
FAR_AWAY = -30000.0
SLOTS = 64
SECTION = SLOTS + CHUNK
EARLY = 2
VMEM = 56 * 1024 * 1024

NT = (((1,), (1,)), ((), ()))
NN = (((1,), (0,)), ((), ()))


def bdot(a, b, dims):
    return lax.dot_general(a, b, dims, preferred_element_type=jnp.float32)


def split_rows(points):
    v = points * POINT_SCALE
    norm = -0.5 * (v[0:1] * v[0:1] + v[1:2] * v[1:2] + v[2:3] * v[2:3])
    full = jnp.concatenate([v, norm], axis=0)
    high = full.astype(jnp.bfloat16).astype(jnp.float32)
    rest = (full - high).astype(jnp.bfloat16).astype(jnp.float32)
    return jnp.concatenate([high, rest], axis=0)


def source_features(rows):
    place = lax.broadcasted_iota(jnp.int32, rows.shape, 0)
    one = jnp.where((place == 3) | (place == 7), 1.0, 0.0)
    return jnp.concatenate([rows, jnp.where(place < 3, rows, one)], axis=0)


def target_features(rows):
    place = lax.broadcasted_iota(jnp.int32, rows.shape, 0)
    turned = jnp.concatenate([rows[4:8], rows[0:4]], axis=0)
    one = jnp.where((place == 3) | (place == 7), 1.0, jnp.where(place < 3, rows, turned))
    return jnp.concatenate([one, turned], axis=0)


def halves(tile):
    lane = lax.broadcasted_iota(jnp.int32, tile.shape, 1)
    turned = pltpu.roll(tile, LANES // 2, 1)
    low = lane < LANES // 2
    return jnp.where(low, tile, turned), jnp.where(low, turned, tile)


def lane_tile(index):
    return pl.ds(pl.multiple_of(index * LANES, LANES), LANES)


def list_slots(
    fine_slots_ref, fine_counts_ref, coarse_slots_ref, coarse_counts_ref, out_ref, *units_refs, owners, caps, splits
):
    fine, coarse = fine_slots_ref.shape[0], coarse_slots_ref.shape[0]
    spare = LANES - fine - coarse
    slots = jnp.concatenate(
        [fine_slots_ref[...], coarse_slots_ref[...], jnp.zeros((spare, SLOTS), jnp.int32)], axis=0
    )
    slots = slots.astype(jnp.float32).T.astype(jnp.int32)
    counts = jnp.concatenate(
        [fine_counts_ref[...], coarse_counts_ref[...], jnp.zeros((1, spare), jnp.int32)], axis=1
    )
    shape = (SLOTS, LANES)
    in_fine = lax.broadcasted_iota(jnp.int32, shape, 1) < fine

    def by_level(values):
        return jnp.where(in_fine, values[0], values[1])

    clusters = by_level((fine, coarse))
    split = by_level(splits)
    live = lax.broadcasted_iota(jnp.int32, shape, 0) < counts
    own = live & (slots < clusters)
    received = live & (slots >= clusters)
    entry = slots - clusters
    source = by_level([entry >> (cap.bit_length() - 1) for cap in caps])
    within = by_level([entry & (cap - 1) for cap in caps])
    later = by_level([cap - first for cap, first in zip(caps, splits)])
    row = lax.broadcasted_iota(jnp.int32, (SLOTS, SLOTS), 0)
    column = lax.broadcasted_iota(jnp.int32, (SLOTS, SLOTS), 1)
    upto = jnp.where(column <= row, 1.0, 0.0).astype(jnp.bfloat16)
    turns = []
    for side, (chosen, value, blank) in enumerate(
        (
            (own, slots, clusters),
            (received & (within < split), source * split + within, owners * split),
            (received & (within >= split), source * later + within - split, owners * later),
        )
    ):
        start = side * SECTION
        rank = bdot(upto, jnp.where(chosen, 1.0, 0.0).astype(jnp.bfloat16), NN).astype(jnp.int32)
        spot = jnp.where(chosen, rank - 1, -1)
        value = value - blank
        for first in range(0, SLOTS, 8):
            rows = [
                blank[:1] + jnp.sum(jnp.where(spot == place, value, 0), axis=0, keepdims=True)
                for place in range(first, first + 8)
            ]
            out_ref[start + first:start + first + 8] = jnp.concatenate(rows, axis=0)
        out_ref[start + SLOTS:start + SLOTS + CHUNK] = jnp.broadcast_to(blank[:1], (CHUNK, LANES))
        turns.append(jnp.maximum((rank[SLOTS - 1:] + CHUNK - 1) // CHUNK, 1))
    turns = jnp.concatenate(turns + [jnp.zeros((5, LANES), jnp.int32)], axis=0).astype(jnp.float32).T
    row = lax.broadcasted_iota(jnp.int32, (LANES, LANES), 0)
    column = lax.broadcasted_iota(jnp.int32, (LANES, LANES), 1)
    upto = (column <= row) & ((row < fine) == (column < fine))
    ends = bdot(jnp.where(upto, 1.0, 0.0).astype(jnp.bfloat16), turns.astype(jnp.bfloat16), NN)
    ends, turns = ends.astype(jnp.int32), turns.astype(jnp.int32)
    for side in range(3):
        for level, (low, count) in enumerate(((0, fine), (fine, coarse))):
            if side == 2 and level == 1:
                continue
            units_ref = units_refs[2 * side + level]
            end = ends[low:low + count, side:side + 1]
            took = turns[low:low + count, side:side + 1]
            lane = lax.broadcasted_iota(jnp.int32, (1, LANES), 1)
            for tile in range(units_ref.shape[0]):
                place = tile * LANES + lane
                passed = end <= place
                target = jnp.sum(jnp.where(passed, 1, 0), axis=0, keepdims=True)
                turn = place - jnp.sum(jnp.where(passed, took, 0), axis=0, keepdims=True)
                over = target >= count
                start = side * SECTION + jnp.where(over, SLOTS, turn * CHUNK)
                code = start * LANES + low + jnp.where(over, count - 1, target)
                if tile == units_ref.shape[0] - 1:
                    code = jnp.where(lane == LANES - 1, end[count - 1:], code)
                units_ref[tile:tile + 1] = code


def sent_rows(pairs, px):
    return pairs * px + -(-pairs // 2) * 16


def pack_send(send_ref, out_ref, dup_coef, dup_rows, px, pairs, base=0, entry_first=False):
    owners = out_ref.shape[0]
    points = base + len(pairs) * px
    lane = lax.broadcasted_iota(jnp.int32, (px, LANES), 1) < LANES // 2
    lane8 = lax.broadcasted_iota(jnp.int32, (8, LANES), 1) < LANES // 2

    def one_owner(owner, carry):
        rows = []
        for place, pair in enumerate(pairs):
            first, second = [
                send_ref[0, entry, owner] if entry_first else send_ref[0, owner, entry]
                for entry in (2 * pair, 2 * pair + 1)
            ]
            start = base + place * px
            out_ref[owner, start:start + px, :] = jnp.where(lane, dup_coef[first], dup_coef[second])
            rows.append(jnp.where(lane8, dup_rows[first], dup_rows[second]))
        if len(rows) % 2:
            rows.append(rows[-1])
        for place in range(0, len(rows), 2):
            start = points + place * 8
            out_ref[owner, start:start + 16, :] = jnp.concatenate(rows[place:place + 2], axis=0).astype(
                jnp.bfloat16
            )
        return carry

    lax.fori_loop(0, owners, one_owner, 0, unroll=4)


def double_fine(coef_ref, rows_ref, dup_coef, dup_rows):
    def one_tile(index, carry):
        a, b = halves(coef_ref[:, lane_tile(index)].astype(jnp.float32))
        dup_coef[2 * index] = a.astype(jnp.bfloat16)
        dup_coef[2 * index + 1] = b.astype(jnp.bfloat16)
        a, b = halves(rows_ref[:, lane_tile(index)])
        dup_rows[2 * index] = a
        dup_rows[2 * index + 1] = b
        return carry

    lax.fori_loop(0, coef_ref.shape[1] // LANES, one_tile, 0, unroll=8)


def pack_kernel(
    send_ref,
    send_fine_ref,
    coef_ref,
    transfer_ref,
    points_ref,
    points_fine_ref,
    out_ref,
    rows_ref,
    coarse_ref,
    fine_rows_ref,
    dup_coef,
    dup_rows,
    dup_fine,
    dup_fine_rows,
    *,
    early,
):
    px = coef_ref.shape[0]
    pairs = send_ref.shape[1] // 2
    rows_ref[...] = split_rows(points_ref[...])
    fine_rows_ref[...] = split_rows(points_fine_ref[...])
    double_fine(coef_ref, fine_rows_ref, dup_fine, dup_fine_rows)

    def one_tile(index, carry):
        doubled = []
        for part in range(2):
            q = 2 * index + part
            a, b = halves(transfer_ref[:, lane_tile(q)].astype(jnp.float32))
            matrix = jnp.concatenate([a, b], axis=0).astype(jnp.bfloat16)
            block = bdot(coef_ref[:, lane_tile(q)], matrix, NN).astype(jnp.bfloat16)
            dup_coef[q] = block
            doubled.append(block)
        lane = lax.broadcasted_iota(jnp.int32, (px, LANES), 1) < LANES // 2
        coarse_ref[:, lane_tile(index)] = jnp.where(lane, doubled[0], doubled[1])
        a, b = halves(rows_ref[:, lane_tile(index)])
        dup_rows[2 * index] = a
        dup_rows[2 * index + 1] = b
        return carry

    lax.fori_loop(0, coef_ref.shape[1] // (2 * LANES), one_tile, 0, unroll=8)
    pack_send(send_ref, out_ref, dup_coef, dup_rows, px, range(pairs), entry_first=True)
    pack_send(send_fine_ref, out_ref, dup_fine, dup_fine_rows, px, range(early), base=sent_rows(pairs, px))


def turned(rows):
    row = lax.broadcasted_iota(jnp.int32, (LANES, LANES), 0)
    column = lax.broadcasted_iota(jnp.int32, (LANES, LANES), 1)
    unit = jnp.where(row == column, 1.0, 0.0).astype(jnp.bfloat16)
    return bdot(unit, rows, NT).astype(jnp.bfloat16)


def put_pair(entry, coef, rows, coef_table, feature_table):
    a, b = halves(coef.astype(jnp.float32))
    coef_table[entry] = a.astype(jnp.bfloat16)
    coef_table[entry + 1] = b.astype(jnp.bfloat16)
    features = turned(jnp.concatenate([source_features(rows).astype(jnp.bfloat16)] * QUAD, axis=0))
    feature_table[entry] = features[:64]
    feature_table[entry + 1] = features[64:]


def put_nothing(entry, coef_table, feature_table):
    coef_table[entry] = jnp.zeros(coef_table.shape[1:], jnp.bfloat16)
    place = lax.broadcasted_iota(jnp.int32, (8, LANES), 0)
    nothing = source_features(jnp.where(place == 3, FAR_AWAY, 0.0)).astype(jnp.bfloat16)
    feature_table[entry] = turned(jnp.concatenate([nothing] * QUAD, axis=0))[:64]


def build_own(coef_ref, rows_ref, coef_table, feature_table):
    tiles = coef_ref.shape[1] // LANES

    def one_tile(index, carry):
        tile = lane_tile(index)
        put_pair(2 * index, coef_ref[:, tile], rows_ref[:, tile], coef_table, feature_table)
        return carry

    lax.fori_loop(0, tiles, one_tile, 0, unroll=16)
    put_nothing(2 * tiles, coef_table, feature_table)


def build_received(recv_ref, base, pairs, coef_table, feature_table):
    owners = recv_ref.shape[0]
    px = coef_table.shape[1]
    points = base + pairs * px

    def one_owner(owner, carry):
        for pair in range(0, pairs, 2):
            start = points + pair * 8
            both = recv_ref[owner, start:start + 16, :].astype(jnp.float32)
            for part in range(min(2, pairs - pair)):
                where = pair + part
                start = base + where * px
                put_pair(
                    owner * (2 * pairs) + 2 * where,
                    recv_ref[owner, start:start + px, :],
                    both[8 * part:8 * part + 8],
                    coef_table,
                    feature_table,
                )
        return carry

    lax.fori_loop(0, owners, one_owner, 0, unroll=8 if pairs <= 4 else 4)
    put_nothing(owners * pairs * 2, coef_table, feature_table)


def build_targets(rows_ref, target_table):
    def one_tile(index, carry):
        a, b = halves(target_features(rows_ref[:, lane_tile(index)]))
        target_table[2 * index] = a.astype(jnp.bfloat16)
        target_table[2 * index + 1] = b.astype(jnp.bfloat16)
        return carry

    lax.fori_loop(0, rows_ref.shape[1] // LANES, one_tile, 0, unroll=16)


def sweep(list_ref, units_ref, first, coef_table, feature_table, target_table, first_buffer, second_buffer, acc):
    px = coef_table.shape[1]
    lane = lax.broadcasted_iota(jnp.int32, (64, 16 * QUAD), 1) // 16
    lane_t = lax.broadcasted_iota(jnp.int32, (16, LANES), 1) // 64
    lane_x = lax.broadcasted_iota(jnp.int32, (px, LANES), 1) < 64
    blank = jnp.zeros((16, LANES), jnp.bfloat16)
    acc[...] = jnp.zeros_like(acc)

    def partners(unit):
        row, column = unit
        return [list_ref[row + m, column] for m in range(CHUNK)]

    def units_of(place):
        codes = [units_ref[place >> 7, (place & (LANES - 1)) + u] for u in range(UNITS)]
        return [(code >> 7, code & (LANES - 1)) for code in codes]

    def tiles(units, buffer):
        for start in range(0, UNITS, QUAD):
            quad = units[start:start + QUAD]
            weights = []
            for u in range(QUAD):
                own = jnp.where(lane_t == u % 2, target_table[quad[u][1] - first], blank)
                weights.append(jnp.concatenate([own if v == u // 2 else blank for v in range(QUAD // 2)], axis=1))
            weights = jnp.concatenate(weights, axis=0)
            ids = [partners(unit) for unit in quad]
            for part in range(0, CHUNK, 4):
                rows = []
                for m in range(part, part + 4):
                    tile = feature_table[ids[0][m]]
                    for u in range(1, QUAD):
                        tile = jnp.where(lane == u, feature_table[ids[u][m]], tile)
                    rows.append(tile)
                power = bdot(jnp.concatenate(rows, axis=0), weights, NN)
                buffer[start // QUAD, part * 64:(part + 4) * 64] = jnp.exp2(power).astype(jnp.bfloat16)

    def products(units, buffer):
        for start in range(0, UNITS, QUAD):
            quad = units[start:start + QUAD]
            coefs = []
            for unit in quad:
                ids = partners(unit)
                coefs.append(
                    jnp.concatenate(
                        [
                            jnp.where(lane_x, coef_table[ids[m]], coef_table[ids[m + 1]])
                            for m in range(0, CHUNK, 2)
                        ],
                        axis=1,
                    )
                )
            product = bdot(jnp.concatenate(coefs, axis=0), buffer[start // QUAD], NN)
            for u in range(QUAD):
                side = (u // 2) * LANES
                acc[u % 2, quad[u][1] - first] += product[u * px:(u + 1) * px, side:side + LANES]

    def two_sets(index, carry):
        here = index * (2 * UNITS)
        second = units_of(here + UNITS)
        tiles(second, second_buffer)
        products(units_of(here), first_buffer)
        tiles(units_of(here + 2 * UNITS), first_buffer)
        products(second, second_buffer)
        return carry

    total = units_ref[units_ref.shape[0] - 1, LANES - 1]
    sets = (total + UNITS - 1) // UNITS
    bodies = (sets - 1) // 2
    last = bodies * (2 * UNITS)
    tiles(units_of(0), first_buffer)
    lax.fori_loop(0, bodies, two_sets, 0)

    @pl.when(sets == 2 * bodies + 2)
    def _():
        second = units_of(last + UNITS)
        tiles(second, second_buffer)
        products(units_of(last), first_buffer)
        products(second, second_buffer)

    @pl.when(sets == 2 * bodies + 1)
    def _():
        products(units_of(last), first_buffer)


def summed(acc, target):
    low = lax.broadcasted_iota(jnp.int32, acc.shape[2:], 1) < 64
    here = jnp.where(low, acc[0, target], acc[1, target])
    return here + pltpu.roll(here, 64, 1)


def put_sums(acc, clusters, out_ref, before_ref=None):
    low = lax.broadcasted_iota(jnp.int32, acc.shape[2:], 1) < 64

    def one_tile(index, carry):
        tile = lane_tile(index)
        sums = jnp.where(low, summed(acc, 2 * index), summed(acc, 2 * index + 1))
        out_ref[:, tile] = sums if before_ref is None else before_ref[:, tile] + sums
        return carry

    lax.fori_loop(0, clusters // 2, one_tile, 0, unroll=8)


def prepare_kernel(
    send_ref,
    fine_slots_ref,
    fine_counts_ref,
    coarse_slots_ref,
    coarse_counts_ref,
    coef_ref,
    fine_rows_ref,
    coarse_coef_ref,
    coarse_rows_ref,
    send_out_ref,
    list_out_ref,
    early_units_ref,
    coarse_units_ref,
    fine_units_ref,
    fine_out_ref,
    coarse_out_ref,
    dup_coef,
    dup_rows,
    fine_own_ref,
    coarse_own_ref,
    list_ref,
    fine_own_units,
    coarse_own_units,
    list_sem,
    fine_sem,
    coarse_sem,
    *scratch,
    owners,
    caps,
    splits,
):
    list_slots(
        fine_slots_ref,
        fine_counts_ref,
        coarse_slots_ref,
        coarse_counts_ref,
        list_out_ref,
        fine_own_ref,
        coarse_own_ref,
        early_units_ref,
        coarse_units_ref,
        fine_units_ref,
        owners=owners,
        caps=caps,
        splits=splits,
    )
    copies = [
        pltpu.make_async_copy(list_out_ref, list_ref, list_sem),
        pltpu.make_async_copy(fine_own_ref, fine_own_units, fine_sem),
        pltpu.make_async_copy(coarse_own_ref, coarse_own_units, coarse_sem),
    ]
    for copy in copies:
        copy.start()
    double_fine(coef_ref, fine_rows_ref, dup_coef, dup_rows)
    pack_send(
        send_ref, send_out_ref, dup_coef, dup_rows, coef_ref.shape[0], range(splits[0] // 2, caps[0] // 2)
    )
    for copy in copies:
        copy.wait()
    first = 0
    for units_ref, source_ref, rows_ref, out_ref in (
        (fine_own_units, coef_ref, fine_rows_ref, fine_out_ref),
        (coarse_own_units, coarse_coef_ref, coarse_rows_ref, coarse_out_ref),
    ):
        clusters = rows_ref.shape[1] // 64
        build_own(source_ref, rows_ref, *scratch[:2])
        build_targets(rows_ref, scratch[2])
        sweep(list_ref, units_ref, first, *scratch)
        put_sums(scratch[-1], clusters, out_ref)
        first += clusters


def first_kernel(
    list_ref,
    early_units_ref,
    units_ref,
    recv_ref,
    fine_rows_ref,
    rows_ref,
    fine_own_ref,
    own_ref,
    fine_out_ref,
    out_ref,
    *scratch,
    pairs,
    early,
):
    px = own_ref.shape[0]
    fine = fine_rows_ref.shape[1] // 64
    build_received(recv_ref, 0, pairs, *scratch[:2])
    build_targets(rows_ref, scratch[2])
    sweep(list_ref, units_ref, fine, *scratch)
    put_sums(scratch[-1], rows_ref.shape[1] // 64, out_ref, own_ref)
    build_received(recv_ref, sent_rows(pairs, px), early, *scratch[:2])
    build_targets(fine_rows_ref, scratch[2])
    sweep(list_ref, early_units_ref, 0, *scratch)
    put_sums(scratch[-1], fine, fine_out_ref, fine_own_ref)


def fine_kernel(groups, pairs, *refs):
    late = 3 + groups
    list_ref, units_ref, recv_ref, rows_ref = refs[:4]
    out_ref, terms_ref = refs[4 + late:6 + late]
    late_refs = refs[6 + late:6 + 2 * late]
    late_sems = refs[6 + 2 * late:6 + 3 * late]
    gram_ref, split_ref, *scratch = refs[6 + 3 * late:]
    copies = [pltpu.make_async_copy(*pair) for pair in zip(refs[4:4 + late], late_refs, late_sems)]
    for copy in copies:
        copy.start()
    own_ref, coarse_ref, transfer_ref, *probes_refs = late_refs
    px = split_ref.shape[0] // 2
    probes = probes_refs[0].shape[0]
    acc = scratch[-1]
    build_received(recv_ref, 0, pairs, *scratch[:2])
    build_targets(rows_ref, scratch[2])
    sweep(list_ref, units_ref, 0, *scratch)
    for copy in copies:
        copy.wait()
    low_x = lax.broadcasted_iota(jnp.int32, (px, LANES), 1) < 64

    def one_parent(q, carry):
        far = halves(coarse_ref[:, lane_tile(q >> 1)])
        twice = jnp.where((q & 1) == 0, far[0], far[1]).astype(jnp.bfloat16)
        matrix = transfer_ref[:, lane_tile(q)].astype(jnp.float32)
        low = lax.broadcasted_iota(jnp.int32, matrix.shape, 1) < 64
        matrix = jnp.concatenate(
            [jnp.where(low, matrix, 0.0), jnp.where(low, 0.0, matrix)], axis=0
        ).astype(jnp.bfloat16)
        sums = jnp.where(low_x, summed(acc, 2 * q), summed(acc, 2 * q + 1))
        total = own_ref[:, lane_tile(q)] + sums + bdot(twice, matrix, NT)
        out_ref[:, lane_tile(q)] = total
        high = total.astype(jnp.bfloat16)
        split_ref[:px, lane_tile(q)] = high
        split_ref[px:, lane_tile(q)] = (total - high.astype(jnp.float32)).astype(jnp.bfloat16)
        return carry

    lax.fori_loop(0, coarse_ref.shape[1] // 64, one_parent, 0, unroll=8)
    for block, probes_ref in enumerate(probes_refs):
        term = bdot(probes_ref[...], split_ref[...], NT)
        gram_ref[block] = term[:, :px] + term[:, px:]
    place = lax.axis_index("probe")
    for b in range(groups):
        block = gram_ref[lax.rem(place - b + groups, groups)]
        packed = jnp.concatenate([block[i:i + 8, :probes] for i in range(0, probes, 8)], axis=1)

        def one_owner(owner, carry):
            terms_ref[owner * groups + b] = packed
            return carry

        lax.fori_loop(0, terms_ref.shape[0] // groups, one_owner, 0)


def gram_kernel(terms_ref, out_ref, *, groups, scale):
    probes = out_ref.shape[0]
    columns = []
    for b in range(groups):
        total = terms_ref[b]
        for owner in range(1, terms_ref.shape[0] // groups):
            total = total + terms_ref[owner * groups + b]
        columns.append(
            jnp.concatenate([total[:, i * probes:(i + 1) * probes] for i in range(probes // 8)], axis=0)
        )
    out_ref[...] = jnp.concatenate(columns, axis=1) * scale


def sweep_scratch(total, clusters, px):
    return [
        pltpu.VMEM((total + 1, px, LANES), jnp.bfloat16),
        pltpu.VMEM((total + 1, 64, 16 * QUAD), jnp.bfloat16),
        pltpu.VMEM((clusters, 16, LANES), jnp.bfloat16),
        pltpu.VMEM((UNITS // QUAD, CHUNK * 64, QUAD * 64), jnp.bfloat16),
        pltpu.VMEM((UNITS // QUAD, CHUNK * 64, QUAD * 64), jnp.bfloat16),
        pltpu.VMEM((2, clusters, px, LANES), jnp.float32),
    ]


def shards(
    coef_fine,
    points_fine,
    points_coarse,
    transfer,
    send_fine,
    slots_fine,
    counts_fine,
    send_coarse,
    slots_coarse,
    counts_coarse,
):
    probes = coef_fine.shape[0]
    fine_count = counts_fine.shape[0]
    coarse_count = counts_coarse.shape[0]
    owners = lax.axis_size("leaf")
    groups = lax.axis_size("probe")
    px = -(-probes // 16) * 16
    coef = coef_fine if px == probes else jnp.pad(coef_fine, ((0, px - probes), (0, 0)))
    cap_fine = send_fine.shape[2]
    cap_coarse = send_coarse.shape[2]

    whole_vmem = pltpu.CompilerParams(vmem_limit_bytes=VMEM)
    smem = pl.BlockSpec(memory_space=pltpu.SMEM)
    vmem = pl.BlockSpec(memory_space=pltpu.VMEM)
    bf16, f32 = jnp.bfloat16, jnp.float32

    coarse_pairs = cap_coarse // 2
    early_pairs = EARLY * (cap_fine // 2) // 8
    late_pairs = cap_fine // 2 - early_pairs
    early_total = owners * 2 * early_pairs
    late_total = owners * 2 * late_pairs
    coarse_total = owners * cap_coarse
    unit_rows = [-(-(count * (SLOTS // CHUNK) + 2 * UNITS + 1) // LANES) for count in (fine_count, coarse_count)]
    list_shape = (3 * SECTION, LANES)
    i32 = jnp.int32
    fine_units_shape, coarse_units_shape = [(rows, LANES) for rows in unit_rows]
    fine_columns, coarse_columns = points_fine.shape[1], points_coarse.shape[1]
    heavy = pl.CostEstimate(flops=10**10, bytes_accessed=10**7, transcendentals=10**7)

    first_send, coarse_rows, coarse_coef, fine_rows = pl.pallas_call(
        functools.partial(pack_kernel, early=early_pairs),
        out_shape=(
            jax.ShapeDtypeStruct(
                (owners, sent_rows(coarse_pairs, px) + sent_rows(early_pairs, px), LANES), bf16
            ),
            jax.ShapeDtypeStruct((8, coarse_columns), f32),
            jax.ShapeDtypeStruct((px, coarse_columns), bf16),
            jax.ShapeDtypeStruct((8, fine_columns), f32),
        ),
        in_specs=[smem] * 2 + [vmem] * 4,
        out_specs=[vmem] * 4,
        scratch_shapes=[
            pltpu.VMEM((coarse_count, px, LANES), bf16),
            pltpu.VMEM((coarse_count, 8, LANES), f32),
            pltpu.VMEM((fine_count, px, LANES), bf16),
            pltpu.VMEM((fine_count, 8, LANES), f32),
        ],
        compiler_params=whole_vmem,
        name="pack_first",
    )(jnp.swapaxes(send_coarse, 1, 2), send_fine, coef, transfer, points_coarse, points_fine)
    first_recv = lax.all_to_all(first_send, "leaf", split_axis=0, concat_axis=0, tiled=True)

    turned = [coef_fine]
    for step in range(1, groups):
        turned.append(lax.ppermute(coef_fine, "probe", [(i, (i + step) % groups) for i in range(groups)]))

    fine_send, slot_list, early_units, coarse_units, fine_units, fine_own_sums, coarse_own_sums = pl.pallas_call(
        functools.partial(
            prepare_kernel,
            owners=owners,
            caps=(cap_fine, cap_coarse),
            splits=(2 * early_pairs, cap_coarse),
        ),
        out_shape=(
            jax.ShapeDtypeStruct((owners, sent_rows(late_pairs, px), LANES), bf16),
            jax.ShapeDtypeStruct(list_shape, i32),
            jax.ShapeDtypeStruct(fine_units_shape, i32),
            jax.ShapeDtypeStruct(coarse_units_shape, i32),
            jax.ShapeDtypeStruct(fine_units_shape, i32),
            jax.ShapeDtypeStruct((px, fine_columns), f32),
            jax.ShapeDtypeStruct((px, coarse_columns), f32),
        ),
        in_specs=[smem] + [vmem] * 8,
        out_specs=[vmem] * 7,
        scratch_shapes=[
            pltpu.VMEM((fine_count, px, LANES), bf16),
            pltpu.VMEM((fine_count, 8, LANES), f32),
            pltpu.VMEM(fine_units_shape, i32),
            pltpu.VMEM(coarse_units_shape, i32),
            pltpu.SMEM(list_shape, i32),
            pltpu.SMEM(fine_units_shape, i32),
            pltpu.SMEM(coarse_units_shape, i32),
            pltpu.SemaphoreType.DMA,
            pltpu.SemaphoreType.DMA,
            pltpu.SemaphoreType.DMA,
        ]
        + sweep_scratch(fine_count, fine_count, px),
        compiler_params=whole_vmem,
        cost_estimate=heavy,
        name="prepare",
    )(
        send_fine,
        slots_fine,
        counts_fine.reshape(1, -1),
        slots_coarse,
        counts_coarse.reshape(1, -1),
        coef,
        fine_rows,
        coarse_coef,
        coarse_rows,
    )
    fine_recv = lax.all_to_all(fine_send, "leaf", split_axis=0, concat_axis=0, tiled=True)

    fine_sums, coarse_far = pl.pallas_call(
        functools.partial(first_kernel, pairs=coarse_pairs, early=early_pairs),
        out_shape=(
            jax.ShapeDtypeStruct((px, fine_columns), f32),
            jax.ShapeDtypeStruct((px, coarse_columns), f32),
        ),
        in_specs=[smem] * 3 + [vmem] * 5,
        out_specs=[vmem, vmem],
        scratch_shapes=sweep_scratch(max(early_total, coarse_total), fine_count, px),
        compiler_params=whole_vmem,
        cost_estimate=heavy,
        name="first_sweep",
    )(slot_list, early_units, coarse_units, first_recv, fine_rows, coarse_rows, fine_own_sums, coarse_own_sums)

    late = (fine_sums, coarse_far, transfer, *turned)
    term_shape = (owners * groups, 8, probes * probes // 8)
    far, terms = pl.pallas_call(
        functools.partial(fine_kernel, groups, late_pairs),
        out_shape=(
            jax.ShapeDtypeStruct((px, points_fine.shape[1]), f32),
            jax.ShapeDtypeStruct(term_shape, f32),
        ),
        in_specs=[smem] * 2 + [vmem] * 2 + [pl.BlockSpec(memory_space=pl.ANY)] * (3 + groups),
        out_specs=[vmem, vmem],
        scratch_shapes=[pltpu.VMEM(operand.shape, operand.dtype) for operand in late]
        + [pltpu.SemaphoreType.DMA] * len(late)
        + [
            pltpu.VMEM((groups, probes, px), f32),
            pltpu.VMEM((2 * px, points_fine.shape[1]), bf16),
        ]
        + sweep_scratch(late_total, fine_count, px),
        compiler_params=whole_vmem,
        name="fine_sweep",
    )(slot_list, fine_units, fine_recv, fine_rows, *late)

    terms = lax.all_to_all(terms, ("leaf", "probe"), split_axis=0, concat_axis=0, tiled=True)
    probe_gram = pl.pallas_call(
        functools.partial(
            gram_kernel, groups=groups, scale=1.0 / math.sqrt(owners * fine_count * 64)
        ),
        out_shape=jax.ShapeDtypeStruct((probes, groups * probes), f32),
        in_specs=[vmem],
        out_specs=vmem,
        name="gram_sum",
    )(terms)
    return (far[:probes], probe_gram)


def solution(mesh):
    return jax.shard_map(
        shards,
        mesh=mesh,
        in_specs=(
            P("probe", "leaf"),
            P(None, "leaf"),
            P(None, "leaf"),
            P(None, "leaf"),
            P("leaf", None, None),
            P("leaf", None),
            P("leaf"),
            P("leaf", None, None),
            P("leaf", None),
            P("leaf"),
        ),
        out_specs=(P("probe", "leaf"), P("probe", None)),
        check_vma=False,
    )
```

```python
import functools
import functools
import math

import jax
import jax.numpy as jnp
from jax import lax
from jax.experimental import pallas as pl
from jax.experimental.pallas import tpu as pltpu
from jax.sharding import PartitionSpec as P

KERNEL_RATE = 1.5
POINT_SCALE = math.sqrt(2.0 * KERNEL_RATE * math.log2(math.e))
LANES = 128
UNITS = 16
QUAD = 4
CHUNK = 8
FAR_AWAY = -30000.0
SLOTS = 64
SECTION = SLOTS + CHUNK
EARLY = 2
VMEM = 56 * 1024 * 1024

NT = (((1,), (1,)), ((), ()))
NN = (((1,), (0,)), ((), ()))


def bdot(a, b, dims):
    return lax.dot_general(a, b, dims, preferred_element_type=jnp.float32)


def split_rows(points):
    v = points * POINT_SCALE
    norm = -0.5 * (v[0:1] * v[0:1] + v[1:2] * v[1:2] + v[2:3] * v[2:3])
    full = jnp.concatenate([v, norm], axis=0)
    high = full.astype(jnp.bfloat16).astype(jnp.float32)
    rest = (full - high).astype(jnp.bfloat16).astype(jnp.float32)
    return jnp.concatenate([high, rest], axis=0)


def source_features(rows):
    place = lax.broadcasted_iota(jnp.int32, rows.shape, 0)
    one = jnp.where((place == 3) | (place == 7), 1.0, 0.0)
    return jnp.concatenate([rows, jnp.where(place < 3, rows, one)], axis=0)


def target_features(rows):
    place = lax.broadcasted_iota(jnp.int32, rows.shape, 0)
    turned = jnp.concatenate([rows[4:8], rows[0:4]], axis=0)
    one = jnp.where((place == 3) | (place == 7), 1.0, jnp.where(place < 3, rows, turned))
    return jnp.concatenate([one, turned], axis=0)


def halves(tile):
    lane = lax.broadcasted_iota(jnp.int32, tile.shape, 1)
    turned = pltpu.roll(tile, LANES // 2, 1)
    low = lane < LANES // 2
    return jnp.where(low, tile, turned), jnp.where(low, turned, tile)


def lane_tile(index):
    return pl.ds(pl.multiple_of(index * LANES, LANES), LANES)


def list_slots(
    fine_slots_ref, fine_counts_ref, coarse_slots_ref, coarse_counts_ref, out_ref, *units_refs, owners, caps, splits
):
    fine, coarse = fine_slots_ref.shape[0], coarse_slots_ref.shape[0]
    spare = LANES - fine - coarse
    slots = jnp.concatenate(
        [fine_slots_ref[...], coarse_slots_ref[...], jnp.zeros((spare, SLOTS), jnp.int32)], axis=0
    )
    slots = slots.astype(jnp.float32).T.astype(jnp.int32)
    counts = jnp.concatenate(
        [fine_counts_ref[...], coarse_counts_ref[...], jnp.zeros((1, spare), jnp.int32)], axis=1
    )
    shape = (SLOTS, LANES)
    in_fine = lax.broadcasted_iota(jnp.int32, shape, 1) < fine

    def by_level(values):
        return jnp.where(in_fine, values[0], values[1])

    clusters = by_level((fine, coarse))
    split = by_level(splits)
    live = lax.broadcasted_iota(jnp.int32, shape, 0) < counts
    own = live & (slots < clusters)
    received = live & (slots >= clusters)
    entry = slots - clusters
    source = by_level([entry >> (cap.bit_length() - 1) for cap in caps])
    within = by_level([entry & (cap - 1) for cap in caps])
    later = by_level([cap - first for cap, first in zip(caps, splits)])
    row = lax.broadcasted_iota(jnp.int32, (SLOTS, SLOTS), 0)
    column = lax.broadcasted_iota(jnp.int32, (SLOTS, SLOTS), 1)
    upto = jnp.where(column <= row, 1.0, 0.0).astype(jnp.bfloat16)
    turns = []
    for side, (chosen, value, blank) in enumerate(
        (
            (own, slots, clusters),
            (received & (within < split), source * split + within, owners * split),
            (received & (within >= split), source * later + within - split, owners * later),
        )
    ):
        start = side * SECTION
        rank = bdot(upto, jnp.where(chosen, 1.0, 0.0).astype(jnp.bfloat16), NN).astype(jnp.int32)
        spot = jnp.where(chosen, rank - 1, -1)
        value = value - blank
        for first in range(0, SLOTS, 8):
            rows = [
                blank[:1] + jnp.sum(jnp.where(spot == place, value, 0), axis=0, keepdims=True)
                for place in range(first, first + 8)
            ]
            out_ref[start + first:start + first + 8] = jnp.concatenate(rows, axis=0)
        out_ref[start + SLOTS:start + SLOTS + CHUNK] = jnp.broadcast_to(blank[:1], (CHUNK, LANES))
        turns.append(jnp.maximum((rank[SLOTS - 1:] + CHUNK - 1) // CHUNK, 1))
    turns = jnp.concatenate(turns + [jnp.zeros((5, LANES), jnp.int32)], axis=0).astype(jnp.float32).T
    row = lax.broadcasted_iota(jnp.int32, (LANES, LANES), 0)
    column = lax.broadcasted_iota(jnp.int32, (LANES, LANES), 1)
    upto = (column <= row) & ((row < fine) == (column < fine))
    ends = bdot(jnp.where(upto, 1.0, 0.0).astype(jnp.bfloat16), turns.astype(jnp.bfloat16), NN)
    ends, turns = ends.astype(jnp.int32), turns.astype(jnp.int32)
    for side in range(3):
        for level, (low, count) in enumerate(((0, fine), (fine, coarse))):
            if side == 2 and level == 1:
                continue
            units_ref = units_refs[2 * side + level]
            end = ends[low:low + count, side:side + 1]
            took = turns[low:low + count, side:side + 1]
            lane = lax.broadcasted_iota(jnp.int32, (1, LANES), 1)
            for tile in range(units_ref.shape[0]):
                place = tile * LANES + lane
                passed = end <= place
                target = jnp.sum(jnp.where(passed, 1, 0), axis=0, keepdims=True)
                turn = place - jnp.sum(jnp.where(passed, took, 0), axis=0, keepdims=True)
                over = target >= count
                start = side * SECTION + jnp.where(over, SLOTS, turn * CHUNK)
                code = start * LANES + low + jnp.where(over, count - 1, target)
                if tile == units_ref.shape[0] - 1:
                    code = jnp.where(lane == LANES - 1, end[count - 1:], code)
                units_ref[tile:tile + 1] = code


def sent_rows(pairs, px):
    return pairs * px + -(-pairs // 2) * 16


def pack_send(send_ref, out_ref, dup_coef, dup_rows, px, pairs, base=0, entry_first=False):
    owners = out_ref.shape[0]
    points = base + len(pairs) * px
    lane = lax.broadcasted_iota(jnp.int32, (px, LANES), 1) < LANES // 2
    lane8 = lax.broadcasted_iota(jnp.int32, (8, LANES), 1) < LANES // 2

    def one_owner(owner, carry):
        rows = []
        for place, pair in enumerate(pairs):
            first, second = [
                send_ref[0, entry, owner] if entry_first else send_ref[0, owner, entry]
                for entry in (2 * pair, 2 * pair + 1)
            ]
            start = base + place * px
            out_ref[owner, start:start + px, :] = jnp.where(lane, dup_coef[first], dup_coef[second])
            rows.append(jnp.where(lane8, dup_rows[first], dup_rows[second]))
        if len(rows) % 2:
            rows.append(rows[-1])
        for place in range(0, len(rows), 2):
            start = points + place * 8
            out_ref[owner, start:start + 16, :] = jnp.concatenate(rows[place:place + 2], axis=0).astype(
                jnp.bfloat16
            )
        return carry

    lax.fori_loop(0, owners, one_owner, 0, unroll=4)


def double_fine(coef_ref, rows_ref, dup_coef, dup_rows):
    def one_tile(index, carry):
        a, b = halves(coef_ref[:, lane_tile(index)].astype(jnp.float32))
        dup_coef[2 * index] = a.astype(jnp.bfloat16)
        dup_coef[2 * index + 1] = b.astype(jnp.bfloat16)
        a, b = halves(rows_ref[:, lane_tile(index)])
        dup_rows[2 * index] = a
        dup_rows[2 * index + 1] = b
        return carry

    lax.fori_loop(0, coef_ref.shape[1] // LANES, one_tile, 0, unroll=8)


def pack_kernel(
    send_ref,
    send_fine_ref,
    coef_ref,
    transfer_ref,
    points_ref,
    points_fine_ref,
    out_ref,
    rows_ref,
    coarse_ref,
    fine_rows_ref,
    dup_coef,
    dup_rows,
    dup_fine,
    dup_fine_rows,
    *,
    early,
):
    px = coef_ref.shape[0]
    pairs = send_ref.shape[1] // 2
    rows_ref[...] = split_rows(points_ref[...])
    fine_rows_ref[...] = split_rows(points_fine_ref[...])
    double_fine(coef_ref, fine_rows_ref, dup_fine, dup_fine_rows)

    def one_tile(index, carry):
        doubled = []
        for part in range(2):
            q = 2 * index + part
            a, b = halves(transfer_ref[:, lane_tile(q)].astype(jnp.float32))
            matrix = jnp.concatenate([a, b], axis=0).astype(jnp.bfloat16)
            block = bdot(coef_ref[:, lane_tile(q)], matrix, NN).astype(jnp.bfloat16)
            dup_coef[q] = block
            doubled.append(block)
        lane = lax.broadcasted_iota(jnp.int32, (px, LANES), 1) < LANES // 2
        coarse_ref[:, lane_tile(index)] = jnp.where(lane, doubled[0], doubled[1])
        a, b = halves(rows_ref[:, lane_tile(index)])
        dup_rows[2 * index] = a
        dup_rows[2 * index + 1] = b
        return carry

    lax.fori_loop(0, coef_ref.shape[1] // (2 * LANES), one_tile, 0, unroll=8)
    pack_send(send_ref, out_ref, dup_coef, dup_rows, px, range(pairs), entry_first=True)
    pack_send(send_fine_ref, out_ref, dup_fine, dup_fine_rows, px, range(early), base=sent_rows(pairs, px))


def turned(rows):
    row = lax.broadcasted_iota(jnp.int32, (LANES, LANES), 0)
    column = lax.broadcasted_iota(jnp.int32, (LANES, LANES), 1)
    unit = jnp.where(row == column, 1.0, 0.0).astype(jnp.bfloat16)
    return bdot(unit, rows, NT).astype(jnp.bfloat16)


def put_pair(entry, coef, rows, coef_table, feature_table):
    a, b = halves(coef.astype(jnp.float32))
    coef_table[entry] = a.astype(jnp.bfloat16)
    coef_table[entry + 1] = b.astype(jnp.bfloat16)
    features = turned(jnp.concatenate([source_features(rows).astype(jnp.bfloat16)] * QUAD, axis=0))
    feature_table[entry] = features[:64]
    feature_table[entry + 1] = features[64:]


def put_nothing(entry, coef_table, feature_table):
    coef_table[entry] = jnp.zeros(coef_table.shape[1:], jnp.bfloat16)
    place = lax.broadcasted_iota(jnp.int32, (8, LANES), 0)
    nothing = source_features(jnp.where(place == 3, FAR_AWAY, 0.0)).astype(jnp.bfloat16)
    feature_table[entry] = turned(jnp.concatenate([nothing] * QUAD, axis=0))[:64]


def build_own(coef_ref, rows_ref, coef_table, feature_table):
    tiles = coef_ref.shape[1] // LANES

    def one_tile(index, carry):
        tile = lane_tile(index)
        put_pair(2 * index, coef_ref[:, tile], rows_ref[:, tile], coef_table, feature_table)
        return carry

    lax.fori_loop(0, tiles, one_tile, 0, unroll=16)
    put_nothing(2 * tiles, coef_table, feature_table)


def build_received(recv_ref, base, pairs, coef_table, feature_table):
    owners = recv_ref.shape[0]
    px = coef_table.shape[1]
    points = base + pairs * px

    def one_owner(owner, carry):
        for pair in range(0, pairs, 2):
            start = points + pair * 8
            both = recv_ref[owner, start:start + 16, :].astype(jnp.float32)
            for part in range(min(2, pairs - pair)):
                where = pair + part
                start = base + where * px
                put_pair(
                    owner * (2 * pairs) + 2 * where,
                    recv_ref[owner, start:start + px, :],
                    both[8 * part:8 * part + 8],
                    coef_table,
                    feature_table,
                )
        return carry

    lax.fori_loop(0, owners, one_owner, 0, unroll=8 if pairs <= 4 else 4)
    put_nothing(owners * pairs * 2, coef_table, feature_table)


def build_targets(rows_ref, target_table):
    def one_tile(index, carry):
        a, b = halves(target_features(rows_ref[:, lane_tile(index)]))
        target_table[2 * index] = a.astype(jnp.bfloat16)
        target_table[2 * index + 1] = b.astype(jnp.bfloat16)
        return carry

    lax.fori_loop(0, rows_ref.shape[1] // LANES, one_tile, 0, unroll=16)


def sweep(list_ref, units_ref, first, coef_table, feature_table, target_table, first_buffer, second_buffer, acc):
    px = coef_table.shape[1]
    lane = lax.broadcasted_iota(jnp.int32, (64, 16 * QUAD), 1) // 16
    lane_t = lax.broadcasted_iota(jnp.int32, (16, LANES), 1) // 64
    lane_x = lax.broadcasted_iota(jnp.int32, (px, LANES), 1) < 64
    blank = jnp.zeros((16, LANES), jnp.bfloat16)
    acc[...] = jnp.zeros_like(acc)

    def partners(unit):
        row, column = unit
        return [list_ref[row + m, column] for m in range(CHUNK)]

    def units_of(place):
        codes = [units_ref[place >> 7, (place & (LANES - 1)) + u] for u in range(UNITS)]
        return [(code >> 7, code & (LANES - 1)) for code in codes]

    def tiles(units, buffer, starts=range(0, UNITS, QUAD)):
        for start in starts:
            quad = units[start:start + QUAD]
            weights = []
            for u in range(QUAD):
                own = jnp.where(lane_t == u % 2, target_table[quad[u][1] - first], blank)
                weights.append(jnp.concatenate([own if v == u // 2 else blank for v in range(QUAD // 2)], axis=1))
            weights = jnp.concatenate(weights, axis=0)
            ids = [partners(unit) for unit in quad]
            for part in range(0, CHUNK, 4):
                rows = []
                for m in range(part, part + 4):
                    tile = feature_table[ids[0][m]]
                    for u in range(1, QUAD):
                        tile = jnp.where(lane == u, feature_table[ids[u][m]], tile)
                    rows.append(tile)
                power = bdot(jnp.concatenate(rows, axis=0), weights, NN)
                buffer[start // QUAD, part * 64:(part + 4) * 64] = jnp.exp2(power).astype(jnp.bfloat16)

    def products(units, buffer, starts=range(0, UNITS, QUAD)):
        for start in starts:
            quad = units[start:start + QUAD]
            coefs = []
            for unit in quad:
                ids = partners(unit)
                coefs.append(
                    jnp.concatenate(
                        [
                            jnp.where(lane_x, coef_table[ids[m]], coef_table[ids[m + 1]])
                            for m in range(0, CHUNK, 2)
                        ],
                        axis=1,
                    )
                )
            product = bdot(jnp.concatenate(coefs, axis=0), buffer[start // QUAD], NN)
            for u in range(QUAD):
                side = (u // 2) * LANES
                acc[u % 2, quad[u][1] - first] += product[u * px:(u + 1) * px, side:side + LANES]

    def phase(later, later_buffer, units, buffer):
        for start in range(0, UNITS, QUAD):
            tiles(later, later_buffer, [start])
            products(units, buffer, [start])

    def two_sets(index, carry):
        here = index * (2 * UNITS)
        second = units_of(here + UNITS)
        phase(second, second_buffer, units_of(here), first_buffer)
        phase(units_of(here + 2 * UNITS), first_buffer, second, second_buffer)
        return carry

    total = units_ref[units_ref.shape[0] - 1, LANES - 1]
    sets = (total + UNITS - 1) // UNITS
    bodies = (sets - 1) // 2
    last = bodies * (2 * UNITS)
    tiles(units_of(0), first_buffer)
    lax.fori_loop(0, bodies, two_sets, 0)

    @pl.when(sets == 2 * bodies + 2)
    def _():
        second = units_of(last + UNITS)
        phase(second, second_buffer, units_of(last), first_buffer)
        products(second, second_buffer)

    @pl.when(sets == 2 * bodies + 1)
    def _():
        products(units_of(last), first_buffer)


def summed(acc, target):
    low = lax.broadcasted_iota(jnp.int32, acc.shape[2:], 1) < 64
    here = jnp.where(low, acc[0, target], acc[1, target])
    return here + pltpu.roll(here, 64, 1)


def put_sums(acc, clusters, out_ref, before_ref=None):
    low = lax.broadcasted_iota(jnp.int32, acc.shape[2:], 1) < 64

    def one_tile(index, carry):
        tile = lane_tile(index)
        sums = jnp.where(low, summed(acc, 2 * index), summed(acc, 2 * index + 1))
        out_ref[:, tile] = sums if before_ref is None else before_ref[:, tile] + sums
        return carry

    lax.fori_loop(0, clusters // 2, one_tile, 0, unroll=8)


def prepare_kernel(
    send_ref,
    fine_slots_ref,
    fine_counts_ref,
    coarse_slots_ref,
    coarse_counts_ref,
    coef_ref,
    fine_rows_ref,
    coarse_coef_ref,
    coarse_rows_ref,
    send_out_ref,
    list_out_ref,
    early_units_ref,
    coarse_units_ref,
    fine_units_ref,
    fine_out_ref,
    coarse_out_ref,
    dup_coef,
    dup_rows,
    fine_own_ref,
    coarse_own_ref,
    list_ref,
    fine_own_units,
    coarse_own_units,
    list_sem,
    fine_sem,
    coarse_sem,
    *scratch,
    owners,
    caps,
    splits,
):
    list_slots(
        fine_slots_ref,
        fine_counts_ref,
        coarse_slots_ref,
        coarse_counts_ref,
        list_out_ref,
        fine_own_ref,
        coarse_own_ref,
        early_units_ref,
        coarse_units_ref,
        fine_units_ref,
        owners=owners,
        caps=caps,
        splits=splits,
    )
    copies = [
        pltpu.make_async_copy(list_out_ref, list_ref, list_sem),
        pltpu.make_async_copy(fine_own_ref, fine_own_units, fine_sem),
        pltpu.make_async_copy(coarse_own_ref, coarse_own_units, coarse_sem),
    ]
    for copy in copies:
        copy.start()
    double_fine(coef_ref, fine_rows_ref, dup_coef, dup_rows)
    pack_send(
        send_ref, send_out_ref, dup_coef, dup_rows, coef_ref.shape[0], range(splits[0] // 2, caps[0] // 2)
    )
    for copy in copies:
        copy.wait()
    first = 0
    for units_ref, source_ref, rows_ref, out_ref in (
        (fine_own_units, coef_ref, fine_rows_ref, fine_out_ref),
        (coarse_own_units, coarse_coef_ref, coarse_rows_ref, coarse_out_ref),
    ):
        clusters = rows_ref.shape[1] // 64
        build_own(source_ref, rows_ref, *scratch[:2])
        build_targets(rows_ref, scratch[2])
        sweep(list_ref, units_ref, first, *scratch)
        put_sums(scratch[-1], clusters, out_ref)
        first += clusters


def first_kernel(
    list_ref,
    early_units_ref,
    units_ref,
    recv_ref,
    fine_rows_ref,
    rows_ref,
    fine_own_ref,
    own_ref,
    fine_out_ref,
    out_ref,
    *scratch,
    pairs,
    early,
):
    px = own_ref.shape[0]
    fine = fine_rows_ref.shape[1] // 64
    build_received(recv_ref, 0, pairs, *scratch[:2])
    build_targets(rows_ref, scratch[2])
    sweep(list_ref, units_ref, fine, *scratch)
    put_sums(scratch[-1], rows_ref.shape[1] // 64, out_ref, own_ref)
    build_received(recv_ref, sent_rows(pairs, px), early, *scratch[:2])
    build_targets(fine_rows_ref, scratch[2])
    sweep(list_ref, early_units_ref, 0, *scratch)
    put_sums(scratch[-1], fine, fine_out_ref, fine_own_ref)


def fine_kernel(groups, pairs, *refs):
    late = 3 + groups
    list_ref, units_ref, recv_ref, rows_ref = refs[:4]
    out_ref, terms_ref = refs[4 + late:6 + late]
    late_refs = refs[6 + late:6 + 2 * late]
    late_sems = refs[6 + 2 * late:6 + 3 * late]
    gram_ref, split_ref, *scratch = refs[6 + 3 * late:]
    copies = [pltpu.make_async_copy(*pair) for pair in zip(refs[4:4 + late], late_refs, late_sems)]
    for copy in copies:
        copy.start()
    own_ref, coarse_ref, transfer_ref, *probes_refs = late_refs
    px = split_ref.shape[0] // 2
    probes = probes_refs[0].shape[0]
    acc = scratch[-1]
    build_received(recv_ref, 0, pairs, *scratch[:2])
    build_targets(rows_ref, scratch[2])
    sweep(list_ref, units_ref, 0, *scratch)
    for copy in copies:
        copy.wait()
    low_x = lax.broadcasted_iota(jnp.int32, (px, LANES), 1) < 64

    def one_parent(q, carry):
        far = halves(coarse_ref[:, lane_tile(q >> 1)])
        twice = jnp.where((q & 1) == 0, far[0], far[1]).astype(jnp.bfloat16)
        matrix = transfer_ref[:, lane_tile(q)].astype(jnp.float32)
        low = lax.broadcasted_iota(jnp.int32, matrix.shape, 1) < 64
        matrix = jnp.concatenate(
            [jnp.where(low, matrix, 0.0), jnp.where(low, 0.0, matrix)], axis=0
        ).astype(jnp.bfloat16)
        sums = jnp.where(low_x, summed(acc, 2 * q), summed(acc, 2 * q + 1))
        total = own_ref[:, lane_tile(q)] + sums + bdot(twice, matrix, NT)
        out_ref[:, lane_tile(q)] = total
        high = total.astype(jnp.bfloat16)
        split_ref[:px, lane_tile(q)] = high
        split_ref[px:, lane_tile(q)] = (total - high.astype(jnp.float32)).astype(jnp.bfloat16)
        return carry

    lax.fori_loop(0, coarse_ref.shape[1] // 64, one_parent, 0, unroll=8)
    for block, probes_ref in enumerate(probes_refs):
        term = bdot(probes_ref[...], split_ref[...], NT)
        gram_ref[block] = term[:, :px] + term[:, px:]
    place = lax.axis_index("probe")
    for b in range(groups):
        block = gram_ref[lax.rem(place - b + groups, groups)]
        packed = jnp.concatenate([block[i:i + 8, :probes] for i in range(0, probes, 8)], axis=1)

        def one_owner(owner, carry):
            terms_ref[owner * groups + b] = packed
            return carry

        lax.fori_loop(0, terms_ref.shape[0] // groups, one_owner, 0)


def gram_kernel(terms_ref, out_ref, *, groups, scale):
    probes = out_ref.shape[0]
    columns = []
    for b in range(groups):
        total = terms_ref[b]
        for owner in range(1, terms_ref.shape[0] // groups):
            total = total + terms_ref[owner * groups + b]
        columns.append(
            jnp.concatenate([total[:, i * probes:(i + 1) * probes] for i in range(probes // 8)], axis=0)
        )
    out_ref[...] = jnp.concatenate(columns, axis=1) * scale


def sweep_scratch(total, clusters, px):
    return [
        pltpu.VMEM((total + 1, px, LANES), jnp.bfloat16),
        pltpu.VMEM((total + 1, 64, 16 * QUAD), jnp.bfloat16),
        pltpu.VMEM((clusters, 16, LANES), jnp.bfloat16),
        pltpu.VMEM((UNITS // QUAD, CHUNK * 64, QUAD * 64), jnp.bfloat16),
        pltpu.VMEM((UNITS // QUAD, CHUNK * 64, QUAD * 64), jnp.bfloat16),
        pltpu.VMEM((2, clusters, px, LANES), jnp.float32),
    ]


def shards(
    coef_fine,
    points_fine,
    points_coarse,
    transfer,
    send_fine,
    slots_fine,
    counts_fine,
    send_coarse,
    slots_coarse,
    counts_coarse,
):
    probes = coef_fine.shape[0]
    fine_count = counts_fine.shape[0]
    coarse_count = counts_coarse.shape[0]
    owners = lax.axis_size("leaf")
    groups = lax.axis_size("probe")
    px = -(-probes // 16) * 16
    coef = coef_fine if px == probes else jnp.pad(coef_fine, ((0, px - probes), (0, 0)))
    cap_fine = send_fine.shape[2]
    cap_coarse = send_coarse.shape[2]

    whole_vmem = pltpu.CompilerParams(vmem_limit_bytes=VMEM)
    smem = pl.BlockSpec(memory_space=pltpu.SMEM)
    vmem = pl.BlockSpec(memory_space=pltpu.VMEM)
    bf16, f32 = jnp.bfloat16, jnp.float32

    coarse_pairs = cap_coarse // 2
    early_pairs = EARLY * (cap_fine // 2) // 8
    late_pairs = cap_fine // 2 - early_pairs
    early_total = owners * 2 * early_pairs
    late_total = owners * 2 * late_pairs
    coarse_total = owners * cap_coarse
    unit_rows = [-(-(count * (SLOTS // CHUNK) + 2 * UNITS + 1) // LANES) for count in (fine_count, coarse_count)]
    list_shape = (3 * SECTION, LANES)
    i32 = jnp.int32
    fine_units_shape, coarse_units_shape = [(rows, LANES) for rows in unit_rows]
    fine_columns, coarse_columns = points_fine.shape[1], points_coarse.shape[1]
    heavy = pl.CostEstimate(flops=10**10, bytes_accessed=10**7, transcendentals=10**7)

    first_send, coarse_rows, coarse_coef, fine_rows = pl.pallas_call(
        functools.partial(pack_kernel, early=early_pairs),
        out_shape=(
            jax.ShapeDtypeStruct(
                (owners, sent_rows(coarse_pairs, px) + sent_rows(early_pairs, px), LANES), bf16
            ),
            jax.ShapeDtypeStruct((8, coarse_columns), f32),
            jax.ShapeDtypeStruct((px, coarse_columns), bf16),
            jax.ShapeDtypeStruct((8, fine_columns), f32),
        ),
        in_specs=[smem] * 2 + [vmem] * 4,
        out_specs=[vmem] * 4,
        scratch_shapes=[
            pltpu.VMEM((coarse_count, px, LANES), bf16),
            pltpu.VMEM((coarse_count, 8, LANES), f32),
            pltpu.VMEM((fine_count, px, LANES), bf16),
            pltpu.VMEM((fine_count, 8, LANES), f32),
        ],
        compiler_params=whole_vmem,
        name="pack_first",
    )(jnp.swapaxes(send_coarse, 1, 2), send_fine, coef, transfer, points_coarse, points_fine)
    first_recv = lax.all_to_all(first_send, "leaf", split_axis=0, concat_axis=0, tiled=True)

    turned = [coef_fine]
    for step in range(1, groups):
        turned.append(lax.ppermute(coef_fine, "probe", [(i, (i + step) % groups) for i in range(groups)]))

    fine_send, slot_list, early_units, coarse_units, fine_units, fine_own_sums, coarse_own_sums = pl.pallas_call(
        functools.partial(
            prepare_kernel,
            owners=owners,
            caps=(cap_fine, cap_coarse),
            splits=(2 * early_pairs, cap_coarse),
        ),
        out_shape=(
            jax.ShapeDtypeStruct((owners, sent_rows(late_pairs, px), LANES), bf16),
            jax.ShapeDtypeStruct(list_shape, i32),
            jax.ShapeDtypeStruct(fine_units_shape, i32),
            jax.ShapeDtypeStruct(coarse_units_shape, i32),
            jax.ShapeDtypeStruct(fine_units_shape, i32),
            jax.ShapeDtypeStruct((px, fine_columns), f32),
            jax.ShapeDtypeStruct((px, coarse_columns), f32),
        ),
        in_specs=[smem] + [vmem] * 8,
        out_specs=[vmem] * 7,
        scratch_shapes=[
            pltpu.VMEM((fine_count, px, LANES), bf16),
            pltpu.VMEM((fine_count, 8, LANES), f32),
            pltpu.VMEM(fine_units_shape, i32),
            pltpu.VMEM(coarse_units_shape, i32),
            pltpu.SMEM(list_shape, i32),
            pltpu.SMEM(fine_units_shape, i32),
            pltpu.SMEM(coarse_units_shape, i32),
            pltpu.SemaphoreType.DMA,
            pltpu.SemaphoreType.DMA,
            pltpu.SemaphoreType.DMA,
        ]
        + sweep_scratch(fine_count, fine_count, px),
        compiler_params=whole_vmem,
        cost_estimate=heavy,
        name="prepare",
    )(
        send_fine,
        slots_fine,
        counts_fine.reshape(1, -1),
        slots_coarse,
        counts_coarse.reshape(1, -1),
        coef,
        fine_rows,
        coarse_coef,
        coarse_rows,
    )
    fine_recv = lax.all_to_all(fine_send, "leaf", split_axis=0, concat_axis=0, tiled=True)

    fine_sums, coarse_far = pl.pallas_call(
        functools.partial(first_kernel, pairs=coarse_pairs, early=early_pairs),
        out_shape=(
            jax.ShapeDtypeStruct((px, fine_columns), f32),
            jax.ShapeDtypeStruct((px, coarse_columns), f32),
        ),
        in_specs=[smem] * 3 + [vmem] * 5,
        out_specs=[vmem, vmem],
        scratch_shapes=sweep_scratch(max(early_total, coarse_total), fine_count, px),
        compiler_params=whole_vmem,
        cost_estimate=heavy,
        name="first_sweep",
    )(slot_list, early_units, coarse_units, first_recv, fine_rows, coarse_rows, fine_own_sums, coarse_own_sums)

    late = (fine_sums, coarse_far, transfer, *turned)
    term_shape = (owners * groups, 8, probes * probes // 8)
    far, terms = pl.pallas_call(
        functools.partial(fine_kernel, groups, late_pairs),
        out_shape=(
            jax.ShapeDtypeStruct((px, points_fine.shape[1]), f32),
            jax.ShapeDtypeStruct(term_shape, f32),
        ),
        in_specs=[smem] * 2 + [vmem] * 2 + [pl.BlockSpec(memory_space=pl.ANY)] * (3 + groups),
        out_specs=[vmem, vmem],
        scratch_shapes=[pltpu.VMEM(operand.shape, operand.dtype) for operand in late]
        + [pltpu.SemaphoreType.DMA] * len(late)
        + [
            pltpu.VMEM((groups, probes, px), f32),
            pltpu.VMEM((2 * px, points_fine.shape[1]), bf16),
        ]
        + sweep_scratch(late_total, fine_count, px),
        compiler_params=whole_vmem,
        name="fine_sweep",
    )(slot_list, fine_units, fine_recv, fine_rows, *late)

    terms = lax.all_to_all(terms, ("leaf", "probe"), split_axis=0, concat_axis=0, tiled=True)
    probe_gram = pl.pallas_call(
        functools.partial(
            gram_kernel, groups=groups, scale=1.0 / math.sqrt(owners * fine_count * 64)
        ),
        out_shape=jax.ShapeDtypeStruct((probes, groups * probes), f32),
        in_specs=[vmem],
        out_specs=vmem,
        name="gram_sum",
    )(terms)
    return (far[:probes], probe_gram)


def solution(mesh):
    return jax.shard_map(
        shards,
        mesh=mesh,
        in_specs=(
            P("probe", "leaf"),
            P(None, "leaf"),
            P(None, "leaf"),
            P(None, "leaf"),
            P("leaf", None, None),
            P("leaf", None),
            P("leaf"),
            P("leaf", None, None),
            P("leaf", None),
            P("leaf"),
        ),
        out_specs=(P("probe", "leaf"), P("probe", None)),
        check_vma=False,
    )
```

```python
import functools
import functools
import math

import jax
import jax.numpy as jnp
from jax import lax
from jax.experimental import pallas as pl
from jax.experimental.pallas import tpu as pltpu
from jax.sharding import PartitionSpec as P

KERNEL_RATE = 1.5
POINT_SCALE = math.sqrt(2.0 * KERNEL_RATE * math.log2(math.e))
LANES = 128
UNITS = 16
QUAD = 4
CHUNK = 8
FAR_AWAY = -30000.0
SLOTS = 64
SECTION = SLOTS + CHUNK
EARLY = 2
VMEM = 56 * 1024 * 1024

NT = (((1,), (1,)), ((), ()))
NN = (((1,), (0,)), ((), ()))


def bdot(a, b, dims):
    return lax.dot_general(a, b, dims, preferred_element_type=jnp.float32)


def split_rows(points):
    v = points * POINT_SCALE
    norm = -0.5 * (v[0:1] * v[0:1] + v[1:2] * v[1:2] + v[2:3] * v[2:3])
    full = jnp.concatenate([v, norm], axis=0)
    high = full.astype(jnp.bfloat16).astype(jnp.float32)
    rest = (full - high).astype(jnp.bfloat16).astype(jnp.float32)
    return jnp.concatenate([high, rest], axis=0)


def source_features(rows):
    place = lax.broadcasted_iota(jnp.int32, rows.shape, 0)
    one = jnp.where((place == 3) | (place == 7), 1.0, 0.0)
    return jnp.concatenate([rows, jnp.where(place < 3, rows, one)], axis=0)


def target_features(rows):
    place = lax.broadcasted_iota(jnp.int32, rows.shape, 0)
    turned = jnp.concatenate([rows[4:8], rows[0:4]], axis=0)
    one = jnp.where((place == 3) | (place == 7), 1.0, jnp.where(place < 3, rows, turned))
    return jnp.concatenate([one, turned], axis=0)


def halves(tile):
    lane = lax.broadcasted_iota(jnp.int32, tile.shape, 1)
    turned = pltpu.roll(tile, LANES // 2, 1)
    low = lane < LANES // 2
    return jnp.where(low, tile, turned), jnp.where(low, turned, tile)


def lane_tile(index):
    return pl.ds(pl.multiple_of(index * LANES, LANES), LANES)


def list_slots(
    fine_slots_ref, fine_counts_ref, coarse_slots_ref, coarse_counts_ref, out_ref, *units_refs, owners, caps, splits
):
    fine, coarse = fine_slots_ref.shape[0], coarse_slots_ref.shape[0]
    spare = LANES - fine - coarse
    slots = jnp.concatenate(
        [fine_slots_ref[...], coarse_slots_ref[...], jnp.zeros((spare, SLOTS), jnp.int32)], axis=0
    )
    slots = slots.astype(jnp.float32).T.astype(jnp.int32)
    counts = jnp.concatenate(
        [fine_counts_ref[...], coarse_counts_ref[...], jnp.zeros((1, spare), jnp.int32)], axis=1
    )
    shape = (SLOTS, LANES)
    in_fine = lax.broadcasted_iota(jnp.int32, shape, 1) < fine

    def by_level(values):
        return jnp.where(in_fine, values[0], values[1])

    clusters = by_level((fine, coarse))
    split = by_level(splits)
    live = lax.broadcasted_iota(jnp.int32, shape, 0) < counts
    own = live & (slots < clusters)
    received = live & (slots >= clusters)
    entry = slots - clusters
    source = by_level([entry >> (cap.bit_length() - 1) for cap in caps])
    within = by_level([entry & (cap - 1) for cap in caps])
    later = by_level([cap - first for cap, first in zip(caps, splits)])
    row = lax.broadcasted_iota(jnp.int32, (SLOTS, SLOTS), 0)
    column = lax.broadcasted_iota(jnp.int32, (SLOTS, SLOTS), 1)
    upto = jnp.where(column <= row, 1.0, 0.0).astype(jnp.bfloat16)
    turns = []
    for side, (chosen, value, blank) in enumerate(
        (
            (own, slots, clusters),
            (received & (within < split), source * split + within, owners * split),
            (received & (within >= split), source * later + within - split, owners * later),
        )
    ):
        start = side * SECTION
        rank = bdot(upto, jnp.where(chosen, 1.0, 0.0).astype(jnp.bfloat16), NN).astype(jnp.int32)
        spot = jnp.where(chosen, rank - 1, -1)
        value = value - blank
        for first in range(0, SLOTS, 8):
            rows = [
                blank[:1] + jnp.sum(jnp.where(spot == place, value, 0), axis=0, keepdims=True)
                for place in range(first, first + 8)
            ]
            out_ref[start + first:start + first + 8] = jnp.concatenate(rows, axis=0)
        out_ref[start + SLOTS:start + SLOTS + CHUNK] = jnp.broadcast_to(blank[:1], (CHUNK, LANES))
        turns.append(jnp.maximum((rank[SLOTS - 1:] + CHUNK - 1) // CHUNK, 1))
    turns = jnp.concatenate(turns + [jnp.zeros((5, LANES), jnp.int32)], axis=0).astype(jnp.float32).T
    row = lax.broadcasted_iota(jnp.int32, (LANES, LANES), 0)
    column = lax.broadcasted_iota(jnp.int32, (LANES, LANES), 1)
    upto = (column <= row) & ((row < fine) == (column < fine))
    ends = bdot(jnp.where(upto, 1.0, 0.0).astype(jnp.bfloat16), turns.astype(jnp.bfloat16), NN)
    ends, turns = ends.astype(jnp.int32), turns.astype(jnp.int32)
    for side in range(3):
        for level, (low, count) in enumerate(((0, fine), (fine, coarse))):
            if side == 2 and level == 1:
                continue
            units_ref = units_refs[2 * side + level]
            end = ends[low:low + count, side:side + 1]
            took = turns[low:low + count, side:side + 1]
            lane = lax.broadcasted_iota(jnp.int32, (1, LANES), 1)
            for tile in range(units_ref.shape[0]):
                place = tile * LANES + lane
                passed = end <= place
                target = jnp.sum(jnp.where(passed, 1, 0), axis=0, keepdims=True)
                turn = place - jnp.sum(jnp.where(passed, took, 0), axis=0, keepdims=True)
                over = target >= count
                start = side * SECTION + jnp.where(over, SLOTS, turn * CHUNK)
                code = start * LANES + low + jnp.where(over, count - 1, target)
                if tile == units_ref.shape[0] - 1:
                    code = jnp.where(lane == LANES - 1, end[count - 1:], code)
                units_ref[tile:tile + 1] = code


def sent_rows(pairs, px):
    return pairs * px + -(-pairs // 2) * 16


def pack_send(send_ref, out_ref, dup_coef, dup_rows, px, pairs, base=0, entry_first=False):
    owners = out_ref.shape[0]
    points = base + len(pairs) * px
    lane = lax.broadcasted_iota(jnp.int32, (px, LANES), 1) < LANES // 2
    lane8 = lax.broadcasted_iota(jnp.int32, (8, LANES), 1) < LANES // 2

    def one_owner(owner, carry):
        rows = []
        for place, pair in enumerate(pairs):
            first, second = [
                send_ref[0, entry, owner] if entry_first else send_ref[0, owner, entry]
                for entry in (2 * pair, 2 * pair + 1)
            ]
            start = base + place * px
            out_ref[owner, start:start + px, :] = jnp.where(lane, dup_coef[first], dup_coef[second])
            rows.append(jnp.where(lane8, dup_rows[first], dup_rows[second]))
        if len(rows) % 2:
            rows.append(rows[-1])
        for place in range(0, len(rows), 2):
            start = points + place * 8
            out_ref[owner, start:start + 16, :] = jnp.concatenate(rows[place:place + 2], axis=0).astype(
                jnp.bfloat16
            )
        return carry

    lax.fori_loop(0, owners, one_owner, 0, unroll=4)


def double_fine(coef_ref, rows_ref, dup_coef, dup_rows):
    def one_tile(index, carry):
        a, b = halves(coef_ref[:, lane_tile(index)].astype(jnp.float32))
        dup_coef[2 * index] = a.astype(jnp.bfloat16)
        dup_coef[2 * index + 1] = b.astype(jnp.bfloat16)
        a, b = halves(rows_ref[:, lane_tile(index)])
        dup_rows[2 * index] = a
        dup_rows[2 * index + 1] = b
        return carry

    lax.fori_loop(0, coef_ref.shape[1] // LANES, one_tile, 0, unroll=8)


def pack_kernel(
    send_ref,
    send_fine_ref,
    coef_ref,
    transfer_ref,
    points_ref,
    points_fine_ref,
    out_ref,
    rows_ref,
    coarse_ref,
    fine_rows_ref,
    dup_coef,
    dup_rows,
    dup_fine,
    dup_fine_rows,
    *,
    early,
):
    px = coef_ref.shape[0]
    pairs = send_ref.shape[1] // 2
    rows_ref[...] = split_rows(points_ref[...])
    fine_rows_ref[...] = split_rows(points_fine_ref[...])
    double_fine(coef_ref, fine_rows_ref, dup_fine, dup_fine_rows)

    def one_tile(index, carry):
        doubled = []
        for part in range(2):
            q = 2 * index + part
            a, b = halves(transfer_ref[:, lane_tile(q)].astype(jnp.float32))
            matrix = jnp.concatenate([a, b], axis=0).astype(jnp.bfloat16)
            block = bdot(coef_ref[:, lane_tile(q)], matrix, NN).astype(jnp.bfloat16)
            dup_coef[q] = block
            doubled.append(block)
        lane = lax.broadcasted_iota(jnp.int32, (px, LANES), 1) < LANES // 2
        coarse_ref[:, lane_tile(index)] = jnp.where(lane, doubled[0], doubled[1])
        a, b = halves(rows_ref[:, lane_tile(index)])
        dup_rows[2 * index] = a
        dup_rows[2 * index + 1] = b
        return carry

    lax.fori_loop(0, coef_ref.shape[1] // (2 * LANES), one_tile, 0, unroll=8)
    pack_send(send_ref, out_ref, dup_coef, dup_rows, px, range(pairs), entry_first=True)
    pack_send(send_fine_ref, out_ref, dup_fine, dup_fine_rows, px, range(early), base=sent_rows(pairs, px))


def turned(rows):
    row = lax.broadcasted_iota(jnp.int32, (LANES, LANES), 0)
    column = lax.broadcasted_iota(jnp.int32, (LANES, LANES), 1)
    unit = jnp.where(row == column, 1.0, 0.0).astype(jnp.bfloat16)
    return bdot(unit, rows, NT).astype(jnp.bfloat16)


def put_pair(entry, coef, rows, coef_table, feature_table):
    a, b = halves(coef.astype(jnp.float32))
    coef_table[entry] = a.astype(jnp.bfloat16)
    coef_table[entry + 1] = b.astype(jnp.bfloat16)
    features = turned(jnp.concatenate([source_features(rows).astype(jnp.bfloat16)] * QUAD, axis=0))
    feature_table[entry] = features[:64]
    feature_table[entry + 1] = features[64:]


def put_nothing(entry, coef_table, feature_table):
    coef_table[entry] = jnp.zeros(coef_table.shape[1:], jnp.bfloat16)
    place = lax.broadcasted_iota(jnp.int32, (8, LANES), 0)
    nothing = source_features(jnp.where(place == 3, FAR_AWAY, 0.0)).astype(jnp.bfloat16)
    feature_table[entry] = turned(jnp.concatenate([nothing] * QUAD, axis=0))[:64]


def build_own(coef_ref, rows_ref, coef_table, feature_table):
    tiles = coef_ref.shape[1] // LANES

    def one_tile(index, carry):
        tile = lane_tile(index)
        put_pair(2 * index, coef_ref[:, tile], rows_ref[:, tile], coef_table, feature_table)
        return carry

    lax.fori_loop(0, tiles, one_tile, 0, unroll=16)
    put_nothing(2 * tiles, coef_table, feature_table)


def build_received(recv_ref, base, pairs, coef_table, feature_table):
    owners = recv_ref.shape[0]
    px = coef_table.shape[1]
    points = base + pairs * px

    def one_owner(owner, carry):
        for pair in range(0, pairs, 2):
            start = points + pair * 8
            both = recv_ref[owner, start:start + 16, :].astype(jnp.float32)
            for part in range(min(2, pairs - pair)):
                where = pair + part
                start = base + where * px
                put_pair(
                    owner * (2 * pairs) + 2 * where,
                    recv_ref[owner, start:start + px, :],
                    both[8 * part:8 * part + 8],
                    coef_table,
                    feature_table,
                )
        return carry

    lax.fori_loop(0, owners, one_owner, 0, unroll=8 if pairs <= 4 else 4)
    put_nothing(owners * pairs * 2, coef_table, feature_table)


def build_targets(rows_ref, target_table):
    def one_tile(index, carry):
        a, b = halves(target_features(rows_ref[:, lane_tile(index)]))
        target_table[2 * index] = a.astype(jnp.bfloat16)
        target_table[2 * index + 1] = b.astype(jnp.bfloat16)
        return carry

    lax.fori_loop(0, rows_ref.shape[1] // LANES, one_tile, 0, unroll=16)


def sweep(list_ref, units_ref, first, coef_table, feature_table, target_table, first_buffer, second_buffer, acc):
    px = coef_table.shape[1]
    lane = lax.broadcasted_iota(jnp.int32, (64, 16 * QUAD), 1) // 16
    lane_t = lax.broadcasted_iota(jnp.int32, (16, LANES), 1) // 64
    lane_x = lax.broadcasted_iota(jnp.int32, (px, LANES), 1) < 64
    blank = jnp.zeros((16, LANES), jnp.bfloat16)
    acc[...] = jnp.zeros_like(acc)

    def partners(unit):
        row, column = unit
        return [list_ref[row + m, column] for m in range(CHUNK)]

    def units_of(place):
        codes = [units_ref[place >> 7, (place & (LANES - 1)) + u] for u in range(UNITS)]
        return [(code >> 7, code & (LANES - 1)) for code in codes]

    def tiles(units, buffer):
        for start in range(0, UNITS, QUAD):
            quad = units[start:start + QUAD]
            weights = []
            for u in range(QUAD):
                own = jnp.where(lane_t == u % 2, target_table[quad[u][1] - first], blank)
                weights.append(jnp.concatenate([own if v == u // 2 else blank for v in range(QUAD // 2)], axis=1))
            weights = jnp.concatenate(weights, axis=0)
            ids = [partners(unit) for unit in quad]
            for part in range(0, CHUNK, CHUNK):
                rows = []
                for m in range(part, part + CHUNK):
                    tile = feature_table[ids[0][m]]
                    for u in range(1, QUAD):
                        tile = jnp.where(lane == u, feature_table[ids[u][m]], tile)
                    rows.append(tile)
                power = bdot(jnp.concatenate(rows, axis=0), weights, NN)
                buffer[start // QUAD, part * 64:(part + CHUNK) * 64] = jnp.exp2(power).astype(jnp.bfloat16)

    def products(units, buffer):
        for start in range(0, UNITS, QUAD):
            quad = units[start:start + QUAD]
            coefs = []
            for unit in quad:
                ids = partners(unit)
                coefs.append(
                    jnp.concatenate(
                        [
                            jnp.where(lane_x, coef_table[ids[m]], coef_table[ids[m + 1]])
                            for m in range(0, CHUNK, 2)
                        ],
                        axis=1,
                    )
                )
            product = bdot(jnp.concatenate(coefs, axis=0), buffer[start // QUAD], NN)
            for u in range(QUAD):
                side = (u // 2) * LANES
                acc[u % 2, quad[u][1] - first] += product[u * px:(u + 1) * px, side:side + LANES]

    def two_sets(index, carry):
        here = index * (2 * UNITS)
        second = units_of(here + UNITS)
        tiles(second, second_buffer)
        products(units_of(here), first_buffer)
        tiles(units_of(here + 2 * UNITS), first_buffer)
        products(second, second_buffer)
        return carry

    total = units_ref[units_ref.shape[0] - 1, LANES - 1]
    sets = (total + UNITS - 1) // UNITS
    bodies = (sets - 1) // 2
    last = bodies * (2 * UNITS)
    tiles(units_of(0), first_buffer)
    lax.fori_loop(0, bodies, two_sets, 0)

    @pl.when(sets == 2 * bodies + 2)
    def _():
        second = units_of(last + UNITS)
        tiles(second, second_buffer)
        products(units_of(last), first_buffer)
        products(second, second_buffer)

    @pl.when(sets == 2 * bodies + 1)
    def _():
        products(units_of(last), first_buffer)


def summed(acc, target):
    low = lax.broadcasted_iota(jnp.int32, acc.shape[2:], 1) < 64
    here = jnp.where(low, acc[0, target], acc[1, target])
    return here + pltpu.roll(here, 64, 1)


def put_sums(acc, clusters, out_ref, before_ref=None):
    low = lax.broadcasted_iota(jnp.int32, acc.shape[2:], 1) < 64

    def one_tile(index, carry):
        tile = lane_tile(index)
        sums = jnp.where(low, summed(acc, 2 * index), summed(acc, 2 * index + 1))
        out_ref[:, tile] = sums if before_ref is None else before_ref[:, tile] + sums
        return carry

    lax.fori_loop(0, clusters // 2, one_tile, 0, unroll=8)


def prepare_kernel(
    send_ref,
    fine_slots_ref,
    fine_counts_ref,
    coarse_slots_ref,
    coarse_counts_ref,
    coef_ref,
    fine_rows_ref,
    coarse_coef_ref,
    coarse_rows_ref,
    send_out_ref,
    list_out_ref,
    early_units_ref,
    coarse_units_ref,
    fine_units_ref,
    fine_out_ref,
    coarse_out_ref,
    dup_coef,
    dup_rows,
    fine_own_ref,
    coarse_own_ref,
    list_ref,
    fine_own_units,
    coarse_own_units,
    list_sem,
    fine_sem,
    coarse_sem,
    *scratch,
    owners,
    caps,
    splits,
):
    list_slots(
        fine_slots_ref,
        fine_counts_ref,
        coarse_slots_ref,
        coarse_counts_ref,
        list_out_ref,
        fine_own_ref,
        coarse_own_ref,
        early_units_ref,
        coarse_units_ref,
        fine_units_ref,
        owners=owners,
        caps=caps,
        splits=splits,
    )
    copies = [
        pltpu.make_async_copy(list_out_ref, list_ref, list_sem),
        pltpu.make_async_copy(fine_own_ref, fine_own_units, fine_sem),
        pltpu.make_async_copy(coarse_own_ref, coarse_own_units, coarse_sem),
    ]
    for copy in copies:
        copy.start()
    double_fine(coef_ref, fine_rows_ref, dup_coef, dup_rows)
    pack_send(
        send_ref, send_out_ref, dup_coef, dup_rows, coef_ref.shape[0], range(splits[0] // 2, caps[0] // 2)
    )
    for copy in copies:
        copy.wait()
    first = 0
    for units_ref, source_ref, rows_ref, out_ref in (
        (fine_own_units, coef_ref, fine_rows_ref, fine_out_ref),
        (coarse_own_units, coarse_coef_ref, coarse_rows_ref, coarse_out_ref),
    ):
        clusters = rows_ref.shape[1] // 64
        build_own(source_ref, rows_ref, *scratch[:2])
        build_targets(rows_ref, scratch[2])
        sweep(list_ref, units_ref, first, *scratch)
        put_sums(scratch[-1], clusters, out_ref)
        first += clusters


def first_kernel(
    list_ref,
    early_units_ref,
    units_ref,
    recv_ref,
    fine_rows_ref,
    rows_ref,
    fine_own_ref,
    own_ref,
    fine_out_ref,
    out_ref,
    *scratch,
    pairs,
    early,
):
    px = own_ref.shape[0]
    fine = fine_rows_ref.shape[1] // 64
    build_received(recv_ref, 0, pairs, *scratch[:2])
    build_targets(rows_ref, scratch[2])
    sweep(list_ref, units_ref, fine, *scratch)
    put_sums(scratch[-1], rows_ref.shape[1] // 64, out_ref, own_ref)
    build_received(recv_ref, sent_rows(pairs, px), early, *scratch[:2])
    build_targets(fine_rows_ref, scratch[2])
    sweep(list_ref, early_units_ref, 0, *scratch)
    put_sums(scratch[-1], fine, fine_out_ref, fine_own_ref)


def fine_kernel(groups, pairs, *refs):
    late = 3 + groups
    list_ref, units_ref, recv_ref, rows_ref = refs[:4]
    out_ref, terms_ref = refs[4 + late:6 + late]
    late_refs = refs[6 + late:6 + 2 * late]
    late_sems = refs[6 + 2 * late:6 + 3 * late]
    gram_ref, split_ref, *scratch = refs[6 + 3 * late:]
    copies = [pltpu.make_async_copy(*pair) for pair in zip(refs[4:4 + late], late_refs, late_sems)]
    for copy in copies:
        copy.start()
    own_ref, coarse_ref, transfer_ref, *probes_refs = late_refs
    px = split_ref.shape[0] // 2
    probes = probes_refs[0].shape[0]
    acc = scratch[-1]
    build_received(recv_ref, 0, pairs, *scratch[:2])
    build_targets(rows_ref, scratch[2])
    sweep(list_ref, units_ref, 0, *scratch)
    for copy in copies:
        copy.wait()
    low_x = lax.broadcasted_iota(jnp.int32, (px, LANES), 1) < 64

    def one_parent(q, carry):
        far = halves(coarse_ref[:, lane_tile(q >> 1)])
        twice = jnp.where((q & 1) == 0, far[0], far[1]).astype(jnp.bfloat16)
        matrix = transfer_ref[:, lane_tile(q)].astype(jnp.float32)
        low = lax.broadcasted_iota(jnp.int32, matrix.shape, 1) < 64
        matrix = jnp.concatenate(
            [jnp.where(low, matrix, 0.0), jnp.where(low, 0.0, matrix)], axis=0
        ).astype(jnp.bfloat16)
        sums = jnp.where(low_x, summed(acc, 2 * q), summed(acc, 2 * q + 1))
        total = own_ref[:, lane_tile(q)] + sums + bdot(twice, matrix, NT)
        out_ref[:, lane_tile(q)] = total
        high = total.astype(jnp.bfloat16)
        split_ref[:px, lane_tile(q)] = high
        split_ref[px:, lane_tile(q)] = (total - high.astype(jnp.float32)).astype(jnp.bfloat16)
        return carry

    lax.fori_loop(0, coarse_ref.shape[1] // 64, one_parent, 0, unroll=8)
    for block, probes_ref in enumerate(probes_refs):
        term = bdot(probes_ref[...], split_ref[...], NT)
        gram_ref[block] = term[:, :px] + term[:, px:]
    place = lax.axis_index("probe")
    for b in range(groups):
        block = gram_ref[lax.rem(place - b + groups, groups)]
        packed = jnp.concatenate([block[i:i + 8, :probes] for i in range(0, probes, 8)], axis=1)

        def one_owner(owner, carry):
            terms_ref[owner * groups + b] = packed
            return carry

        lax.fori_loop(0, terms_ref.shape[0] // groups, one_owner, 0)


def gram_kernel(terms_ref, out_ref, *, groups, scale):
    probes = out_ref.shape[0]
    columns = []
    for b in range(groups):
        total = terms_ref[b]
        for owner in range(1, terms_ref.shape[0] // groups):
            total = total + terms_ref[owner * groups + b]
        columns.append(
            jnp.concatenate([total[:, i * probes:(i + 1) * probes] for i in range(probes // 8)], axis=0)
        )
    out_ref[...] = jnp.concatenate(columns, axis=1) * scale


def sweep_scratch(total, clusters, px):
    return [
        pltpu.VMEM((total + 1, px, LANES), jnp.bfloat16),
        pltpu.VMEM((total + 1, 64, 16 * QUAD), jnp.bfloat16),
        pltpu.VMEM((clusters, 16, LANES), jnp.bfloat16),
        pltpu.VMEM((UNITS // QUAD, CHUNK * 64, QUAD * 64), jnp.bfloat16),
        pltpu.VMEM((UNITS // QUAD, CHUNK * 64, QUAD * 64), jnp.bfloat16),
        pltpu.VMEM((2, clusters, px, LANES), jnp.float32),
    ]


def shards(
    coef_fine,
    points_fine,
    points_coarse,
    transfer,
    send_fine,
    slots_fine,
    counts_fine,
    send_coarse,
    slots_coarse,
    counts_coarse,
):
    probes = coef_fine.shape[0]
    fine_count = counts_fine.shape[0]
    coarse_count = counts_coarse.shape[0]
    owners = lax.axis_size("leaf")
    groups = lax.axis_size("probe")
    px = -(-probes // 16) * 16
    coef = coef_fine if px == probes else jnp.pad(coef_fine, ((0, px - probes), (0, 0)))
    cap_fine = send_fine.shape[2]
    cap_coarse = send_coarse.shape[2]

    whole_vmem = pltpu.CompilerParams(vmem_limit_bytes=VMEM)
    smem = pl.BlockSpec(memory_space=pltpu.SMEM)
    vmem = pl.BlockSpec(memory_space=pltpu.VMEM)
    bf16, f32 = jnp.bfloat16, jnp.float32

    coarse_pairs = cap_coarse // 2
    early_pairs = EARLY * (cap_fine // 2) // 8
    late_pairs = cap_fine // 2 - early_pairs
    early_total = owners * 2 * early_pairs
    late_total = owners * 2 * late_pairs
    coarse_total = owners * cap_coarse
    unit_rows = [-(-(count * (SLOTS // CHUNK) + 2 * UNITS + 1) // LANES) for count in (fine_count, coarse_count)]
    list_shape = (3 * SECTION, LANES)
    i32 = jnp.int32
    fine_units_shape, coarse_units_shape = [(rows, LANES) for rows in unit_rows]
    fine_columns, coarse_columns = points_fine.shape[1], points_coarse.shape[1]
    heavy = pl.CostEstimate(flops=10**10, bytes_accessed=10**7, transcendentals=10**7)

    first_send, coarse_rows, coarse_coef, fine_rows = pl.pallas_call(
        functools.partial(pack_kernel, early=early_pairs),
        out_shape=(
            jax.ShapeDtypeStruct(
                (owners, sent_rows(coarse_pairs, px) + sent_rows(early_pairs, px), LANES), bf16
            ),
            jax.ShapeDtypeStruct((8, coarse_columns), f32),
            jax.ShapeDtypeStruct((px, coarse_columns), bf16),
            jax.ShapeDtypeStruct((8, fine_columns), f32),
        ),
        in_specs=[smem] * 2 + [vmem] * 4,
        out_specs=[vmem] * 4,
        scratch_shapes=[
            pltpu.VMEM((coarse_count, px, LANES), bf16),
            pltpu.VMEM((coarse_count, 8, LANES), f32),
            pltpu.VMEM((fine_count, px, LANES), bf16),
            pltpu.VMEM((fine_count, 8, LANES), f32),
        ],
        compiler_params=whole_vmem,
        name="pack_first",
    )(jnp.swapaxes(send_coarse, 1, 2), send_fine, coef, transfer, points_coarse, points_fine)
    first_recv = lax.all_to_all(first_send, "leaf", split_axis=0, concat_axis=0, tiled=True)

    turned = [coef_fine]
    for step in range(1, groups):
        turned.append(lax.ppermute(coef_fine, "probe", [(i, (i + step) % groups) for i in range(groups)]))

    fine_send, slot_list, early_units, coarse_units, fine_units, fine_own_sums, coarse_own_sums = pl.pallas_call(
        functools.partial(
            prepare_kernel,
            owners=owners,
            caps=(cap_fine, cap_coarse),
            splits=(2 * early_pairs, cap_coarse),
        ),
        out_shape=(
            jax.ShapeDtypeStruct((owners, sent_rows(late_pairs, px), LANES), bf16),
            jax.ShapeDtypeStruct(list_shape, i32),
            jax.ShapeDtypeStruct(fine_units_shape, i32),
            jax.ShapeDtypeStruct(coarse_units_shape, i32),
            jax.ShapeDtypeStruct(fine_units_shape, i32),
            jax.ShapeDtypeStruct((px, fine_columns), f32),
            jax.ShapeDtypeStruct((px, coarse_columns), f32),
        ),
        in_specs=[smem] + [vmem] * 8,
        out_specs=[vmem] * 7,
        scratch_shapes=[
            pltpu.VMEM((fine_count, px, LANES), bf16),
            pltpu.VMEM((fine_count, 8, LANES), f32),
            pltpu.VMEM(fine_units_shape, i32),
            pltpu.VMEM(coarse_units_shape, i32),
            pltpu.SMEM(list_shape, i32),
            pltpu.SMEM(fine_units_shape, i32),
            pltpu.SMEM(coarse_units_shape, i32),
            pltpu.SemaphoreType.DMA,
            pltpu.SemaphoreType.DMA,
            pltpu.SemaphoreType.DMA,
        ]
        + sweep_scratch(fine_count, fine_count, px),
        compiler_params=whole_vmem,
        cost_estimate=heavy,
        name="prepare",
    )(
        send_fine,
        slots_fine,
        counts_fine.reshape(1, -1),
        slots_coarse,
        counts_coarse.reshape(1, -1),
        coef,
        fine_rows,
        coarse_coef,
        coarse_rows,
    )
    fine_recv = lax.all_to_all(fine_send, "leaf", split_axis=0, concat_axis=0, tiled=True)

    fine_sums, coarse_far = pl.pallas_call(
        functools.partial(first_kernel, pairs=coarse_pairs, early=early_pairs),
        out_shape=(
            jax.ShapeDtypeStruct((px, fine_columns), f32),
            jax.ShapeDtypeStruct((px, coarse_columns), f32),
        ),
        in_specs=[smem] * 3 + [vmem] * 5,
        out_specs=[vmem, vmem],
        scratch_shapes=sweep_scratch(max(early_total, coarse_total), fine_count, px),
        compiler_params=whole_vmem,
        cost_estimate=heavy,
        name="first_sweep",
    )(slot_list, early_units, coarse_units, first_recv, fine_rows, coarse_rows, fine_own_sums, coarse_own_sums)

    late = (fine_sums, coarse_far, transfer, *turned)
    term_shape = (owners * groups, 8, probes * probes // 8)
    far, terms = pl.pallas_call(
        functools.partial(fine_kernel, groups, late_pairs),
        out_shape=(
            jax.ShapeDtypeStruct((px, points_fine.shape[1]), f32),
            jax.ShapeDtypeStruct(term_shape, f32),
        ),
        in_specs=[smem] * 2 + [vmem] * 2 + [pl.BlockSpec(memory_space=pl.ANY)] * (3 + groups),
        out_specs=[vmem, vmem],
        scratch_shapes=[pltpu.VMEM(operand.shape, operand.dtype) for operand in late]
        + [pltpu.SemaphoreType.DMA] * len(late)
        + [
            pltpu.VMEM((groups, probes, px), f32),
            pltpu.VMEM((2 * px, points_fine.shape[1]), bf16),
        ]
        + sweep_scratch(late_total, fine_count, px),
        compiler_params=whole_vmem,
        name="fine_sweep",
    )(slot_list, fine_units, fine_recv, fine_rows, *late)

    terms = lax.all_to_all(terms, ("leaf", "probe"), split_axis=0, concat_axis=0, tiled=True)
    probe_gram = pl.pallas_call(
        functools.partial(
            gram_kernel, groups=groups, scale=1.0 / math.sqrt(owners * fine_count * 64)
        ),
        out_shape=jax.ShapeDtypeStruct((probes, groups * probes), f32),
        in_specs=[vmem],
        out_specs=vmem,
        name="gram_sum",
    )(terms)
    return (far[:probes], probe_gram)


def solution(mesh):
    return jax.shard_map(
        shards,
        mesh=mesh,
        in_specs=(
            P("probe", "leaf"),
            P(None, "leaf"),
            P(None, "leaf"),
            P(None, "leaf"),
            P("leaf", None, None),
            P("leaf", None),
            P("leaf"),
            P("leaf", None, None),
            P("leaf", None),
            P("leaf"),
        ),
        out_specs=(P("probe", "leaf"), P("probe", None)),
        check_vma=False,
    )
```
